32 devices in a mesh: dp: 8 (over y, x, core), head: 4 (over z).
Axes of the slice: x: 2, y: 2, z: 4, core: 2. Of those that a mesh axis runs over, the one named last changes fastest.
Arguments:
- text: bfloat16 [16, 2, 492, 768], P('dp', None, 'head'), may hold values from -6 to 6
- boundary: int32 [16, 2, 492], P('dp'), may hold values from 0 to 1, as said below
- reset: int32 [16, 2], P('dp'), may hold values 0 or 1
- memory_in: bfloat16 [16, 10, 768], P('dp'), may hold values from -6 to 6
- init_memory: bfloat16 [10, 768], P(None, ('dp', 'head')), may hold values from -6 to 6
- w_qkv: bfloat16 [768, 3, 768], P(None, None, 'head'), may hold values from -0.21875 to 0.21875
- b_qv: bfloat16 [2, 12, 64], P(None, 'head'), may hold values from -3 to 3
- w_out: bfloat16 [768, 768], P('head'), may hold values from -0.875 to 0.875
- w_in: bfloat16 [768, 3072], P(None, ('dp', 'head')), may hold values from -0.21875 to 0.21875
- w_back: bfloat16 [3072, 768], P(('dp', 'head')), may hold values from -0.109375 to 0.109375
- b_in: bfloat16 [3072], P(('dp', 'head')), may hold values from -3 to 3
- norm_gains: bfloat16 [2, 768], P(None, ('dp', 'head')), may hold values from 0.5 to 1.5
- biases: bfloat16 [4, 768], P(None, ('dp', 'head')), may hold values from -2 to 2
- cotangent: bfloat16 [16, 2, 512, 768], P('dp', None, 'head'), may hold values from -6 to 6
Outputs:
- activations: bfloat16 [16, 2, 512, 768], P('dp', None, 'head')
- d_text: bfloat16 [16, 2, 492, 768], P('dp', None, 'head')
- d_init: float32 [10, 768], P(None, ('dp', 'head'))
- d_w_qkv: float32 [768, 3, 768], P('dp', None, 'head')
- d_b_qv: float32 [2, 12, 64], P(None, 'head', 'dp')
- d_w_out: float32 [768, 768], P('head', 'dp')
- d_w_in: float32 [768, 3072], P(None, ('dp', 'head'))
- d_w_back: float32 [3072, 768], P(('dp', 'head'))
- d_b_in: float32 [3072], P(('dp', 'head'))
- d_norm_gains: float32 [2, 768], P(None, ('dp', 'head'))
- d_biases: float32 [4, 768], P(None, ('dp', 'head'))
The draws below stay inside these ranges and needn't reach their ends.
Inputs may be any that keep to these rules, and one draw needn't show every extreme that they name: `boundary`: in each aligned block of 2 sequences, one is a single document (it has no document start in either segment), as the data loader pairs one long document with one packed sequence.
All inputs are finite; a program needn't handle non-finite values. No bound on the sum of `reset` on one device may be relied on, other than what follows from the above.
Results may differ from the reference program's by a relative error of at most 0.024.
Values may be sent and summed in bfloat16 or wider, within the bound.
A program may use at most 192 MiB of HBM per device.

```python
import jax
import jax.numpy as jnp
from jax import lax

D = 768
NH = 12
HD = 64
FF = 3072
MEM = 10
TEXT = 492
SEQ_DEV = 2
SEQS = 16
SEG = 512


def draw_boundary(key, part):
    key = jax.random.fold_in(key, 7)
    key_marks = jax.random.fold_in(key, 1)
    key_pick = jax.random.fold_in(key, 2)
    marks = (jax.random.randint(key_marks, (SEQS, 2, TEXT), 0, 64) == 0).astype(jnp.int32)
    picked = jax.random.randint(key_pick, (SEQS // SEQ_DEV,), 0, SEQ_DEV)
    clear = jnp.arange(SEQS) % SEQ_DEV == jnp.repeat(picked, SEQ_DEV)
    return jnp.where(clear[:, None, None], 0, marks).astype(jnp.int32)


def with_ends(drawn, key, smallest, high):
    index_at = [jax.random.randint(jax.random.fold_in(key, axis), (), 0, length) for axis, length in enumerate(drawn.shape)]
    longest = drawn.shape.index(max(drawn.shape))
    neighbour = index_at[:longest] + [(index_at[longest] + 1) % drawn.shape[longest]] + index_at[longest + 1:]
    return drawn.at[tuple(index_at)].set(smallest).at[tuple(neighbour)].set(high)


def block_levels(key, extent, pieces, least, top_value):
    def one(axis_at, parts):
        steps = jax.random.uniform(jax.random.fold_in(jax.random.fold_in(key, 6), axis_at), (parts,), jnp.float32, least / len(pieces), top_value / len(pieces))
        return jnp.repeat(jnp.exp(steps), extent[axis_at] // parts).reshape((-1,) + (1,) * (len(extent) - axis_at - 1))

    level = one(*pieces[0])
    for cut in pieces[1:]:
        level = level * one(*cut)
    return level


def centred(stream_key, dims, deviation, bound, cuts=(), kind=jnp.bfloat16):
    gain = block_levels(stream_key, dims, cuts, -0.22, 0.18) if cuts else 1.0
    entries = jax.random.normal(stream_key, dims, jnp.float32) * deviation * gain
    return jnp.minimum(jnp.maximum(entries, -bound), bound).astype(kind)


def setup_inputs(seed: int = 0) -> dict:
    splits = jax.random.split(jax.random.key(seed), 15)
    return {
        "text": centred(splits[0], (SEQS, 2, TEXT, D), 1.0, 6.0, ((0, 8), (2, 4))),
        "boundary": draw_boundary(jax.random.fold_in(splits[14], 71), 0),
        "reset": with_ends((jax.random.randint(splits[2], (SEQS, 2), 0, 2) < 1).astype(jnp.int32), jax.random.fold_in(splits[2], 1), 0, 1),
        "memory_in": centred(splits[3], (SEQS, MEM, D), 1.0, 6.0, ((0, 8),)),
        "init_memory": centred(splits[4], (MEM, D), 1.0, 6.0, ((1, 32),)),
        "w_qkv": centred(splits[5], (D, 3, D), D ** -0.5, 0.21875, ((2, 4),)),
        "b_qv": centred(splits[6], (2, NH, HD), 0.5, 3.0, ((1, 4),)),
        "w_out": centred(splits[7], (D, D), (D // 16) ** -0.5, 0.875, ((0, 4),)),
        "w_in": centred(splits[8], (D, FF), D ** -0.5, 0.21875, ((1, 32),)),
        "w_back": centred(splits[9], (FF, D), FF ** -0.5, 0.109375, ((0, 32),)),
        "b_in": centred(splits[10], (FF,), 0.5, 3.0, ((0, 32),)),
        "norm_gains": jnp.clip(1.0 + 0.1 * jax.random.normal(splits[11], (2, D), jnp.float32), 0.5, 1.5).astype(jnp.bfloat16),
        "biases": centred(splits[12], (4, D), 0.3, 2.0, ((1, 32),)),
        "cotangent": centred(splits[13], (SEQS, 2, SEG, D), 1.0, 6.0, ((0, 8), (2, 4))),
    }


@jax.custom_vjp
def low(v):
    return lax.optimization_barrier(v.astype(jnp.bfloat16)).astype(jnp.float32)

@jax.custom_vjp
def low_back(v):
    return v

def low_keep(v):
    return (low(v), None)

def low_pass(kept, grad):
    return (grad,)

def back_keep(v):
    return (v, None)

def back_low(kept, grad):
    return (low(grad),)
low.defvjp(low_keep, low_pass)
low_back.defvjp(back_keep, back_low)
HIGHEST = lax.Precision.HIGHEST

def layer_norm(values, gain_row, shift_row):
    center = values - lax.optimization_barrier(jnp.mean(values, axis=-1, keepdims=True))
    spread = lax.optimization_barrier(jnp.mean(center * center, axis=-1, keepdims=True))
    return center * lax.rsqrt(spread + 1e-05) * gain_row + shift_row

def segment(rows_in, visible, params):
    init, w_qkv, b_qv, w_out, w_in, w_back, b_in, gains, biases = params
    mixed = jnp.einsum('rd,dce->rce', rows_in, w_qkv, precision=HIGHEST)
    bias_pair = b_qv.reshape(2, D)
    query = low_back(low(mixed[:, 0] + bias_pair[0])).reshape(SEG, NH, HD)
    key_rows = low_back(low(mixed[:, 1])).reshape(SEG, NH, HD)
    value = low_back(low(mixed[:, 2] + bias_pair[1])).reshape(SEG, NH, HD)
    scores = low_back(jnp.einsum('qhe,khe->hqk', query, key_rows, precision=HIGHEST) * 0.125)
    masked = jnp.where(visible[None], scores, -1e+30)
    weights = jax.nn.softmax(masked, axis=-1)
    attended = jnp.einsum('hqk,khe->qhe', low(weights), value, precision=HIGHEST)
    attended = low_back(low(attended)).reshape(SEG, D)
    branch = low_back(jnp.dot(attended, w_out, precision=HIGHEST)) + biases[1]
    hidden = layer_norm(rows_in + branch, gains[0], biases[0])
    inner = low_back(jnp.dot(low(hidden), w_in, precision=HIGHEST) + b_in)
    active = low(jax.nn.gelu(inner, approximate=True))
    outer = low_back(jnp.dot(active, w_back, precision=HIGHEST)) + biases[2]
    return layer_norm(hidden + outer, gains[1], biases[3])

def visibility(bounds):
    doc_ids = jnp.cumsum(bounds, axis=-1).astype(jnp.int32)
    marks = jnp.full((2, MEM), -1, jnp.int32)
    labels = jnp.concatenate([marks, doc_ids, marks], axis=1)
    left = labels[:, :, None]
    right = labels[:, None, :]
    return (left == right) | (left < 0) | (right < 0)

def chain(text_seq, memory_seq, visible, flags, params):
    init = params[0]
    first_mem = jnp.where(flags[0] > 0, init, memory_seq)
    out_one = segment(jnp.concatenate([first_mem, text_seq[0], first_mem], axis=0), visible[0], params)
    second_mem = jnp.where(flags[1] > 0, init, low(out_one[SEG - MEM:]))
    out_two = segment(jnp.concatenate([second_mem, text_seq[1], second_mem], axis=0), visible[1], params)
    return jnp.stack([out_one, out_two])

def reference(text, boundary, reset, memory_in, init_memory, w_qkv, b_qv, w_out, w_in, w_back, b_in, norm_gains, biases, cotangent):
    params = tuple((p.astype(jnp.float32) for p in (init_memory, w_qkv, b_qv, w_out, w_in, w_back, b_in, norm_gains, biases)))

    def one_seq(totals, items):
        text_seq, memory_seq, bounds, flags, grad_seq = items
        visible = visibility(bounds)
        memory_f = memory_seq.astype(jnp.float32)

        def forward(text_f, prm):
            return chain(text_f, memory_f, visible, flags, prm)
        result, pull = jax.vjp(forward, text_seq.astype(jnp.float32), params)
        grad_text, grad_params = pull(grad_seq.astype(jnp.float32))
        totals = jax.tree.map(lambda a, b: a + b, totals, grad_params)
        return (totals, (result.astype(jnp.bfloat16), grad_text.astype(jnp.bfloat16)))
    zeros = jax.tree.map(jnp.zeros_like, params)
    grads, (outputs, grad_texts) = lax.scan(one_seq, zeros, (text, memory_in, boundary, reset, cotangent))
    g_init, g_qkv, g_bqv, g_out, g_in, g_back, g_bin, g_gains, g_biases = grads
    return (outputs, grad_texts, g_init, g_qkv, g_bqv, g_out, g_in, g_back, g_bin, g_gains, g_biases)
```

```python
import functools

import jax
import jax.numpy as jnp
from jax import lax
from jax.experimental import pallas as pl
from jax.experimental.pallas import tpu as pltpu
from jax.sharding import PartitionSpec as P

HD = 64
MESH = pl.DeviceIdType.MESH
BF = jnp.bfloat16
F32 = jnp.float32
VMEM_LIMIT = 64 * 1024 * 1024


def nn(a, b):
    return lax.dot_general(a, b, (((1,), (0,)), ((), ())), preferred_element_type=F32)


def nt(a, b):
    return lax.dot_general(a, b, (((1,), (1,)), ((), ())), preferred_element_type=F32)


def tn(a, b):
    return lax.dot_general(a, b, (((0,), (0,)), ((), ())), preferred_element_type=F32)


def place():
    dp, z = lax.axis_index("dp"), lax.axis_index("head")
    core, plane = dp % 2, dp // 2
    return core, plane % 2, plane // 2, z


def device(core, x, y, z):
    return ((y * 2 + x) * 2 + core, z)


def push(src, dst, send, recv, target):
    return pltpu.make_async_remote_copy(
        src_ref=src, dst_ref=dst, send_sem=send, recv_sem=recv, device_id=target, device_id_type=MESH
    )


def greet(targets):
    barrier = pltpu.get_barrier_semaphore()
    for target in targets:
        pl.semaphore_signal(barrier, inc=1, device_id=target, device_id_type=MESH)
    pl.semaphore_wait(barrier, len(targets))


def from_root(x, axis, root):
    mine = lax.axis_index(axis) == root
    return lax.psum(jnp.where(mine, x, jnp.zeros_like(x)), axis)


def layer_norm(values, gain_row, shift_row):
    center = values - jnp.mean(values, axis=-1, keepdims=True)
    spread = jnp.mean(center * center, axis=-1, keepdims=True)
    return center * lax.rsqrt(spread + 1e-05) * gain_row + shift_row


def gelu_tanh(values):
    return jax.nn.gelu(values, approximate=True)


def head_major(array, dim, dp_count, head_count):
    shape = array.shape
    size = shape[dim]
    split = array.reshape(
        shape[:dim] + (dp_count, head_count, size // (dp_count * head_count)) + shape[dim + 1 :]
    )
    return jnp.swapaxes(split, dim, dim + 1).reshape(shape)


def local(
    text,
    boundary,
    reset,
    memory_in,
    init_memory,
    w_qkv,
    b_qv,
    w_out,
    w_in,
    w_back,
    b_in,
    norm_gains,
    biases,
    cotangent,
):
    head_count = lax.axis_size("head")
    dp_count = lax.axis_size("dp")
    head_idx = lax.axis_index("head")
    batch_size = text.shape[0]
    width = text.shape[3]
    seg_rows = cotangent.shape[2]
    seg_len = seg_rows * head_count
    mem_rows = memory_in.shape[1]
    text_len = seg_len - 2 * mem_rows
    local_width = w_qkv.shape[2]
    local_heads = local_width // HD
    row_start = head_idx * seg_rows
    is_first = (head_idx == 0).astype(jnp.float32)
    is_final = (head_idx == head_count - 1).astype(jnp.float32)
    grad_dims = (1, 0, 0, 1, 1, 1)
    doc_ids = jnp.cumsum(boundary, axis=2)
    marks = jnp.full((batch_size, 2, mem_rows), -1, jnp.int32)
    labels = jnp.concatenate([marks, doc_ids, marks], axis=2)
    visible = (
        (labels[..., :, None] == labels[..., None, :])
        | (labels[..., :, None] < 0)
        | (labels[..., None, :] < 0)
    )
    bias_query = b_qv[0].reshape(local_width).astype(jnp.float32)
    bias_value = b_qv[1].reshape(local_width).astype(jnp.float32)
    shared = (
        lax.all_gather(w_in, ("dp", "head"), axis=1, tiled=True),
        lax.all_gather(w_back, ("dp", "head"), axis=0, tiled=True),
        lax.all_gather(b_in, ("dp", "head"), axis=0, tiled=True),
        lax.all_gather(norm_gains, ("dp", "head"), axis=1, tiled=True),
        lax.all_gather(biases, ("dp", "head"), axis=1, tiled=True),
        lax.all_gather(init_memory, ("dp", "head"), axis=1, tiled=True),
    )

    def fetch():
        return shared

    def attention_probs(query, key_rows, seg):
        scores = (
            jnp.einsum("sqhe,skhe->shqk", query, key_rows, preferred_element_type=jnp.float32)
            * 0.125
        )
        return jnp.where(visible[:, seg][:, None], scores, -1e30)

    def forward(seg, memory, ffn):
        w_in_all, w_back_all, b_in_all, gains_all, biases_all, unused = ffn
        gains_f = gains_all.astype(jnp.float32)
        biases_f = biases_all.astype(jnp.float32)
        local_text = lax.all_gather(text[:, seg], "head", axis=1, tiled=True)
        x_rows = jnp.concatenate([memory, local_text, memory], axis=1)
        mixed = jnp.einsum("srd,dce->srce", x_rows, w_qkv, preferred_element_type=jnp.float32)
        query = (
            (mixed[:, :, 0] + bias_query)
            .astype(jnp.bfloat16)
            .reshape(batch_size, seg_len, local_heads, HD)
        )
        key_rows = mixed[:, :, 1].astype(jnp.bfloat16).reshape(batch_size, seg_len, local_heads, HD)
        value = (
            (mixed[:, :, 2] + bias_value)
            .astype(jnp.bfloat16)
            .reshape(batch_size, seg_len, local_heads, HD)
        )
        masked = attention_probs(query, key_rows, seg)
        row_max = jnp.max(masked, axis=-1, keepdims=True)
        exp_terms = jnp.exp(masked - row_max)
        row_total = jnp.sum(exp_terms, axis=-1, keepdims=True)
        log_total = row_max + jnp.log(row_total)
        probs = (exp_terms / row_total).astype(jnp.bfloat16)
        attended = jnp.einsum("shqk,skhe->sqhe", probs, value, preferred_element_type=jnp.float32)
        attended = attended.astype(jnp.bfloat16).reshape(batch_size, seg_len, local_width)
        partial_out = jnp.einsum("srl,ld->srd", attended, w_out, preferred_element_type=jnp.float32)
        summed = lax.psum_scatter(
            partial_out.astype(jnp.bfloat16), "head", scatter_dimension=1, tiled=True
        ).astype(jnp.float32)
        own_rows = lax.dynamic_slice_in_dim(x_rows, row_start, seg_rows, 1).astype(jnp.float32)
        pre_norm = own_rows + summed + biases_f[1]
        hidden = layer_norm(pre_norm, gains_f[0], biases_f[0])
        hidden_low = hidden.astype(jnp.bfloat16)
        inner = jnp.einsum(
            "srd,df->srf", hidden_low, w_in_all, preferred_element_type=jnp.float32
        ) + b_in_all.astype(jnp.float32)
        active = gelu_tanh(inner).astype(jnp.bfloat16)
        outer = (
            jnp.einsum("srf,fd->srd", active, w_back_all, preferred_element_type=jnp.float32)
            + biases_f[2]
        )
        post_norm = hidden + outer
        result = layer_norm(post_norm, gains_f[1], biases_f[3])
        kept = (
            x_rows,
            query,
            key_rows,
            value,
            log_total,
            attended,
            pre_norm,
            hidden_low,
            inner,
            active,
            post_norm,
        )
        return (result, kept)

    def backward(seg, grad_out, kept, ffn):
        (
            x_rows,
            query,
            key_rows,
            value,
            log_total,
            attended,
            pre_norm,
            hidden_low,
            inner,
            active,
            post_norm,
        ) = kept
        w_in_all, w_back_all, b_in_all, gains_all, biases_all, unused = ffn
        gains_f = gains_all.astype(jnp.float32)
        biases_f = biases_all.astype(jnp.float32)
        unused_two, pull_two = jax.vjp(layer_norm, post_norm, gains_f[1], biases_f[3])
        grad_post, grad_gain_two, grad_shift_two = pull_two(grad_out)
        grad_outer = grad_post.astype(jnp.bfloat16)
        grad_ffn_bias = jnp.sum(grad_post, axis=(0, 1))
        grad_w_back = jnp.einsum(
            "srf,srd->fd", active, grad_outer, preferred_element_type=jnp.float32
        )
        grad_active = jnp.einsum(
            "srd,fd->srf", grad_outer, w_back_all, preferred_element_type=jnp.float32
        )
        unused_gelu, pull_gelu = jax.vjp(gelu_tanh, inner)
        grad_inner = pull_gelu(grad_active)[0].astype(jnp.bfloat16)
        grad_b_in = jnp.sum(grad_inner, axis=(0, 1), dtype=jnp.float32)
        grad_w_in = jnp.einsum(
            "srd,srf->df", hidden_low, grad_inner, preferred_element_type=jnp.float32
        )
        grad_hidden = grad_post + jnp.einsum(
            "srf,df->srd", grad_inner, w_in_all, preferred_element_type=jnp.float32
        )
        unused_one, pull_one = jax.vjp(layer_norm, pre_norm, gains_f[0], biases_f[0])
        grad_pre, grad_gain_one, grad_shift_one = pull_one(grad_hidden)
        grad_out_bias = jnp.sum(grad_pre, axis=(0, 1))
        grad_branch = lax.all_gather(grad_pre.astype(jnp.bfloat16), "head", axis=1, tiled=True)
        grad_w_out = jnp.einsum(
            "srl,srd->ld", attended, grad_branch, preferred_element_type=jnp.float32
        )
        grad_att = jnp.einsum("srd,ld->srl", grad_branch, w_out, preferred_element_type=jnp.float32)
        grad_att = grad_att.astype(jnp.bfloat16).reshape(batch_size, seg_len, local_heads, HD)
        masked = attention_probs(query, key_rows, seg)
        probs = jnp.exp(masked - log_total)
        grad_value = jnp.einsum(
            "shqk,sqhe->skhe",
            probs.astype(jnp.bfloat16),
            grad_att,
            preferred_element_type=jnp.float32,
        )
        grad_probs = jnp.einsum(
            "sqhe,skhe->shqk", grad_att, value, preferred_element_type=jnp.float32
        )
        grad_scores = probs * (grad_probs - jnp.sum(grad_probs * probs, axis=-1, keepdims=True))
        grad_scores = grad_scores.astype(jnp.bfloat16)
        grad_query = (
            jnp.einsum("shqk,skhe->sqhe", grad_scores, key_rows, preferred_element_type=jnp.float32)
            * 0.125
        )
        grad_key = (
            jnp.einsum("shqk,sqhe->skhe", grad_scores, query, preferred_element_type=jnp.float32)
            * 0.125
        )
        grad_mixed = jnp.stack([grad_query, grad_key, grad_value], axis=2).astype(jnp.bfloat16)
        grad_mixed = grad_mixed.reshape(batch_size, seg_len, 3, local_width)
        grad_bias_qv = jnp.stack(
            [
                jnp.sum(grad_mixed[:, :, 0], axis=(0, 1), dtype=jnp.float32),
                jnp.sum(grad_mixed[:, :, 2], axis=(0, 1), dtype=jnp.float32),
            ]
        ).reshape(2, local_heads, HD)
        grad_w_qkv = jnp.einsum(
            "srd,srce->dce", x_rows, grad_mixed, preferred_element_type=jnp.float32
        )
        grad_rows = jnp.einsum(
            "srce,dce->srd", grad_mixed, w_qkv, preferred_element_type=jnp.float32
        )
        placed = lax.dynamic_update_slice_in_dim(jnp.zeros_like(grad_rows), grad_pre, row_start, 1)
        grad_rows = grad_rows + placed
        grad_text_part = lax.psum_scatter(
            grad_rows[:, mem_rows : mem_rows + text_len].astype(jnp.bfloat16),
            "head",
            scatter_dimension=1,
            tiled=True,
        ).astype(jnp.float32)
        grad_memory = lax.psum(
            (grad_rows[:, :mem_rows] + grad_rows[:, seg_len - mem_rows :]).astype(jnp.bfloat16),
            "head",
        ).astype(jnp.float32)
        reset_flag = reset[:, seg] > 0
        grad_init = (
            jnp.sum(jnp.where(reset_flag[:, None, None], grad_memory, 0.0), axis=0) * is_first
        )
        ffn_grads = (
            grad_w_in,
            grad_w_back,
            grad_b_in,
            jnp.stack([grad_gain_one, grad_gain_two]),
            jnp.stack([grad_shift_one, grad_out_bias, grad_ffn_bias, grad_shift_two]),
            grad_init,
        )
        return (grad_text_part, grad_memory, (grad_w_qkv, grad_bias_qv, grad_w_out), ffn_grads)

    ffn_first = fetch()
    init_all = ffn_first[5]
    memory_one = jnp.where(reset[:, 0, None, None] > 0, init_all[None], memory_in)
    out_one, kept_one = forward(0, memory_one, ffn_first)
    tail_rows = out_one[:, seg_rows - mem_rows :].astype(jnp.bfloat16)
    carried = from_root(tail_rows, "head", head_count - 1)
    ffn_second = fetch()
    memory_two = jnp.where(reset[:, 1, None, None] > 0, ffn_second[5][None], carried)
    out_two, kept_two = forward(1, memory_two, ffn_second)
    activations = jnp.stack([out_one, out_two], axis=1).astype(jnp.bfloat16)
    ffn_third = fetch()
    text_two, memory_grad_two, attn_two, ffn_two = backward(
        1, cotangent[:, 1].astype(jnp.float32), kept_two, ffn_third
    )
    keep_flag = reset[:, 1, None, None] <= 0
    carried_grad = jnp.where(keep_flag, memory_grad_two, 0.0) * is_final
    grad_one = cotangent[:, 0].astype(jnp.float32) + jnp.concatenate(
        [jnp.zeros((batch_size, seg_rows - mem_rows, width), jnp.float32), carried_grad], axis=1
    )
    ffn_fourth = fetch()
    text_one, memory_grad_one, attn_one, ffn_one = backward(0, grad_one, kept_one, ffn_fourth)
    grads = jax.tree.map(lambda a, b: a + b, ffn_one, ffn_two)
    ffn_total = tuple((head_major(g, d, dp_count, head_count) for g, d in zip(grads, grad_dims)))
    partial_sums = (
        lax.psum_scatter(
            ffn_total[0].astype(jnp.bfloat16), "head", scatter_dimension=1, tiled=True
        ).astype(jnp.float32),
        lax.psum_scatter(
            ffn_total[1].astype(jnp.bfloat16), "head", scatter_dimension=0, tiled=True
        ).astype(jnp.float32),
        lax.psum_scatter(
            ffn_total[2].astype(jnp.bfloat16), "head", scatter_dimension=0, tiled=True
        ).astype(jnp.float32),
        lax.psum_scatter(
            ffn_total[3].astype(jnp.bfloat16), "head", scatter_dimension=1, tiled=True
        ).astype(jnp.float32),
        lax.psum_scatter(
            ffn_total[4].astype(jnp.bfloat16), "head", scatter_dimension=1, tiled=True
        ).astype(jnp.float32),
        lax.psum_scatter(
            ffn_total[5].astype(jnp.bfloat16), "head", scatter_dimension=1, tiled=True
        ).astype(jnp.float32),
    )
    reduced = (
        lax.psum_scatter(partial_sums[0], "dp", scatter_dimension=1, tiled=True),
        lax.psum_scatter(partial_sums[1], "dp", scatter_dimension=0, tiled=True),
        lax.psum_scatter(partial_sums[2], "dp", scatter_dimension=0, tiled=True),
        lax.psum_scatter(partial_sums[3], "dp", scatter_dimension=1, tiled=True),
        lax.psum_scatter(partial_sums[4], "dp", scatter_dimension=1, tiled=True),
        lax.psum_scatter(partial_sums[5], "dp", scatter_dimension=1, tiled=True),
    )
    attn_total = jax.tree.map(lambda a, b: a + b, attn_one, attn_two)
    grad_qkv, grad_bqv, grad_wout = (
        lax.psum_scatter(attn_total[0], "dp", scatter_dimension=0, tiled=True),
        lax.psum_scatter(attn_total[1], "dp", scatter_dimension=2, tiled=True),
        lax.psum_scatter(attn_total[2], "dp", scatter_dimension=1, tiled=True),
    )
    grad_text = jnp.stack([text_one, text_two], axis=1).astype(jnp.bfloat16)
    grad_win, grad_wback, grad_bin, grad_gains, grad_biases, grad_init = reduced
    return (
        activations,
        grad_text,
        grad_init,
        grad_qkv,
        grad_bqv,
        grad_wout,
        grad_win,
        grad_wback,
        grad_bin,
        grad_gains,
        grad_biases,
    )


def layer_kernel(
    mem_rows,
    rows_ref, wa, wf, lab_row, lab_col, par, bqv, bin_ref, mem_a, mem_b, init_a, init_b, flags,
    y_out, dt_out, ffg_out, agq_out, ago_out, sg_out, dinit_out, dbin_out, dbqv_out,
    x, qkv, pt, ot, mask, hf, acc, xh1, rs1, hb, u, gp, xh2, rs2, gf, gz, ga, got, gq,
    send_buf, recv_buf, cur_a, cur_b, carry, stage, send_sem, recv_sem, stage_sem,
):
    core, px, py, z = place()
    sibling = device(1 - core, px, py, z)
    greet([sibling])
    seg_len, width = x.shape[1], x.shape[2]
    hidden = u.shape[2]
    heads = pt.shape[1]
    local = ot.shape[2]
    per_block = local // HD
    step = 128
    row_steps = seg_len // step
    hid = 256
    hid_steps = hidden // hid
    text_rows = (seg_len - 2 * mem_rows) // row_steps
    tail = 16

    def rows(r):
        return pl.ds(pl.multiple_of(r * step, step), step)

    def cols(i):
        return pl.ds(pl.multiple_of(i * hid, hid), hid)

    def head_rows(h, part):
        return pl.ds(pl.multiple_of((h % per_block) * HD + part * local, HD), HD)

    def exchange(slot, r):
        return push(
            send_buf.at[slot, r], recv_buf.at[slot, r], send_sem.at[slot, r], recv_sem.at[slot, r], sibling
        )

    def place_rows(start, count):
        nat = lax.broadcasted_iota(jnp.int32, (count, seg_len), 0) + start
        pad = lax.broadcasted_iota(jnp.int32, (count, seg_len), 1)
        inside = pad & (step - 1)
        target = (pad >> 7) * text_rows + inside + mem_rows
        return jnp.where((nat == target) & (inside < text_rows), 1.0, 0.0).astype(BF)

    def take_rows(r):
        inside = lax.broadcasted_iota(jnp.int32, (step, seg_len), 0)
        nat = lax.broadcasted_iota(jnp.int32, (step, seg_len), 1)
        target = r * text_rows + inside + mem_rows
        return jnp.where((nat == target) & (inside < text_rows), 1.0, 0.0).astype(BF)

    def loop(count, body):
        def run(i, unused):
            body(i)
            return unused

        lax.fori_loop(0, count, run, 0)

    sg_out[...] = jnp.zeros_like(sg_out)
    dinit_out[...] = jnp.zeros_like(dinit_out)
    dbin_out[...] = jnp.zeros_like(dbin_out)
    dbqv_out[...] = jnp.zeros_like(dbqv_out)
    carry[...] = jnp.zeros_like(carry)
    cur_a[...] = mem_a[...]
    cur_b[...] = mem_b[...]
    tail_row = lax.broadcasted_iota(jnp.int32, (tail, width), 0)
    is_mem = tail_row >= tail - mem_rows

    def forward(seg):
        def build(r):
            x[seg, rows(r), :] = nn(place_rows(r * step, step), rows_ref[seg]).astype(BF)

        loop(row_steps, build)
        x[seg, 0:tail, :] = x[seg, 0:tail, :] + cur_a[...]
        x[seg, seg_len - tail : seg_len, :] = x[seg, seg_len - tail : seg_len, :] + cur_b[...]
        left, right = lab_col[seg], lab_row[seg]
        mask[...] = jnp.where((left == right) | (left < 0) | (right < 0), 0.0, -1e30)

        def project(i):
            j, t = i // 3, i % 3
            at = pl.ds(pl.multiple_of(t * local, local), local)
            value = nt(wa[j, at, :], x[seg]) + bqv[j, at, :]
            qkv[seg, j, at, :] = (value * jnp.where(t == 0, 0.125, 1.0)).astype(BF)

        loop(6, project)

        def attend(h):
            j = h // per_block
            q, k, v = (qkv[seg, j, head_rows(h, part), :] for part in range(3))
            s = tn(k, q) + mask[...]
            e = jnp.exp(s - jnp.max(s, axis=0, keepdims=True))
            p = (e * (1.0 / jnp.sum(e, axis=0, keepdims=True))).astype(BF)
            pt[seg, h] = p
            ot[seg, j, head_rows(h, 0), :] = nn(v, p).astype(BF)

        loop(heads, attend)

        def out_proj(r):
            part = tn(ot[seg, 0, :, rows(r)], wa[0, 3 * local :, :]) + tn(
                ot[seg, 1, :, rows(r)], wa[1, 3 * local :, :]
            )
            acc[rows(r), :] = part
            send_buf[0, r] = part.astype(BF)
            exchange(0, r).start()

        loop(row_steps, out_proj)

        def norm(v):
            center = v - jnp.mean(v, axis=-1, keepdims=True)
            scale = lax.rsqrt(jnp.mean(center * center, axis=-1, keepdims=True) + 1e-05)
            return center * scale, scale

        def norm_one(r):
            exchange(0, r).wait()
            h0 = (
                x[seg, rows(r), :].astype(F32)
                + acc[rows(r), :]
                + recv_buf[0, r].astype(F32)
                + par[3:4, :]
            )
            hat, scale = norm(h0)
            xh1[seg, rows(r), :] = hat.astype(BF)
            rs1[seg, rows(r), :] = scale
            h = hat * par[0:1, :] + par[2:3, :]
            hf[rows(r), :] = h
            hb[seg, rows(r), :] = h.astype(BF)

        loop(row_steps, norm_one)

        def inner(i):
            v = nt(hb[seg], wf[0, cols(i), :]) + bin_ref[:, cols(i)]
            c0 = 0.7978845608028654
            sq = v * v
            th = jnp.tanh(v * (c0 + (c0 * 0.044715) * sq))
            half = 0.5 + 0.5 * th
            u[seg, :, cols(i)] = (v * half).astype(BF)
            slope = half + (0.5 * v) * (1.0 - th * th) * (c0 + (3 * c0 * 0.044715) * sq)
            gp[seg, :, cols(i)] = slope.astype(BF)

        loop(hid_steps, inner)

        def outer(r):
            part = nn(u[seg, rows(r), :], wf[1])
            acc[rows(r), :] = part
            send_buf[1, r] = part.astype(BF)
            exchange(1, r).start()

        loop(row_steps, outer)

        def norm_two(r):
            exchange(1, r).wait()
            post = hf[rows(r), :] + acc[rows(r), :] + recv_buf[1, r].astype(F32) + par[4:5, :]
            hat, scale = norm(post)
            xh2[seg, rows(r), :] = hat.astype(BF)
            rs2[seg, rows(r), :] = scale
            y_out[seg, rows(r), :] = (hat * par[1:2, :] + par[5:6, :]).astype(BF)

        loop(row_steps, norm_two)
        last = y_out[seg, seg_len - tail : seg_len, :].astype(F32)
        chosen = jnp.where(flags[1:2, :] > 0, init_b[...].astype(F32), last)
        memory = jnp.where(is_mem, chosen, 0.0)
        cur_b[...] = memory.astype(BF)
        cur_a[...] = pltpu.roll(memory, mem_rows, 0).astype(BF)

    def backward(seg):
        def pull_two(r):
            g_y = rows_ref[2 + seg, rows(r), :].astype(F32) + jnp.where(r == row_steps - 1, carry[...], 0.0)
            hat = xh2[seg, rows(r), :].astype(F32)
            g = g_y * par[1:2, :]
            m1 = jnp.mean(g, axis=-1, keepdims=True)
            m2 = jnp.mean(g * hat, axis=-1, keepdims=True)
            pre = rs2[seg, rows(r), :] * (g - m1 - hat * m2)
            hf[rows(r), :] = pre
            gf[seg, rows(r), :] = pre.astype(BF)
            sg_out[1:2, :] += jnp.sum(g_y * hat, axis=0, keepdims=True)
            sg_out[5:6, :] += jnp.sum(g_y, axis=0, keepdims=True)
            sg_out[4:5, :] += jnp.sum(pre, axis=0, keepdims=True)

        loop(row_steps, pull_two)

        def pull_inner(i):
            g_u = nt(gf[seg], wf[1, cols(i), :])
            g_z = (g_u * gp[seg, :, cols(i)].astype(F32)).astype(BF)
            gz[seg, :, cols(i)] = g_z
            dbin_out[0:1, cols(i)] += jnp.sum(g_z.astype(F32), axis=0, keepdims=True)

        loop(hid_steps, pull_inner)

        def pull_hidden(r):
            part = nn(gz[seg, rows(r), :], wf[0])
            acc[rows(r), :] = part
            send_buf[0, r] = part.astype(BF)
            exchange(0, r).start()

        loop(row_steps, pull_hidden)

        def pull_one(r):
            exchange(0, r).wait()
            g_h = hf[rows(r), :] + acc[rows(r), :] + recv_buf[0, r].astype(F32)
            hat = xh1[seg, rows(r), :].astype(F32)
            g = g_h * par[0:1, :]
            m1 = jnp.mean(g, axis=-1, keepdims=True)
            m2 = jnp.mean(g * hat, axis=-1, keepdims=True)
            pre = rs1[seg, rows(r), :] * (g - m1 - hat * m2)
            hf[rows(r), :] = pre
            ga[seg, rows(r), :] = pre.astype(BF)
            sg_out[0:1, :] += jnp.sum(g_h * hat, axis=0, keepdims=True)
            sg_out[2:3, :] += jnp.sum(g_h, axis=0, keepdims=True)
            sg_out[3:4, :] += jnp.sum(pre, axis=0, keepdims=True)

        loop(row_steps, pull_one)

        def pull_out(j):
            got[j] = nt(wa[j, 3 * local :, :], ga[seg]).astype(BF)

        loop(2, pull_out)

        def pull_head(h):
            j = h // per_block
            q, k, v = (qkv[seg, j, head_rows(h, part), :] for part in range(3))
            g_o = got[j, head_rows(h, 0), :]
            p = pt[seg, h]
            d_v = nt(g_o, p).astype(BF)
            total = jnp.sum(
                g_o.astype(F32) * ot[seg, j, head_rows(h, 0), :].astype(F32), axis=0, keepdims=True
            )
            d_s = (p.astype(F32) * (tn(v, g_o) - total)).astype(BF)
            d_q = (nn(k, d_s) * 0.125).astype(BF)
            d_k = nt(q, d_s).astype(BF)
            for part, value in enumerate((d_q, d_k, d_v)):
                gq[seg, j, head_rows(h, part), :] = value
            for part, value in ((0, d_q), (2, d_v)):
                dbqv_out[j, head_rows(h, part), :] += jnp.sum(value.astype(F32), axis=1, keepdims=True)

        loop(heads, pull_head)

        def pull_rows(r):
            part = tn(gq[seg, 0, :, rows(r)], wa[0, : 3 * local, :]) + tn(
                gq[seg, 1, :, rows(r)], wa[1, : 3 * local, :]
            )
            acc[rows(r), :] = part
            send_buf[1, r] = part.astype(BF)
            exchange(1, r).start()

        loop(row_steps, pull_rows)

        def pull_x(r):
            exchange(1, r).wait()
            total = hf[rows(r), :] + acc[rows(r), :] + recv_buf[1, r].astype(F32)
            acc[rows(r), :] = total
            xh1[seg, rows(r), :] = total.astype(BF)

        loop(row_steps, pull_x)

        def out_text(r):
            dt_out[seg, rows(r), :] = nn(take_rows(r), xh1[seg]).astype(BF)

        loop(row_steps, out_text)
        both = pltpu.roll(acc[0:tail, :], tail - mem_rows, 0) + acc[seg_len - tail : seg_len, :]
        memory = jnp.where(is_mem, both, 0.0)
        flag = jnp.where(seg == 0, flags[0:1, :], flags[1:2, :])
        dinit_out[...] += jnp.where(flag > 0, memory, 0.0)
        carry[step - tail : step, :] = jnp.where(flag > 0, 0.0, memory)

    loop(2, forward)
    loop(2, lambda i: backward(1 - i))

    def stored(kind, i):
        return pltpu.make_async_copy(stage.at[kind], ffg_out.at[kind, cols(i), :], stage_sem.at[kind])

    def ffn_grads(i):
        for kind, (left, right) in enumerate(((gz, hb), (u, gf))):
            value = tn(left[0, :, cols(i)], right[0]) + tn(left[1, :, cols(i)], right[1])

            @pl.when(i > 0)
            def _():
                stored(kind, i - 1).wait()

            stage[kind] = value.astype(BF)
            stored(kind, i).start()

    loop(hid_steps, ffn_grads)
    for kind in range(2):
        stored(kind, hid_steps - 1).wait()

    def attention_grads(i):
        xt = [x[s, :, cols(i)].T for s in range(2)]
        gt = [ga[s, :, cols(i)].T for s in range(2)]
        for j in range(2):
            agq_out[j, cols(i), :] = (nt(xt[0], gq[0, j]) + nt(xt[1], gq[1, j])).astype(BF)
            ago_out[j, cols(i), :] = (nt(gt[0], ot[0, j]) + nt(gt[1], ot[1, j])).astype(BF)

    loop(width // hid, attention_grads)


def start_kernel(
    dp_count, head_count,
    small, seqf, memp, rows, wa, wf,
    small_o, seqf_o, memp_o, rows_o, wa_o, wf_o,
    small_s, small_r, pair_s, pair_r, rows_s, rows_r, fwd_s, fwd_r, att_s, att_r, plane_s, plane_r,
    ffn_s, ffn_r, side_s, side_r, local_sem,
):
    core, px, py, z = place()
    plane = py * 2 + px
    me = (plane * 2 + core) * head_count + z
    total = dp_count * head_count
    sibling = device(1 - core, px, py, z)
    x_mate, y_mate = device(core, 1 - px, py, z), device(core, px, 1 - py, z)
    x_plane, y_plane, far_plane = py * 2 + 1 - px, (1 - py) * 2 + px, (1 - py) * 2 + 1 - px

    def other(i):
        t = (me + 1 + i) % total
        return t, (t // head_count, t % head_count)

    def loop(count, body):
        def run(i, unused):
            body(i)
            return unused

        lax.fori_loop(0, count, run, 0)

    barrier = pltpu.get_barrier_semaphore()
    loop(
        total - 1,
        lambda i: pl.semaphore_signal(barrier, inc=1, device_id=other(i)[1], device_id_type=MESH),
    )
    pl.semaphore_wait(barrier, total - 1)

    locals_ = [
        pltpu.make_async_copy(small, small_o.at[me], local_sem.at[0]),
        pltpu.make_async_copy(wf, wf_o.at[:, plane * head_count + z], local_sem.at[1]),
    ]
    for copy in locals_:
        copy.start()
    own_attention = pltpu.make_async_copy(wa, wa_o.at[z % 2], local_sem.at[2])
    is_home = core == z // 2

    @pl.when(is_home)
    def _():
        own_attention.start()

    share = wa.shape[0] // 4
    half = share // 2
    mine = pl.ds(share * plane + half * core, half)

    def attention_out(i):
        zt = (z + 1 + i) % head_count
        return push(
            wa.at[mine],
            wa_o.at[z % 2, mine],
            att_s.at[i],
            att_r.at[z % 2, core],
            device(z // 2, px, py, zt),
        )

    for i in range(head_count - 1):
        attention_out(i).start()

    piece = rows.shape[2] // 2

    def rows_out(j, h):
        span = pl.ds(h * piece, piece)
        return push(
            rows.at[j, :, span],
            rows_o.at[:, z, span],
            rows_s.at[j, h],
            rows_r.at[z],
            device(h, px, py, 2 * core + j),
        )

    def rows_here(j, h):
        span = pl.ds(h * piece, piece)
        return pltpu.make_async_copy(rows.at[j, :, span], rows_o.at[:, z, span], local_sem.at[3])

    for j in range(2):
        for h in range(2):
            here = (core == h) & (z == 2 * core + j)

            @pl.when(here)
            def _():
                rows_here(j, h).start()

            @pl.when(jnp.logical_not(here))
            def _():
                rows_out(j, h).start()

    def ffn_out(i):
        zt = (z + 1 + i) % head_count
        return push(
            wf,
            wf_o.at[:, plane * head_count + z],
            ffn_s.at[i],
            ffn_r.at[z],
            device(core, px, py, zt),
        )

    for i in range(head_count - 1):
        ffn_out(i).start()

    pair = [
        push(seqf, seqf_o, pair_s.at[0], pair_r.at[0], sibling),
        push(memp, memp_o, pair_s.at[1], pair_r.at[1], sibling),
    ]
    for copy in pair:
        copy.start()

    def small_out(i):
        return push(small, small_o.at[me], small_s.at[i], small_r.at[me], other(i)[1])

    loop(total - 1, lambda i: small_out(i).start())

    def plane_copy(k, which):
        block = pl.ds(share * plane, share)
        if which == 0:
            return push(wa_o.at[k, block], wa_o.at[k, block], plane_s.at[k, 0], plane_r.at[k, 0], x_mate)
        if which == 1:
            return push(wa_o.at[k, block], wa_o.at[k, block], plane_s.at[k, 1], plane_r.at[k, 1], y_mate)
        if which == 2:
            block = pl.ds(share * x_plane, half)
            return push(wa_o.at[k, block], wa_o.at[k, block], plane_s.at[k, 2], plane_r.at[k, 2], y_mate)
        block = pl.ds(share * y_plane + half, half)
        return push(wa_o.at[k, block], wa_o.at[k, block], plane_s.at[k, 3], plane_r.at[k, 3], x_mate)

    foreign = [jnp.logical_not(is_home & (z % 2 == k)) for k in range(2)]

    def arrived(k, h):
        span = pl.ds(share * plane + half * h, half)
        return push(wa.at[mine], wa_o.at[k, span], att_s.at[0], att_r.at[k, h], sibling)

    for k in range(2):

        @pl.when(foreign[k])
        def _():
            for h in range(2):
                arrived(k, h).wait_recv()
            plane_copy(k, 0).start()
            plane_copy(k, 1).start()

    def forward(zs):
        span = pl.ds(core * piece, piece)
        return push(
            rows_o.at[:, zs, span], rows_o.at[:, zs, span], fwd_s.at[zs], fwd_r.at[zs], sibling
        )

    def rows_arrived(zs):
        span = pl.ds(core * piece, piece)
        return push(rows.at[0, :, span], rows_o.at[:, zs, span], rows_s.at[0, 0], rows_r.at[zs], sibling)

    for zs in range(head_count):
        here = is_home & (z == zs)

        @pl.when(here)
        def _():
            rows_here(z % 2, core).wait()

        @pl.when(jnp.logical_not(here))
        def _():
            rows_arrived(zs).wait_recv()

        forward(zs).start()

    def side(kind, zi, first):
        own, x_at, y_at = (p * head_count + zi for p in (plane, x_plane, y_plane))
        if first == 0:
            return push(wf_o.at[kind, own], wf_o.at[kind, own], side_s.at[zi, kind, 0], side_r.at[zi, kind, 0], x_mate)
        if first == 1:
            return push(wf_o.at[kind, own], wf_o.at[kind, own], side_s.at[zi, kind, 1], side_r.at[zi, kind, 1], y_mate)
        if kind == 0:
            return push(wf_o.at[0, x_at], wf_o.at[0, x_at], side_s.at[zi, 0, 2], side_r.at[zi, 0, 2], y_mate)
        return push(wf_o.at[1, y_at], wf_o.at[1, y_at], side_s.at[zi, 1, 2], side_r.at[zi, 1, 2], x_mate)

    def ffn_arrived(zs):
        return push(wf, wf_o.at[:, plane * head_count + zs], ffn_s.at[0], ffn_r.at[zs], sibling)

    for d in range(head_count):
        zi = (z + d) % head_count
        if d == 0:
            locals_[1].wait()
        else:
            ffn_arrived(zi).wait_recv()
        for kind in range(2):
            side(kind, zi, 0).start()
            side(kind, zi, 1).start()

    for k in range(2):

        @pl.when(foreign[k])
        def _():
            plane_copy(k, 0).wait_recv()
            plane_copy(k, 2).start()
            plane_copy(k, 1).wait_recv()
            plane_copy(k, 3).start()

    for d in range(head_count):
        zi = (z + d) % head_count
        side(0, zi, 0).wait_recv()
        side(0, zi, 2).start()
        side(1, zi, 1).wait_recv()
        side(1, zi, 2).start()

    locals_[0].wait()

    @pl.when(is_home)
    def _():
        own_attention.wait()

    for i in range(head_count - 1):
        attention_out(i).wait_send()
        ffn_out(i).wait_send()
    for j in range(2):
        for h in range(2):

            @pl.when(jnp.logical_not((core == h) & (z == 2 * core + j)))
            def _():
                rows_out(j, h).wait_send()

    for copy in pair:
        copy.wait()
    for k in range(2):

        @pl.when(foreign[k])
        def _():
            plane_copy(k, 0).wait_send()
            plane_copy(k, 1).wait_send()
            plane_copy(k, 2).wait()
            plane_copy(k, 3).wait()

    for zs in range(head_count):
        forward(zs).wait_send()
        span = pl.ds((1 - core) * piece, piece)
        push(rows_o.at[:, zs, span], rows_o.at[:, zs, span], fwd_s.at[zs], fwd_r.at[zs], sibling).wait_recv()

    for d in range(head_count):
        zi = (z + d) % head_count
        for kind in range(2):
            side(kind, zi, 0).wait_send()
            side(kind, zi, 1).wait_send()
        side(0, zi, 1).wait_recv()
        side(1, zi, 0).wait_recv()
        for kind in range(2):
            side(kind, zi, 2).wait()

    def small_in(i):
        t = other(i)[0]
        push(small, small_o.at[t], small_s.at[i], small_r.at[t], sibling).wait_recv()

    loop(total - 1, lambda i: small_out(i).wait_send())
    loop(total - 1, small_in)


def finish_kernel(
    dp_count, head_count,
    fa, fb, at, y, dt,
    fa_o, fb_o, at_o, y_o, dt_o,
    fa_b, fb_b, at_b, fa_1, fa_2, fb_1, fb_2, at_1, at_2, fa_z, fb_z, at_z,
    one_s, one_r, two_s, two_r, z_s, z_r, a_s, a_r, out_s, out_r, local_sem,
):
    core, px, py, z = place()
    sibling = device(1 - core, px, py, z)
    x_mate, y_mate = device(core, 1 - px, py, z), device(core, px, 1 - py, z)
    far = [device(h, px, py, (z + 1 + i) % head_count) for h in range(2) for i in range(head_count - 1)]
    greet([sibling, x_mate, y_mate] + far)

    def add(dst, src):
        count = dst.shape[0]

        def run(i, unused):
            dst[i] = (dst[i].astype(F32) + src[i].astype(F32)).astype(BF)
            return unused

        lax.fori_loop(0, count, run, 0)

    piece = y_o.shape[2] // 2
    block = y_o.shape[2]

    def row_copy(which, zt):
        src, dst = ((y, y_o), (dt, dt_o))[which]
        span = pl.ds(core * piece, piece)
        return src.at[:, pl.ds(pl.multiple_of(zt * block + core * piece, piece), piece)], dst.at[z % 2, :, span]

    def row_out(which, i):
        zt = (z + i) % head_count
        src, dst = row_copy(which, zt)
        return push(src, dst, out_s.at[which, i], out_r.at[which, z % 2, core], device(z // 2, px, py, zt))

    def row_here(which):
        src, dst = row_copy(which, z)
        return pltpu.make_async_copy(src, dst, local_sem.at[which])

    is_home = core == z // 2

    def first(name, i):
        if name == 0:
            oy = 1 - py if i == 0 else py
            return push(fa_b.at[oy, 1 - px], fa_1.at[i], one_s.at[0, i], one_r.at[0, i], x_mate)
        if name == 1:
            ox = 1 - px if i == 0 else px
            return push(fb_b.at[1 - py, ox], fb_1.at[i], one_s.at[1, i], one_r.at[1, i], y_mate)
        if name == 2:
            oy = 1 - py if i == 0 else py
            return push(at_b.at[0, oy, 1 - px], at_1.at[0, i], one_s.at[2, i], one_r.at[2, i], x_mate)
        ox = 1 - px if i == 0 else px
        return push(at_b.at[1, 1 - py, ox], at_1.at[1, i], one_s.at[3, i], one_r.at[3, i], y_mate)

    def second(name):
        if name == 0:
            return push(fa_b.at[1 - py, px], fa_2, two_s.at[0], two_r.at[0], y_mate)
        if name == 1:
            return push(fb_b.at[py, 1 - px], fb_2, two_s.at[1], two_r.at[1], x_mate)
        if name == 2:
            return push(at_b.at[0, 1 - py, px], at_2.at[0], two_s.at[2], two_r.at[2], y_mate)
        return push(at_b.at[1, py, 1 - px], at_2.at[1], two_s.at[3], two_r.at[3], x_mate)

    def on_way(name):
        return (fa_b.at[1 - py, px], fb_b.at[py, 1 - px], at_b.at[0, 1 - py, px], at_b.at[1, py, 1 - px])[name]

    def kept(name):
        return (fa_b.at[py, px], fb_b.at[py, px], at_b.at[0, py, px], at_b.at[1, py, px])[name]

    def got_one(name, i):
        return (fa_1.at[i], fb_1.at[i], at_1.at[0, i], at_1.at[1, i])[name]

    def got_two(name):
        return (fa_2, fb_2, at_2.at[0], at_2.at[1])[name]

    loads = [
        pltpu.make_async_copy(fa, fa_b, local_sem.at[3]),
        pltpu.make_async_copy(fb, fb_b, local_sem.at[4]),
        pltpu.make_async_copy(at, at_b, local_sem.at[5]),
    ]
    for copy in loads:
        copy.start()
    names = (0, 1, 2, 3)
    for copy in loads:
        copy.wait()
    for i in range(2):
        for name in names:
            first(name, i).start()

    for which in range(2):
        for i in range(head_count):
            if i == 0:

                @pl.when(is_home)
                def _():
                    row_here(which).start()

                @pl.when(jnp.logical_not(is_home))
                def _():
                    row_out(which, 0).start()

            else:
                row_out(which, i).start()

    for name in names:
        first(name, 0).wait_recv()
        add(on_way(name), got_one(name, 0))
        second(name).start()
    for name in names:
        first(name, 1).wait_recv()
        add(kept(name), got_one(name, 1))

    def z_out(name, i):
        zt = (z + 1 + i) % head_count
        buf, dst = ((fa_b, fa_z), (fb_b, fb_z))[name]
        return push(buf.at[py, px, zt], dst.at[z], z_s.at[name, i], z_r.at[name, z], device(core, px, py, zt))

    def z_in(name, i):
        zs = (z + 1 + i) % head_count
        buf, dst = ((fa_b, fa_z), (fb_b, fb_z))[name]
        return push(buf.at[py, px, z], dst.at[zs], z_s.at[name, i], z_r.at[name, zs], sibling)

    def a_out(k, h):
        return push(
            at_b.at[k, py, px, h], at_z.at[z], a_s.at[k, h], a_r.at[z], device(h, px, py, 2 * core + k)
        )

    def a_here(k):
        return pltpu.make_async_copy(at_b.at[k, py, px, core], at_z.at[z], local_sem.at[2])

    for name in names:
        second(name).wait_recv()
        add(kept(name), got_two(name))
        if name < 2:
            for i in range(head_count - 1):
                z_out(name, i).start()
        else:
            k = name - 2
            for h in range(2):
                here = (core == h) & (z == 2 * core + k)

                @pl.when(here)
                def _():
                    a_here(k).start()

                @pl.when(jnp.logical_not(here))
                def _():
                    a_out(k, h).start()

    for name in range(2):
        for i in range(head_count - 1):
            z_in(name, i).wait_recv()
    for buf, got, out in ((fa_b, fa_z, fa_o), (fb_b, fb_z, fb_o)):
        value = buf[py, px, z].astype(F32)
        for i in range(head_count - 1):
            value = value + got[(z + 1 + i) % head_count].astype(F32)
        out[...] = value
    for zs in range(head_count):
        here = is_home & (z == zs)

        @pl.when(here)
        def _():
            a_here(z % 2).wait()

        @pl.when(jnp.logical_not(here))
        def _():
            push(at_b.at[0, 0, 0, 0], at_z.at[zs], a_s.at[0, 0], a_r.at[zs], sibling).wait_recv()

    value = at_z[0].astype(F32)
    for zs in range(1, head_count):
        value = value + at_z[zs].astype(F32)
    at_o[...] = value

    for name in names:
        for i in range(2):
            first(name, i).wait_send()
        second(name).wait_send()
    for name in range(2):
        for i in range(head_count - 1):
            z_out(name, i).wait_send()
    for k in range(2):
        for h in range(2):

            @pl.when(jnp.logical_not((core == h) & (z == 2 * core + k)))
            def _():
                a_out(k, h).wait_send()

    for which in range(2):
        for i in range(head_count):
            if i == 0:

                @pl.when(is_home)
                def _():
                    row_here(which).wait()

                @pl.when(jnp.logical_not(is_home))
                def _():
                    row_out(which, 0).wait_send()

            else:
                row_out(which, i).wait_send()
        src, dst = ((y, y_o), (dt, dt_o))[which]
        for j in range(2):
            for h in range(2):
                span = pl.ds(h * piece, piece)

                @pl.when(jnp.logical_not((core == h) & (z == 2 * core + j)))
                def _():
                    push(
                        src.at[:, pl.ds(0, piece)], dst.at[j, :, span], out_s.at[which, 0],
                        out_r.at[which, j, h], sibling,
                    ).wait_recv()


def vmem(shape, dtype=BF):
    return pltpu.VMEM(shape, dtype)


def sds(shape, dtype=BF):
    return jax.ShapeDtypeStruct(shape, dtype)


def dma(*shape):
    return pltpu.SemaphoreType.DMA(shape)


ANY = pl.BlockSpec(memory_space=pl.ANY)
INV = pl.BlockSpec(memory_space=pltpu.VMEM)


def by_chip(
    text, boundary, reset, memory_in, init_memory, w_qkv, b_qv, w_out, w_in, w_back, b_in, norm_gains, biases,
    cotangent,
):
    head_count = lax.axis_size("head")
    dp_count = lax.axis_size("dp")
    core = lax.axis_index("dp") % 2
    z = lax.axis_index("head")
    planes = dp_count // 2
    total = dp_count * head_count
    text_rows, width = text.shape[2], text.shape[3]
    block = cotangent.shape[2]
    seg_len = block * head_count
    mem_rows = memory_in.shape[1]
    local = w_qkv.shape[2]
    hid = w_in.shape[1]
    lanes = norm_gains.shape[1]
    heads = 2 * local // HD
    hidden = hid * planes * head_count

    small = jnp.zeros((32, 128), BF)
    small = small.at[0:16, 0:lanes].set(jnp.concatenate([norm_gains, biases, init_memory], axis=0))
    small = small.at[16, 0:hid].set(b_in)
    small = small.at[17:20].set(b_qv.reshape(3, 128))
    j = z % 2
    doc_ids = jnp.cumsum(boundary[j], axis=1).astype(F32)
    marks = jnp.full((2, mem_rows), -1.0, F32)
    labels = jnp.concatenate([marks, doc_ids, marks], axis=1)
    flag_rows = jnp.broadcast_to(reset[j].astype(F32)[:, None], (2, seg_len))
    seqf = jnp.concatenate([labels, flag_rows, jnp.zeros((4, seg_len), F32)], axis=0)
    memp = jnp.pad(memory_in[j], ((0, 16 - mem_rows), (0, 0)))
    text_pad = jnp.pad(text, ((0, 0), (0, 0), (0, block - text_rows), (0, 0)))
    rows = jnp.concatenate([text_pad, cotangent], axis=1)
    wa = jnp.concatenate([w_qkv.transpose(1, 2, 0).reshape(3 * local, width), w_out], axis=0)
    wf = jnp.stack([w_in.T, w_back])

    small_all, seq_pair, mem_pair, rows_all, wa_all, wf_all = pl.pallas_call(
        functools.partial(start_kernel, dp_count, head_count),
        out_shape=(
            sds((total, 32, 128)),
            sds((8, seg_len), F32),
            sds((16, width)),
            sds((4, head_count, block, width)),
            sds((2, 4 * local, width)),
            sds((2, planes * head_count, hid, width)),
        ),
        in_specs=[ANY] * 6,
        out_specs=[ANY] * 6,
        scratch_shapes=[
            dma(total), dma(total), dma(2), dma(2), dma(2, 2), dma(4), dma(4), dma(4), dma(3), dma(2, 2),
            dma(2, 4), dma(2, 4), dma(3), dma(4), dma(4, 2, 3), dma(4, 2, 3), dma(4),
        ],
        compiler_params=pltpu.CompilerParams(collective_id=0, has_side_effects=True),
        name="start",
    )(small, seqf, memp, rows, wa, wf)

    home = core == z // 2
    seqf = jnp.where(home, seqf, seq_pair)
    mem_one = jnp.where(home, memp, mem_pair)
    by_device = small_all.reshape(planes, 2, head_count, 32, 128)
    vectors = by_device[:, :, :, 0:16, 0:lanes].transpose(3, 0, 1, 2, 4).reshape(16, width)
    par = vectors.astype(F32)
    own_core = lax.dynamic_index_in_dim(by_device, core, 1, keepdims=False)
    bin_row = own_core[:, :, 16, 0:hid].reshape(1, hidden).astype(F32)
    qv = lax.dynamic_slice_in_dim(own_core[0], 2 * core, 2, 0)[:, 17:20].reshape(2, 2, local).astype(F32)
    bqv = jnp.concatenate([qv[:, 0], jnp.zeros((2, local), F32), qv[:, 1]], axis=1)[:, :, None]
    init = vectors[6 : 6 + mem_rows]
    init_a = jnp.pad(init, ((0, 16 - mem_rows), (0, 0)))
    init_b = jnp.pad(init, ((16 - mem_rows, 0), (0, 0)))
    flags = jnp.broadcast_to(seqf[2:4, 0:1], (2, width))
    flags = jnp.concatenate([flags, jnp.zeros((6, width), F32)], axis=0)
    mem_a = jnp.where(flags[0:1] > 0, init_a, mem_one)
    mem_b = jnp.roll(mem_a, 16 - mem_rows, axis=0)
    lab_row = seqf[0:2, None, :]
    lab_col = seqf[0:2, :, None]
    rows_nat = rows_all.reshape(4, seg_len, width)
    wf_nat = wf_all.reshape(2, hidden, width)

    y, dt, ffg, agq, ago, sg, dinit, dbin, dbqv = pl.pallas_call(
        functools.partial(layer_kernel, mem_rows),
        out_shape=(
            sds((2, seg_len, width)),
            sds((2, seg_len, width)),
            sds((2, hidden, width)),
            sds((2, width, 3 * local)),
            sds((2, width, local)),
            sds((8, width), F32),
            sds((16, width), F32),
            sds((8, hidden), F32),
            sds((2, 3 * local, 1), F32),
        ),
        in_specs=[INV] * 13,
        out_specs=[INV, INV, ANY] + [INV] * 6,
        scratch_shapes=[
            vmem((2, seg_len, width)),
            vmem((2, 2, 3 * local, seg_len)),
            vmem((2, heads, seg_len, seg_len)),
            vmem((2, 2, local, seg_len)),
            vmem((seg_len, seg_len), F32),
            vmem((seg_len, width), F32),
            vmem((seg_len, width), F32),
            vmem((2, seg_len, width)),
            vmem((2, seg_len, 1), F32),
            vmem((2, seg_len, width)),
            vmem((2, seg_len, hidden)),
            vmem((2, seg_len, hidden)),
            vmem((2, seg_len, width)),
            vmem((2, seg_len, 1), F32),
            vmem((2, seg_len, width)),
            vmem((2, seg_len, hidden)),
            vmem((2, seg_len, width)),
            vmem((2, local, seg_len)),
            vmem((2, 2, 3 * local, seg_len)),
            vmem((2, 4, 128, width)),
            vmem((2, 4, 128, width)),
            vmem((16, width)),
            vmem((16, width)),
            vmem((128, width), F32),
            vmem((2, 256, width)),
            dma(2, 4),
            dma(2, 4),
            dma(2),
        ],
        compiler_params=pltpu.CompilerParams(
            collective_id=1, has_side_effects=True, vmem_limit_bytes=VMEM_LIMIT
        ),
        name="layer",
    )(rows_nat, wa_all, wf_nat, lab_row, lab_col, par, bqv, bin_row, mem_a, mem_b, init_a, init_b, flags)

    vec = jnp.concatenate([sg[0:6], dinit[16 - mem_rows : 16]], axis=0)
    vec = vec.reshape(16, planes, 2, head_count, lanes)
    vec = lax.dynamic_index_in_dim(vec, core, 2, keepdims=False).transpose(1, 2, 0, 3)
    bin_part = jnp.pad(
        dbin[0].reshape(planes, head_count, 1, hid), ((0, 0), (0, 0), (0, 15), (128, width - 128 - hid))
    )
    vec = jnp.pad(vec, ((0, 0), (0, 0), (0, 0), (0, width - lanes))) + bin_part
    ffg = ffg.reshape(2, planes, head_count, hid, width)
    fa = jnp.concatenate([ffg[0], vec.astype(BF)], axis=2)
    dqv = jnp.stack([dbqv[:, 0:local, 0], dbqv[:, 2 * local :, 0]], axis=1)
    slice_b = HD // dp_count
    dqv = dqv.reshape(2, 2, local // HD, dp_count, slice_b).transpose(0, 3, 1, 2, 4)
    dqv = dqv.reshape(2, dp_count, 1, -1)
    dqv = jnp.pad(dqv, ((0, 0), (0, 0), (0, 15), (0, width - dqv.shape[3])))
    share = width // dp_count
    att = jnp.concatenate([agq, ago], axis=2).reshape(2, dp_count, share, width)
    att = jnp.concatenate([att, dqv.astype(BF)], axis=2)
    plane_shape = (2, 2)
    fa = fa.reshape(plane_shape + fa.shape[1:])
    fb = ffg[1].reshape(plane_shape + ffg.shape[2:])
    att = att.reshape((2,) + plane_shape + (2,) + att.shape[2:])
    hc, ra, rb, rt = head_count, hid + 16, hid, share + 16

    fa_o, fb_o, at_o, acts, grad_text = pl.pallas_call(
        functools.partial(finish_kernel, dp_count, head_count),
        out_shape=(
            sds((ra, width), F32),
            sds((rb, width), F32),
            sds((rt, width), F32),
            sds((2, 2, block, width)),
            sds((2, 2, block, width)),
        ),
        in_specs=[ANY] * 5,
        out_specs=[INV, INV, INV, ANY, ANY],
        scratch_shapes=[
            vmem((2, 2, hc, ra, width)),
            vmem((2, 2, hc, rb, width)),
            vmem((2, 2, 2, 2, rt, width)),
            vmem((2, hc, ra, width)),
            vmem((hc, ra, width)),
            vmem((2, hc, rb, width)),
            vmem((hc, rb, width)),
            vmem((2, 2, 2, rt, width)),
            vmem((2, 2, rt, width)),
            vmem((hc, ra, width)),
            vmem((hc, rb, width)),
            vmem((hc, rt, width)),
            dma(4, 2), dma(4, 2), dma(4), dma(4), dma(2, 3), dma(2, 4), dma(2, 2), dma(4), dma(2, 4),
            dma(2, 2, 2), dma(6),
        ],
        compiler_params=pltpu.CompilerParams(
            collective_id=2, has_side_effects=True, vmem_limit_bytes=VMEM_LIMIT
        ),
        name="finish",
    )(fa, fb, att, y, dt)

    d_vec = fa_o[hid:, 0:lanes]
    d_bqv = at_o[share, 0 : 2 * (local // HD) * slice_b].reshape(2, local // HD, slice_b)
    return (
        acts,
        grad_text[:, :, 0:text_rows],
        d_vec[6:16],
        at_o[:share, 0 : 3 * local].reshape(share, 3, local),
        d_bqv,
        at_o[:share, 3 * local :].T,
        fa_o[:hid].T,
        fb_o,
        fa_o[hid, 128 : 128 + hid],
        d_vec[0:2],
        d_vec[2:6],
    )


def solution(mesh):
    body = by_chip if mesh.shape["dp"] == 8 and mesh.shape["head"] == 4 else local
    return jax.shard_map(
        body,
        mesh=mesh,
        in_specs=(
            P("dp", None, "head", None),
            P("dp", None, None),
            P("dp", None),
            P("dp", None, None),
            P(None, ("dp", "head")),
            P(None, None, "head"),
            P(None, "head", None),
            P("head", None),
            P(None, ("dp", "head")),
            P(("dp", "head"), None),
            P(("dp", "head")),
            P(None, ("dp", "head")),
            P(None, ("dp", "head")),
            P("dp", None, "head", None),
        ),
        out_specs=(
            P("dp", None, "head", None),
            P("dp", None, "head", None),
            P(None, ("dp", "head")),
            P("dp", None, "head"),
            P(None, "head", "dp"),
            P("head", "dp"),
            P(None, ("dp", "head")),
            P(("dp", "head"), None),
            P(("dp", "head")),
            P(None, ("dp", "head")),
            P(None, ("dp", "head")),
        ),
        check_vma=False,
    )
```

```python
import functools

import jax
import jax.numpy as jnp
from jax import lax
from jax.experimental import pallas as pl
from jax.experimental.pallas import tpu as pltpu
from jax.sharding import PartitionSpec as P

HD = 64
MESH = pl.DeviceIdType.MESH
BF = jnp.bfloat16
F32 = jnp.float32
VMEM_LIMIT = 64 * 1024 * 1024


def nn(a, b):
    return lax.dot_general(a, b, (((1,), (0,)), ((), ())), preferred_element_type=F32)


def nt(a, b):
    return lax.dot_general(a, b, (((1,), (1,)), ((), ())), preferred_element_type=F32)


def tn(a, b):
    return lax.dot_general(a, b, (((0,), (0,)), ((), ())), preferred_element_type=F32)


def place():
    dp, z = lax.axis_index("dp"), lax.axis_index("head")
    core, plane = dp % 2, dp // 2
    return core, plane % 2, plane // 2, z


def device(core, x, y, z):
    return ((y * 2 + x) * 2 + core, z)


def push(src, dst, send, recv, target):
    return pltpu.make_async_remote_copy(
        src_ref=src, dst_ref=dst, send_sem=send, recv_sem=recv, device_id=target, device_id_type=MESH
    )


def from_root(x, axis, root):
    mine = lax.axis_index(axis) == root
    return lax.psum(jnp.where(mine, x, jnp.zeros_like(x)), axis)


def layer_norm(values, gain_row, shift_row):
    center = values - jnp.mean(values, axis=-1, keepdims=True)
    spread = jnp.mean(center * center, axis=-1, keepdims=True)
    return center * lax.rsqrt(spread + 1e-05) * gain_row + shift_row


def gelu_tanh(values):
    return jax.nn.gelu(values, approximate=True)


def head_major(array, dim, dp_count, head_count):
    shape = array.shape
    size = shape[dim]
    split = array.reshape(
        shape[:dim] + (dp_count, head_count, size // (dp_count * head_count)) + shape[dim + 1 :]
    )
    return jnp.swapaxes(split, dim, dim + 1).reshape(shape)


def local(
    text,
    boundary,
    reset,
    memory_in,
    init_memory,
    w_qkv,
    b_qv,
    w_out,
    w_in,
    w_back,
    b_in,
    norm_gains,
    biases,
    cotangent,
):
    head_count = lax.axis_size("head")
    dp_count = lax.axis_size("dp")
    head_idx = lax.axis_index("head")
    batch_size = text.shape[0]
    width = text.shape[3]
    seg_rows = cotangent.shape[2]
    seg_len = seg_rows * head_count
    mem_rows = memory_in.shape[1]
    text_len = seg_len - 2 * mem_rows
    local_width = w_qkv.shape[2]
    local_heads = local_width // HD
    row_start = head_idx * seg_rows
    is_first = (head_idx == 0).astype(jnp.float32)
    is_final = (head_idx == head_count - 1).astype(jnp.float32)
    grad_dims = (1, 0, 0, 1, 1, 1)
    doc_ids = jnp.cumsum(boundary, axis=2)
    marks = jnp.full((batch_size, 2, mem_rows), -1, jnp.int32)
    labels = jnp.concatenate([marks, doc_ids, marks], axis=2)
    visible = (
        (labels[..., :, None] == labels[..., None, :])
        | (labels[..., :, None] < 0)
        | (labels[..., None, :] < 0)
    )
    bias_query = b_qv[0].reshape(local_width).astype(jnp.float32)
    bias_value = b_qv[1].reshape(local_width).astype(jnp.float32)
    shared = (
        lax.all_gather(w_in, ("dp", "head"), axis=1, tiled=True),
        lax.all_gather(w_back, ("dp", "head"), axis=0, tiled=True),
        lax.all_gather(b_in, ("dp", "head"), axis=0, tiled=True),
        lax.all_gather(norm_gains, ("dp", "head"), axis=1, tiled=True),
        lax.all_gather(biases, ("dp", "head"), axis=1, tiled=True),
        lax.all_gather(init_memory, ("dp", "head"), axis=1, tiled=True),
    )

    def fetch():
        return shared

    def attention_probs(query, key_rows, seg):
        scores = (
            jnp.einsum("sqhe,skhe->shqk", query, key_rows, preferred_element_type=jnp.float32)
            * 0.125
        )
        return jnp.where(visible[:, seg][:, None], scores, -1e30)

    def forward(seg, memory, ffn):
        w_in_all, w_back_all, b_in_all, gains_all, biases_all, unused = ffn
        gains_f = gains_all.astype(jnp.float32)
        biases_f = biases_all.astype(jnp.float32)
        local_text = lax.all_gather(text[:, seg], "head", axis=1, tiled=True)
        x_rows = jnp.concatenate([memory, local_text, memory], axis=1)
        mixed = jnp.einsum("srd,dce->srce", x_rows, w_qkv, preferred_element_type=jnp.float32)
        query = (
            (mixed[:, :, 0] + bias_query)
            .astype(jnp.bfloat16)
            .reshape(batch_size, seg_len, local_heads, HD)
        )
        key_rows = mixed[:, :, 1].astype(jnp.bfloat16).reshape(batch_size, seg_len, local_heads, HD)
        value = (
            (mixed[:, :, 2] + bias_value)
            .astype(jnp.bfloat16)
            .reshape(batch_size, seg_len, local_heads, HD)
        )
        masked = attention_probs(query, key_rows, seg)
        row_max = jnp.max(masked, axis=-1, keepdims=True)
        exp_terms = jnp.exp(masked - row_max)
        row_total = jnp.sum(exp_terms, axis=-1, keepdims=True)
        log_total = row_max + jnp.log(row_total)
        probs = (exp_terms / row_total).astype(jnp.bfloat16)
        attended = jnp.einsum("shqk,skhe->sqhe", probs, value, preferred_element_type=jnp.float32)
        attended = attended.astype(jnp.bfloat16).reshape(batch_size, seg_len, local_width)
        partial_out = jnp.einsum("srl,ld->srd", attended, w_out, preferred_element_type=jnp.float32)
        summed = lax.psum_scatter(
            partial_out.astype(jnp.bfloat16), "head", scatter_dimension=1, tiled=True
        ).astype(jnp.float32)
        own_rows = lax.dynamic_slice_in_dim(x_rows, row_start, seg_rows, 1).astype(jnp.float32)
        pre_norm = own_rows + summed + biases_f[1]
        hidden = layer_norm(pre_norm, gains_f[0], biases_f[0])
        hidden_low = hidden.astype(jnp.bfloat16)
        inner = jnp.einsum(
            "srd,df->srf", hidden_low, w_in_all, preferred_element_type=jnp.float32
        ) + b_in_all.astype(jnp.float32)
        active = gelu_tanh(inner).astype(jnp.bfloat16)
        outer = (
            jnp.einsum("srf,fd->srd", active, w_back_all, preferred_element_type=jnp.float32)
            + biases_f[2]
        )
        post_norm = hidden + outer
        result = layer_norm(post_norm, gains_f[1], biases_f[3])
        kept = (
            x_rows,
            query,
            key_rows,
            value,
            log_total,
            attended,
            pre_norm,
            hidden_low,
            inner,
            active,
            post_norm,
        )
        return (result, kept)

    def backward(seg, grad_out, kept, ffn):
        (
            x_rows,
            query,
            key_rows,
            value,
            log_total,
            attended,
            pre_norm,
            hidden_low,
            inner,
            active,
            post_norm,
        ) = kept
        w_in_all, w_back_all, b_in_all, gains_all, biases_all, unused = ffn
        gains_f = gains_all.astype(jnp.float32)
        biases_f = biases_all.astype(jnp.float32)
        unused_two, pull_two = jax.vjp(layer_norm, post_norm, gains_f[1], biases_f[3])
        grad_post, grad_gain_two, grad_shift_two = pull_two(grad_out)
        grad_outer = grad_post.astype(jnp.bfloat16)
        grad_ffn_bias = jnp.sum(grad_post, axis=(0, 1))
        grad_w_back = jnp.einsum(
            "srf,srd->fd", active, grad_outer, preferred_element_type=jnp.float32
        )
        grad_active = jnp.einsum(
            "srd,fd->srf", grad_outer, w_back_all, preferred_element_type=jnp.float32
        )
        unused_gelu, pull_gelu = jax.vjp(gelu_tanh, inner)
        grad_inner = pull_gelu(grad_active)[0].astype(jnp.bfloat16)
        grad_b_in = jnp.sum(grad_inner, axis=(0, 1), dtype=jnp.float32)
        grad_w_in = jnp.einsum(
            "srd,srf->df", hidden_low, grad_inner, preferred_element_type=jnp.float32
        )
        grad_hidden = grad_post + jnp.einsum(
            "srf,df->srd", grad_inner, w_in_all, preferred_element_type=jnp.float32
        )
        unused_one, pull_one = jax.vjp(layer_norm, pre_norm, gains_f[0], biases_f[0])
        grad_pre, grad_gain_one, grad_shift_one = pull_one(grad_hidden)
        grad_out_bias = jnp.sum(grad_pre, axis=(0, 1))
        grad_branch = lax.all_gather(grad_pre.astype(jnp.bfloat16), "head", axis=1, tiled=True)
        grad_w_out = jnp.einsum(
            "srl,srd->ld", attended, grad_branch, preferred_element_type=jnp.float32
        )
        grad_att = jnp.einsum("srd,ld->srl", grad_branch, w_out, preferred_element_type=jnp.float32)
        grad_att = grad_att.astype(jnp.bfloat16).reshape(batch_size, seg_len, local_heads, HD)
        masked = attention_probs(query, key_rows, seg)
        probs = jnp.exp(masked - log_total)
        grad_value = jnp.einsum(
            "shqk,sqhe->skhe",
            probs.astype(jnp.bfloat16),
            grad_att,
            preferred_element_type=jnp.float32,
        )
        grad_probs = jnp.einsum(
            "sqhe,skhe->shqk", grad_att, value, preferred_element_type=jnp.float32
        )
        grad_scores = probs * (grad_probs - jnp.sum(grad_probs * probs, axis=-1, keepdims=True))
        grad_scores = grad_scores.astype(jnp.bfloat16)
        grad_query = (
            jnp.einsum("shqk,skhe->sqhe", grad_scores, key_rows, preferred_element_type=jnp.float32)
            * 0.125
        )
        grad_key = (
            jnp.einsum("shqk,sqhe->skhe", grad_scores, query, preferred_element_type=jnp.float32)
            * 0.125
        )
        grad_mixed = jnp.stack([grad_query, grad_key, grad_value], axis=2).astype(jnp.bfloat16)
        grad_mixed = grad_mixed.reshape(batch_size, seg_len, 3, local_width)
        grad_bias_qv = jnp.stack(
            [
                jnp.sum(grad_mixed[:, :, 0], axis=(0, 1), dtype=jnp.float32),
                jnp.sum(grad_mixed[:, :, 2], axis=(0, 1), dtype=jnp.float32),
            ]
        ).reshape(2, local_heads, HD)
        grad_w_qkv = jnp.einsum(
            "srd,srce->dce", x_rows, grad_mixed, preferred_element_type=jnp.float32
        )
        grad_rows = jnp.einsum(
            "srce,dce->srd", grad_mixed, w_qkv, preferred_element_type=jnp.float32
        )
        placed = lax.dynamic_update_slice_in_dim(jnp.zeros_like(grad_rows), grad_pre, row_start, 1)
        grad_rows = grad_rows + placed
        grad_text_part = lax.psum_scatter(
            grad_rows[:, mem_rows : mem_rows + text_len].astype(jnp.bfloat16),
            "head",
            scatter_dimension=1,
            tiled=True,
        ).astype(jnp.float32)
        grad_memory = lax.psum(
            (grad_rows[:, :mem_rows] + grad_rows[:, seg_len - mem_rows :]).astype(jnp.bfloat16),
            "head",
        ).astype(jnp.float32)
        reset_flag = reset[:, seg] > 0
        grad_init = (
            jnp.sum(jnp.where(reset_flag[:, None, None], grad_memory, 0.0), axis=0) * is_first
        )
        ffn_grads = (
            grad_w_in,
            grad_w_back,
            grad_b_in,
            jnp.stack([grad_gain_one, grad_gain_two]),
            jnp.stack([grad_shift_one, grad_out_bias, grad_ffn_bias, grad_shift_two]),
            grad_init,
        )
        return (grad_text_part, grad_memory, (grad_w_qkv, grad_bias_qv, grad_w_out), ffn_grads)

    ffn_first = fetch()
    init_all = ffn_first[5]
    memory_one = jnp.where(reset[:, 0, None, None] > 0, init_all[None], memory_in)
    out_one, kept_one = forward(0, memory_one, ffn_first)
    tail_rows = out_one[:, seg_rows - mem_rows :].astype(jnp.bfloat16)
    carried = from_root(tail_rows, "head", head_count - 1)
    ffn_second = fetch()
    memory_two = jnp.where(reset[:, 1, None, None] > 0, ffn_second[5][None], carried)
    out_two, kept_two = forward(1, memory_two, ffn_second)
    activations = jnp.stack([out_one, out_two], axis=1).astype(jnp.bfloat16)
    ffn_third = fetch()
    text_two, memory_grad_two, attn_two, ffn_two = backward(
        1, cotangent[:, 1].astype(jnp.float32), kept_two, ffn_third
    )
    keep_flag = reset[:, 1, None, None] <= 0
    carried_grad = jnp.where(keep_flag, memory_grad_two, 0.0) * is_final
    grad_one = cotangent[:, 0].astype(jnp.float32) + jnp.concatenate(
        [jnp.zeros((batch_size, seg_rows - mem_rows, width), jnp.float32), carried_grad], axis=1
    )
    ffn_fourth = fetch()
    text_one, memory_grad_one, attn_one, ffn_one = backward(0, grad_one, kept_one, ffn_fourth)
    grads = jax.tree.map(lambda a, b: a + b, ffn_one, ffn_two)
    ffn_total = tuple((head_major(g, d, dp_count, head_count) for g, d in zip(grads, grad_dims)))
    partial_sums = (
        lax.psum_scatter(
            ffn_total[0].astype(jnp.bfloat16), "head", scatter_dimension=1, tiled=True
        ).astype(jnp.float32),
        lax.psum_scatter(
            ffn_total[1].astype(jnp.bfloat16), "head", scatter_dimension=0, tiled=True
        ).astype(jnp.float32),
        lax.psum_scatter(
            ffn_total[2].astype(jnp.bfloat16), "head", scatter_dimension=0, tiled=True
        ).astype(jnp.float32),
        lax.psum_scatter(
            ffn_total[3].astype(jnp.bfloat16), "head", scatter_dimension=1, tiled=True
        ).astype(jnp.float32),
        lax.psum_scatter(
            ffn_total[4].astype(jnp.bfloat16), "head", scatter_dimension=1, tiled=True
        ).astype(jnp.float32),
        lax.psum_scatter(
            ffn_total[5].astype(jnp.bfloat16), "head", scatter_dimension=1, tiled=True
        ).astype(jnp.float32),
    )
    reduced = (
        lax.psum_scatter(partial_sums[0], "dp", scatter_dimension=1, tiled=True),
        lax.psum_scatter(partial_sums[1], "dp", scatter_dimension=0, tiled=True),
        lax.psum_scatter(partial_sums[2], "dp", scatter_dimension=0, tiled=True),
        lax.psum_scatter(partial_sums[3], "dp", scatter_dimension=1, tiled=True),
        lax.psum_scatter(partial_sums[4], "dp", scatter_dimension=1, tiled=True),
        lax.psum_scatter(partial_sums[5], "dp", scatter_dimension=1, tiled=True),
    )
    attn_total = jax.tree.map(lambda a, b: a + b, attn_one, attn_two)
    grad_qkv, grad_bqv, grad_wout = (
        lax.psum_scatter(attn_total[0], "dp", scatter_dimension=0, tiled=True),
        lax.psum_scatter(attn_total[1], "dp", scatter_dimension=2, tiled=True),
        lax.psum_scatter(attn_total[2], "dp", scatter_dimension=1, tiled=True),
    )
    grad_text = jnp.stack([text_one, text_two], axis=1).astype(jnp.bfloat16)
    grad_win, grad_wback, grad_bin, grad_gains, grad_biases, grad_init = reduced
    return (
        activations,
        grad_text,
        grad_init,
        grad_qkv,
        grad_bqv,
        grad_wout,
        grad_win,
        grad_wback,
        grad_bin,
        grad_gains,
        grad_biases,
    )


class Refs:
    pass


def by_name(names, values):
    refs = Refs()
    for name, value in zip(names, values, strict=True):
        setattr(refs, name, value)
    return refs


def loop(count, body):
    def run(i, unused):
        body(i)
        return unused

    lax.fori_loop(0, count, run, 0)


def add_blocks(dst, src):
    def body(i):
        dst[i] = (dst[i].astype(F32) + src[i].astype(F32)).astype(BF)

    loop(dst.shape[0], body)


def add_block(dst, src):
    dst[...] = (dst[...].astype(F32) + src[...].astype(F32)).astype(BF)


def as_column(row):
    n = row.shape[1]
    down = lax.broadcasted_iota(jnp.int32, (n, n), 0)
    across = lax.broadcasted_iota(jnp.int32, (n, n), 1)
    return jnp.sum(jnp.where(down == across, row, 0.0), axis=1, keepdims=True)


def norm(v):
    center = v - jnp.mean(v, axis=-1, keepdims=True)
    scale = lax.rsqrt(jnp.mean(center * center, axis=-1, keepdims=True) + 1e-05)
    return center * scale, scale


def pull_norm(g, hat, scale):
    m1 = jnp.mean(g, axis=-1, keepdims=True)
    m2 = jnp.mean(g * hat, axis=-1, keepdims=True)
    return scale * (g - m1 - hat * m2)


def row_sum(v):
    return jnp.sum(v, axis=0, keepdims=True)


def main_kernel(names, dp_count, head_count, *values):
    r_ = by_name(names, values)
    core, px, py, z = place()
    plane = py * 2 + px
    x_plane, y_plane = py * 2 + 1 - px, (1 - py) * 2 + px
    me = (plane * 2 + core) * head_count + z
    total = dp_count * head_count
    planes = dp_count // 2
    is_home = core == z // 2
    away = jnp.logical_not(is_home)
    sibling = device(1 - core, px, py, z)
    x_mate, y_mate = device(core, 1 - px, py, z), device(core, px, 1 - py, z)
    mirror = z // 2

    def from_end(i):
        return i + mirror * (head_count - 1 - 2 * i)

    depth = from_end(z)
    inside = depth == 1
    order = [from_end(i) for i in (depth, 1 - depth, 2, 3)]

    x, qkv, pt, ot, wa, wf = r_.x, r_.qkv, r_.pt, r_.ot, r_.wa, r_.wf
    hf, acc, par = r_.hf, r_.acc, r_.par
    seg_len, width = x.shape[1], x.shape[2]
    hidden = r_.u.shape[2]
    heads = pt.shape[1]
    local = ot.shape[2]
    hid = r_.w_back.shape[0]
    lanes = r_.norm_gains.shape[1]
    mem_rows = r_.memory_in.shape[0]
    text_rows = r_.text.shape[2]
    per_block = local // HD
    step = seg_len // head_count
    piece = step // 2
    chunk = hidden // head_count
    tail = 16

    def rows(r):
        return pl.ds(pl.multiple_of(r * step, step), step)

    def cols(i):
        return pl.ds(pl.multiple_of(i * chunk, chunk), chunk)

    def head_rows(h, part):
        return pl.ds(pl.multiple_of((h % per_block) * HD + part * local, HD), HD)

    def column(i):
        h = core if i < head_count - 1 else 1 - core
        zt = (z + 1 + i) % head_count
        return (plane * 2 + h) * head_count + zt, device(h, px, py, zt)

    column_size = 2 * head_count - 1

    def when_not(cond, body):
        pl.when(jnp.logical_not(cond))(body)

    share = local
    half = share // 2

    def attention_out(i, which):
        zt = (z + 1 + i) % head_count
        at = pl.multiple_of((share * jnp.minimum(plane, planes - 2) if which == 0 else 0) + half * core, half)
        src = (r_.wq_t, r_.w_out)[which]
        return push(
            src.at[pl.ds(at, half)], wa.at[z % 2, pl.ds(pl.multiple_of(share * plane + half * core, half), half)],
            r_.att_s.at[i], r_.att_r.at[z % 2, core], device(z // 2, px, py, zt),
        )

    def attention_outs(do):
        for which, mine in enumerate((plane < planes - 1, plane == planes - 1)):

            def each():
                for i in range(head_count - 1):
                    do(attention_out(i, which))

            pl.when(mine)(each)

    def attention_in(k, h):
        span = pl.ds(pl.multiple_of(share * plane + half * h, half), half)
        return push(r_.w_out.at[pl.ds(0, half)], wa.at[k, span], r_.att_s.at[0], r_.att_r.at[k, h], sibling)

    def attention_plane(k, which):
        at, count, mate = (
            (share * plane, share, x_mate),
            (share * plane, share, y_mate),
            (share * x_plane, half, y_mate),
            (share * y_plane + half, half, x_mate),
        )[which]
        block = pl.ds(pl.multiple_of(at, half), count)
        return push(
            wa.at[k, block], wa.at[k, block], r_.plane_s.at[k, which], r_.plane_r.at[k, which], mate
        )

    own_attention = [
        pltpu.make_async_copy(r_.wq_t, wa.at[z % 2, pl.ds(0, 3 * local)], r_.local_sem.at[0]),
        pltpu.make_async_copy(r_.w_out, wa.at[z % 2, pl.ds(3 * local, local)], r_.local_sem.at[1]),
    ]
    foreign = [jnp.logical_not(is_home & (z % 2 == k)) for k in range(2)]

    def rows_src(a, j, h):
        src = r_.text_pad if a < 2 else r_.cotangent
        return src.at[j, a % 2, pl.ds(h * piece, piece)]

    def rows_dst(a, zs, h):
        dst = r_.text_all if a < 2 else r_.cot_all
        return dst.at[a % 2, pl.ds(pl.multiple_of(zs * step + h * piece, piece), piece)]

    def rows_out(a, j, h):
        return push(
            rows_src(a, j, h), rows_dst(a, z, h), r_.rows_s.at[a, j, h], r_.rows_r.at[a, z],
            device(h, px, py, 2 * core + j),
        )

    def rows_here(a, j, h):
        return pltpu.make_async_copy(rows_src(a, j, h), rows_dst(a, z, h), r_.here_sem.at[a])

    def rows_send(a):
        for j in range(2):
            for h in range(2):
                here = (core == h) & (z == 2 * core + j)
                pl.when(here)(lambda: rows_here(a, j, h).start())
                when_not(here, lambda: rows_out(a, j, h).start())

    def rows_forward(a, zs, h):
        ref = rows_dst(a, zs, h)
        return push(ref, ref, r_.fwd_s.at[a, zs], r_.fwd_r.at[a, zs], sibling)

    def rows_pass(a):
        for zs in range(head_count):
            here = is_home & (z == zs)
            pl.when(here)(lambda: rows_here(a, z % 2, core).wait())
            when_not(
                here,
                lambda: push(
                    rows_src(a, 0, 0), rows_dst(a, zs, core), r_.rows_s.at[a, 0, 0], r_.rows_r.at[a, zs], sibling
                ).wait_recv(),
            )
            rows_forward(a, zs, core).start()

    def rows_ready(a):
        for zs in range(head_count):
            rows_forward(a, zs, 1 - core).wait_recv()

    def rows_done(a):
        for j in range(2):
            for h in range(2):
                when_not((core == h) & (z == 2 * core + j), lambda: rows_out(a, j, h).wait_send())
        for zs in range(head_count):
            rows_forward(a, zs, core).wait_send()

    def hidden_block(p, zi):
        return pl.ds(pl.multiple_of((zi * planes + p) * hid, hid), hid)

    def ffn_push(zi, to, slot):
        ref = wf.at[:, hidden_block(plane, zi)]
        return push(ref, ref, r_.ffn_s.at[slot], r_.ffn_r.at[zi], device(core, px, py, to))

    ffn_hops = [(0, from_end(1 - depth)), (0, from_end(2)), (1, from_end(2)), (2, from_end(0)), (3, from_end(0))]

    def ffn_hop(i):
        which, to = ffn_hops[i]
        return ffn_push(order[which], to, i)

    def ffn_own():
        ffn_hop(0).start()
        pl.when(inside)(ffn_hop(1).start)

    def ffn_one(n):
        ffn_push(order[n], z, 0).wait_recv()
        pl.when(inside)(ffn_hop(n + 1).start)
        side_first(order[n])

    def ffn_sent():
        ffn_hop(0).wait_send()

        def rest():
            for i in range(1, 5):
                ffn_hop(i).wait_send()

        pl.when(inside)(rest)

    def side(kind, zi, which):
        p, mate = (
            (plane, x_mate),
            (plane, y_mate),
            (x_plane, y_mate) if kind == 0 else (y_plane, x_mate),
        )[which]
        ref = wf.at[kind, hidden_block(p, zi)]
        return push(ref, ref, r_.side_s.at[zi, kind, which], r_.side_r.at[zi, kind, which], mate)

    def side_first(zi):
        for kind in range(2):
            side(kind, zi, 0).start()
            side(kind, zi, 1).start()

    def ffn_two(n):
        zi = order[n]
        side(0, zi, 0).wait_recv()
        side(0, zi, 2).start()
        side(1, zi, 1).wait_recv()
        side(1, zi, 2).start()

    def ffn_ready(n):
        zi = order[n]
        side(0, zi, 1).wait_recv()
        side(1, zi, 0).wait_recv()
        side(0, zi, 2).wait_recv()
        side(1, zi, 2).wait_recv()

    def small_out(i):
        return push(r_.small, r_.small_all.at[me], r_.small_s.at[i], r_.small_r.at[z, core], column(i)[1])

    def small_in(i):
        at, (dp_i, z_i) = column(i)
        return push(r_.small, r_.small_all.at[at], r_.small_s.at[i], r_.small_r.at[z_i, dp_i % 2], sibling)

    def small_plane(i):
        p, mate = ((plane, x_mate), (plane, y_mate), (x_plane, y_mate))[i]
        ref = r_.small_all.at[pl.ds(p * 2 * head_count, 2 * head_count)]
        return push(ref, ref, r_.small_ps.at[i], r_.small_pr.at[i], mate)

    pair = [
        push(r_.seqf, r_.seqf_in, r_.pair_s.at[0], r_.pair_r.at[0], sibling),
        push(r_.memp, r_.memp_in, r_.pair_s.at[1], r_.pair_r.at[1], sibling),
    ]

    barrier = pltpu.get_barrier_semaphore()
    mates = [x_mate, y_mate] + [column(i)[1] for i in range(column_size)]
    for mate in mates:
        pl.semaphore_signal(barrier, inc=1, device_id=mate, device_id_type=MESH)
    for j in range(2):
        for s in range(2):
            r_.text_pad[j, s, 0:text_rows, :] = r_.text[j, s]
            r_.text_pad[j, s, text_rows:step, :] = jnp.zeros((step - text_rows, width), BF)
    wf[0, hidden_block(plane, z), :] = r_.w_in_t[...]
    wf[1, hidden_block(plane, z), :] = r_.w_back[...]
    vtmp = r_.vtmp
    vtmp[...] = jnp.zeros_like(vtmp)
    vtmp[0:2, 0:lanes] = r_.norm_gains[...].astype(F32)
    vtmp[2:6, 0:lanes] = r_.biases[...].astype(F32)
    vtmp[6 : 6 + mem_rows, 0:lanes] = r_.init_memory[...].astype(F32)
    vtmp[0:1, 32 : 32 + hid] = r_.b_in[...].astype(F32)
    for b in range(per_block):
        pair_b = r_.b_qv[b].astype(F32)
        for part in range(2):
            vtmp[1 + part * per_block + b : 2 + part * per_block + b, 32 : 32 + HD] = pair_b[part : part + 1, :]
    r_.small[...] = vtmp[...].astype(BF)
    r_.small_all[me] = r_.small[...]
    seqf = r_.seqf
    marks = r_.boundary[z % 2].astype(F32).astype(BF)
    text_len = marks.shape[1]
    n_from = lax.broadcasted_iota(jnp.int32, (text_len, seg_len), 0)
    n_to = lax.broadcasted_iota(jnp.int32, (text_len, seg_len), 1) - mem_rows
    counts = nn(marks, jnp.where(n_from <= n_to, 1.0, 0.0).astype(BF))
    at_row = lax.broadcasted_iota(jnp.int32, (2, seg_len), 1)
    seqf[...] = jnp.zeros_like(seqf)
    seqf[0:2, :] = jnp.where((at_row >= mem_rows) & (at_row < seg_len - mem_rows), counts, -1.0)
    for s in range(2):
        seqf[2 + s : 3 + s, :] = jnp.full((1, seg_len), r_.reset[z % 2, s].astype(F32))
    r_.memp[...] = jnp.zeros_like(r_.memp)
    both_in = r_.memory_in[...].astype(F32)
    r_.memp[0:mem_rows, :] = jnp.where(z % 2 == 0, both_in[:, 0, :], both_in[:, 1, :]).astype(BF)
    for ref in (r_.sg, r_.dinit, r_.dbin, r_.carry):
        ref[...] = jnp.zeros_like(ref)
    pl.semaphore_wait(barrier, len(mates))

    attention_outs(lambda c: c.start())

    def keep_own():
        for copy in own_attention:
            copy.start()

    pl.when(is_home)(keep_own)
    rows_send(0)
    for i in range(column_size):
        small_out(i).start()
    for copy in pair:
        copy.start()
    side_first(z)

    def attention_to_plane(k):
        for h in range(2):
            attention_in(k, h).wait_recv()
        attention_plane(k, 0).start()
        attention_plane(k, 1).start()

    def attention_across(k):
        attention_plane(k, 0).wait_recv()
        attention_plane(k, 2).start()
        attention_plane(k, 1).wait_recv()
        attention_plane(k, 3).start()

    for i in range(column_size):
        small_in(i).wait_recv()
    small_plane(0).start()
    small_plane(1).start()
    for k in range(2):
        pl.when(foreign[k])(lambda: attention_to_plane(k))
    ffn_own()
    small_plane(0).wait_recv()
    small_plane(2).start()
    ffn_two(0)
    rows_pass(0)
    for k in range(2):
        pl.when(foreign[k])(lambda: attention_across(k))

    for copy in pair:
        copy.wait_recv()
    small_plane(1).wait_recv()
    small_plane(2).wait_recv()
    for i in range(total):
        par[0:16, lanes * i : lanes * (i + 1)] = r_.small_all[i, 0:16, 0:lanes].astype(F32)
    for zi in range(head_count):
        for p in range(planes):
            at = (zi * planes + p) * hid
            line = r_.small_all[(2 * p + core) * head_count + zi].astype(F32)
            r_.bin_row[0:1, at : at + hid] = line[0:1, 32 : 32 + hid]
    r_.bqv[...] = jnp.zeros_like(r_.bqv)
    for k in range(2):
        lines = r_.small_all[2 * core + k].astype(F32)
        for part in range(2):
            for b in range(per_block):
                line = lines[1 + part * per_block + b : 2 + part * per_block + b, 32 : 32 + HD]
                at = 2 * part * local + b * HD
                r_.bqv[k, at : at + HD, :] = as_column(line)
    seq = jnp.where(is_home, seqf[...], r_.seqf_in[...])
    seqf_out = r_.seq
    seqf_out[...] = seq
    flags = [seqf_out[2 + s : 3 + s, 0:1] for s in range(2)]
    tail_row = lax.broadcasted_iota(jnp.int32, (tail, width), 0)
    is_mem = tail_row >= tail - mem_rows
    init_b = jnp.where(is_mem, par[...], 0.0)
    given = jnp.where(is_home, r_.memp[...].astype(F32), r_.memp_in[...].astype(F32))
    first_b = jnp.where(flags[0] > 0, init_b, pltpu.roll(given, tail - mem_rows, 0))
    r_.cur_b[...] = first_b.astype(BF)
    r_.cur_a[...] = pltpu.roll(first_b, mem_rows, 0).astype(BF)

    def take_rows(r):
        inside = lax.broadcasted_iota(jnp.int32, (step, seg_len), 0)
        nat = lax.broadcasted_iota(jnp.int32, (step, seg_len), 1)
        return jnp.where((nat == r * text_rows + inside + mem_rows) & (inside < text_rows), 1.0, 0.0).astype(BF)

    def place_rows(r):
        nat = lax.broadcasted_iota(jnp.int32, (step, seg_len), 0) + r * step
        pad = lax.broadcasted_iota(jnp.int32, (step, seg_len), 1)
        inside = pad & (step - 1)
        target = (pad // step) * text_rows + inside + mem_rows
        return jnp.where((nat == target) & (inside < text_rows), 1.0, 0.0).astype(BF)

    def exchange(slot, r):
        return push(
            r_.send_buf.at[slot, r], r_.recv_buf.at[slot, r], r_.send_sem.at[slot, r], r_.recv_sem.at[slot, r],
            sibling,
        )

    def give(slot, r, part):
        acc[rows(r), :] = part
        r_.send_buf[slot, r] = part.astype(BF)
        exchange(slot, r).start()

    def taken(slot, r):
        exchange(slot, r).wait()
        return acc[rows(r), :] + r_.recv_buf[slot, r].astype(F32)

    def back_copy(which, seg, zt):
        src, dst = ((r_.y, r_.acts_o), (r_.text_all, r_.dt_all))[which]
        span = pl.ds(pl.multiple_of(zt * step + core * piece, piece), piece)
        return src.at[seg, span], dst.at[z % 2, seg, pl.ds(core * piece, piece)]

    def back_out(which, seg, i):
        zt = (z + i) % head_count
        src, dst = back_copy(which, seg, zt)
        return push(
            src, dst, r_.back_s.at[which, seg, i], r_.back_r.at[which, seg, z % 2, core], device(z // 2, px, py, zt)
        )

    def back_here(which, seg):
        src, dst = back_copy(which, seg, z)
        return pltpu.make_async_copy(src, dst, r_.back_here_sem.at[which, seg])

    def back_send(which, seg):
        pl.when(is_home)(lambda: back_here(which, seg).start())
        pl.when(away)(lambda: back_out(which, seg, 0).start())
        for i in range(1, head_count):
            back_out(which, seg, i).start()

    def back_done(which, seg):
        pl.when(is_home)(lambda: back_here(which, seg).wait())
        pl.when(away)(lambda: back_out(which, seg, 0).wait_send())
        for i in range(1, head_count):
            back_out(which, seg, i).wait_send()
        src, dst = ((r_.y, r_.acts_o), (r_.text_all, r_.dt_all))[which]
        for j in range(2):
            for h in range(2):
                when_not(
                    (core == h) & (z == 2 * core + j),
                    lambda: push(
                        src.at[seg, pl.ds(0, piece)], dst.at[j, seg, pl.ds(h * piece, piece)],
                        r_.back_s.at[which, seg, 0], r_.back_r.at[which, seg, j, h], sibling,
                    ).wait_recv(),
                )

    def build(seg):
        def one(r):
            x[seg, rows(r), :] = nn(place_rows(r), r_.text_all[seg]).astype(BF)

        loop(head_count, one)
        x[seg, 0:tail, :] = x[seg, 0:tail, :] + r_.cur_a[...]
        x[seg, seg_len - tail : seg_len, :] = x[seg, seg_len - tail : seg_len, :] + r_.cur_b[...]
        right = r_.seq[seg : seg + 1, :]
        left = as_column(right)
        acc[:, 0:seg_len] = jnp.where((left == right) | (left < 0) | (right < 0), 0.0, -1e30)

    def project(seg):
        def one(i):
            j, t = i // 3, i % 3
            at = pl.ds(pl.multiple_of(t * local, local), local)
            value = nt(wa[j, at, :], x[seg]) + r_.bqv[j, at, :]
            qkv[seg, j, at, :] = (value * jnp.where(t == 0, 0.125, 1.0)).astype(BF)

        loop(6, one)

    def attend(seg, first, count):
        def one(i):
            h = first + i
            j = h // per_block
            q, k, v = (qkv[seg, j, head_rows(h, part), :] for part in range(3))
            s = tn(k, q) + acc[:, 0:seg_len]
            e = jnp.exp(s - jnp.max(s, axis=0, keepdims=True))
            p = (e * (1.0 / jnp.sum(e, axis=0, keepdims=True))).astype(BF)
            pt[seg, h] = p
            ot[seg, j, head_rows(h, 0), :] = nn(v, p).astype(BF)

        loop(count, one)

    def out_project(seg):
        def one(r):
            give(
                0, r,
                tn(ot[seg, 0, :, rows(r)], wa[0, 3 * local :, :]) + tn(ot[seg, 1, :, rows(r)], wa[1, 3 * local :, :]),
            )

        loop(head_count, one)

    def norm_one(seg):
        def one(r):
            hat, scale = norm(x[seg, rows(r), :].astype(F32) + taken(0, r) + par[3:4, :])
            r_.xh1[seg, rows(r), :] = hat.astype(BF)
            r_.rs[rows(r), 2 * seg : 2 * seg + 1] = scale
            h = hat * par[0:1, :] + par[2:3, :]
            hf[rows(r), :] = h
            r_.hb[seg, rows(r), :] = h.astype(BF)

        loop(head_count, one)

    def inner(seg, i):
        v = nt(r_.hb[seg], wf[0, cols(i), :]) + r_.bin_row[:, cols(i)]
        c0 = 0.7978845608028654
        sq = v * v
        th = jnp.tanh(v * (c0 + (c0 * 0.044715) * sq))
        up = 0.5 + 0.5 * th
        r_.u[seg, :, cols(i)] = (v * up).astype(BF)
        slope = up + (0.5 * v) * (1.0 - th * th) * (c0 + (3 * c0 * 0.044715) * sq)
        r_.gp[seg, :, cols(i)] = slope.astype(BF)

    def outer(seg):
        loop(head_count, lambda r: give(1, r, nn(r_.u[seg, rows(r), :], wf[1])))

    def norm_two(seg):
        def one(r):
            hat, scale = norm(hf[rows(r), :] + taken(1, r) + par[4:5, :])
            r_.xh2[seg, rows(r), :] = hat.astype(BF)
            r_.rs[rows(r), 2 * seg + 1 : 2 * seg + 2] = scale
            r_.y[seg, rows(r), :] = (hat * par[1:2, :] + par[5:6, :]).astype(BF)

        loop(head_count, one)

    def next_memory():
        last = r_.y[0, seg_len - tail : seg_len, :].astype(F32)
        memory = jnp.where(is_mem, jnp.where(flags[1] > 0, par[...], last), 0.0)
        r_.cur_b[...] = memory.astype(BF)
        r_.cur_a[...] = pltpu.roll(memory, mem_rows, 0).astype(BF)

    rows_ready(0)
    build(0)
    ffn_one(1)
    for k in range(2):

        def last_part():
            attention_plane(k, 2).wait_recv()
            attention_plane(k, 3).wait_recv()

        pl.when(foreign[k])(last_part)

    def kept_own():
        for copy in own_attention:
            copy.wait()

    pl.when(is_home)(kept_own)
    project(0)
    ffn_one(2)
    attend(0, 0, 2)
    ffn_two(1)
    attend(0, 2, 2)
    ffn_one(3)
    rows_send(1)
    attend(0, 4, heads - 4)
    out_project(0)
    ffn_two(2)
    norm_one(0)
    for n in range(2):
        ffn_ready(n)
        inner(0, order[n])
    ffn_two(3)
    for n in range(2, head_count):
        ffn_ready(n)
        inner(0, order[n])
    outer(0)
    rows_pass(1)
    rows_done(0)
    rows_send(3)
    rows_send(2)
    norm_two(0)
    next_memory()
    back_send(0, 0)

    rows_ready(1)
    build(1)
    project(1)
    attend(1, 0, heads)
    rows_pass(3)
    rows_done(1)
    out_project(1)
    norm_one(1)
    loop(head_count, lambda i: inner(1, i))
    rows_pass(2)
    outer(1)
    norm_two(1)
    back_send(0, 1)
    rows_ready(3)
    rows_ready(2)

    def pull_two(seg):
        def one(r):
            g_y = r_.cot_all[seg, rows(r), :].astype(F32)
            if seg == 0:
                g_y = g_y + jnp.where(r == head_count - 1, r_.carry[...], 0.0)
            hat = r_.xh2[seg, rows(r), :].astype(F32)
            pre = pull_norm(g_y * par[1:2, :], hat, r_.rs[rows(r), 2 * seg + 1 : 2 * seg + 2])
            hf[rows(r), :] = pre
            r_.xh2[seg, rows(r), :] = pre.astype(BF)
            r_.sg[1:2, :] += row_sum(g_y * hat)
            r_.sg[5:6, :] += row_sum(g_y)
            r_.sg[4:5, :] += row_sum(pre)

        loop(head_count, one)

    def pull_inner(seg, i):
        g_u = nt(r_.xh2[seg], wf[1, cols(i), :])
        g_z = (g_u * r_.gp[seg, :, cols(i)].astype(F32)).astype(BF)
        r_.gp[seg, :, cols(i)] = g_z
        r_.dbin[0:1, cols(i)] += row_sum(g_z.astype(F32))

    def pull_hidden(seg):
        loop(head_count, lambda r: give(0, r, nn(r_.gp[seg, rows(r), :], wf[0])))

    def pull_one(seg):
        def one(r):
            g_h = hf[rows(r), :] + taken(0, r)
            hat = r_.xh1[seg, rows(r), :].astype(F32)
            pre = pull_norm(g_h * par[0:1, :], hat, r_.rs[rows(r), 2 * seg : 2 * seg + 1])
            hf[rows(r), :] = pre
            r_.xh1[seg, rows(r), :] = pre.astype(BF)
            r_.sg[0:1, :] += row_sum(g_h * hat)
            r_.sg[2:3, :] += row_sum(g_h)
            r_.sg[3:4, :] += row_sum(pre)

        loop(head_count, one)

        def out(j):
            r_.got[j] = nt(wa[j, 3 * local :, :], r_.xh1[seg]).astype(BF)

        loop(2, out)

    def pull_heads(seg, first, count):
        def one(i):
            h = first + i
            j = h // per_block
            q, k, v = (qkv[seg, j, head_rows(h, part), :] for part in range(3))
            g_o = r_.got[j, head_rows(h, 0), :]
            p = pt[seg, h]
            d_v = nt(g_o, p).astype(BF)
            total_p = row_sum(g_o.astype(F32) * ot[seg, j, head_rows(h, 0), :].astype(F32))
            d_s = (p.astype(F32) * (tn(v, g_o) - total_p)).astype(BF)
            d_q = (nn(k, d_s) * 0.125).astype(BF)
            d_k = nt(q, d_s).astype(BF)
            for part, value in enumerate((d_q, d_k, d_v)):
                qkv[seg, j, head_rows(h, part), :] = value

        loop(count, one)

    def pull_rows(seg):
        def one(r):
            give(
                1, r,
                tn(qkv[seg, 0, :, rows(r)], wa[0, : 3 * local, :]) + tn(qkv[seg, 1, :, rows(r)], wa[1, : 3 * local, :]),
            )

        loop(head_count, one)

    def pull_x(seg):
        def one(r):
            value = hf[rows(r), :] + taken(1, r)
            acc[rows(r), :] = value
            r_.send_buf[1, r] = value.astype(BF)

        loop(head_count, one)
        both = pltpu.roll(acc[0:tail, :], tail - mem_rows, 0) + acc[seg_len - tail : seg_len, :]
        memory = jnp.where(is_mem, both, 0.0)
        r_.dinit[...] += jnp.where(flags[seg] > 0, memory, 0.0)
        if seg == 1:
            r_.carry[step - tail : step, :] = jnp.where(flags[1] > 0, 0.0, memory)

    def text_grad(seg):
        def one(r):
            r_.text_all[seg, rows(r), :] = nn(take_rows(r), r_.send_buf[1].reshape(seg_len, width)).astype(BF)

        loop(head_count, one)

    pull_two(1)
    loop(head_count, lambda i: pull_inner(1, i))
    pull_hidden(1)
    pull_one(1)
    pull_heads(1, 0, heads)
    pull_rows(1)
    pull_x(1)
    text_grad(1)
    back_send(1, 1)

    def cut(buf, kind, a, b):
        first, second = (px, py) if kind == 0 else (py, px)
        first = first if a == 0 else 1 - first
        second = second if b == 0 else 1 - second
        return buf.at[second, first] if kind == 0 else buf.at[first, second]

    sum_mates = ((x_mate, y_mate), (y_mate, x_mate))

    def sum_one(name, kind, b):
        buf, got, s, r = sums[name](kind)
        return push(cut(buf, kind, 1, b), got[0].at[b], s.at[b], r.at[b], sum_mates[kind][0])

    def sum_two(name, kind):
        buf, got, s, r = sums[name](kind)
        return push(cut(buf, kind, 0, 1), got[1], s.at[2], r.at[2], sum_mates[kind][1])

    def ffn_sum(d):
        zi = (z + d) % head_count

        def parts(kind):
            return (
                r_.fsend.at[kind, zi], (r_.f_one.at[kind, zi], r_.f_two.at[kind, zi]),
                r_.fsum_s.at[kind, zi], r_.fsum_r.at[kind, zi],
            )

        return parts

    sums = {d: ffn_sum(d) for d in range(head_count)}
    sums["a"] = lambda kind: (
        r_.asend.at[kind], (r_.a_one.at[kind], r_.a_two.at[kind]), r_.asum_s.at[kind], r_.asum_r.at[kind]
    )
    sums["v"] = lambda kind: (
        r_.vsend.at[kind], (r_.v_one.at[kind], r_.v_two.at[kind]), r_.vsum_s.at[kind], r_.vsum_r.at[kind]
    )

    def start_sum(name):
        for b in (1, 0):
            for kind in range(2):
                sum_one(name, kind, b).start()

    def adder(name):
        return add_block if isinstance(name, int) else add_blocks

    def go_on(name):
        for kind in range(2):
            buf, got, _, _ = sums[name](kind)
            sum_one(name, kind, 1).wait_recv()
            adder(name)(cut(buf, kind, 0, 1), got[0].at[1])
            sum_two(name, kind).start()
        for kind in range(2):
            buf, got, _, _ = sums[name](kind)
            sum_one(name, kind, 0).wait_recv()
            adder(name)(cut(buf, kind, 0, 0), got[0].at[0])

    def end_plane(name):
        for kind in range(2):
            buf, got, _, _ = sums[name](kind)
            sum_two(name, kind).wait_recv()
            adder(name)(cut(buf, kind, 0, 0), got[1])

    def sum_sent(name):
        for kind in range(2):
            for b in range(2):
                sum_one(name, kind, b).wait_send()
            sum_two(name, kind).wait_send()

    def z_out(kind, d):
        zi = (z + d) % head_count
        return push(
            cut(r_.fsend.at[kind, zi], kind, 0, 0), r_.f_z.at[kind, z], r_.fz_s.at[kind, d], r_.fz_r.at[kind, z],
            device(core, px, py, zi),
        )

    def z_in(kind, zs):
        return push(
            cut(r_.fsend.at[kind, z], kind, 0, 0), r_.f_z.at[kind, zs], r_.fz_s.at[kind, 0], r_.fz_r.at[kind, zs], sibling
        )

    def end_ffn(d):
        end_plane(d)
        if d > 0:
            for kind in range(2):
                z_out(kind, d).start()

    def last_out(name, k, h):
        buf, dst, s, r = last[name]
        return push(
            cut(buf.at[k], k, 0, 0).at[h], dst.at[z], s.at[k, h], r.at[z], device(h, px, py, 2 * core + k)
        )

    def last_here(name, k):
        buf, dst, _, _ = last[name]
        return pltpu.make_async_copy(cut(buf.at[k], k, 0, 0).at[core], dst.at[z], r_.last_sem.at["av".index(name)])

    last = {
        "a": (r_.asend, r_.a_z, r_.az_s, r_.az_r),
        "v": (r_.vsend, r_.v_z, r_.vz_s, r_.vz_r),
    }

    def last_each(name, here_do, away_do):
        for k in range(2):
            for h in range(2):
                here = (core == h) & (z == 2 * core + k)
                if here_do is not None:
                    pl.when(here)(lambda: here_do(last_here(name, k)))
                when_not(here, lambda: away_do(last_out(name, k, h)))

    def last_total(name):
        buf, dst, s, r = last[name]
        for zs in range(head_count):
            here = is_home & (z == zs)
            pl.when(here)(lambda: last_here(name, 0).wait())
            when_not(
                here, lambda: push(buf.at[0, 0, 0, 0], dst.at[zs], s.at[0, 0], r.at[zs], sibling).wait_recv()
            )
        value = dst[0].astype(F32)
        for zs in range(1, head_count):
            value = value + dst[zs].astype(F32)
        return value

    def ffn_grads(d):
        i = (z + d) % head_count
        pull_inner(0, i)
        for kind, (left, right) in enumerate(((r_.gp, r_.hb), (r_.u, r_.xh2))):
            value = tn(left[0, :, cols(i)], right[0]) + tn(left[1, :, cols(i)], right[1])
            for p in range(planes):
                r_.fsend[kind, i, p // 2, p % 2] = value[p * hid : (p + 1) * hid, :].astype(BF)
        start_sum(d)

    pull_two(0)
    ffn_grads(1)
    ffn_grads(2)
    go_on(1)
    ffn_grads(3)
    go_on(2)
    end_ffn(1)
    ffn_grads(0)
    dbin_pair = push(r_.dbin, r_.dbin_in, r_.pair_s.at[2], r_.pair_r.at[2], sibling)
    dbin_pair.start()
    pull_hidden(0)
    go_on(3)
    end_ffn(2)
    pull_one(0)
    pull_heads(0, 0, 3)
    go_on(0)
    end_ffn(3)
    pull_heads(0, 3, heads - 3)
    end_ffn(0)

    def attention_grads(i):
        wide = width // 2
        span = pl.ds(pl.multiple_of(i * wide, wide), wide)
        xt = [x[s, :, span].T for s in range(2)]
        gt = [r_.xh1[s, :, span].T for s in range(2)]
        part = hid_rows
        for k in range(2):
            qkv_g = nt(xt[0], qkv[0, k]) + nt(xt[1], qkv[1, k])
            out_g = nt(gt[0], ot[0, k]) + nt(gt[1], ot[1, k])
            for b in range(4):
                at = slice(b * part, (b + 1) * part)
                r_.asend[k, i, b // 2, b % 2, :, 0 : 3 * local] = qkv_g[at, :].astype(BF)
                r_.asend[k, i, b // 2, b % 2, :, 3 * local :] = out_g[at, :].astype(BF)

    hid_rows = width // dp_count
    attention_grads(1 - py)
    attention_grads(py)
    start_sum("a")
    pull_rows(0)
    pull_x(0)
    text_grad(0)
    back_send(1, 0)
    dbin_pair.wait()

    dbin_both = [jnp.where(core == h, r_.dbin[0:1, :], r_.dbin_in[0:1, :]) for h in range(2)]
    for k in range(2):
        r_.bqv[k] = sum(jnp.sum(qkv[s, k].astype(F32), axis=1, keepdims=True) for s in range(2))
    sg, dinit = r_.sg, r_.dinit
    r_.vec[...] = jnp.where(is_mem, dinit[...], 0.0)
    r_.vec[0:6, :] = sg[0:6, :]
    vtmp[...] = jnp.zeros_like(vtmp)

    def by_core(cut_of):
        return jnp.where(core == 0, cut_of(0), cut_of(1))

    qv_rows = [
        [
            jnp.sum(
                jnp.where(
                    lax.broadcasted_iota(jnp.int32, (HD, HD), 0) == lax.broadcasted_iota(jnp.int32, (HD, HD), 1),
                    r_.bqv[k, 2 * part * local + b * HD : 2 * part * local + (b + 1) * HD, :],
                    0.0,
                ),
                axis=0,
                keepdims=True,
            )
            for part in range(2)
            for b in range(per_block)
        ]
        for k in range(2)
    ]
    piece_b = HD // dp_count
    vec = r_.vec[...]

    def small_cut(k, p, h):
        dp_t = 2 * p + h

        def from_vec(c):
            at = (dp_t * head_count + 2 * c + k) * lanes
            return vec[:, at : at + lanes]

        def from_bin(c):
            at = ((2 * c + k) * planes + p) * hid
            return dbin_both[h][:, at : at + hid]

        vtmp[0:16, 0:lanes] = by_core(from_vec)
        vtmp[0:1, 32 : 32 + hid] = by_core(from_bin)
        for n, line in enumerate(qv_rows[k]):
            vtmp[1:2, 32 + n * piece_b : 32 + (n + 1) * piece_b] = line[:, dp_t * piece_b : (dp_t + 1) * piece_b]
        r_.vsend[k, p // 2, p % 2, h] = vtmp[...].astype(BF)

    for k in range(2):
        for p in range(planes):
            for h in range(2):
                small_cut(k, p, h)
    start_sum("v")
    go_on("a")
    go_on("v")
    end_plane("a")
    last_each("a", lambda c: c.start(), lambda c: c.start())
    end_plane("v")
    last_each("v", lambda c: c.start(), lambda c: c.start())

    for kind, out in enumerate((r_.win_o, r_.wback_o)):
        value = cut(r_.fsend.at[kind, z], kind, 0, 0)[...].astype(F32)
        for d in range(1, head_count):
            zs = (z + d) % head_count
            z_in(kind, zs).wait_recv()
            value = value + r_.f_z[kind, zs].astype(F32)
        out[...] = value
    r_.att_o[...] = last_total("a")
    r_.vec_o[...] = last_total("v")

    for name in (0, 1, 2, 3, "a", "v"):
        sum_sent(name)
    for d in range(1, head_count):
        for kind in range(2):
            z_out(kind, d).wait_send()
    for name in "av":
        last_each(name, None, lambda c: c.wait_send())
    for which in range(2):
        for seg in range(2):
            back_done(which, seg)
    for a in range(2, 4):
        rows_done(a)
    attention_outs(lambda c: c.wait_send())
    ffn_sent()
    for copy in pair:
        copy.wait_send()
    for k in range(2):

        def sent():
            for which in range(4):
                attention_plane(k, which).wait_send()

        pl.when(foreign[k])(sent)
    for zi in range(head_count):
        for kind in range(2):
            for which in range(3):
                side(kind, zi, which).wait_send()
    for i in range(column_size):
        small_out(i).wait_send()
    for i in range(3):
        small_plane(i).wait_send()
    r_.dt_o[...] = r_.dt_all[...]


def vmem(*shape, dtype=BF):
    return pltpu.VMEM(shape, dtype)


def f32(*shape):
    return pltpu.VMEM(shape, F32)


def sds(*shape, dtype=BF):
    return jax.ShapeDtypeStruct(shape, dtype)


def dma(*shape):
    return pltpu.SemaphoreType.DMA(shape)


ANY = pl.BlockSpec(memory_space=pl.ANY)
INV = pl.BlockSpec(memory_space=pltpu.VMEM)
INS = pl.BlockSpec(memory_space=pltpu.SMEM)


def end_kernel(mem_rows, hid, lanes, acts, dt, win, wback, att, vec, *outs):
    acts_o, dt_o, dinit_o, dqkv_o, dbqv_o, dwout_o, dwin_o, dwback_o, dbin_o, dgains_o, dbiases_o = outs
    acts_o[...] = acts[...]
    text_rows = dt_o.shape[2]
    for j in range(2):
        for s in range(2):
            dt_o[j, s] = dt[j, s, 0:text_rows, :]
    dinit_o[...] = vec[6 : 6 + mem_rows, 0:lanes]
    parts, _, local_width = dqkv_o.shape
    for t in range(parts):
        dqkv_o[t] = att[:, t * local_width : (t + 1) * local_width]
    per_block, _, slice_b = dbqv_o.shape
    for b in range(per_block):
        for part in range(2):
            at = 32 + (part * per_block + b) * slice_b
            dbqv_o[b, part : part + 1, :] = vec[1:2, at : at + slice_b]
    dwout_o[...] = att[:, parts * local_width :].T
    dwin_o[...] = win[...]
    dwback_o[...] = wback[...]
    dbin_o[...] = vec[0:1, 32 : 32 + hid]
    dgains_o[...] = vec[0:2, 0:lanes]
    dbiases_o[...] = vec[2:6, 0:lanes]


def by_chip(
    text, boundary, reset, memory_in, init_memory, w_qkv, b_qv, w_out, w_in, w_back, b_in, norm_gains, biases,
    cotangent,
):
    head_count = lax.axis_size("head")
    dp_count = lax.axis_size("dp")
    planes = dp_count // 2
    total = dp_count * head_count
    text_rows, width = text.shape[2], text.shape[3]
    block = cotangent.shape[2]
    seg_len = block * head_count
    mem_rows = memory_in.shape[1]
    local = w_qkv.shape[2]
    hid = w_in.shape[1]
    lanes = norm_gains.shape[1]
    heads = 2 * local // HD
    hidden = hid * planes * head_count
    share = width // dp_count

    inputs = dict(
        text=(text, INV),
        boundary=(boundary, INV),
        reset=(reset, INS),
        memory_in=(memory_in.transpose(1, 0, 2), INV),
        init_memory=(init_memory, INV),
        wq_t=(w_qkv.transpose(1, 2, 0).reshape(3 * local, width), ANY),
        w_out=(w_out, ANY),
        b_qv=(b_qv.transpose(1, 0, 2), INV),
        w_in_t=(w_in.T, INV),
        w_back=(w_back, INV),
        b_in=(b_in[None, :], INV),
        norm_gains=(norm_gains, INV),
        biases=(biases, INV),
        cotangent=(cotangent, ANY),
    )
    outputs = dict(
        acts_o=(sds(2, 2, block, width), ANY),
        dt_o=(sds(2, 2, block, width), INV),
        win_o=(sds(hid, width, dtype=F32), INV),
        wback_o=(sds(hid, width, dtype=F32), INV),
        att_o=(sds(share, width, dtype=F32), INV),
        vec_o=(sds(16, 128, dtype=F32), INV),
    )
    scratch = dict(
        text_pad=vmem(2, 2, block, width),
        text_all=vmem(2, seg_len, width),
        cot_all=vmem(2, seg_len, width),
        wa=vmem(2, 4 * local, width),
        wf=vmem(2, hidden, width),
        small=vmem(16, 128),
        small_all=vmem(total, 16, 128),
        seqf=f32(8, seg_len),
        seqf_in=f32(8, seg_len),
        seq=f32(8, seg_len),
        memp=vmem(16, width),
        memp_in=vmem(16, width),
        par=f32(16, width),
        bin_row=f32(1, hidden),
        bqv=f32(2, 3 * local, 1),
        x=vmem(2, seg_len, width),
        qkv=vmem(2, 2, 3 * local, seg_len),
        pt=vmem(2, heads, seg_len, seg_len),
        ot=vmem(2, 2, local, seg_len),
        hf=f32(seg_len, width),
        acc=f32(seg_len, width),
        xh1=vmem(2, seg_len, width),
        hb=vmem(2, seg_len, width),
        u=vmem(2, seg_len, hidden),
        gp=vmem(2, seg_len, hidden),
        xh2=vmem(2, seg_len, width),
        rs=f32(seg_len, 4),
        y=vmem(2, seg_len, width),
        got=vmem(2, local, seg_len),
        send_buf=vmem(2, head_count, block, width),
        recv_buf=vmem(2, head_count, block, width),
        cur_a=vmem(16, width),
        cur_b=vmem(16, width),
        carry=f32(block, width),
        sg=f32(8, width),
        dinit=f32(16, width),
        dbin=f32(8, hidden),
        dbin_in=f32(8, hidden),
        vec=f32(16, width),
        vtmp=f32(16, 128),
        dt_all=vmem(2, 2, block, width),
        fsend=vmem(2, head_count, 2, 2, hid, width),
        f_one=vmem(2, head_count, 2, hid, width),
        f_two=vmem(2, head_count, hid, width),
        f_z=vmem(2, head_count, hid, width),
        asend=vmem(2, 2, 2, 2, share, width),
        a_one=vmem(2, 2, 2, share, width),
        a_two=vmem(2, 2, share, width),
        a_z=vmem(head_count, share, width),
        vsend=vmem(2, 2, 2, 2, 16, 128),
        v_one=vmem(2, 2, 2, 16, 128),
        v_two=vmem(2, 2, 16, 128),
        v_z=vmem(head_count, 16, 128),
        small_s=dma(7),
        small_r=dma(4, 2),
        small_ps=dma(3),
        small_pr=dma(3),
        pair_s=dma(3),
        pair_r=dma(3),
        att_s=dma(3),
        att_r=dma(2, 2),
        plane_s=dma(2, 4),
        plane_r=dma(2, 4),
        local_sem=dma(2),
        rows_s=dma(4, 2, 2),
        rows_r=dma(4, 4),
        here_sem=dma(4),
        fwd_s=dma(4, 4),
        fwd_r=dma(4, 4),
        ffn_s=dma(5),
        ffn_r=dma(4),
        side_s=dma(4, 2, 3),
        side_r=dma(4, 2, 3),
        send_sem=dma(2, 4),
        recv_sem=dma(2, 4),
        back_s=dma(2, 2, 4),
        back_r=dma(2, 2, 2, 2),
        back_here_sem=dma(2, 2),
        fsum_s=dma(2, 4, 3),
        fsum_r=dma(2, 4, 3),
        asum_s=dma(2, 3),
        asum_r=dma(2, 3),
        vsum_s=dma(2, 3),
        vsum_r=dma(2, 3),
        fz_s=dma(2, 4),
        fz_r=dma(2, 4),
        az_s=dma(2, 2),
        az_r=dma(4),
        vz_s=dma(2, 2),
        vz_r=dma(4),
        last_sem=dma(2),
    )
    names = tuple(inputs) + tuple(outputs) + tuple(scratch)
    middle = pl.pallas_call(
        functools.partial(main_kernel, names, dp_count, head_count),
        out_shape=tuple(v[0] for v in outputs.values()),
        in_specs=[v[1] for v in inputs.values()],
        out_specs=tuple(v[1] for v in outputs.values()),
        scratch_shapes=list(scratch.values()),
        compiler_params=pltpu.CompilerParams(
            collective_id=0, has_side_effects=True, vmem_limit_bytes=VMEM_LIMIT
        ),
        name="layer",
    )(*(v[0] for v in inputs.values()))

    slice_b = HD // dp_count
    out = pl.pallas_call(
        functools.partial(end_kernel, mem_rows, hid, lanes),
        out_shape=(
            sds(2, 2, block, width),
            sds(2, 2, text_rows, width),
            sds(mem_rows, lanes, dtype=F32),
            sds(3, share, local, dtype=F32),
            sds(local // HD, 2, slice_b, dtype=F32),
            sds(local, share, dtype=F32),
            sds(hid, width, dtype=F32),
            sds(hid, width, dtype=F32),
            sds(1, hid, dtype=F32),
            sds(2, lanes, dtype=F32),
            sds(4, lanes, dtype=F32),
        ),
        in_specs=[INV] * 6,
        out_specs=tuple([INV] * 11),
        name="results",
    )(*middle)
    acts, d_text, d_init, d_qkv, d_bqv, d_wout, d_win, d_wback, d_bin, d_gains, d_biases = out
    return (
        acts, d_text, d_init,
        d_qkv.transpose(1, 0, 2),
        d_bqv.transpose(1, 0, 2),
        d_wout, d_win.T, d_wback, d_bin[0], d_gains, d_biases,
    )


def solution(mesh):
    body = by_chip if mesh.shape["dp"] == 8 and mesh.shape["head"] == 4 else local
    return jax.shard_map(
        body,
        mesh=mesh,
        in_specs=(
            P("dp", None, "head", None),
            P("dp", None, None),
            P("dp", None),
            P("dp", None, None),
            P(None, ("dp", "head")),
            P(None, None, "head"),
            P(None, "head", None),
            P("head", None),
            P(None, ("dp", "head")),
            P(("dp", "head"), None),
            P(("dp", "head")),
            P(None, ("dp", "head")),
            P(None, ("dp", "head")),
            P("dp", None, "head", None),
        ),
        out_specs=(
            P("dp", None, "head", None),
            P("dp", None, "head", None),
            P(None, ("dp", "head")),
            P("dp", None, "head"),
            P(None, "head", "dp"),
            P("head", "dp"),
            P(None, ("dp", "head")),
            P(("dp", "head"), None),
            P(("dp", "head")),
            P(None, ("dp", "head")),
            P(None, ("dp", "head")),
        ),
        check_vma=False,
    )
```

```python
import functools

import jax
import jax.numpy as jnp
from jax import lax
from jax.experimental import pallas as pl
from jax.experimental.pallas import tpu as pltpu
from jax.sharding import PartitionSpec as P

HD = 64
MESH = pl.DeviceIdType.MESH
BF = jnp.bfloat16
F32 = jnp.float32
VMEM_LIMIT = 64 * 1024 * 1024


def nn(a, b):
    return lax.dot_general(a, b, (((1,), (0,)), ((), ())), preferred_element_type=F32)


def nt(a, b):
    return lax.dot_general(a, b, (((1,), (1,)), ((), ())), preferred_element_type=F32)


def tn(a, b):
    return lax.dot_general(a, b, (((0,), (0,)), ((), ())), preferred_element_type=F32)


def place():
    dp, z = lax.axis_index("dp"), lax.axis_index("head")
    core, plane = dp % 2, dp // 2
    return core, plane % 2, plane // 2, z


def device(core, x, y, z):
    return ((y * 2 + x) * 2 + core, z)


def push(src, dst, send, recv, target):
    return pltpu.make_async_remote_copy(
        src_ref=src, dst_ref=dst, send_sem=send, recv_sem=recv, device_id=target, device_id_type=MESH
    )


def from_root(x, axis, root):
    mine = lax.axis_index(axis) == root
    return lax.psum(jnp.where(mine, x, jnp.zeros_like(x)), axis)


def layer_norm(values, gain_row, shift_row):
    center = values - jnp.mean(values, axis=-1, keepdims=True)
    spread = jnp.mean(center * center, axis=-1, keepdims=True)
    return center * lax.rsqrt(spread + 1e-05) * gain_row + shift_row


def gelu_tanh(values):
    return jax.nn.gelu(values, approximate=True)


def head_major(array, dim, dp_count, head_count):
    shape = array.shape
    size = shape[dim]
    split = array.reshape(
        shape[:dim] + (dp_count, head_count, size // (dp_count * head_count)) + shape[dim + 1 :]
    )
    return jnp.swapaxes(split, dim, dim + 1).reshape(shape)


def local(
    text,
    boundary,
    reset,
    memory_in,
    init_memory,
    w_qkv,
    b_qv,
    w_out,
    w_in,
    w_back,
    b_in,
    norm_gains,
    biases,
    cotangent,
):
    head_count = lax.axis_size("head")
    dp_count = lax.axis_size("dp")
    head_idx = lax.axis_index("head")
    batch_size = text.shape[0]
    width = text.shape[3]
    seg_rows = cotangent.shape[2]
    seg_len = seg_rows * head_count
    mem_rows = memory_in.shape[1]
    text_len = seg_len - 2 * mem_rows
    local_width = w_qkv.shape[2]
    local_heads = local_width // HD
    row_start = head_idx * seg_rows
    is_first = (head_idx == 0).astype(jnp.float32)
    is_final = (head_idx == head_count - 1).astype(jnp.float32)
    grad_dims = (1, 0, 0, 1, 1, 1)
    doc_ids = jnp.cumsum(boundary, axis=2)
    marks = jnp.full((batch_size, 2, mem_rows), -1, jnp.int32)
    labels = jnp.concatenate([marks, doc_ids, marks], axis=2)
    visible = (
        (labels[..., :, None] == labels[..., None, :])
        | (labels[..., :, None] < 0)
        | (labels[..., None, :] < 0)
    )
    bias_query = b_qv[0].reshape(local_width).astype(jnp.float32)
    bias_value = b_qv[1].reshape(local_width).astype(jnp.float32)
    shared = (
        lax.all_gather(w_in, ("dp", "head"), axis=1, tiled=True),
        lax.all_gather(w_back, ("dp", "head"), axis=0, tiled=True),
        lax.all_gather(b_in, ("dp", "head"), axis=0, tiled=True),
        lax.all_gather(norm_gains, ("dp", "head"), axis=1, tiled=True),
        lax.all_gather(biases, ("dp", "head"), axis=1, tiled=True),
        lax.all_gather(init_memory, ("dp", "head"), axis=1, tiled=True),
    )

    def fetch():
        return shared

    def attention_probs(query, key_rows, seg):
        scores = (
            jnp.einsum("sqhe,skhe->shqk", query, key_rows, preferred_element_type=jnp.float32)
            * 0.125
        )
        return jnp.where(visible[:, seg][:, None], scores, -1e30)

    def forward(seg, memory, ffn):
        w_in_all, w_back_all, b_in_all, gains_all, biases_all, unused = ffn
        gains_f = gains_all.astype(jnp.float32)
        biases_f = biases_all.astype(jnp.float32)
        local_text = lax.all_gather(text[:, seg], "head", axis=1, tiled=True)
        x_rows = jnp.concatenate([memory, local_text, memory], axis=1)
        mixed = jnp.einsum("srd,dce->srce", x_rows, w_qkv, preferred_element_type=jnp.float32)
        query = (
            (mixed[:, :, 0] + bias_query)
            .astype(jnp.bfloat16)
            .reshape(batch_size, seg_len, local_heads, HD)
        )
        key_rows = mixed[:, :, 1].astype(jnp.bfloat16).reshape(batch_size, seg_len, local_heads, HD)
        value = (
            (mixed[:, :, 2] + bias_value)
            .astype(jnp.bfloat16)
            .reshape(batch_size, seg_len, local_heads, HD)
        )
        masked = attention_probs(query, key_rows, seg)
        row_max = jnp.max(masked, axis=-1, keepdims=True)
        exp_terms = jnp.exp(masked - row_max)
        row_total = jnp.sum(exp_terms, axis=-1, keepdims=True)
        log_total = row_max + jnp.log(row_total)
        probs = (exp_terms / row_total).astype(jnp.bfloat16)
        attended = jnp.einsum("shqk,skhe->sqhe", probs, value, preferred_element_type=jnp.float32)
        attended = attended.astype(jnp.bfloat16).reshape(batch_size, seg_len, local_width)
        partial_out = jnp.einsum("srl,ld->srd", attended, w_out, preferred_element_type=jnp.float32)
        summed = lax.psum_scatter(
            partial_out.astype(jnp.bfloat16), "head", scatter_dimension=1, tiled=True
        ).astype(jnp.float32)
        own_rows = lax.dynamic_slice_in_dim(x_rows, row_start, seg_rows, 1).astype(jnp.float32)
        pre_norm = own_rows + summed + biases_f[1]
        hidden = layer_norm(pre_norm, gains_f[0], biases_f[0])
        hidden_low = hidden.astype(jnp.bfloat16)
        inner = jnp.einsum(
            "srd,df->srf", hidden_low, w_in_all, preferred_element_type=jnp.float32
        ) + b_in_all.astype(jnp.float32)
        active = gelu_tanh(inner).astype(jnp.bfloat16)
        outer = (
            jnp.einsum("srf,fd->srd", active, w_back_all, preferred_element_type=jnp.float32)
            + biases_f[2]
        )
        post_norm = hidden + outer
        result = layer_norm(post_norm, gains_f[1], biases_f[3])
        kept = (
            x_rows,
            query,
            key_rows,
            value,
            log_total,
            attended,
            pre_norm,
            hidden_low,
            inner,
            active,
            post_norm,
        )
        return (result, kept)

    def backward(seg, grad_out, kept, ffn):
        (
            x_rows,
            query,
            key_rows,
            value,
            log_total,
            attended,
            pre_norm,
            hidden_low,
            inner,
            active,
            post_norm,
        ) = kept
        w_in_all, w_back_all, b_in_all, gains_all, biases_all, unused = ffn
        gains_f = gains_all.astype(jnp.float32)
        biases_f = biases_all.astype(jnp.float32)
        unused_two, pull_two = jax.vjp(layer_norm, post_norm, gains_f[1], biases_f[3])
        grad_post, grad_gain_two, grad_shift_two = pull_two(grad_out)
        grad_outer = grad_post.astype(jnp.bfloat16)
        grad_ffn_bias = jnp.sum(grad_post, axis=(0, 1))
        grad_w_back = jnp.einsum(
            "srf,srd->fd", active, grad_outer, preferred_element_type=jnp.float32
        )
        grad_active = jnp.einsum(
            "srd,fd->srf", grad_outer, w_back_all, preferred_element_type=jnp.float32
        )
        unused_gelu, pull_gelu = jax.vjp(gelu_tanh, inner)
        grad_inner = pull_gelu(grad_active)[0].astype(jnp.bfloat16)
        grad_b_in = jnp.sum(grad_inner, axis=(0, 1), dtype=jnp.float32)
        grad_w_in = jnp.einsum(
            "srd,srf->df", hidden_low, grad_inner, preferred_element_type=jnp.float32
        )
        grad_hidden = grad_post + jnp.einsum(
            "srf,df->srd", grad_inner, w_in_all, preferred_element_type=jnp.float32
        )
        unused_one, pull_one = jax.vjp(layer_norm, pre_norm, gains_f[0], biases_f[0])
        grad_pre, grad_gain_one, grad_shift_one = pull_one(grad_hidden)
        grad_out_bias = jnp.sum(grad_pre, axis=(0, 1))
        grad_branch = lax.all_gather(grad_pre.astype(jnp.bfloat16), "head", axis=1, tiled=True)
        grad_w_out = jnp.einsum(
            "srl,srd->ld", attended, grad_branch, preferred_element_type=jnp.float32
        )
        grad_att = jnp.einsum("srd,ld->srl", grad_branch, w_out, preferred_element_type=jnp.float32)
        grad_att = grad_att.astype(jnp.bfloat16).reshape(batch_size, seg_len, local_heads, HD)
        masked = attention_probs(query, key_rows, seg)
        probs = jnp.exp(masked - log_total)
        grad_value = jnp.einsum(
            "shqk,sqhe->skhe",
            probs.astype(jnp.bfloat16),
            grad_att,
            preferred_element_type=jnp.float32,
        )
        grad_probs = jnp.einsum(
            "sqhe,skhe->shqk", grad_att, value, preferred_element_type=jnp.float32
        )
        grad_scores = probs * (grad_probs - jnp.sum(grad_probs * probs, axis=-1, keepdims=True))
        grad_scores = grad_scores.astype(jnp.bfloat16)
        grad_query = (
            jnp.einsum("shqk,skhe->sqhe", grad_scores, key_rows, preferred_element_type=jnp.float32)
            * 0.125
        )
        grad_key = (
            jnp.einsum("shqk,sqhe->skhe", grad_scores, query, preferred_element_type=jnp.float32)
            * 0.125
        )
        grad_mixed = jnp.stack([grad_query, grad_key, grad_value], axis=2).astype(jnp.bfloat16)
        grad_mixed = grad_mixed.reshape(batch_size, seg_len, 3, local_width)
        grad_bias_qv = jnp.stack(
            [
                jnp.sum(grad_mixed[:, :, 0], axis=(0, 1), dtype=jnp.float32),
                jnp.sum(grad_mixed[:, :, 2], axis=(0, 1), dtype=jnp.float32),
            ]
        ).reshape(2, local_heads, HD)
        grad_w_qkv = jnp.einsum(
            "srd,srce->dce", x_rows, grad_mixed, preferred_element_type=jnp.float32
        )
        grad_rows = jnp.einsum(
            "srce,dce->srd", grad_mixed, w_qkv, preferred_element_type=jnp.float32
        )
        placed = lax.dynamic_update_slice_in_dim(jnp.zeros_like(grad_rows), grad_pre, row_start, 1)
        grad_rows = grad_rows + placed
        grad_text_part = lax.psum_scatter(
            grad_rows[:, mem_rows : mem_rows + text_len].astype(jnp.bfloat16),
            "head",
            scatter_dimension=1,
            tiled=True,
        ).astype(jnp.float32)
        grad_memory = lax.psum(
            (grad_rows[:, :mem_rows] + grad_rows[:, seg_len - mem_rows :]).astype(jnp.bfloat16),
            "head",
        ).astype(jnp.float32)
        reset_flag = reset[:, seg] > 0
        grad_init = (
            jnp.sum(jnp.where(reset_flag[:, None, None], grad_memory, 0.0), axis=0) * is_first
        )
        ffn_grads = (
            grad_w_in,
            grad_w_back,
            grad_b_in,
            jnp.stack([grad_gain_one, grad_gain_two]),
            jnp.stack([grad_shift_one, grad_out_bias, grad_ffn_bias, grad_shift_two]),
            grad_init,
        )
        return (grad_text_part, grad_memory, (grad_w_qkv, grad_bias_qv, grad_w_out), ffn_grads)

    ffn_first = fetch()
    init_all = ffn_first[5]
    memory_one = jnp.where(reset[:, 0, None, None] > 0, init_all[None], memory_in)
    out_one, kept_one = forward(0, memory_one, ffn_first)
    tail_rows = out_one[:, seg_rows - mem_rows :].astype(jnp.bfloat16)
    carried = from_root(tail_rows, "head", head_count - 1)
    ffn_second = fetch()
    memory_two = jnp.where(reset[:, 1, None, None] > 0, ffn_second[5][None], carried)
    out_two, kept_two = forward(1, memory_two, ffn_second)
    activations = jnp.stack([out_one, out_two], axis=1).astype(jnp.bfloat16)
    ffn_third = fetch()
    text_two, memory_grad_two, attn_two, ffn_two = backward(
        1, cotangent[:, 1].astype(jnp.float32), kept_two, ffn_third
    )
    keep_flag = reset[:, 1, None, None] <= 0
    carried_grad = jnp.where(keep_flag, memory_grad_two, 0.0) * is_final
    grad_one = cotangent[:, 0].astype(jnp.float32) + jnp.concatenate(
        [jnp.zeros((batch_size, seg_rows - mem_rows, width), jnp.float32), carried_grad], axis=1
    )
    ffn_fourth = fetch()
    text_one, memory_grad_one, attn_one, ffn_one = backward(0, grad_one, kept_one, ffn_fourth)
    grads = jax.tree.map(lambda a, b: a + b, ffn_one, ffn_two)
    ffn_total = tuple((head_major(g, d, dp_count, head_count) for g, d in zip(grads, grad_dims)))
    partial_sums = (
        lax.psum_scatter(
            ffn_total[0].astype(jnp.bfloat16), "head", scatter_dimension=1, tiled=True
        ).astype(jnp.float32),
        lax.psum_scatter(
            ffn_total[1].astype(jnp.bfloat16), "head", scatter_dimension=0, tiled=True
        ).astype(jnp.float32),
        lax.psum_scatter(
            ffn_total[2].astype(jnp.bfloat16), "head", scatter_dimension=0, tiled=True
        ).astype(jnp.float32),
        lax.psum_scatter(
            ffn_total[3].astype(jnp.bfloat16), "head", scatter_dimension=1, tiled=True
        ).astype(jnp.float32),
        lax.psum_scatter(
            ffn_total[4].astype(jnp.bfloat16), "head", scatter_dimension=1, tiled=True
        ).astype(jnp.float32),
        lax.psum_scatter(
            ffn_total[5].astype(jnp.bfloat16), "head", scatter_dimension=1, tiled=True
        ).astype(jnp.float32),
    )
    reduced = (
        lax.psum_scatter(partial_sums[0], "dp", scatter_dimension=1, tiled=True),
        lax.psum_scatter(partial_sums[1], "dp", scatter_dimension=0, tiled=True),
        lax.psum_scatter(partial_sums[2], "dp", scatter_dimension=0, tiled=True),
        lax.psum_scatter(partial_sums[3], "dp", scatter_dimension=1, tiled=True),
        lax.psum_scatter(partial_sums[4], "dp", scatter_dimension=1, tiled=True),
        lax.psum_scatter(partial_sums[5], "dp", scatter_dimension=1, tiled=True),
    )
    attn_total = jax.tree.map(lambda a, b: a + b, attn_one, attn_two)
    grad_qkv, grad_bqv, grad_wout = (
        lax.psum_scatter(attn_total[0], "dp", scatter_dimension=0, tiled=True),
        lax.psum_scatter(attn_total[1], "dp", scatter_dimension=2, tiled=True),
        lax.psum_scatter(attn_total[2], "dp", scatter_dimension=1, tiled=True),
    )
    grad_text = jnp.stack([text_one, text_two], axis=1).astype(jnp.bfloat16)
    grad_win, grad_wback, grad_bin, grad_gains, grad_biases, grad_init = reduced
    return (
        activations,
        grad_text,
        grad_init,
        grad_qkv,
        grad_bqv,
        grad_wout,
        grad_win,
        grad_wback,
        grad_bin,
        grad_gains,
        grad_biases,
    )


class Refs:
    pass


def by_name(names, values):
    refs = Refs()
    for name, value in zip(names, values, strict=True):
        setattr(refs, name, value)
    return refs


def loop(count, body):
    def run(i, unused):
        body(i)
        return unused

    lax.fori_loop(0, count, run, 0)


def add_blocks(dst, src):
    def body(i):
        dst[i] = (dst[i].astype(F32) + src[i].astype(F32)).astype(BF)

    loop(dst.shape[0], body)


def add_block(dst, src):
    dst[...] = (dst[...].astype(F32) + src[...].astype(F32)).astype(BF)


def as_column(row):
    n = row.shape[1]
    down = lax.broadcasted_iota(jnp.int32, (n, n), 0)
    across = lax.broadcasted_iota(jnp.int32, (n, n), 1)
    return jnp.sum(jnp.where(down == across, row, 0.0), axis=1, keepdims=True)


def norm(v):
    center = v - jnp.mean(v, axis=-1, keepdims=True)
    scale = lax.rsqrt(jnp.mean(center * center, axis=-1, keepdims=True) + 1e-05)
    return center * scale, scale


def pull_norm(g, hat, scale):
    m1 = jnp.mean(g, axis=-1, keepdims=True)
    m2 = jnp.mean(g * hat, axis=-1, keepdims=True)
    return scale * (g - m1 - hat * m2)


def row_sum(v):
    return jnp.sum(v, axis=0, keepdims=True)


def main_kernel(names, dp_count, head_count, *values):
    r_ = by_name(names, values)
    core, px, py, z = place()
    plane = py * 2 + px
    x_plane, y_plane = py * 2 + 1 - px, (1 - py) * 2 + px
    me = (plane * 2 + core) * head_count + z
    total = dp_count * head_count
    planes = dp_count // 2
    is_home = core == z // 2
    away = jnp.logical_not(is_home)
    sibling = device(1 - core, px, py, z)
    x_mate, y_mate = device(core, 1 - px, py, z), device(core, px, 1 - py, z)
    mirror = z // 2

    def from_end(i):
        return i + mirror * (head_count - 1 - 2 * i)

    depth = from_end(z)
    inside = depth == 1
    order = [from_end(i) for i in (depth, 1 - depth, 2, 3)]

    x, qkv, pt, ot, wa, wf = r_.x, r_.qkv, r_.pt, r_.ot, r_.wa, r_.wf
    hf, acc, par = r_.hf, r_.acc, r_.par
    seg_len, width = x.shape[1], x.shape[2]
    hidden = r_.u.shape[2]
    heads = pt.shape[1]
    local = ot.shape[2]
    hid = r_.w_back.shape[0]
    lanes = r_.norm_gains.shape[1]
    mem_rows = r_.memory_in.shape[0]
    text_rows = r_.text.shape[1]
    per_block = local // HD
    step = seg_len // head_count
    piece = step // 2
    chunk = hidden // head_count
    tail = 16
    tail_at = pl.ds(seg_len - tail, tail)

    def rows(r):
        return pl.ds(pl.multiple_of(r * step, step), step)

    def cols(i):
        return pl.ds(pl.multiple_of(i * chunk, chunk), chunk)

    def head_rows(h, part):
        return pl.ds(pl.multiple_of((h % per_block) * HD + part * local, HD), HD)

    def column(i):
        h = core if i < head_count - 1 else 1 - core
        zt = (z + 1 + i) % head_count
        return (plane * 2 + h) * head_count + zt, device(h, px, py, zt)

    column_size = 2 * head_count - 1

    def when_not(cond, body):
        pl.when(jnp.logical_not(cond))(body)

    share = local
    half = share // 2

    def attention_out(i, which):
        zt = (z + 1 + i) % head_count
        at = pl.multiple_of((share * jnp.minimum(plane, planes - 2) if which == 0 else 0) + half * core, half)
        src = (r_.wq_t, r_.w_out)[which]
        return push(
            src.at[pl.ds(at, half)], wa.at[z % 2, pl.ds(pl.multiple_of(share * plane + half * core, half), half)],
            r_.att_s.at[i], r_.att_r.at[z % 2, core], device(z // 2, px, py, zt),
        )

    def attention_outs(do):
        for which, mine in enumerate((plane < planes - 1, plane == planes - 1)):

            def each():
                for i in range(head_count - 1):
                    do(attention_out(i, which))

            pl.when(mine)(each)

    def attention_in(k, h):
        span = pl.ds(pl.multiple_of(share * plane + half * h, half), half)
        return push(r_.w_out.at[pl.ds(0, half)], wa.at[k, span], r_.att_s.at[0], r_.att_r.at[k, h], sibling)

    def attention_plane(k, which):
        at, count, mate = (
            (share * plane, share, x_mate),
            (share * plane, share, y_mate),
            (share * x_plane, half, y_mate),
            (share * y_plane + half, half, x_mate),
        )[which]
        block = pl.ds(pl.multiple_of(at, half), count)
        return push(
            wa.at[k, block], wa.at[k, block], r_.plane_s.at[k, which], r_.plane_r.at[k, which], mate
        )

    own_attention = [
        pltpu.make_async_copy(r_.wq_t, wa.at[z % 2, pl.ds(0, 3 * local)], r_.local_sem.at[0]),
        pltpu.make_async_copy(r_.w_out, wa.at[z % 2, pl.ds(3 * local, local)], r_.local_sem.at[1]),
    ]
    foreign = [jnp.logical_not(is_home & (z % 2 == k)) for k in range(2)]

    def rows_src(a, j, h):
        src = r_.text_pad if a < 2 else r_.cotangent
        return src.at[j, a % 2, pl.ds(h * piece, piece)]

    def rows_dst(a, zs, h):
        dst = r_.text_all if a < 2 else r_.cot_all
        return dst.at[a % 2, pl.ds(pl.multiple_of(zs * step + h * piece, piece), piece)]

    def rows_out(a, j, h):
        return push(
            rows_src(a, j, h), rows_dst(a, z, h), r_.rows_s.at[a, j, h], r_.rows_r.at[a, z],
            device(h, px, py, 2 * core + j),
        )

    def rows_here(a, j, h):
        return pltpu.make_async_copy(rows_src(a, j, h), rows_dst(a, z, h), r_.here_sem.at[a])

    def rows_send(a):
        for j in range(2):
            for h in range(2):
                here = (core == h) & (z == 2 * core + j)
                pl.when(here)(lambda: rows_here(a, j, h).start())
                when_not(here, lambda: rows_out(a, j, h).start())

    def rows_forward(a, zs, h):
        ref = rows_dst(a, zs, h)
        return push(ref, ref, r_.fwd_s.at[a, zs], r_.fwd_r.at[a, zs], sibling)

    def rows_pass(a):
        for zs in range(head_count):
            here = is_home & (z == zs)
            pl.when(here)(lambda: rows_here(a, z % 2, core).wait())
            when_not(
                here,
                lambda: push(
                    rows_src(a, 0, 0), rows_dst(a, zs, core), r_.rows_s.at[a, 0, 0], r_.rows_r.at[a, zs], sibling
                ).wait_recv(),
            )
            rows_forward(a, zs, core).start()

    def rows_ready(a):
        for zs in range(head_count):
            rows_forward(a, zs, 1 - core).wait_recv()

    def rows_done(a):
        for j in range(2):
            for h in range(2):
                when_not((core == h) & (z == 2 * core + j), lambda: rows_out(a, j, h).wait_send())
        for zs in range(head_count):
            rows_forward(a, zs, core).wait_send()

    def hidden_block(p, zi):
        return pl.ds(pl.multiple_of((zi * planes + p) * hid, hid), hid)

    def ffn_push(zi, to, slot):
        ref = wf.at[:, hidden_block(plane, zi)]
        return push(ref, ref, r_.ffn_s.at[slot], r_.ffn_r.at[zi], device(core, px, py, to))

    ffn_hops = [(0, from_end(1 - depth)), (0, from_end(2)), (1, from_end(2)), (2, from_end(0)), (3, from_end(0))]

    def ffn_hop(i):
        which, to = ffn_hops[i]
        return ffn_push(order[which], to, i)

    def ffn_own():
        ffn_hop(0).start()
        pl.when(inside)(ffn_hop(1).start)

    def ffn_one(n):
        ffn_push(order[n], z, 0).wait_recv()
        pl.when(inside)(ffn_hop(n + 1).start)
        side_first(order[n])

    def ffn_sent():
        ffn_hop(0).wait_send()

        def rest():
            for i in range(1, 5):
                ffn_hop(i).wait_send()

        pl.when(inside)(rest)

    def side(kind, zi, which):
        p, mate = (
            (plane, x_mate),
            (plane, y_mate),
            (x_plane, y_mate) if kind == 0 else (y_plane, x_mate),
        )[which]
        ref = wf.at[kind, hidden_block(p, zi)]
        return push(ref, ref, r_.side_s.at[zi, kind, which], r_.side_r.at[zi, kind, which], mate)

    def side_first(zi):
        for kind in range(2):
            side(kind, zi, 0).start()
            side(kind, zi, 1).start()

    def ffn_two(n):
        zi = order[n]
        side(0, zi, 0).wait_recv()
        side(0, zi, 2).start()
        side(1, zi, 1).wait_recv()
        side(1, zi, 2).start()

    def ffn_ready(n):
        zi = order[n]
        side(0, zi, 1).wait_recv()
        side(1, zi, 0).wait_recv()
        side(0, zi, 2).wait_recv()
        side(1, zi, 2).wait_recv()

    def small_out(i):
        return push(r_.small, r_.small_all.at[me], r_.small_s.at[i], r_.small_r.at[z, core], column(i)[1])

    def small_in(i):
        at, (dp_i, z_i) = column(i)
        return push(r_.small, r_.small_all.at[at], r_.small_s.at[i], r_.small_r.at[z_i, dp_i % 2], sibling)

    def small_plane(i):
        p, mate = ((plane, x_mate), (plane, y_mate), (x_plane, y_mate))[i]
        ref = r_.small_all.at[pl.ds(p * 2 * head_count, 2 * head_count)]
        return push(ref, ref, r_.small_ps.at[i], r_.small_pr.at[i], mate)

    pair = [
        push(r_.seqf, r_.seqf_in, r_.pair_s.at[0], r_.pair_r.at[0], sibling),
        push(r_.memp, r_.memp_in, r_.pair_s.at[1], r_.pair_r.at[1], sibling),
    ]

    barrier = pltpu.get_barrier_semaphore()
    far = [device(core, px, py, (z + i) % head_count) for i in range(1, head_count)]
    far = far + [device(core, 1 - px, py, (z + i) % head_count) for i in range(head_count)]
    far = far + [device(core, px, 1 - py, (z + i) % head_count) for i in range(head_count)]
    far = far + [device(core, 1 - px, 1 - py, (z + i) % head_count) for i in range(head_count)]
    mates = far + [column(i)[1] for i in range(head_count - 1, column_size)]
    for mate in mates:
        pl.semaphore_signal(barrier, inc=1, device_id=mate, device_id_type=MESH)
    for j in range(2):
        for s in range(2):
            r_.text_pad[j, s, 0:text_rows, :] = r_.text[j].astype(F32)[:, s, :].astype(BF)
            r_.text_pad[j, s, text_rows:step, :] = jnp.zeros((step - text_rows, width), BF)
    wf[0, hidden_block(plane, z), :] = r_.w_in_t[...]
    wf[1, hidden_block(plane, z), :] = r_.w_back[...]
    vtmp = r_.vtmp
    vtmp[...] = jnp.zeros_like(vtmp)
    vtmp[0:2, 0:lanes] = r_.norm_gains[...].astype(F32)
    vtmp[2:6, 0:lanes] = r_.biases[...].astype(F32)
    vtmp[6 : 6 + mem_rows, 0:lanes] = r_.init_memory[...].astype(F32)
    vtmp[0:1, 32 : 32 + hid] = r_.b_in[...].astype(F32)
    for b in range(per_block):
        pair_b = r_.b_qv[b].astype(F32)
        for part in range(2):
            vtmp[1 + part * per_block + b : 2 + part * per_block + b, 32 : 32 + HD] = pair_b[part : part + 1, :]
    r_.small[...] = vtmp[...].astype(BF)
    r_.small_all[me] = r_.small[...]
    seqf = r_.seqf
    marks = r_.boundary[z % 2].astype(F32).astype(BF)
    text_len = marks.shape[1]
    n_from = lax.broadcasted_iota(jnp.int32, (text_len, seg_len), 0)
    n_to = lax.broadcasted_iota(jnp.int32, (text_len, seg_len), 1) - mem_rows
    counts = nn(marks, jnp.where(n_from <= n_to, 1.0, 0.0).astype(BF))
    at_row = lax.broadcasted_iota(jnp.int32, (2, seg_len), 1)
    seqf[...] = jnp.zeros_like(seqf)
    seqf[0:2, :] = jnp.where((at_row >= mem_rows) & (at_row < seg_len - mem_rows), counts, -1.0)
    for s in range(2):
        seqf[2 + s : 3 + s, :] = jnp.full((1, seg_len), r_.reset[z % 2, s].astype(F32))
    r_.memp[...] = jnp.zeros_like(r_.memp)
    both_in = r_.memory_in[...].astype(F32)
    r_.memp[0:mem_rows, :] = jnp.where(z % 2 == 0, both_in[:, 0, :], both_in[:, 1, :]).astype(BF)
    for ref in (r_.sg, r_.dinit, r_.dbin, r_.carry):
        ref[...] = jnp.zeros_like(ref)
    pl.semaphore_wait(barrier, len(mates))

    for i in range(column_size):
        small_out(i).start()
    for copy in pair:
        copy.start()
    side_first(z)
    attention_outs(lambda c: c.start())

    def keep_own():
        for copy in own_attention:
            copy.start()

    pl.when(is_home)(keep_own)
    rows_send(0)
    ffn_own()

    def attention_to_plane(k):
        for h in range(2):
            attention_in(k, h).wait_recv()
        attention_plane(k, 0).start()
        attention_plane(k, 1).start()

    def attention_across(k):
        attention_plane(k, 0).wait_recv()
        attention_plane(k, 2).start()
        attention_plane(k, 1).wait_recv()
        attention_plane(k, 3).start()

    for i in range(column_size):
        small_in(i).wait_recv()
    small_plane(0).start()
    small_plane(1).start()
    ffn_two(0)
    small_plane(0).wait_recv()
    small_plane(2).start()
    for k in range(2):
        pl.when(foreign[k])(lambda: attention_to_plane(k))

    for copy in pair:
        copy.wait_recv()
    small_plane(1).wait_recv()
    small_plane(2).wait_recv()
    for i in range(total):
        par[0:16, lanes * i : lanes * (i + 1)] = r_.small_all[i, 0:16, 0:lanes].astype(F32)
    for zi in range(head_count):
        for p in range(planes):
            at = (zi * planes + p) * hid
            line = r_.small_all[(2 * p + core) * head_count + zi].astype(F32)
            r_.bin_row[0:1, at : at + hid] = line[0:1, 32 : 32 + hid]
    r_.bqv[...] = jnp.zeros_like(r_.bqv)
    for k in range(2):
        lines = r_.small_all[2 * core + k].astype(F32)
        for part in range(2):
            for b in range(per_block):
                line = lines[1 + part * per_block + b : 2 + part * per_block + b, 32 : 32 + HD]
                at = 2 * part * local + b * HD
                r_.bqv[k, at : at + HD, :] = as_column(line)
    seq = jnp.where(is_home, seqf[...], r_.seqf_in[...])
    seqf_out = r_.seq
    seqf_out[...] = seq
    flags = [seqf_out[2 + s : 3 + s, 0:1] for s in range(2)]
    tail_row = lax.broadcasted_iota(jnp.int32, (tail, width), 0)
    is_mem = tail_row >= tail - mem_rows
    init_b = jnp.where(is_mem, par[...], 0.0)
    given = jnp.where(is_home, r_.memp[...].astype(F32), r_.memp_in[...].astype(F32))
    first_b = jnp.where(flags[0] > 0, init_b, pltpu.roll(given, tail - mem_rows, 0))
    r_.cur_b[...] = first_b.astype(BF)
    r_.cur_a[...] = pltpu.roll(first_b, mem_rows, 0).astype(BF)

    def take_rows(r):
        inside = lax.broadcasted_iota(jnp.int32, (step, seg_len), 0)
        nat = lax.broadcasted_iota(jnp.int32, (step, seg_len), 1)
        return jnp.where((nat == r * text_rows + inside + mem_rows) & (inside < text_rows), 1.0, 0.0).astype(BF)

    def place_rows(r):
        nat = lax.broadcasted_iota(jnp.int32, (step, seg_len), 0) + r * step
        pad = lax.broadcasted_iota(jnp.int32, (step, seg_len), 1)
        inside = pad & (step - 1)
        target = (pad // step) * text_rows + inside + mem_rows
        return jnp.where((nat == target) & (inside < text_rows), 1.0, 0.0).astype(BF)

    def exchange(slot, r):
        return push(
            r_.send_buf.at[slot, r], r_.recv_buf.at[slot, r], r_.send_sem.at[slot, r], r_.recv_sem.at[slot, r],
            sibling,
        )

    def give(slot, r, part):
        acc[rows(r), :] = part
        r_.send_buf[slot, r] = part.astype(BF)
        exchange(slot, r).start()

    def taken(slot, r):
        exchange(slot, r).wait()
        return acc[rows(r), :] + r_.recv_buf[slot, r].astype(F32)

    def back_copy(which, seg, zt):
        src, dst = ((r_.y, r_.acts_o), (r_.text_all, r_.text_pad))[which]
        span = pl.ds(pl.multiple_of(zt * step + core * piece, piece), piece)
        return src.at[seg, span], dst.at[z % 2, seg, pl.ds(core * piece, piece)]

    def back_out(which, seg, i):
        zt = (z + i) % head_count
        src, dst = back_copy(which, seg, zt)
        return push(
            src, dst, r_.back_s.at[which, seg, i], r_.back_r.at[which, seg, z % 2, core], device(z // 2, px, py, zt)
        )

    def back_here(which, seg):
        src, dst = back_copy(which, seg, z)
        return pltpu.make_async_copy(src, dst, r_.back_here_sem.at[which, seg])

    def back_send(which, seg):
        pl.when(is_home)(lambda: back_here(which, seg).start())
        pl.when(away)(lambda: back_out(which, seg, 0).start())
        for i in range(1, head_count):
            back_out(which, seg, i).start()

    def back_sent(which, seg):
        pl.when(is_home)(lambda: back_here(which, seg).wait())
        pl.when(away)(lambda: back_out(which, seg, 0).wait_send())
        for i in range(1, head_count):
            back_out(which, seg, i).wait_send()

    def back_done(which, seg):
        dst = (r_.acts_o, r_.text_pad)[which]
        for j in range(2):
            for h in range(2):
                when_not(
                    (core == h) & (z == 2 * core + j),
                    lambda: push(
                        r_.text_all.at[seg, pl.ds(0, piece)], dst.at[j, seg, pl.ds(h * piece, piece)],
                        r_.back_s.at[which, seg, 0], r_.back_r.at[which, seg, j, h], sibling,
                    ).wait_recv(),
                )

    def tail_z(which, i):
        zt = (z + 1 + i) % head_count
        to = device(core, px, py, zt)
        dst = r_.factors.at[which, z, plane]
        return push(r_.factor_out.at[which, zt], dst, r_.tg_s.at[which, i], r_.tg_r.at[which, z], to)

    def tail_z_in(which, i):
        zs = (z + 1 + i) % head_count
        dst = r_.factors.at[which, zs, plane]
        return push(r_.factor_out.at[which, zs], dst, r_.tg_s.at[which, i], r_.tg_r.at[which, zs], sibling)

    def tail_plane(which, i):
        p, to = ((plane, x_mate), (plane, y_mate), (x_plane, y_mate))[i]
        buf = r_.factors.at[which, :, p]
        return push(buf, buf, r_.tg_s.at[which, 3 + i], r_.tg_r.at[which, head_count + i], to)

    def tail_gather(which, stage):
        if stage == 0:
            for i in range(head_count - 1):
                tail_z(which, i).start()
            r_.factors[which, z, plane] = r_.factor_out[which, z]
        elif stage == 1:
            for i in range(head_count - 1):
                tail_z_in(which, i).wait_recv()
            tail_plane(which, 0).start()
            tail_plane(which, 1).start()
        elif stage == 2:
            tail_plane(which, 0).wait_recv()
            tail_plane(which, 2).start()
        elif stage == 3:
            tail_plane(which, 1).wait_recv()
            tail_plane(which, 2).wait_recv()
        else:
            for i in range(head_count - 1):
                tail_z(which, i).wait_send()
            for i in range(3):
                tail_plane(which, i).wait_send()

    def tail_put(which, hidden_rows, units):
        for zt in range(head_count):
            r_.factor_out[which, zt, :, 0:width] = hidden_rows
            r_.factor_out[which, zt, :, width:] = units[:, zt * chunk : (zt + 1) * chunk]
        tail_gather(which, 0)

    def tail_products():
        down = lax.broadcasted_iota(jnp.int32, (chunk, 128), 0)
        across = lax.broadcasted_iota(jnp.int32, (chunk, 128), 1)
        pick = jnp.where((down == plane * hid + across) & (across < hid), 1.0, 0.0).astype(BF)
        all_rows = planes * head_count * tail
        parts = [r_.factors[which].reshape(all_rows, width + chunk) for which in range(2)]
        units = [nn(part[:, width:], pick).astype(BF) for part in parts]
        return [tn(units[1], parts[0][:, 0:width])[0:hid, :], tn(units[0], parts[1][:, 0:width])[0:hid, :]]

    def build(seg):
        def one(r):
            x[seg, rows(r), :] = nn(place_rows(r), r_.text_all[seg]).astype(BF)

        loop(head_count, one)
        x[seg, 0:tail, :] = x[seg, 0:tail, :] + r_.cur_a[...]
        x[seg, seg_len - tail : seg_len, :] = x[seg, seg_len - tail : seg_len, :] + r_.cur_b[...]
        right = r_.seq[seg : seg + 1, :]
        left = as_column(right)
        acc[:, 0:seg_len] = jnp.where((left == right) | (left < 0) | (right < 0), 0.0, -1e30)

    def project(seg):
        def one(i):
            j, t = i // 3, i % 3
            at = pl.ds(pl.multiple_of(t * local, local), local)
            value = nt(wa[j, at, :], x[seg]) + r_.bqv[j, at, :]
            qkv[seg, j, at, :] = (value * jnp.where(t == 0, 0.125, 1.0)).astype(BF)

        loop(6, one)

    def attend(seg, first, count):
        def one(i):
            h = first + i
            j = h // per_block
            q, k, v = (qkv[seg, j, head_rows(h, part), :] for part in range(3))
            s = tn(k, q) + acc[:, 0:seg_len]
            e = jnp.exp(s - jnp.max(s, axis=0, keepdims=True))
            p = (e * (1.0 / jnp.sum(e, axis=0, keepdims=True))).astype(BF)
            pt[seg, h] = p
            ot[seg, j, head_rows(h, 0), :] = nn(v, p).astype(BF)

        loop(count, one)

    def out_project(seg):
        def one(r):
            give(
                0, r,
                tn(ot[seg, 0, :, rows(r)], wa[0, 3 * local :, :]) + tn(ot[seg, 1, :, rows(r)], wa[1, 3 * local :, :]),
            )

        loop(head_count, one)

    def norm_one(seg):
        def one(r):
            hat, scale = norm(x[seg, rows(r), :].astype(F32) + taken(0, r) + par[3:4, :])
            r_.xh1[seg, rows(r), :] = hat.astype(BF)
            r_.rs[rows(r), 2 * seg : 2 * seg + 1] = scale
            h = hat * par[0:1, :] + par[2:3, :]
            hf[rows(r), :] = h
            r_.hb[seg, rows(r), :] = h.astype(BF)

        loop(head_count, one)

    def inner(seg, i):
        v = nt(r_.hb[seg], wf[0, cols(i), :]) + r_.bin_row[:, cols(i)]
        c0 = 0.7978845608028654
        sq = v * v
        th = jnp.tanh(v * (c0 + (c0 * 0.044715) * sq))
        up = 0.5 + 0.5 * th
        r_.u[seg, :, cols(i)] = (v * up).astype(BF)
        slope = up + (0.5 * v) * (1.0 - th * th) * (c0 + (3 * c0 * 0.044715) * sq)
        r_.gp[seg, :, cols(i)] = slope.astype(BF)

    def outer(seg):
        loop(head_count, lambda r: give(1, r, nn(r_.u[seg, rows(r), :], wf[1])))

    def norm_two(seg):
        def one(r):
            hat, scale = norm(hf[rows(r), :] + taken(1, r) + par[4:5, :])
            r_.xh2[seg, rows(r), :] = hat.astype(BF)
            r_.rs[rows(r), 2 * seg + 1 : 2 * seg + 2] = scale
            r_.y[seg, rows(r), :] = (hat * par[1:2, :] + par[5:6, :]).astype(BF)

        loop(head_count, one)

    def next_memory():
        last = r_.y[0, tail_at, :].astype(F32)
        memory = jnp.where(is_mem, jnp.where(flags[1] > 0, par[...], last), 0.0)
        r_.cur_b[...] = memory.astype(BF)
        r_.cur_a[...] = pltpu.roll(memory, mem_rows, 0).astype(BF)

    for k in range(2):
        pl.when(foreign[k])(lambda: attention_across(k))
    rows_pass(0)
    rows_ready(0)
    build(0)
    ffn_one(1)
    for k in range(2):

        def last_part():
            attention_plane(k, 2).wait_recv()
            attention_plane(k, 3).wait_recv()

        pl.when(foreign[k])(last_part)

    def kept_own():
        for copy in own_attention:
            copy.wait()

    pl.when(is_home)(kept_own)
    project(0)
    ffn_one(2)
    attend(0, 0, 2)
    ffn_two(1)
    attend(0, 2, 2)
    ffn_one(3)
    rows_send(1)
    rows_send(3)
    attend(0, 4, heads - 4)
    out_project(0)
    ffn_two(2)
    norm_one(0)
    for n in range(2):
        ffn_ready(n)
        inner(0, order[n])
    ffn_two(3)
    for n in range(2, head_count):
        ffn_ready(n)
        inner(0, order[n])
    outer(0)
    rows_pass(1)
    rows_done(0)
    rows_done(1)
    rows_send(2)
    norm_two(0)
    next_memory()
    tail_put(0, r_.hb[0, tail_at, :], r_.u[0, tail_at, :])

    rows_ready(1)
    build(1)
    project(1)
    attend(1, 0, heads)
    rows_pass(3)
    back_send(0, 0)
    out_project(1)
    norm_one(1)
    loop(head_count, lambda i: inner(1, i))
    rows_pass(2)
    outer(1)
    norm_two(1)
    back_send(0, 1)
    rows_ready(3)
    rows_ready(2)

    def pull_two_part(seg, g_y, hat, scale):
        pre = pull_norm(g_y * par[1:2, :], hat, scale)
        r_.sg[1:2, :] += row_sum(g_y * hat)
        r_.sg[5:6, :] += row_sum(g_y)
        r_.sg[4:5, :] += row_sum(pre)
        return pre.astype(BF)

    def pull_two(seg):
        def one(r):
            g_y = r_.cot_all[seg, rows(r), :].astype(F32)
            if seg == 0:
                below = lax.broadcasted_iota(jnp.int32, (step, width), 0) + r * step
                g_y = jnp.where(below < seg_len - tail, g_y, 0.0)
            hat = r_.xh2[seg, rows(r), :].astype(F32)
            r_.xh2[seg, rows(r), :] = pull_two_part(seg, g_y, hat, r_.rs[rows(r), 2 * seg + 1 : 2 * seg + 2])

        loop(head_count, one)

    def keep_tail():
        r_.xh2_t[...] = r_.xh2[0, tail_at, :]
        r_.gp_t[...] = r_.gp[0, tail_at, :]

    def pull_tail():
        g_y = r_.cot_all[0, tail_at, :].astype(F32) + r_.carry[...]
        pre = pull_two_part(0, g_y, r_.xh2_t[...].astype(F32), r_.rs[tail_at, 1:2])
        r_.xh2[0, tail_at, :] = pre
        g_z = (nt(pre, wf[1]) * r_.gp_t[...].astype(F32)).astype(BF)
        r_.gp[0, tail_at, :] = g_z
        r_.dbin[0:1, :] += row_sum(g_z.astype(F32))
        tail_put(1, pre, g_z)

    def pull_inner(seg, i):
        g_u = nt(r_.xh2[seg], wf[1, cols(i), :])
        g_z = (g_u * r_.gp[seg, :, cols(i)].astype(F32)).astype(BF)
        r_.gp[seg, :, cols(i)] = g_z
        r_.dbin[0:1, cols(i)] += row_sum(g_z.astype(F32))

    def pull_hidden(seg):
        loop(head_count, lambda r: give(0, r, nn(r_.gp[seg, rows(r), :], wf[0])))

    def pull_one(seg):
        def one(r):
            g_h = r_.xh2[seg, rows(r), :].astype(F32) + taken(0, r)
            hat = r_.xh1[seg, rows(r), :].astype(F32)
            pre = pull_norm(g_h * par[0:1, :], hat, r_.rs[rows(r), 2 * seg : 2 * seg + 1])
            hf[rows(r), :] = pre
            r_.xh1[seg, rows(r), :] = pre.astype(BF)
            r_.sg[0:1, :] += row_sum(g_h * hat)
            r_.sg[2:3, :] += row_sum(g_h)
            r_.sg[3:4, :] += row_sum(pre)

        loop(head_count, one)

        def out(j):
            r_.got[j] = nt(wa[j, 3 * local :, :], r_.xh1[seg]).astype(BF)

        loop(2, out)

    def pull_heads(seg, first, count):
        def one(i):
            h = first + i
            j = h // per_block
            q, k, v = (qkv[seg, j, head_rows(h, part), :] for part in range(3))
            g_o = r_.got[j, head_rows(h, 0), :]
            p = pt[seg, h]
            d_v = nt(g_o, p).astype(BF)
            total_p = row_sum(g_o.astype(F32) * ot[seg, j, head_rows(h, 0), :].astype(F32))
            d_s = (p.astype(F32) * (tn(v, g_o) - total_p)).astype(BF)
            d_q = (nn(k, d_s) * 0.125).astype(BF)
            d_k = nt(q, d_s).astype(BF)
            for part, value in enumerate((d_q, d_k, d_v)):
                qkv[seg, j, head_rows(h, part), :] = value

        loop(count, one)

    def pull_rows(seg, which):
        for r in which:
            give(
                1, r,
                tn(qkv[seg, 0, :, rows(r)], wa[0, : 3 * local, :]) + tn(qkv[seg, 1, :, rows(r)], wa[1, : 3 * local, :]),
            )

    def pull_x(seg, which):
        for r in which:
            value = hf[rows(r), :] + taken(1, r)
            acc[rows(r), :] = value
            r_.send_buf[1, r] = value.astype(BF)

    def pull_memory(seg):
        both = pltpu.roll(acc[0:tail, :], tail - mem_rows, 0) + acc[seg_len - tail : seg_len, :]
        memory = jnp.where(is_mem, both, 0.0)
        r_.dinit[...] += jnp.where(flags[seg] > 0, memory, 0.0)
        if seg == 1:
            r_.carry[...] = jnp.where(flags[1] > 0, 0.0, memory)

    ends = (0, head_count - 1)
    middle = tuple(range(1, head_count - 1))

    def text_grad(seg):
        def one(r):
            r_.text_all[seg, rows(r), :] = nn(take_rows(r), r_.send_buf[1].reshape(seg_len, width)).astype(BF)

        loop(head_count, one)

    def cut(buf, kind, a, b):
        first, second = (px, py) if kind == 0 else (py, px)
        first = first if a == 0 else 1 - first
        second = second if b == 0 else 1 - second
        return buf.at[second, first] if kind == 0 else buf.at[first, second]

    sum_mates = ((x_mate, y_mate), (y_mate, x_mate))

    def sum_one(name, kind, b):
        buf, got, s, r = sums[name](kind)
        return push(cut(buf, kind, 1, b), got[0].at[b], s.at[b], r.at[b], sum_mates[kind][0])

    def sum_two(name, kind):
        buf, got, s, r = sums[name](kind)
        return push(cut(buf, kind, 0, 1), got[1], s.at[2], r.at[2], sum_mates[kind][1])

    def ffn_sum(d):
        zi = order[d]

        def parts(kind):
            return (
                r_.fsend.at[kind, zi], (r_.f_one.at[kind, zi], r_.f_two.at[kind, zi]),
                r_.fsum_s.at[kind, zi], r_.fsum_r.at[kind, zi],
            )

        return parts

    sums = {d: ffn_sum(d) for d in range(head_count)}

    def attention_sum(n):
        def parts(kind):
            return (
                r_.asend.at[n, kind], (r_.a_one.at[n, kind], r_.a_two.at[n, kind]),
                r_.asum_s.at[n, kind], r_.asum_r.at[n, kind],
            )

        return parts

    halves = ("a", "b")
    for n, name in enumerate(halves):
        sums[name] = attention_sum(n)
    sums["v"] = lambda kind: (
        r_.vsend.at[kind], (r_.v_one.at[kind], r_.v_two.at[kind]), r_.vsum_s.at[kind], r_.vsum_r.at[kind]
    )

    def start_sum(name, which=((1, 0), (1, 1), (0, 0), (0, 1))):
        for b, kind in which:
            sum_one(name, kind, b).start()

    def adder(name):
        return add_block if isinstance(name, int) else add_blocks

    def go_on(name):
        for kind in range(2):
            buf, got, _, _ = sums[name](kind)
            sum_one(name, kind, 1).wait_recv()
            adder(name)(cut(buf, kind, 0, 1), got[0].at[1])
            sum_two(name, kind).start()
        for kind in range(2):
            buf, got, _, _ = sums[name](kind)
            sum_one(name, kind, 0).wait_recv()
            adder(name)(cut(buf, kind, 0, 0), got[0].at[0])

    def end_plane(name):
        for kind in range(2):
            buf, got, _, _ = sums[name](kind)
            sum_two(name, kind).wait_recv()
            adder(name)(cut(buf, kind, 0, 0), got[1])

    def sum_sent(name):
        for kind in range(2):
            for b in range(2):
                sum_one(name, kind, b).wait_send()
            sum_two(name, kind).wait_send()

    def z_out(kind, d):
        zi = order[d]
        return push(
            cut(r_.fsend.at[kind, zi], kind, 0, 0), r_.f_z.at[kind, z], r_.fz_s.at[kind, d], r_.fz_r.at[kind, z],
            device(core, px, py, zi),
        )

    def z_in(kind, zs):
        return push(
            cut(r_.fsend.at[kind, z], kind, 0, 0), r_.f_z.at[kind, zs], r_.fz_s.at[kind, 0], r_.fz_r.at[kind, zs], sibling
        )

    def end_ffn(d):
        end_plane(d)
        if d > 0:
            for kind in range(2):
                z_out(kind, d).start()

    def last_out(name, k, h):
        buf, dst, s, r = last[name]
        return push(
            cut(buf.at[k], k, 0, 0).at[h], dst.at[z], s.at[k, h], r.at[z], device(h, px, py, 2 * core + k)
        )

    def last_here(name, k):
        buf, dst, _, _ = last[name]
        return pltpu.make_async_copy(cut(buf.at[k], k, 0, 0).at[core], dst.at[z], r_.last_sem.at["abv".index(name)])

    last = {
        "a": (r_.asend.at[0], r_.a_z.at[0], r_.az_s.at[0], r_.az_r.at[0]),
        "b": (r_.asend.at[1], r_.a_z.at[1], r_.az_s.at[1], r_.az_r.at[1]),
        "v": (r_.vsend, r_.v_z, r_.vz_s, r_.vz_r),
    }

    def last_each(name, here_do, away_do):
        for k in range(2):
            for h in range(2):
                here = (core == h) & (z == 2 * core + k)
                if here_do is not None:
                    pl.when(here)(lambda: here_do(last_here(name, k)))
                when_not(here, lambda: away_do(last_out(name, k, h)))

    def last_total(name):
        buf, dst, s, r = last[name]
        for zs in range(head_count):
            here = is_home & (z == zs)
            pl.when(here)(lambda: last_here(name, 0).wait())
            when_not(
                here, lambda: push(buf.at[0, 0, 0, 0], dst.at[zs], s.at[0, 0], r.at[zs], sibling).wait_recv()
            )
        value = dst[0].astype(F32)
        for zs in range(1, head_count):
            value = value + dst[zs].astype(F32)
        return value

    def ffn_grads(d):
        i = order[d]
        pull_inner(1, i)
        pull_inner(0, i)
        for kind, (left, right) in enumerate(((r_.gp, r_.hb), (r_.u, r_.xh2))):
            value = tn(left[0, :, cols(i)], right[0]) + tn(left[1, :, cols(i)], right[1])
            for p in range(planes):
                r_.fsend[kind, i, p // 2, p % 2] = value[p * hid : (p + 1) * hid, :].astype(BF)
        start_sum(d)

    keep_tail()
    pull_two(1)
    pull_two(0)
    tail_gather(0, 1)
    ffn_grads(3)
    ffn_grads(2)
    go_on(3)
    ffn_grads(1)
    ffn_grads(0)

    pull_hidden(1)
    pull_one(1)
    go_on(2)
    pull_heads(1, 0, 3)
    end_ffn(3)
    pull_heads(1, 3, heads - 3)
    pull_rows(1, ends)
    pull_x(1, ends)
    pull_memory(1)
    go_on(1)

    pull_tail()
    dbin_pair = push(r_.dbin, r_.dbin_in, r_.pair_s.at[2], r_.pair_r.at[2], sibling)
    dbin_pair.start()
    pull_rows(1, middle)
    pull_x(1, middle)
    text_grad(1)
    back_send(1, 1)
    pull_hidden(0)
    go_on(0)
    pull_one(0)
    end_ffn(2)
    pull_heads(0, 0, 3)
    end_ffn(1)
    pull_heads(0, 3, heads - 3)

    hid_rows = width // dp_count
    cut_rows = hid_rows // 2

    def attention_grads(i):
        wide = width // 2
        span = pl.ds(pl.multiple_of(i * wide, wide), wide)
        xt = [x[s, :, span].T for s in range(2)]
        gt = [r_.xh1[s, :, span].T for s in range(2)]
        for k in range(2):
            qkv_g = nt(xt[0], qkv[0, k]) + nt(xt[1], qkv[1, k])
            out_g = nt(gt[0], ot[0, k]) + nt(gt[1], ot[1, k])
            for b in range(8):
                at = slice(b * cut_rows, (b + 1) * cut_rows)
                r_.asend[b % 2, k, i, b // 4, (b // 2) % 2, :, 0 : 3 * local] = qkv_g[at, :].astype(BF)
                r_.asend[b % 2, k, i, b // 4, (b // 2) % 2, :, 3 * local :] = out_g[at, :].astype(BF)

    attention_grads(1 - py)
    for name in halves:
        start_sum(name, ((1, 0), (1, 1), (0, 1)))
    attention_grads(py)
    for name in halves:
        start_sum(name, ((0, 0),))
    end_ffn(0)
    tail_gather(0, 2)
    tail_gather(1, 1)
    pull_rows(0, ends + middle)
    pull_x(0, ends + middle)
    pull_memory(0)
    go_on("a")
    text_grad(0)
    back_send(1, 0)
    tail_gather(1, 2)
    dbin_pair.wait()

    dbin_both = [jnp.where(core == h, r_.dbin[0:1, :], r_.dbin_in[0:1, :]) for h in range(2)]
    for k in range(2):
        r_.bqv[k] = sum(jnp.sum(qkv[s, k].astype(F32), axis=1, keepdims=True) for s in range(2))
    sg, dinit = r_.sg, r_.dinit
    r_.vec[...] = jnp.where(is_mem, dinit[...], 0.0)
    r_.vec[0:6, :] = sg[0:6, :]
    vtmp[...] = jnp.zeros_like(vtmp)

    def by_core(cut_of):
        return jnp.where(core == 0, cut_of(0), cut_of(1))

    qv_rows = [
        [
            jnp.sum(
                jnp.where(
                    lax.broadcasted_iota(jnp.int32, (HD, HD), 0) == lax.broadcasted_iota(jnp.int32, (HD, HD), 1),
                    r_.bqv[k, 2 * part * local + b * HD : 2 * part * local + (b + 1) * HD, :],
                    0.0,
                ),
                axis=0,
                keepdims=True,
            )
            for part in range(2)
            for b in range(per_block)
        ]
        for k in range(2)
    ]
    piece_b = HD // dp_count
    vec = r_.vec[...]

    def small_cut(k, p, h):
        dp_t = 2 * p + h

        def from_vec(c):
            at = (dp_t * head_count + 2 * c + k) * lanes
            return vec[:, at : at + lanes]

        def from_bin(c):
            at = ((2 * c + k) * planes + p) * hid
            return dbin_both[h][:, at : at + hid]

        vtmp[0:16, 0:lanes] = by_core(from_vec)
        vtmp[0:1, 32 : 32 + hid] = by_core(from_bin)
        for n, line in enumerate(qv_rows[k]):
            vtmp[1:2, 32 + n * piece_b : 32 + (n + 1) * piece_b] = line[:, dp_t * piece_b : (dp_t + 1) * piece_b]
        r_.vsend[k, p // 2, p % 2, h] = vtmp[...].astype(BF)

    for k in range(2):
        for p in range(planes):
            for h in range(2):
                small_cut(k, p, h)
    start_sum("v")
    go_on("b")
    end_plane("a")
    last_each("a", lambda c: c.start(), lambda c: c.start())
    go_on("v")
    end_plane("b")
    last_each("b", lambda c: c.start(), lambda c: c.start())
    end_plane("v")
    last_each("v", lambda c: c.start(), lambda c: c.start())

    tail_gather(0, 3)
    tail_gather(1, 3)
    extra = tail_products()
    for kind, out in enumerate((r_.win_o, r_.wback_o)):
        value = extra[kind] + cut(r_.fsend.at[kind, z], kind, 0, 0)[...].astype(F32)
        for d in range(1, head_count):
            zs = (z + d) % head_count
            z_in(kind, zs).wait_recv()
            value = value + r_.f_z[kind, zs].astype(F32)
        out[...] = value
    r_.att_o[0:cut_rows, :] = last_total("a")
    r_.att_o[cut_rows:hid_rows, :] = last_total("b")
    r_.vec_o[...] = last_total("v")

    for name in (0, 1, 2, 3, "a", "b", "v"):
        sum_sent(name)
    for d in range(1, head_count):
        for kind in range(2):
            z_out(kind, d).wait_send()
    for name in "abv":
        last_each(name, None, lambda c: c.wait_send())
    for which in range(2):
        for seg in range(2):
            back_sent(which, seg)
            back_done(which, seg)
    for a in range(2, 4):
        rows_done(a)
    attention_outs(lambda c: c.wait_send())
    ffn_sent()
    for which in range(2):
        tail_gather(which, 4)
    for copy in pair:
        copy.wait_send()
    for k in range(2):

        def sent():
            for which in range(4):
                attention_plane(k, which).wait_send()

        pl.when(foreign[k])(sent)
    for zi in range(head_count):
        for kind in range(2):
            for which in range(3):
                side(kind, zi, which).wait_send()
    for i in range(column_size):
        small_out(i).wait_send()
    for i in range(3):
        small_plane(i).wait_send()
    r_.dt_o[...] = r_.text_pad[...]


def vmem(*shape, dtype=BF):
    return pltpu.VMEM(shape, dtype)


def f32(*shape):
    return pltpu.VMEM(shape, F32)


def sds(*shape, dtype=BF):
    return jax.ShapeDtypeStruct(shape, dtype)


def dma(*shape):
    return pltpu.SemaphoreType.DMA(shape)


ANY = pl.BlockSpec(memory_space=pl.ANY)
INV = pl.BlockSpec(memory_space=pltpu.VMEM)
INS = pl.BlockSpec(memory_space=pltpu.SMEM)


def end_kernel(mem_rows, hid, lanes, acts, dt, win, wback, att, vec, *outs):
    acts_o, dt_o, dinit_o, dqkv_o, dbqv_o, dwout_o, dwin_o, dwback_o, dbin_o, dgains_o, dbiases_o = outs
    acts_o[...] = acts[...]
    text_rows = dt_o.shape[1]
    for j in range(2):
        both = [dt[j, s, 0:text_rows, :].astype(F32)[:, None, :] for s in range(2)]
        dt_o[j] = jnp.concatenate(both, axis=1).astype(BF)
    dinit_o[...] = vec[6 : 6 + mem_rows, 0:lanes]
    parts, _, local_width = dqkv_o.shape
    for t in range(parts):
        dqkv_o[t] = att[:, t * local_width : (t + 1) * local_width]
    per_block, _, slice_b = dbqv_o.shape
    for b in range(per_block):
        for part in range(2):
            at = 32 + (part * per_block + b) * slice_b
            dbqv_o[b, part : part + 1, :] = vec[1:2, at : at + slice_b]
    dwout_o[...] = att[:, parts * local_width :].T
    dwin_o[...] = win[...]
    dwback_o[...] = wback[...]
    dbin_o[...] = vec[0:1, 32 : 32 + hid]
    dgains_o[...] = vec[0:2, 0:lanes]
    dbiases_o[...] = vec[2:6, 0:lanes]


def by_chip(
    text, boundary, reset, memory_in, init_memory, w_qkv, b_qv, w_out, w_in, w_back, b_in, norm_gains, biases,
    cotangent,
):
    head_count = lax.axis_size("head")
    dp_count = lax.axis_size("dp")
    planes = dp_count // 2
    total = dp_count * head_count
    text_rows, width = text.shape[2], text.shape[3]
    block = cotangent.shape[2]
    seg_len = block * head_count
    mem_rows = memory_in.shape[1]
    local = w_qkv.shape[2]
    hid = w_in.shape[1]
    lanes = norm_gains.shape[1]
    heads = 2 * local // HD
    hidden = hid * planes * head_count
    share = width // dp_count

    inputs = dict(
        text=(text.transpose(0, 2, 1, 3), INV),
        boundary=(boundary, INV),
        reset=(reset, INS),
        memory_in=(memory_in.transpose(1, 0, 2), INV),
        init_memory=(init_memory, INV),
        wq_t=(w_qkv.transpose(1, 2, 0).reshape(3 * local, width), ANY),
        w_out=(w_out, ANY),
        b_qv=(b_qv.transpose(1, 0, 2), INV),
        w_in_t=(w_in.T, INV),
        w_back=(w_back, INV),
        b_in=(b_in[None, :], INV),
        norm_gains=(norm_gains, INV),
        biases=(biases, INV),
        cotangent=(cotangent, ANY),
    )
    outputs = dict(
        acts_o=(sds(2, 2, block, width), ANY),
        dt_o=(sds(2, 2, block, width), INV),
        win_o=(sds(hid, width, dtype=F32), INV),
        wback_o=(sds(hid, width, dtype=F32), INV),
        att_o=(sds(share, width, dtype=F32), INV),
        vec_o=(sds(16, 128, dtype=F32), INV),
    )
    scratch = dict(
        text_pad=vmem(2, 2, block, width),
        text_all=vmem(2, seg_len, width),
        cot_all=vmem(2, seg_len, width),
        wa=vmem(2, 4 * local, width),
        wf=vmem(2, hidden, width),
        small=vmem(16, 128),
        small_all=vmem(total, 16, 128),
        seqf=f32(8, seg_len),
        seqf_in=f32(8, seg_len),
        seq=f32(8, seg_len),
        memp=vmem(16, width),
        memp_in=vmem(16, width),
        par=f32(16, width),
        bin_row=f32(1, hidden),
        bqv=f32(2, 3 * local, 1),
        x=vmem(2, seg_len, width),
        qkv=vmem(2, 2, 3 * local, seg_len),
        pt=vmem(2, heads, seg_len, seg_len),
        ot=vmem(2, 2, local, seg_len),
        hf=f32(seg_len, width),
        acc=f32(seg_len, width),
        xh1=vmem(2, seg_len, width),
        hb=vmem(2, seg_len, width),
        u=vmem(2, seg_len, hidden),
        gp=vmem(2, seg_len, hidden),
        xh2=vmem(2, seg_len, width),
        rs=f32(seg_len, 4),
        y=vmem(2, seg_len, width),
        got=vmem(2, local, seg_len),
        send_buf=vmem(2, head_count, block, width),
        recv_buf=vmem(2, head_count, block, width),
        cur_a=vmem(16, width),
        cur_b=vmem(16, width),
        carry=f32(16, width),
        xh2_t=vmem(16, width),
        gp_t=vmem(16, hidden),
        factor_out=vmem(2, head_count, 16, width + hidden // head_count),
        factors=vmem(2, head_count, planes, 16, width + hidden // head_count),
        sg=f32(8, width),
        dinit=f32(16, width),
        dbin=f32(8, hidden),
        dbin_in=f32(8, hidden),
        vec=f32(16, width),
        vtmp=f32(16, 128),
        fsend=vmem(2, head_count, 2, 2, hid, width),
        f_one=vmem(2, head_count, 2, hid, width),
        f_two=vmem(2, head_count, hid, width),
        f_z=vmem(2, head_count, hid, width),
        asend=vmem(2, 2, 2, 2, 2, share // 2, width),
        a_one=vmem(2, 2, 2, 2, share // 2, width),
        a_two=vmem(2, 2, 2, share // 2, width),
        a_z=vmem(2, head_count, share // 2, width),
        vsend=vmem(2, 2, 2, 2, 16, 128),
        v_one=vmem(2, 2, 2, 16, 128),
        v_two=vmem(2, 2, 16, 128),
        v_z=vmem(head_count, 16, 128),
        small_s=dma(7),
        small_r=dma(4, 2),
        small_ps=dma(3),
        small_pr=dma(3),
        pair_s=dma(3),
        pair_r=dma(3),
        att_s=dma(3),
        att_r=dma(2, 2),
        plane_s=dma(2, 4),
        plane_r=dma(2, 4),
        local_sem=dma(2),
        rows_s=dma(4, 2, 2),
        rows_r=dma(4, 4),
        here_sem=dma(4),
        fwd_s=dma(4, 4),
        fwd_r=dma(4, 4),
        ffn_s=dma(5),
        ffn_r=dma(4),
        side_s=dma(4, 2, 3),
        side_r=dma(4, 2, 3),
        send_sem=dma(2, 4),
        recv_sem=dma(2, 4),
        back_s=dma(2, 2, 4),
        back_r=dma(2, 2, 2, 2),
        back_here_sem=dma(2, 2),
        fsum_s=dma(2, 4, 3),
        fsum_r=dma(2, 4, 3),
        asum_s=dma(2, 2, 3),
        asum_r=dma(2, 2, 3),
        tg_s=dma(2, 6),
        tg_r=dma(2, 7),
        vsum_s=dma(2, 3),
        vsum_r=dma(2, 3),
        fz_s=dma(2, 4),
        fz_r=dma(2, 4),
        az_s=dma(2, 2, 2),
        az_r=dma(2, 4),
        vz_s=dma(2, 2),
        vz_r=dma(4),
        last_sem=dma(3),
    )
    names = tuple(inputs) + tuple(outputs) + tuple(scratch)
    middle = pl.pallas_call(
        functools.partial(main_kernel, names, dp_count, head_count),
        out_shape=tuple(v[0] for v in outputs.values()),
        in_specs=[v[1] for v in inputs.values()],
        out_specs=tuple(v[1] for v in outputs.values()),
        scratch_shapes=list(scratch.values()),
        compiler_params=pltpu.CompilerParams(
            collective_id=0, has_side_effects=True, vmem_limit_bytes=VMEM_LIMIT
        ),
        name="layer",
    )(*(v[0] for v in inputs.values()))

    slice_b = HD // dp_count
    out = pl.pallas_call(
        functools.partial(end_kernel, mem_rows, hid, lanes),
        out_shape=(
            sds(2, 2, block, width),
            sds(2, text_rows, 2, width),
            sds(mem_rows, lanes, dtype=F32),
            sds(3, share, local, dtype=F32),
            sds(local // HD, 2, slice_b, dtype=F32),
            sds(local, share, dtype=F32),
            sds(hid, width, dtype=F32),
            sds(hid, width, dtype=F32),
            sds(1, hid, dtype=F32),
            sds(2, lanes, dtype=F32),
            sds(4, lanes, dtype=F32),
        ),
        in_specs=[INV] * 6,
        out_specs=tuple([INV] * 11),
        name="results",
    )(*middle)
    acts, d_text, d_init, d_qkv, d_bqv, d_wout, d_win, d_wback, d_bin, d_gains, d_biases = out
    return (
        acts, d_text.transpose(0, 2, 1, 3), d_init,
        d_qkv.transpose(1, 0, 2),
        d_bqv.transpose(1, 0, 2),
        d_wout, d_win.T, d_wback, d_bin[0], d_gains, d_biases,
    )


def solution(mesh):
    body = by_chip if mesh.shape["dp"] == 8 and mesh.shape["head"] == 4 else local
    return jax.shard_map(
        body,
        mesh=mesh,
        in_specs=(
            P("dp", None, "head", None),
            P("dp", None, None),
            P("dp", None),
            P("dp", None, None),
            P(None, ("dp", "head")),
            P(None, None, "head"),
            P(None, "head", None),
            P("head", None),
            P(None, ("dp", "head")),
            P(("dp", "head"), None),
            P(("dp", "head")),
            P(None, ("dp", "head")),
            P(None, ("dp", "head")),
            P("dp", None, "head", None),
        ),
        out_specs=(
            P("dp", None, "head", None),
            P("dp", None, "head", None),
            P(None, ("dp", "head")),
            P("dp", None, "head"),
            P(None, "head", "dp"),
            P("head", "dp"),
            P(None, ("dp", "head")),
            P(("dp", "head"), None),
            P(("dp", "head")),
            P(None, ("dp", "head")),
            P(None, ("dp", "head")),
        ),
        check_vma=False,
    )
```

```python
import functools

import jax
import jax.numpy as jnp
from jax import lax
from jax.experimental import pallas as pl
from jax.experimental.pallas import tpu as pltpu
from jax.sharding import PartitionSpec as P

HD = 64
MESH = pl.DeviceIdType.MESH
BF = jnp.bfloat16
F32 = jnp.float32
VMEM_LIMIT = 64 * 1024 * 1024


def nn(a, b):
    return lax.dot_general(a, b, (((1,), (0,)), ((), ())), preferred_element_type=F32)


def nt(a, b):
    return lax.dot_general(a, b, (((1,), (1,)), ((), ())), preferred_element_type=F32)


def tn(a, b):
    return lax.dot_general(a, b, (((0,), (0,)), ((), ())), preferred_element_type=F32)


def place():
    dp, z = lax.axis_index("dp"), lax.axis_index("head")
    core, plane = dp % 2, dp // 2
    return core, plane % 2, plane // 2, z


def device(core, x, y, z):
    return ((y * 2 + x) * 2 + core, z)


def push(src, dst, send, recv, target):
    return pltpu.make_async_remote_copy(
        src_ref=src, dst_ref=dst, send_sem=send, recv_sem=recv, device_id=target, device_id_type=MESH
    )


def from_root(x, axis, root):
    mine = lax.axis_index(axis) == root
    return lax.psum(jnp.where(mine, x, jnp.zeros_like(x)), axis)


def layer_norm(values, gain_row, shift_row):
    center = values - jnp.mean(values, axis=-1, keepdims=True)
    spread = jnp.mean(center * center, axis=-1, keepdims=True)
    return center * lax.rsqrt(spread + 1e-05) * gain_row + shift_row


def gelu_tanh(values):
    return jax.nn.gelu(values, approximate=True)


def head_major(array, dim, dp_count, head_count):
    shape = array.shape
    size = shape[dim]
    split = array.reshape(
        shape[:dim] + (dp_count, head_count, size // (dp_count * head_count)) + shape[dim + 1 :]
    )
    return jnp.swapaxes(split, dim, dim + 1).reshape(shape)


def local(
    text,
    boundary,
    reset,
    memory_in,
    init_memory,
    w_qkv,
    b_qv,
    w_out,
    w_in,
    w_back,
    b_in,
    norm_gains,
    biases,
    cotangent,
):
    head_count = lax.axis_size("head")
    dp_count = lax.axis_size("dp")
    head_idx = lax.axis_index("head")
    batch_size = text.shape[0]
    width = text.shape[3]
    seg_rows = cotangent.shape[2]
    seg_len = seg_rows * head_count
    mem_rows = memory_in.shape[1]
    text_len = seg_len - 2 * mem_rows
    local_width = w_qkv.shape[2]
    local_heads = local_width // HD
    row_start = head_idx * seg_rows
    is_first = (head_idx == 0).astype(jnp.float32)
    is_final = (head_idx == head_count - 1).astype(jnp.float32)
    grad_dims = (1, 0, 0, 1, 1, 1)
    doc_ids = jnp.cumsum(boundary, axis=2)
    marks = jnp.full((batch_size, 2, mem_rows), -1, jnp.int32)
    labels = jnp.concatenate([marks, doc_ids, marks], axis=2)
    visible = (
        (labels[..., :, None] == labels[..., None, :])
        | (labels[..., :, None] < 0)
        | (labels[..., None, :] < 0)
    )
    bias_query = b_qv[0].reshape(local_width).astype(jnp.float32)
    bias_value = b_qv[1].reshape(local_width).astype(jnp.float32)
    shared = (
        lax.all_gather(w_in, ("dp", "head"), axis=1, tiled=True),
        lax.all_gather(w_back, ("dp", "head"), axis=0, tiled=True),
        lax.all_gather(b_in, ("dp", "head"), axis=0, tiled=True),
        lax.all_gather(norm_gains, ("dp", "head"), axis=1, tiled=True),
        lax.all_gather(biases, ("dp", "head"), axis=1, tiled=True),
        lax.all_gather(init_memory, ("dp", "head"), axis=1, tiled=True),
    )

    def fetch():
        return shared

    def attention_probs(query, key_rows, seg):
        scores = (
            jnp.einsum("sqhe,skhe->shqk", query, key_rows, preferred_element_type=jnp.float32)
            * 0.125
        )
        return jnp.where(visible[:, seg][:, None], scores, -1e30)

    def forward(seg, memory, ffn):
        w_in_all, w_back_all, b_in_all, gains_all, biases_all, unused = ffn
        gains_f = gains_all.astype(jnp.float32)
        biases_f = biases_all.astype(jnp.float32)
        local_text = lax.all_gather(text[:, seg], "head", axis=1, tiled=True)
        x_rows = jnp.concatenate([memory, local_text, memory], axis=1)
        mixed = jnp.einsum("srd,dce->srce", x_rows, w_qkv, preferred_element_type=jnp.float32)
        query = (
            (mixed[:, :, 0] + bias_query)
            .astype(jnp.bfloat16)
            .reshape(batch_size, seg_len, local_heads, HD)
        )
        key_rows = mixed[:, :, 1].astype(jnp.bfloat16).reshape(batch_size, seg_len, local_heads, HD)
        value = (
            (mixed[:, :, 2] + bias_value)
            .astype(jnp.bfloat16)
            .reshape(batch_size, seg_len, local_heads, HD)
        )
        masked = attention_probs(query, key_rows, seg)
        row_max = jnp.max(masked, axis=-1, keepdims=True)
        exp_terms = jnp.exp(masked - row_max)
        row_total = jnp.sum(exp_terms, axis=-1, keepdims=True)
        log_total = row_max + jnp.log(row_total)
        probs = (exp_terms / row_total).astype(jnp.bfloat16)
        attended = jnp.einsum("shqk,skhe->sqhe", probs, value, preferred_element_type=jnp.float32)
        attended = attended.astype(jnp.bfloat16).reshape(batch_size, seg_len, local_width)
        partial_out = jnp.einsum("srl,ld->srd", attended, w_out, preferred_element_type=jnp.float32)
        summed = lax.psum_scatter(
            partial_out.astype(jnp.bfloat16), "head", scatter_dimension=1, tiled=True
        ).astype(jnp.float32)
        own_rows = lax.dynamic_slice_in_dim(x_rows, row_start, seg_rows, 1).astype(jnp.float32)
        pre_norm = own_rows + summed + biases_f[1]
        hidden = layer_norm(pre_norm, gains_f[0], biases_f[0])
        hidden_low = hidden.astype(jnp.bfloat16)
        inner = jnp.einsum(
            "srd,df->srf", hidden_low, w_in_all, preferred_element_type=jnp.float32
        ) + b_in_all.astype(jnp.float32)
        active = gelu_tanh(inner).astype(jnp.bfloat16)
        outer = (
            jnp.einsum("srf,fd->srd", active, w_back_all, preferred_element_type=jnp.float32)
            + biases_f[2]
        )
        post_norm = hidden + outer
        result = layer_norm(post_norm, gains_f[1], biases_f[3])
        kept = (
            x_rows,
            query,
            key_rows,
            value,
            log_total,
            attended,
            pre_norm,
            hidden_low,
            inner,
            active,
            post_norm,
        )
        return (result, kept)

    def backward(seg, grad_out, kept, ffn):
        (
            x_rows,
            query,
            key_rows,
            value,
            log_total,
            attended,
            pre_norm,
            hidden_low,
            inner,
            active,
            post_norm,
        ) = kept
        w_in_all, w_back_all, b_in_all, gains_all, biases_all, unused = ffn
        gains_f = gains_all.astype(jnp.float32)
        biases_f = biases_all.astype(jnp.float32)
        unused_two, pull_two = jax.vjp(layer_norm, post_norm, gains_f[1], biases_f[3])
        grad_post, grad_gain_two, grad_shift_two = pull_two(grad_out)
        grad_outer = grad_post.astype(jnp.bfloat16)
        grad_ffn_bias = jnp.sum(grad_post, axis=(0, 1))
        grad_w_back = jnp.einsum(
            "srf,srd->fd", active, grad_outer, preferred_element_type=jnp.float32
        )
        grad_active = jnp.einsum(
            "srd,fd->srf", grad_outer, w_back_all, preferred_element_type=jnp.float32
        )
        unused_gelu, pull_gelu = jax.vjp(gelu_tanh, inner)
        grad_inner = pull_gelu(grad_active)[0].astype(jnp.bfloat16)
        grad_b_in = jnp.sum(grad_inner, axis=(0, 1), dtype=jnp.float32)
        grad_w_in = jnp.einsum(
            "srd,srf->df", hidden_low, grad_inner, preferred_element_type=jnp.float32
        )
        grad_hidden = grad_post + jnp.einsum(
            "srf,df->srd", grad_inner, w_in_all, preferred_element_type=jnp.float32
        )
        unused_one, pull_one = jax.vjp(layer_norm, pre_norm, gains_f[0], biases_f[0])
        grad_pre, grad_gain_one, grad_shift_one = pull_one(grad_hidden)
        grad_out_bias = jnp.sum(grad_pre, axis=(0, 1))
        grad_branch = lax.all_gather(grad_pre.astype(jnp.bfloat16), "head", axis=1, tiled=True)
        grad_w_out = jnp.einsum(
            "srl,srd->ld", attended, grad_branch, preferred_element_type=jnp.float32
        )
        grad_att = jnp.einsum("srd,ld->srl", grad_branch, w_out, preferred_element_type=jnp.float32)
        grad_att = grad_att.astype(jnp.bfloat16).reshape(batch_size, seg_len, local_heads, HD)
        masked = attention_probs(query, key_rows, seg)
        probs = jnp.exp(masked - log_total)
        grad_value = jnp.einsum(
            "shqk,sqhe->skhe",
            probs.astype(jnp.bfloat16),
            grad_att,
            preferred_element_type=jnp.float32,
        )
        grad_probs = jnp.einsum(
            "sqhe,skhe->shqk", grad_att, value, preferred_element_type=jnp.float32
        )
        grad_scores = probs * (grad_probs - jnp.sum(grad_probs * probs, axis=-1, keepdims=True))
        grad_scores = grad_scores.astype(jnp.bfloat16)
        grad_query = (
            jnp.einsum("shqk,skhe->sqhe", grad_scores, key_rows, preferred_element_type=jnp.float32)
            * 0.125
        )
        grad_key = (
            jnp.einsum("shqk,sqhe->skhe", grad_scores, query, preferred_element_type=jnp.float32)
            * 0.125
        )
        grad_mixed = jnp.stack([grad_query, grad_key, grad_value], axis=2).astype(jnp.bfloat16)
        grad_mixed = grad_mixed.reshape(batch_size, seg_len, 3, local_width)
        grad_bias_qv = jnp.stack(
            [
                jnp.sum(grad_mixed[:, :, 0], axis=(0, 1), dtype=jnp.float32),
                jnp.sum(grad_mixed[:, :, 2], axis=(0, 1), dtype=jnp.float32),
            ]
        ).reshape(2, local_heads, HD)
        grad_w_qkv = jnp.einsum(
            "srd,srce->dce", x_rows, grad_mixed, preferred_element_type=jnp.float32
        )
        grad_rows = jnp.einsum(
            "srce,dce->srd", grad_mixed, w_qkv, preferred_element_type=jnp.float32
        )
        placed = lax.dynamic_update_slice_in_dim(jnp.zeros_like(grad_rows), grad_pre, row_start, 1)
        grad_rows = grad_rows + placed
        grad_text_part = lax.psum_scatter(
            grad_rows[:, mem_rows : mem_rows + text_len].astype(jnp.bfloat16),
            "head",
            scatter_dimension=1,
            tiled=True,
        ).astype(jnp.float32)
        grad_memory = lax.psum(
            (grad_rows[:, :mem_rows] + grad_rows[:, seg_len - mem_rows :]).astype(jnp.bfloat16),
            "head",
        ).astype(jnp.float32)
        reset_flag = reset[:, seg] > 0
        grad_init = (
            jnp.sum(jnp.where(reset_flag[:, None, None], grad_memory, 0.0), axis=0) * is_first
        )
        ffn_grads = (
            grad_w_in,
            grad_w_back,
            grad_b_in,
            jnp.stack([grad_gain_one, grad_gain_two]),
            jnp.stack([grad_shift_one, grad_out_bias, grad_ffn_bias, grad_shift_two]),
            grad_init,
        )
        return (grad_text_part, grad_memory, (grad_w_qkv, grad_bias_qv, grad_w_out), ffn_grads)

    ffn_first = fetch()
    init_all = ffn_first[5]
    memory_one = jnp.where(reset[:, 0, None, None] > 0, init_all[None], memory_in)
    out_one, kept_one = forward(0, memory_one, ffn_first)
    tail_rows = out_one[:, seg_rows - mem_rows :].astype(jnp.bfloat16)
    carried = from_root(tail_rows, "head", head_count - 1)
    ffn_second = fetch()
    memory_two = jnp.where(reset[:, 1, None, None] > 0, ffn_second[5][None], carried)
    out_two, kept_two = forward(1, memory_two, ffn_second)
    activations = jnp.stack([out_one, out_two], axis=1).astype(jnp.bfloat16)
    ffn_third = fetch()
    text_two, memory_grad_two, attn_two, ffn_two = backward(
        1, cotangent[:, 1].astype(jnp.float32), kept_two, ffn_third
    )
    keep_flag = reset[:, 1, None, None] <= 0
    carried_grad = jnp.where(keep_flag, memory_grad_two, 0.0) * is_final
    grad_one = cotangent[:, 0].astype(jnp.float32) + jnp.concatenate(
        [jnp.zeros((batch_size, seg_rows - mem_rows, width), jnp.float32), carried_grad], axis=1
    )
    ffn_fourth = fetch()
    text_one, memory_grad_one, attn_one, ffn_one = backward(0, grad_one, kept_one, ffn_fourth)
    grads = jax.tree.map(lambda a, b: a + b, ffn_one, ffn_two)
    ffn_total = tuple((head_major(g, d, dp_count, head_count) for g, d in zip(grads, grad_dims)))
    partial_sums = (
        lax.psum_scatter(
            ffn_total[0].astype(jnp.bfloat16), "head", scatter_dimension=1, tiled=True
        ).astype(jnp.float32),
        lax.psum_scatter(
            ffn_total[1].astype(jnp.bfloat16), "head", scatter_dimension=0, tiled=True
        ).astype(jnp.float32),
        lax.psum_scatter(
            ffn_total[2].astype(jnp.bfloat16), "head", scatter_dimension=0, tiled=True
        ).astype(jnp.float32),
        lax.psum_scatter(
            ffn_total[3].astype(jnp.bfloat16), "head", scatter_dimension=1, tiled=True
        ).astype(jnp.float32),
        lax.psum_scatter(
            ffn_total[4].astype(jnp.bfloat16), "head", scatter_dimension=1, tiled=True
        ).astype(jnp.float32),
        lax.psum_scatter(
            ffn_total[5].astype(jnp.bfloat16), "head", scatter_dimension=1, tiled=True
        ).astype(jnp.float32),
    )
    reduced = (
        lax.psum_scatter(partial_sums[0], "dp", scatter_dimension=1, tiled=True),
        lax.psum_scatter(partial_sums[1], "dp", scatter_dimension=0, tiled=True),
        lax.psum_scatter(partial_sums[2], "dp", scatter_dimension=0, tiled=True),
        lax.psum_scatter(partial_sums[3], "dp", scatter_dimension=1, tiled=True),
        lax.psum_scatter(partial_sums[4], "dp", scatter_dimension=1, tiled=True),
        lax.psum_scatter(partial_sums[5], "dp", scatter_dimension=1, tiled=True),
    )
    attn_total = jax.tree.map(lambda a, b: a + b, attn_one, attn_two)
    grad_qkv, grad_bqv, grad_wout = (
        lax.psum_scatter(attn_total[0], "dp", scatter_dimension=0, tiled=True),
        lax.psum_scatter(attn_total[1], "dp", scatter_dimension=2, tiled=True),
        lax.psum_scatter(attn_total[2], "dp", scatter_dimension=1, tiled=True),
    )
    grad_text = jnp.stack([text_one, text_two], axis=1).astype(jnp.bfloat16)
    grad_win, grad_wback, grad_bin, grad_gains, grad_biases, grad_init = reduced
    return (
        activations,
        grad_text,
        grad_init,
        grad_qkv,
        grad_bqv,
        grad_wout,
        grad_win,
        grad_wback,
        grad_bin,
        grad_gains,
        grad_biases,
    )


class Refs:
    pass


def by_name(names, values):
    refs = Refs()
    for name, value in zip(names, values, strict=True):
        setattr(refs, name, value)
    return refs


def loop(count, body, unroll=1):
    def run(i, unused):
        body(i)
        return unused

    lax.fori_loop(0, count, run, 0, unroll=unroll)


def add_all(dst, *sources):
    def body(at):
        dst[at] = sum([src[at].astype(F32) for src in sources], dst[at].astype(F32)).astype(BF)

    if len(dst.shape) == 2:
        body(...)
    else:
        loop(dst.shape[0], body)


def as_column(row):
    n = row.shape[1]
    down = lax.broadcasted_iota(jnp.int32, (n, n), 0)
    across = lax.broadcasted_iota(jnp.int32, (n, n), 1)
    return jnp.sum(jnp.where(down == across, row, 0.0), axis=1, keepdims=True)


def norm(v):
    center = v - jnp.mean(v, axis=-1, keepdims=True)
    scale = lax.rsqrt(jnp.mean(center * center, axis=-1, keepdims=True) + 1e-05)
    return center * scale, scale


def pull_norm(g, hat, scale):
    m1 = jnp.mean(g, axis=-1, keepdims=True)
    m2 = jnp.mean(g * hat, axis=-1, keepdims=True)
    return scale * (g - m1 - hat * m2)


def row_sum(v):
    return jnp.sum(v, axis=0, keepdims=True)


def main_kernel(names, dp_count, head_count, *values):
    r_ = by_name(names, values)
    core, px, py, z = place()
    plane = py * 2 + px
    x_plane, y_plane = py * 2 + 1 - px, (1 - py) * 2 + px
    me = (plane * 2 + core) * head_count + z
    total = dp_count * head_count
    planes = dp_count // 2
    is_home = core == z // 2
    away = jnp.logical_not(is_home)
    sibling = device(1 - core, px, py, z)
    x_mate, y_mate = device(core, 1 - px, py, z), device(core, px, 1 - py, z)
    mirror = z // 2

    def from_end(i):
        return i + mirror * (head_count - 1 - 2 * i)

    depth = from_end(z)
    inside = depth == 1
    order = [from_end(i) for i in (depth, 1 - depth, 2, 3)]

    def order_at(n):
        return from_end(jnp.where(n == 0, depth, jnp.where(n == 1, 1 - depth, n)))

    x, qkv, pt, ot, wa, wf = r_.x, r_.qkv, r_.pt, r_.ot, r_.wa, r_.wf
    hf, acc, par = r_.hf, r_.acc, r_.par
    seg_len, width = x.shape[1], x.shape[2]
    hidden = r_.u.shape[2]
    heads = pt.shape[1]
    local = ot.shape[2]
    hid = r_.w_back.shape[0]
    lanes = r_.norm_gains.shape[1]
    mem_rows = r_.memory_in.shape[0]
    text_rows = r_.text.shape[1]
    per_block = local // HD
    step = seg_len // head_count
    piece = step // 2
    chunk = hidden // head_count
    tail = 16
    tail_at = pl.ds(seg_len - tail, tail)

    def rows(r):
        return pl.ds(pl.multiple_of(r * step, step), step)

    def cols(i):
        return pl.ds(pl.multiple_of(i * chunk, chunk), chunk)

    def head_rows(h, part):
        return pl.ds(pl.multiple_of((h % per_block) * HD + part * local, HD), HD)

    def column(i):
        h = core if i < head_count - 1 else 1 - core
        zt = (z + 1 + i) % head_count
        return (plane * 2 + h) * head_count + zt, device(h, px, py, zt)

    column_size = 2 * head_count - 1

    def when_not(cond, body):
        pl.when(jnp.logical_not(cond))(body)

    share = local
    half = share // 2

    def attention_out(i, which):
        zt = (z + 1 + i) % head_count
        at = pl.multiple_of((share * jnp.minimum(plane, planes - 2) if which == 0 else 0) + half * core, half)
        src = (r_.wq_t, r_.w_out)[which]
        return push(
            src.at[pl.ds(at, half)], wa.at[z % 2, pl.ds(pl.multiple_of(share * plane + half * core, half), half)],
            r_.att_s.at[i], r_.att_r.at[z % 2, core], device(z // 2, px, py, zt),
        )

    def attention_outs(do):
        for which, mine in enumerate((plane < planes - 1, plane == planes - 1)):

            def each():
                for i in range(head_count - 1):
                    do(attention_out(i, which))

            pl.when(mine)(each)

    def attention_in(k, h):
        span = pl.ds(pl.multiple_of(share * plane + half * h, half), half)
        return push(r_.w_out.at[pl.ds(0, half)], wa.at[k, span], r_.att_s.at[0], r_.att_r.at[k, h], sibling)

    def attention_plane(k, which):
        at, count, mate = (
            (share * plane, share, x_mate),
            (share * plane, share, y_mate),
            (share * x_plane, half, y_mate),
            (share * y_plane + half, half, x_mate),
        )[which]
        block = pl.ds(pl.multiple_of(at, half), count)
        return push(
            wa.at[k, block], wa.at[k, block], r_.plane_s.at[k, which], r_.plane_r.at[k, which], mate
        )

    own_attention = [
        pltpu.make_async_copy(r_.wq_t, wa.at[z % 2, pl.ds(0, 3 * local)], r_.local_sem.at[0]),
        pltpu.make_async_copy(r_.w_out, wa.at[z % 2, pl.ds(3 * local, local)], r_.local_sem.at[1]),
    ]
    foreign = [jnp.logical_not(is_home & (z % 2 == k)) for k in range(2)]

    def rows_src(a, j, h):
        src = r_.text_pad if a < 2 else r_.cotangent
        return src.at[j, a % 2, pl.ds(h * piece, piece)]

    def rows_dst(a, zs, h):
        dst = r_.text_all if a < 2 else r_.cot_all
        return dst.at[a % 2, pl.ds(pl.multiple_of(zs * step + h * piece, piece), piece)]

    def rows_out(a, j, h):
        return push(
            rows_src(a, j, h), rows_dst(a, z, h), r_.rows_s.at[a, j, h], r_.rows_r.at[a, z],
            device(h, px, py, 2 * core + j),
        )

    def rows_here(a, j, h):
        return pltpu.make_async_copy(rows_src(a, j, h), rows_dst(a, z, h), r_.here_sem.at[a])

    def rows_send(a):
        for j in range(2):
            for h in range(2):
                here = (core == h) & (z == 2 * core + j)
                pl.when(here)(lambda: rows_here(a, j, h).start())
                when_not(here, lambda: rows_out(a, j, h).start())

    def rows_forward(a, zs, h):
        ref = rows_dst(a, zs, h)
        return push(ref, ref, r_.fwd_s.at[a, zs], r_.fwd_r.at[a, zs], sibling)

    def rows_pass(a):
        for zs in range(head_count):
            here = is_home & (z == zs)
            pl.when(here)(lambda: rows_here(a, z % 2, core).wait())
            when_not(
                here,
                lambda: push(
                    rows_src(a, 0, 0), rows_dst(a, zs, core), r_.rows_s.at[a, 0, 0], r_.rows_r.at[a, zs], sibling
                ).wait_recv(),
            )
            rows_forward(a, zs, core).start()

    def rows_ready(a):
        for zs in range(head_count):
            rows_forward(a, zs, 1 - core).wait_recv()

    def rows_done(a):
        for j in range(2):
            for h in range(2):
                when_not((core == h) & (z == 2 * core + j), lambda: rows_out(a, j, h).wait_send())
        for zs in range(head_count):
            rows_forward(a, zs, core).wait_send()

    def hidden_block(p, zi):
        return pl.ds(pl.multiple_of((zi * planes + p) * hid, hid), hid)

    def ffn_push(zi, to, slot):
        ref = wf.at[:, hidden_block(plane, zi)]
        return push(ref, ref, r_.ffn_s.at[slot], r_.ffn_r.at[zi], device(core, px, py, to))

    ffn_hops = [(0, from_end(1 - depth)), (0, from_end(2)), (1, from_end(2)), (2, from_end(0)), (3, from_end(0))]

    def ffn_hop(i):
        which, to = ffn_hops[i]
        return ffn_push(order[which], to, i)

    def ffn_own():
        ffn_hop(0).start()
        pl.when(inside)(ffn_hop(1).start)

    def ffn_hop_on(n):
        ffn_push(order[n], z, 0).wait_recv()
        pl.when(inside)(ffn_hop(n + 1).start)

    def ffn_sent():
        ffn_hop(0).wait_send()

        def rest():
            for i in range(1, 5):
                ffn_hop(i).wait_send()

        pl.when(inside)(rest)

    def side(kind, zi, which):
        p, mate = (
            (plane, x_mate),
            (plane, y_mate),
            (x_plane, y_mate) if kind == 0 else (y_plane, x_mate),
        )[which]
        ref = wf.at[kind, hidden_block(p, zi)]
        return push(ref, ref, r_.side_s.at[zi, kind, which], r_.side_r.at[zi, kind, which], mate)

    def side_first(zi):
        for kind in range(2):
            side(kind, zi, 0).start()
            side(kind, zi, 1).start()

    def ffn_two(n):
        zi = order_at(n)
        side(0, zi, 0).wait_recv()
        side(0, zi, 2).start()
        side(1, zi, 1).wait_recv()
        side(1, zi, 2).start()

    def ffn_ready(n):
        zi = order_at(n)
        side(0, zi, 1).wait_recv()
        side(1, zi, 0).wait_recv()
        side(0, zi, 2).wait_recv()
        side(1, zi, 2).wait_recv()

    def small_out(i):
        return push(r_.small, r_.small_all.at[me], r_.small_s.at[i], r_.small_r.at[z, core], column(i)[1])

    def small_in(i):
        at, (dp_i, z_i) = column(i)
        return push(r_.small, r_.small_all.at[at], r_.small_s.at[i], r_.small_r.at[z_i, dp_i % 2], sibling)

    def small_plane(i):
        p, mate = ((plane, x_mate), (plane, y_mate), (x_plane, y_mate))[i]
        ref = r_.small_all.at[pl.ds(p * 2 * head_count, 2 * head_count)]
        return push(ref, ref, r_.small_ps.at[i], r_.small_pr.at[i], mate)

    pair = [
        push(r_.seqf, r_.seqf_in, r_.pair_s.at[0], r_.pair_r.at[0], sibling),
        push(r_.memp, r_.memp_in, r_.pair_s.at[1], r_.pair_r.at[1], sibling),
    ]

    barrier = pltpu.get_barrier_semaphore()
    mates = [x_mate, y_mate] + [column(i)[1] for i in range(column_size)]
    for mate in mates:
        pl.semaphore_signal(barrier, inc=1, device_id=mate, device_id_type=MESH)
    wf[0, hidden_block(plane, z), :] = r_.w_in_t[...]
    wf[1, hidden_block(plane, z), :] = r_.w_back[...]
    vtmp = r_.vtmp
    vtmp[...] = jnp.zeros_like(vtmp)
    vtmp[0:2, 0:lanes] = r_.norm_gains[...].astype(F32)
    vtmp[2:6, 0:lanes] = r_.biases[...].astype(F32)
    vtmp[6 : 6 + mem_rows, 0:lanes] = r_.init_memory[...].astype(F32)
    vtmp[0:1, 32 : 32 + hid] = r_.b_in[...].astype(F32)
    for b in range(per_block):
        pair_b = r_.b_qv[b].astype(F32)
        for part in range(2):
            vtmp[1 + part * per_block + b : 2 + part * per_block + b, 32 : 32 + HD] = pair_b[part : part + 1, :]
    r_.small[...] = vtmp[...].astype(BF)
    r_.small_all[me] = r_.small[...]
    pl.semaphore_wait(barrier, len(mates))

    for i in range(column_size):
        small_out(i).start()
    side_first(z)
    ffn_own()
    attention_outs(lambda c: c.start())

    def keep_own():
        for copy in own_attention:
            copy.start()

    pl.when(is_home)(keep_own)
    seqf = r_.seqf
    marks = r_.boundary[z % 2].astype(F32).astype(BF)
    text_len = marks.shape[1]
    n_from = lax.broadcasted_iota(jnp.int32, (text_len, seg_len), 0)
    n_to = lax.broadcasted_iota(jnp.int32, (text_len, seg_len), 1) - mem_rows
    counts = nn(marks, jnp.where(n_from <= n_to, 1.0, 0.0).astype(BF))
    at_row = lax.broadcasted_iota(jnp.int32, (2, seg_len), 1)
    seqf[...] = jnp.zeros_like(seqf)
    seqf[0:2, :] = jnp.where((at_row >= mem_rows) & (at_row < seg_len - mem_rows), counts, -1.0)
    for s in range(2):
        seqf[2 + s : 3 + s, :] = jnp.full((1, seg_len), r_.reset[z % 2, s].astype(F32))
    r_.memp[...] = jnp.zeros_like(r_.memp)
    both_in = r_.memory_in[...].astype(F32)
    r_.memp[0:mem_rows, :] = jnp.where(z % 2 == 0, both_in[:, 0, :], both_in[:, 1, :]).astype(BF)
    for copy in pair:
        copy.start()

    def pad_text(j):
        both = r_.text[j].astype(F32)
        for s in range(2):
            r_.text_pad[j, s, 0:text_rows, :] = both[:, s, :].astype(BF)
            r_.text_pad[j, s, text_rows:step, :] = jnp.zeros((step - text_rows, width), BF)

    loop(2, pad_text)
    for ref in (r_.sg, r_.dinit, r_.dbin, r_.carry, r_.rs):
        ref[...] = jnp.zeros_like(ref)

    def attention_to_plane(k):
        for h in range(2):
            attention_in(k, h).wait_recv()
        attention_plane(k, 0).start()
        attention_plane(k, 1).start()

    def attention_across(k):
        attention_plane(k, 0).wait_recv()
        attention_plane(k, 2).start()
        attention_plane(k, 1).wait_recv()
        attention_plane(k, 3).start()

    for i in range(column_size):
        small_in(i).wait_recv()
    small_plane(0).start()
    small_plane(1).start()
    ffn_two(0)
    ffn_hop_on(1)
    pl.when(inside)(lambda: ffn_hop_on(2))
    side_first(order[1])
    rows_send(0)
    small_plane(0).wait_recv()
    small_plane(2).start()
    for k in range(2):
        pl.when(foreign[k] & is_home)(lambda: attention_to_plane(k))
    ffn_two(1)
    for k in range(2):
        pl.when(foreign[k] & away)(lambda: attention_to_plane(k))

    for copy in pair:
        copy.wait_recv()
    small_plane(1).wait_recv()
    small_plane(2).wait_recv()
    for i in range(total):
        par[0:16, lanes * i : lanes * (i + 1)] = r_.small_all[i, 0:16, 0:lanes].astype(F32)
    for zi in range(head_count):
        for p in range(planes):
            at = (zi * planes + p) * hid
            line = r_.small_all[(2 * p + core) * head_count + zi].astype(F32)
            r_.bin_row[0:1, at : at + hid] = line[0:1, 32 : 32 + hid]
    r_.bqv[...] = jnp.zeros_like(r_.bqv)
    for k in range(2):
        lines = r_.small_all[2 * core + k].astype(F32)
        for part in range(2):
            for b in range(per_block):
                line = lines[1 + part * per_block + b : 2 + part * per_block + b, 32 : 32 + HD]
                at = 2 * part * local + b * HD
                r_.bqv[k, at : at + HD, :] = as_column(line)
    seq = jnp.where(is_home, seqf[...], r_.seqf_in[...])
    seqf_out = r_.seq
    seqf_out[...] = seq
    flags = [seqf_out[2 + s : 3 + s, 0:1] for s in range(2)]
    tail_row = lax.broadcasted_iota(jnp.int32, (tail, width), 0)
    is_mem = tail_row >= tail - mem_rows
    init_b = jnp.where(is_mem, par[...], 0.0)
    given = jnp.where(is_home, r_.memp[...].astype(F32), r_.memp_in[...].astype(F32))
    first_b = jnp.where(flags[0] > 0, init_b, pltpu.roll(given, tail - mem_rows, 0))
    r_.cur_b[...] = first_b.astype(BF)
    r_.cur_a[...] = pltpu.roll(first_b, mem_rows, 0).astype(BF)

    def take_rows(r):
        inside = lax.broadcasted_iota(jnp.int32, (step, seg_len), 0)
        nat = lax.broadcasted_iota(jnp.int32, (step, seg_len), 1)
        return jnp.where((nat == r * text_rows + inside + mem_rows) & (inside < text_rows), 1.0, 0.0).astype(BF)

    def place_rows(r):
        nat = lax.broadcasted_iota(jnp.int32, (step, seg_len), 0) + r * step
        pad = lax.broadcasted_iota(jnp.int32, (step, seg_len), 1)
        inside = pad & (step - 1)
        target = (pad // step) * text_rows + inside + mem_rows
        return jnp.where((nat == target) & (inside < text_rows), 1.0, 0.0).astype(BF)

    wide = 2 * step

    def half_span(i):
        return pl.ds(pl.multiple_of(i * wide, wide), wide), i

    def end_span(i):
        return pl.ds(pl.multiple_of(i * (seg_len - step), step), step), i

    def middle_span(i):
        return pl.ds(step, wide), 2

    def exchange(slot, span):
        at, n = span
        return push(
            r_.send_buf.at[slot, at], r_.recv_buf.at[slot, at], r_.send_sem.at[slot, n], r_.recv_sem.at[slot, n],
            sibling,
        )

    def give(slot, span, part):
        at = span[0]
        acc[at, :] = part
        r_.send_buf[slot, at, :] = part.astype(BF)
        exchange(slot, span).start()

    def taken(slot, at):
        return acc[at, :] + r_.recv_buf[slot, at, :].astype(F32)

    def by_half(slot, body):
        def one(r):
            pl.when(r % 2 == 0)(lambda: exchange(slot, half_span(r // 2)).wait())
            body(rows(r))

        loop(head_count, one)

    def keep_scale(first, seg, at, scale):
        pair_at = slice(2 * first, 2 * first + 2)
        lane = lax.broadcasted_iota(jnp.int32, (1, 2), 1)
        r_.rs[at, pair_at] = jnp.where(lane == seg, scale, r_.rs[at, pair_at])

    def kept_scale(first, seg, at):
        lane = lax.broadcasted_iota(jnp.int32, (1, 2), 1)
        both = r_.rs[at, 2 * first : 2 * first + 2]
        return jnp.sum(jnp.where(lane == seg, both, 0.0), axis=1, keepdims=True)

    def back_copy(which, seg, zt):
        src, dst = ((r_.y, r_.acts_o), (r_.text_all, r_.text_pad))[which]
        span = pl.ds(pl.multiple_of(zt * step + core * piece, piece), piece)
        return src.at[seg, span], dst.at[z % 2, seg, pl.ds(core * piece, piece)]

    def back_out(which, seg, i):
        zt = (z + i) % head_count
        src, dst = back_copy(which, seg, zt)
        return push(
            src, dst, r_.back_s.at[which, seg, i], r_.back_r.at[which, seg, z % 2, core], device(z // 2, px, py, zt)
        )

    def back_here(which, seg):
        src, dst = back_copy(which, seg, z)
        return pltpu.make_async_copy(src, dst, r_.back_here_sem.at[which, seg])

    def back_send(which, seg):
        pl.when(is_home)(lambda: back_here(which, seg).start())
        pl.when(away)(lambda: back_out(which, seg, 0).start())
        for i in range(1, head_count):
            back_out(which, seg, i).start()

    def back_sent(which, seg):
        pl.when(is_home)(lambda: back_here(which, seg).wait())
        pl.when(away)(lambda: back_out(which, seg, 0).wait_send())
        for i in range(1, head_count):
            back_out(which, seg, i).wait_send()

    def back_done(which, seg):
        dst = (r_.acts_o, r_.text_pad)[which]
        for j in range(2):
            for h in range(2):
                when_not(
                    (core == h) & (z == 2 * core + j),
                    lambda: push(
                        r_.text_all.at[seg, pl.ds(0, piece)], dst.at[j, seg, pl.ds(h * piece, piece)],
                        r_.back_s.at[which, seg, 0], r_.back_r.at[which, seg, j, h], sibling,
                    ).wait_recv(),
                )

    def tail_z(which, i):
        zt = (z + 1 + i) % head_count
        to = device(core, px, py, zt)
        dst = r_.factors.at[which, z, plane]
        return push(r_.factor_out.at[which, zt], dst, r_.tg_s.at[which, i], r_.tg_r.at[which, z], to)

    def tail_z_in(which, i):
        zs = (z + 1 + i) % head_count
        dst = r_.factors.at[which, zs, plane]
        return push(r_.factor_out.at[which, zs], dst, r_.tg_s.at[which, i], r_.tg_r.at[which, zs], sibling)

    def tail_plane(which, i):
        p, zs, to = (
            (plane, slice(None), x_mate), (plane, slice(None), y_mate),
            (x_plane, pl.ds(0, 2), y_mate), (y_plane, pl.ds(2, 2), x_mate),
        )[i]
        buf = r_.factors.at[which, zs, p]
        return push(buf, buf, r_.tg_s.at[which, 3 + i], r_.tg_r.at[which, head_count + i], to)

    def tail_pair(which):
        src = r_.factors.at[which, :, :, :, pl.ds(0, half_width)]
        return push(src, r_.factors_in.at[which], r_.tp_s.at[which], r_.tp_r.at[which], sibling)

    def tail_gather(which, stage):
        if stage == 0:
            for i in range(head_count - 1):
                tail_z(which, i).start()
            r_.factors[which, z, plane] = r_.factor_out[which, z]
        elif stage == 1:
            for i in range(head_count - 1):
                tail_z_in(which, i).wait_recv()
            tail_plane(which, 0).start()
            tail_plane(which, 1).start()
        elif stage == 2:
            for i in range(2):
                tail_plane(which, i).wait_recv()
                tail_plane(which, 2 + i).start()
        elif stage == 3:
            for i in range(2):
                tail_plane(which, 2 + i).wait_recv()
            tail_pair(which).start()
        else:
            for i in range(head_count - 1):
                tail_z(which, i).wait_send()
            for i in range(4):
                tail_plane(which, i).wait_send()

    half_width = width // 2

    def half_of(h):
        return pl.ds(pl.multiple_of(h * half_width, half_width), half_width)

    def tail_put(which, hidden_ref, units):
        part = hidden_ref[0, tail_at, half_of(core)]
        for zt in range(head_count):
            r_.factor_out[which, zt, :, 0:half_width] = part
            r_.factor_out[which, zt, :, half_width:] = units[:, zt * chunk : (zt + 1) * chunk]
        tail_gather(which, 0)

    def tail_products():
        down = lax.broadcasted_iota(jnp.int32, (chunk, 128), 0)
        across = lax.broadcasted_iota(jnp.int32, (chunk, 128), 1)
        pick = jnp.where((down == plane * hid + across) & (across < hid), 1.0, 0.0).astype(BF)
        all_rows = planes * head_count * tail
        units = [
            nn(r_.factors[which, :, :, :, half_width:].reshape(all_rows, chunk), pick).astype(BF) for which in range(2)
        ]
        for which in range(2):
            tail_pair(which).wait()
        out = []
        for kind in range(2):
            mine = tn(units[1 - kind], r_.factors[kind, :, :, :, 0:half_width].reshape(all_rows, half_width))[0:hid, :]
            theirs = tn(units[1 - kind], r_.factors_in[kind].reshape(all_rows, half_width))[0:hid, :]
            out.append((mine, theirs))
        return out

    def build(seg):
        def one(r):
            x[seg, rows(r), :] = nn(place_rows(r), r_.text_all[seg]).astype(BF)

        loop(head_count, one)

    def add_memory(seg):
        x[seg, 0:tail, :] = x[seg, 0:tail, :] + r_.cur_a[...]
        x[seg, tail_at, :] = x[seg, tail_at, :] + r_.cur_b[...]

    def make_mask(seg):
        right = r_.seq[pl.ds(seg, 1), :]
        left = as_column(right)
        acc[:, 0:seg_len] = jnp.where((left == right) | (left < 0) | (right < 0), 0.0, -1e30)

    def keep_projected(seg, j, at, value):
        value = value + r_.bqv[j]
        qkv[seg, j, 0:local, at] = (value[0:local, :] * 0.125).astype(BF)
        qkv[seg, j, local:, at] = value[local:, :].astype(BF)

    def project(seg):
        def one(j):
            keep_projected(seg, j, slice(None), nt(wa[j, 0 : 3 * local, :], x[seg]))

        loop(2, one)

    def project_ends(seg):
        both = jnp.concatenate([x[seg, 0:step, :], x[seg, seg_len - step :, :]], axis=0)

        def one(j):
            value = nt(wa[j, 0 : 3 * local, :], both)
            keep_projected(seg, j, slice(0, step), value[:, 0:step])
            keep_projected(seg, j, slice(seg_len - step, seg_len), value[:, step:])

        loop(2, one)

    def attend(seg):
        def one(h):
            j = h // per_block
            q, k, v = (qkv[seg, j, head_rows(h, part), :] for part in range(3))
            s = tn(k, q) + acc[:, 0:seg_len]
            e = jnp.exp(s - jnp.max(s, axis=0, keepdims=True))
            p = (e * (1.0 / jnp.sum(e, axis=0, keepdims=True))).astype(BF)
            pt[seg, h] = p
            ot[seg, j, head_rows(h, 0), :] = nn(v, p).astype(BF)

        loop(heads, one, unroll=2)

    def out_project(seg):
        def one(i):
            span = half_span(i)
            at = span[0]
            give(
                0, span, tn(ot[seg, 0, :, at], wa[0, 3 * local :, :]) + tn(ot[seg, 1, :, at], wa[1, 3 * local :, :])
            )

        loop(2, one)

    def norm_one(seg):
        def one(at):
            hat, scale = norm(x[seg, at, :].astype(F32) + taken(0, at) + par[3:4, :])
            r_.xh1[seg, at, :] = hat.astype(BF)
            keep_scale(0, seg, at, scale)
            h = hat * par[0:1, :] + par[2:3, :]
            hf[at, :] = h
            r_.hb[seg, at, :] = h.astype(BF)

        by_half(0, one)

    def inner(seg, at):
        v = nt(r_.hb[seg], wf[0, at, :]) + r_.bin_row[:, at]
        c0 = 0.7978845608028654
        sq = v * v
        th = jnp.tanh(v * (c0 + (c0 * 0.044715) * sq))
        up = 0.5 + 0.5 * th
        active = v * up
        r_.u[seg, :, at] = active.astype(BF)
        slope = up + active * (1.0 - up) * (2 * c0 + (6 * c0 * 0.044715) * sq)
        r_.gp[seg, :, at] = slope.astype(BF)

    def outer(seg):
        def one(i):
            span = half_span(i)
            give(1, span, nn(r_.u[seg, span[0], :], wf[1]))

        loop(2, one)

    def norm_two(seg):
        def one(at):
            hat, scale = norm(hf[at, :] + taken(1, at) + par[4:5, :])
            r_.xh2[seg, at, :] = hat.astype(BF)
            keep_scale(1, seg, at, scale)
            r_.y[seg, at, :] = (hat * par[1:2, :] + par[5:6, :]).astype(BF)

        by_half(1, one)

    def next_memory():
        last = r_.y[0, tail_at, :].astype(F32)
        memory = jnp.where(is_mem, jnp.where(flags[1] > 0, par[...], last), 0.0)
        r_.cur_b[...] = memory.astype(BF)
        r_.cur_a[...] = pltpu.roll(memory, mem_rows, 0).astype(BF)

    pl.when(inside)(lambda: ffn_hop_on(3))
    pl.when(depth == 0)(lambda: ffn_hop_on(2))
    for k in range(2):
        pl.when(foreign[k])(lambda: attention_across(k))
    side_first(order[2])
    rows_pass(0)
    rows_ready(0)
    build(0)
    add_memory(0)
    for k in range(2):

        def last_part():
            attention_plane(k, 2).wait_recv()
            attention_plane(k, 3).wait_recv()

        pl.when(foreign[k])(last_part)

    def kept_own():
        for copy in own_attention:
            copy.wait()

    pl.when(is_home)(kept_own)
    project(0)
    pl.when(depth == 0)(lambda: ffn_hop_on(3))
    side_first(order[3])
    rows_send(1)

    def forward(seg):
        make_mask(seg)
        attend(seg)

        def between():
            rows_pass(3)
            back_send(0, 0)

        pl.when(seg == 1)(between)
        out_project(seg)

        def rows_next():
            ffn_two(2)
            rows_send(3)
            rows_send(2)

        pl.when(seg == 0)(rows_next)
        norm_one(seg)

        def units(n):
            def start_two():
                ffn_two(3)
                rows_ready(1)
                build(1)
                project(1)

            def rows_on():
                rows_pass(1)

            pl.when(n == 2)(rows_on)
            pl.when(n == 3)(start_two)
            ffn_ready(n)
            inner(0, cols(order_at(n)))

        def wide_units():
            loop(2, lambda n: inner(1, pl.ds(pl.multiple_of(n * 2 * chunk, 2 * chunk), 2 * chunk)))

        pl.when(seg == 0)(lambda: loop(head_count, units))
        pl.when(seg == 1)(wide_units)
        outer(seg)
        pl.when(seg == 1)(lambda: rows_pass(2))
        norm_two(seg)

        def on_to_two():
            rows_done(0)
            rows_done(1)
            next_memory()
            add_memory(1)
            project_ends(1)
            tail_put(0, r_.hb, r_.u[0, tail_at, :])

        pl.when(seg == 0)(on_to_two)

    loop(2, forward)
    back_send(0, 1)
    rows_ready(3)

    def pull_two_part(g_y, hat, scale):
        pre = pull_norm(g_y * par[1:2, :], hat, scale)
        r_.sg[1:2, :] += row_sum(g_y * hat)
        r_.sg[5:6, :] += row_sum(g_y)
        r_.sg[4:5, :] += row_sum(pre)
        return pre.astype(BF)

    def pull_two():
        def one(n):
            seg, r = 1 - n // head_count, n % head_count
            pl.when(n == head_count)(lambda: rows_ready(2))
            below = lax.broadcasted_iota(jnp.int32, (step, width), 0) + r * step
            held = (below >= seg_len - tail) & (seg == 0)
            g_y = jnp.where(held, 0.0, r_.cot_all[seg, rows(r), :].astype(F32))
            hat = r_.xh2[seg, rows(r), :].astype(F32)
            r_.xh2[seg, rows(r), :] = pull_two_part(g_y, hat, kept_scale(1, seg, rows(r)))

        loop(2 * head_count, one)

    def keep_tail():
        r_.xh2_t[...] = r_.xh2[0, tail_at, :]
        r_.gp_t[...] = r_.gp[0, tail_at, :]

    def pull_tail():
        g_y = r_.cot_all[0, tail_at, :].astype(F32) + r_.carry[...]
        pre = pull_two_part(g_y, r_.xh2_t[...].astype(F32), kept_scale(1, 0, tail_at))
        r_.xh2[0, tail_at, :] = pre
        g_z = (nt(pre, wf[1]) * r_.gp_t[...].astype(F32)).astype(BF)
        r_.gp[0, tail_at, :] = g_z
        r_.dbin[0:1, :] += row_sum(g_z.astype(F32))
        tail_put(1, r_.xh2, g_z)

    def pull_inner(i):
        both = r_.xh2[...].reshape(2 * seg_len, width)
        g_u = nt(both, wf[1, cols(i), :])
        for seg in range(2):
            g_z = (g_u[seg * seg_len : (seg + 1) * seg_len, :] * r_.gp[seg, :, cols(i)].astype(F32)).astype(BF)
            r_.gp[seg, :, cols(i)] = g_z
            r_.dbin[0:1, cols(i)] += row_sum(g_z.astype(F32))

    def pull_hidden(seg):
        def one(i):
            span = half_span(i)
            give(0, span, nn(r_.gp[seg, span[0], :], wf[0]))

        loop(2, one)

    def pull_one(seg):
        def one(at):
            g_h = r_.xh2[seg, at, :].astype(F32) + taken(0, at)
            hat = r_.xh1[seg, at, :].astype(F32)
            pre = pull_norm(g_h * par[0:1, :], hat, kept_scale(0, seg, at))
            hf[at, :] = pre
            r_.xh1[seg, at, :] = pre.astype(BF)
            r_.sg[0:1, :] += row_sum(g_h * hat)
            r_.sg[2:3, :] += row_sum(g_h)
            r_.sg[3:4, :] += row_sum(pre)

        by_half(0, one)

        def out(j):
            r_.got[j] = nt(wa[j, 3 * local :, :], r_.xh1[seg]).astype(BF)

        loop(2, out)

    def pull_heads(seg):
        def one(h):
            j = h // per_block
            q, k, v = (qkv[seg, j, head_rows(h, part), :] for part in range(3))
            g_o = r_.got[j, head_rows(h, 0), :]
            p = pt[seg, h]
            d_v = nt(g_o, p).astype(BF)
            total_p = row_sum(g_o.astype(F32) * ot[seg, j, head_rows(h, 0), :].astype(F32))
            d_s = (p.astype(F32) * (tn(v, g_o) - total_p)).astype(BF)
            d_q = (nn(k, d_s) * 0.125).astype(BF)
            d_k = nt(q, d_s).astype(BF)
            for part, value in enumerate((d_q, d_k, d_v)):
                qkv[seg, j, head_rows(h, part), :] = value

        loop(heads, one, unroll=2)

    def pull_rows(seg, span):
        at = span[0]
        give(
            1, span,
            tn(qkv[seg, 0, :, at], wa[0, 0 : 3 * local, :]) + tn(qkv[seg, 1, :, at], wa[1, 0 : 3 * local, :]),
        )

    def pull_x(at):
        value = hf[at, :] + taken(1, at)
        acc[at, :] = value
        r_.send_buf[1, at, :] = value.astype(BF)

    def pull_memory(seg):
        both = pltpu.roll(acc[0:tail, :], tail - mem_rows, 0) + acc[seg_len - tail : seg_len, :]
        memory = jnp.where(is_mem, both, 0.0)
        r_.dinit[...] += jnp.where(flags[seg] > 0, memory, 0.0)
        if seg == 1:
            r_.carry[...] = jnp.where(flags[1] > 0, 0.0, memory)

    def text_grad(seg):
        def one(r):
            r_.text_all[seg, rows(r), :] = nn(take_rows(r), r_.send_buf[1]).astype(BF)

        loop(head_count, one)

    def cut(buf, kind, a, b):
        first, second = (px, py) if kind == 0 else (py, px)
        first = first if a == 0 else 1 - first
        second = second if b == 0 else 1 - second
        return buf.at[second, first] if kind == 0 else buf.at[first, second]

    def parts_of(name):
        return sums[name] if isinstance(name, str) else ffn_sum(name)

    sum_mates = ((x_mate, y_mate), (y_mate, x_mate))

    def sum_one(name, kind, b):
        buf, got, s, r = parts_of(name)(kind)
        return push(cut(buf, kind, 1, b), got[0].at[b], s.at[b], r.at[b], sum_mates[kind][0])

    def sum_two(name, kind):
        buf, got, s, r = parts_of(name)(kind)
        return push(cut(buf, kind, 0, 1), got[1], s.at[2], r.at[2], sum_mates[kind][1])

    def ffn_sum(d):
        zi = order_at(d)

        def parts(kind):
            return (
                r_.fsend.at[kind, zi], (r_.f_one.at[kind, zi], r_.f_two.at[kind, zi]),
                r_.fsum_s.at[kind, zi], r_.fsum_r.at[kind, zi],
            )

        return parts

    sums = {}

    def attention_sum(n):
        def parts(kind):
            return (
                r_.asend.at[n, kind], (r_.a_one.at[n, kind], r_.a_two.at[n, kind]),
                r_.asum_s.at[n, kind], r_.asum_r.at[n, kind],
            )

        return parts

    halves = ("a", "b")
    for n, name in enumerate(halves):
        sums[name] = attention_sum(n)
    sums["v"] = lambda kind: (
        r_.vsend.at[kind], (r_.v_one.at[kind], r_.v_two.at[kind]), r_.vsum_s.at[kind], r_.vsum_r.at[kind]
    )

    def start_sum(name, which=((1, 0), (1, 1), (0, 0), (0, 1))):
        for b, kind in which:
            sum_one(name, kind, b).start()

    def travel(name):
        for kind in range(2):
            buf, got, _, _ = parts_of(name)(kind)
            sum_one(name, kind, 1).wait_recv()
            add_all(cut(buf, kind, 0, 1), got[0].at[1])
            sum_two(name, kind).start()

    def end_plane(name):
        for kind in range(2):
            buf, got, _, _ = parts_of(name)(kind)
            sum_one(name, kind, 0).wait_recv()
            sum_two(name, kind).wait_recv()
            add_all(cut(buf, kind, 0, 0), got[0].at[0], got[1])

    def sum_sent(name):
        for kind in range(2):
            for b in range(2):
                sum_one(name, kind, b).wait_send()
            sum_two(name, kind).wait_send()

    def z_out(kind, d):
        slot = jnp.where(inside, jnp.where(d == 1, 0, jnp.where(d == 2, 4, 1)), jnp.where(d == 1, 0, d))
        to = from_end(jnp.where(inside, jnp.where(d == 1, 0, 2), 1))
        return push(
            cut(r_.fsend.at[kind, order_at(d)], kind, 0, 0), r_.f_z.at[kind, slot], r_.fz_s.at[kind, d],
            r_.fz_r.at[kind, slot], device(core, px, py, to),
        )

    def z_in(kind, slot):
        return push(
            cut(r_.fsend.at[kind, z], kind, 0, 0), r_.f_z.at[kind, slot], r_.fz_s.at[kind, 0], r_.fz_r.at[kind, slot],
            sibling,
        )

    def end_ffn(d):
        end_plane(d)

        def send():
            for kind in range(2):
                z_out(kind, d).start()

        if d > 0:
            pl.when(depth == 0)(send)

    def z_pass(d):
        def add_and_send():
            for kind in range(2):
                z_in(kind, d).wait_recv()
                add_all(cut(r_.fsend.at[kind, order_at(d)], kind, 0, 0), r_.f_z.at[kind, d])
                z_out(kind, d).start()

        pl.when(inside)(add_and_send)

    def last_out(name, k, h):
        buf, dst, s, r = last[name]
        return push(
            cut(buf.at[k], k, 0, 0).at[h], dst.at[z], s.at[k, h], r.at[z], device(h, px, py, 2 * core + k)
        )

    def last_here(name, k):
        buf, dst, _, _ = last[name]
        return pltpu.make_async_copy(cut(buf.at[k], k, 0, 0).at[core], dst.at[z], r_.last_sem.at["abv".index(name)])

    last = {
        "a": (r_.asend.at[0], r_.a_z.at[0], r_.az_s.at[0], r_.az_r.at[0]),
        "b": (r_.asend.at[1], r_.a_z.at[1], r_.az_s.at[1], r_.az_r.at[1]),
        "v": (r_.vsend, r_.v_z, r_.vz_s, r_.vz_r),
    }

    def last_each(name, here_do, away_do):
        for k in range(2):
            for h in range(2):
                here = (core == h) & (z == 2 * core + k)
                if here_do is not None:
                    pl.when(here)(lambda: here_do(last_here(name, k)))
                when_not(here, lambda: away_do(last_out(name, k, h)))

    def last_total(name):
        buf, dst, s, r = last[name]
        for zs in range(head_count):
            here = is_home & (z == zs)
            pl.when(here)(lambda: last_here(name, 0).wait())
            when_not(
                here, lambda: push(buf.at[0, 0, 0, 0], dst.at[zs], s.at[0, 0], r.at[zs], sibling).wait_recv()
            )
        value = dst[0].astype(F32)
        for zs in range(1, head_count):
            value = value + dst[zs].astype(F32)
        return value

    def ffn_grads(d):
        i = order_at(d)

        def grads(kind, left, right):
            value = tn(left[0, :, cols(i)], right[0]) + tn(left[1, :, cols(i)], right[1])
            for p in range(planes):
                r_.fsend[kind, i, p // 2, p % 2] = value[p * hid : (p + 1) * hid, :].astype(BF)

        grads(1, r_.u, r_.xh2)

        def first_kind():
            pl.when(d == 2)(lambda: travel(3))
            start_sum(d, ((1, 1), (0, 1)))

        pl.when(d >= 2)(first_kind)
        pull_inner(i)
        grads(0, r_.gp, r_.hb)
        pl.when(d >= 2)(lambda: start_sum(d, ((1, 0), (0, 0))))

    keep_tail()
    pull_two()
    tail_gather(0, 1)
    loop(head_count, lambda n: ffn_grads(head_count - 1 - n))
    dbin_pair = push(r_.dbin, r_.dbin_in, r_.pair_s.at[2], r_.pair_r.at[2], sibling)

    def backward(n):
        seg = 1 - n
        pull_hidden(seg)

        pull_one(seg)

        def first_events():
            end_ffn(3)
            travel(2)
            start_sum(1)
            start_sum(0)
            tail_gather(0, 2)

        pl.when(seg == 1)(first_events)
        pull_heads(seg)

        def segment_two():
            loop(2, lambda i: pull_rows(1, end_span(i)))

            def one(i):
                exchange(1, end_span(i)).wait()
                pull_x(end_span(i)[0])

            loop(2, one)
            pull_memory(1)
            pull_tail()
            dbin_pair.start()
            pull_rows(1, middle_span(0))
            z_pass(3)
            end_ffn(2)
            travel(1)
            exchange(1, middle_span(0)).wait()
            pull_x(middle_span(0)[0])
            text_grad(1)
            back_send(1, 1)

        pl.when(seg == 1)(segment_two)

    loop(2, backward)
    travel(0)
    z_pass(2)
    hid_rows = width // dp_count
    cut_rows = hid_rows // 2

    def attention_grads(i):
        wide = width // 2
        span = pl.ds(pl.multiple_of(i * wide, wide), wide)
        xt = [x[s, :, span].T for s in range(2)]
        gt = [r_.xh1[s, :, span].T for s in range(2)]
        for k in range(2):
            qkv_g = nt(xt[0], qkv[0, k]) + nt(xt[1], qkv[1, k])
            out_g = nt(gt[0], ot[0, k]) + nt(gt[1], ot[1, k])
            for b in range(8):
                at = slice(b * cut_rows, (b + 1) * cut_rows)
                r_.asend[b % 2, k, i, b // 4, (b // 2) % 2, :, 0 : 3 * local] = qkv_g[at, :].astype(BF)
                r_.asend[b % 2, k, i, b // 4, (b // 2) % 2, :, 3 * local :] = out_g[at, :].astype(BF)

    def both_planes(n):
        attention_grads(jnp.where(n == 0, 1 - py, py))

        def travelling():
            for name in halves:
                start_sum(name, ((1, 0), (1, 1)))

        pl.when(n == 0)(travelling)

    loop(2, both_planes)
    start_sum("a", ((0, 1), (0, 0)))
    tail_gather(1, 1)
    end_ffn(1)
    loop(2, lambda i: pull_rows(0, half_span(i)))
    by_half(1, pull_x)
    pull_memory(0)
    dbin_pair.wait()

    dbin_both = [jnp.where(core == h, r_.dbin[0:1, :], r_.dbin_in[0:1, :]) for h in range(2)]
    for k in range(2):
        r_.bqv[k] = sum(jnp.sum(qkv[s, k].astype(F32), axis=1, keepdims=True) for s in range(2))
    sg, dinit = r_.sg, r_.dinit
    r_.vec[...] = jnp.where(is_mem, dinit[...], 0.0)
    r_.vec[0:6, :] = sg[0:6, :]
    vtmp[...] = jnp.zeros_like(vtmp)

    def by_core(cut_of):
        return jnp.where(core == 0, cut_of(0), cut_of(1))

    qv_rows = [
        [
            jnp.sum(
                jnp.where(
                    lax.broadcasted_iota(jnp.int32, (HD, HD), 0) == lax.broadcasted_iota(jnp.int32, (HD, HD), 1),
                    r_.bqv[k, 2 * part * local + b * HD : 2 * part * local + (b + 1) * HD, :],
                    0.0,
                ),
                axis=0,
                keepdims=True,
            )
            for part in range(2)
            for b in range(per_block)
        ]
        for k in range(2)
    ]
    piece_b = HD // dp_count
    vec = r_.vec[...]

    def small_cut(k, p, h):
        dp_t = 2 * p + h

        def from_vec(c):
            at = (dp_t * head_count + 2 * c + k) * lanes
            return vec[:, at : at + lanes]

        def from_bin(c):
            at = ((2 * c + k) * planes + p) * hid
            return dbin_both[h][:, at : at + hid]

        vtmp[0:16, 0:lanes] = by_core(from_vec)
        vtmp[0:1, 32 : 32 + hid] = by_core(from_bin)
        for n, line in enumerate(qv_rows[k]):
            vtmp[1:2, 32 + n * piece_b : 32 + (n + 1) * piece_b] = line[:, dp_t * piece_b : (dp_t + 1) * piece_b]
        r_.vsend[k, p // 2, p % 2, h] = vtmp[...].astype(BF)

    for k in range(2):
        for p in range(planes):
            for h in range(2):
                small_cut(k, p, h)
    start_sum("v")
    end_ffn(0)
    z_pass(1)
    travel("a")
    start_sum("b", ((0, 1), (0, 0)))
    text_grad(0)
    back_send(1, 0)
    travel("b")
    travel("v")
    end_plane("a")
    last_each("a", lambda c: c.start(), lambda c: c.start())
    tail_gather(1, 2)
    end_plane("v")
    last_each("v", lambda c: c.start(), lambda c: c.start())
    end_plane("b")
    last_each("b", lambda c: c.start(), lambda c: c.start())

    tail_gather(0, 3)
    tail_gather(1, 3)
    extra = tail_products()
    for kind, out in enumerate((r_.win_o, r_.wback_o)):
        value = cut(r_.fsend.at[kind, z], kind, 0, 0)[...].astype(F32)
        z_in(kind, 0).wait_recv()
        out[...] = value + r_.f_z[kind, 0].astype(F32)

        def other_side():
            z_in(kind, 4).wait_recv()
            out[...] += r_.f_z[kind, 4].astype(F32)

        pl.when(inside)(other_side)
        out[:, half_of(core)] += extra[kind][0]
        out[:, half_of(1 - core)] += extra[kind][1]


    for name in (0, 1, 2, 3, "a", "b", "v"):
        sum_sent(name)
    for d in range(1, head_count):
        for kind in range(2):
            z_out(kind, d).wait_send()
    for which in range(2):
        for seg in range(2):
            back_sent(which, seg)
            back_done(which, seg)
    for a in range(2, 4):
        rows_done(a)
    attention_outs(lambda c: c.wait_send())
    ffn_sent()
    for which in range(2):
        tail_gather(which, 4)
    for copy in pair:
        copy.wait_send()
    for k in range(2):

        def sent():
            for which in range(4):
                attention_plane(k, which).wait_send()

        pl.when(foreign[k])(sent)
    for zi in range(head_count):
        for kind in range(2):
            for which in range(3):
                side(kind, zi, which).wait_send()
    for i in range(column_size):
        small_out(i).wait_send()
    for i in range(3):
        small_plane(i).wait_send()
    for j in range(2):
        both = [r_.text_pad[j, s, 0:text_rows, :].astype(F32)[:, None, :] for s in range(2)]
        r_.dt_o[j] = jnp.concatenate(both, axis=1).astype(BF)
    r_.att_o[0:cut_rows, :] = last_total("a")
    r_.att_o[cut_rows:hid_rows, :] = last_total("b")
    r_.vec_o[...] = last_total("v")
    for name in "abv":
        last_each(name, None, lambda c: c.wait_send())


def vmem(*shape, dtype=BF):
    return pltpu.VMEM(shape, dtype)


def f32(*shape):
    return pltpu.VMEM(shape, F32)


def sds(*shape, dtype=BF):
    return jax.ShapeDtypeStruct(shape, dtype)


def dma(*shape):
    return pltpu.SemaphoreType.DMA(shape)


ANY = pl.BlockSpec(memory_space=pl.ANY)
INV = pl.BlockSpec(memory_space=pltpu.VMEM)
INS = pl.BlockSpec(memory_space=pltpu.SMEM)


def end_kernel(mem_rows, hid, lanes, acts, dt, win, wback, att, vec, *outs):
    acts_o, dt_o, dinit_o, dqkv_o, dbqv_o, dwout_o, dwin_o, dwback_o, dbin_o, dgains_o, dbiases_o = outs
    acts_o[...] = acts[...]
    dt_o[...] = dt[...]
    dinit_o[...] = vec[6 : 6 + mem_rows, 0:lanes]
    parts, _, local_width = dqkv_o.shape
    for t in range(parts):
        dqkv_o[t] = att[:, t * local_width : (t + 1) * local_width]
    per_block, _, slice_b = dbqv_o.shape
    for b in range(per_block):
        for part in range(2):
            at = 32 + (part * per_block + b) * slice_b
            dbqv_o[b, part : part + 1, :] = vec[1:2, at : at + slice_b]
    dwout_o[...] = att[:, parts * local_width :].T
    dwin_o[...] = win[...]
    dwback_o[...] = wback[...]
    dbin_o[...] = vec[0:1, 32 : 32 + hid]
    dgains_o[...] = vec[0:2, 0:lanes]
    dbiases_o[...] = vec[2:6, 0:lanes]


def by_chip(
    text, boundary, reset, memory_in, init_memory, w_qkv, b_qv, w_out, w_in, w_back, b_in, norm_gains, biases,
    cotangent,
):
    head_count = lax.axis_size("head")
    dp_count = lax.axis_size("dp")
    planes = dp_count // 2
    total = dp_count * head_count
    text_rows, width = text.shape[2], text.shape[3]
    block = cotangent.shape[2]
    seg_len = block * head_count
    mem_rows = memory_in.shape[1]
    local = w_qkv.shape[2]
    hid = w_in.shape[1]
    lanes = norm_gains.shape[1]
    heads = 2 * local // HD
    hidden = hid * planes * head_count
    share = width // dp_count

    inputs = dict(
        text=(text.transpose(0, 2, 1, 3), INV),
        boundary=(boundary, INV),
        reset=(reset, INS),
        memory_in=(memory_in.transpose(1, 0, 2), INV),
        init_memory=(init_memory, INV),
        wq_t=(w_qkv.transpose(1, 2, 0).reshape(3 * local, width), ANY),
        w_out=(w_out, ANY),
        b_qv=(b_qv.transpose(1, 0, 2), INV),
        w_in_t=(w_in.T, INV),
        w_back=(w_back, INV),
        b_in=(b_in[None, :], INV),
        norm_gains=(norm_gains, INV),
        biases=(biases, INV),
        cotangent=(cotangent, ANY),
    )
    outputs = dict(
        acts_o=(sds(2, 2, block, width), ANY),
        dt_o=(sds(2, text_rows, 2, width), INV),
        win_o=(sds(hid, width, dtype=F32), INV),
        wback_o=(sds(hid, width, dtype=F32), INV),
        att_o=(sds(share, width, dtype=F32), INV),
        vec_o=(sds(16, 128, dtype=F32), INV),
    )
    scratch = dict(
        text_pad=vmem(2, 2, block, width),
        text_all=vmem(2, seg_len, width),
        cot_all=vmem(2, seg_len, width),
        wa=vmem(2, 4 * local, width),
        wf=vmem(2, hidden, width),
        small=vmem(16, 128),
        small_all=vmem(total, 16, 128),
        seqf=f32(8, seg_len),
        seqf_in=f32(8, seg_len),
        seq=f32(8, seg_len),
        memp=vmem(16, width),
        memp_in=vmem(16, width),
        par=f32(16, width),
        bin_row=f32(1, hidden),
        bqv=f32(2, 3 * local, 1),
        x=vmem(2, seg_len, width),
        qkv=vmem(2, 2, 3 * local, seg_len),
        pt=vmem(2, heads, seg_len, seg_len),
        ot=vmem(2, 2, local, seg_len),
        hf=f32(seg_len, width),
        acc=f32(seg_len, width),
        xh1=vmem(2, seg_len, width),
        hb=vmem(2, seg_len, width),
        u=vmem(2, seg_len, hidden),
        gp=vmem(2, seg_len, hidden),
        xh2=vmem(2, seg_len, width),
        rs=f32(seg_len, 4),
        y=vmem(2, seg_len, width),
        got=vmem(2, local, seg_len),
        send_buf=vmem(2, seg_len, width),
        recv_buf=vmem(2, seg_len, width),
        cur_a=vmem(16, width),
        cur_b=vmem(16, width),
        carry=f32(16, width),
        xh2_t=vmem(16, width),
        gp_t=vmem(16, hidden),
        factor_out=vmem(2, head_count, 16, width // 2 + hidden // head_count),
        factors=vmem(2, head_count, planes, 16, width // 2 + hidden // head_count),
        factors_in=vmem(2, head_count, planes, 16, width // 2),
        sg=f32(8, width),
        dinit=f32(16, width),
        dbin=f32(8, hidden),
        dbin_in=f32(8, hidden),
        vec=f32(16, width),
        vtmp=f32(16, 128),
        fsend=vmem(2, head_count, 2, 2, hid, width),
        f_one=vmem(2, head_count, 2, hid, width),
        f_two=vmem(2, head_count, hid, width),
        f_z=vmem(2, head_count + 1, hid, width),
        asend=vmem(2, 2, 2, 2, 2, share // 2, width),
        a_one=vmem(2, 2, 2, 2, share // 2, width),
        a_two=vmem(2, 2, 2, share // 2, width),
        a_z=vmem(2, head_count, share // 2, width),
        vsend=vmem(2, 2, 2, 2, 16, 128),
        v_one=vmem(2, 2, 2, 16, 128),
        v_two=vmem(2, 2, 16, 128),
        v_z=vmem(head_count, 16, 128),
        small_s=dma(7),
        small_r=dma(4, 2),
        small_ps=dma(3),
        small_pr=dma(3),
        pair_s=dma(3),
        pair_r=dma(3),
        att_s=dma(3),
        att_r=dma(2, 2),
        plane_s=dma(2, 4),
        plane_r=dma(2, 4),
        local_sem=dma(2),
        rows_s=dma(4, 2, 2),
        rows_r=dma(4, 4),
        here_sem=dma(4),
        fwd_s=dma(4, 4),
        fwd_r=dma(4, 4),
        ffn_s=dma(5),
        ffn_r=dma(4),
        side_s=dma(4, 2, 3),
        side_r=dma(4, 2, 3),
        send_sem=dma(2, 4),
        recv_sem=dma(2, 4),
        back_s=dma(2, 2, 4),
        back_r=dma(2, 2, 2, 2),
        back_here_sem=dma(2, 2),
        fsum_s=dma(2, 4, 3),
        fsum_r=dma(2, 4, 3),
        asum_s=dma(2, 2, 3),
        asum_r=dma(2, 2, 3),
        tg_s=dma(2, 7),
        tg_r=dma(2, 8),
        tp_s=dma(2),
        tp_r=dma(2),
        vsum_s=dma(2, 3),
        vsum_r=dma(2, 3),
        fz_s=dma(2, 4),
        fz_r=dma(2, 5),
        az_s=dma(2, 2, 2),
        az_r=dma(2, 4),
        vz_s=dma(2, 2),
        vz_r=dma(4),
        last_sem=dma(3),
    )
    names = tuple(inputs) + tuple(outputs) + tuple(scratch)
    middle = pl.pallas_call(
        functools.partial(main_kernel, names, dp_count, head_count),
        out_shape=tuple(v[0] for v in outputs.values()),
        in_specs=[v[1] for v in inputs.values()],
        out_specs=tuple(v[1] for v in outputs.values()),
        scratch_shapes=list(scratch.values()),
        compiler_params=pltpu.CompilerParams(
            collective_id=0, has_side_effects=True, vmem_limit_bytes=VMEM_LIMIT
        ),
        name="layer",
    )(*(v[0] for v in inputs.values()))

    slice_b = HD // dp_count
    out = pl.pallas_call(
        functools.partial(end_kernel, mem_rows, hid, lanes),
        out_shape=(
            sds(2, 2, block, width),
            sds(2, text_rows, 2, width),
            sds(mem_rows, lanes, dtype=F32),
            sds(3, share, local, dtype=F32),
            sds(local // HD, 2, slice_b, dtype=F32),
            sds(local, share, dtype=F32),
            sds(hid, width, dtype=F32),
            sds(hid, width, dtype=F32),
            sds(1, hid, dtype=F32),
            sds(2, lanes, dtype=F32),
            sds(4, lanes, dtype=F32),
        ),
        in_specs=[INV] * 6,
        out_specs=tuple([INV] * 11),
        name="results",
    )(*middle)
    acts, d_text, d_init, d_qkv, d_bqv, d_wout, d_win, d_wback, d_bin, d_gains, d_biases = out
    return (
        acts, d_text.transpose(0, 2, 1, 3), d_init,
        d_qkv.transpose(1, 0, 2),
        d_bqv.transpose(1, 0, 2),
        d_wout, d_win.T, d_wback, d_bin[0], d_gains, d_biases,
    )


def solution(mesh):
    body = by_chip if mesh.shape["dp"] == 8 and mesh.shape["head"] == 4 else local
    return jax.shard_map(
        body,
        mesh=mesh,
        in_specs=(
            P("dp", None, "head", None),
            P("dp", None, None),
            P("dp", None),
            P("dp", None, None),
            P(None, ("dp", "head")),
            P(None, None, "head"),
            P(None, "head", None),
            P("head", None),
            P(None, ("dp", "head")),
            P(("dp", "head"), None),
            P(("dp", "head")),
            P(None, ("dp", "head")),
            P(None, ("dp", "head")),
            P("dp", None, "head", None),
        ),
        out_specs=(
            P("dp", None, "head", None),
            P("dp", None, "head", None),
            P(None, ("dp", "head")),
            P("dp", None, "head"),
            P(None, "head", "dp"),
            P("head", "dp"),
            P(None, ("dp", "head")),
            P(("dp", "head"), None),
            P(("dp", "head")),
            P(None, ("dp", "head")),
            P(None, ("dp", "head")),
        ),
        check_vma=False,
    )
```

```python
import functools

import jax
import jax.numpy as jnp
from jax import lax
from jax.experimental import pallas as pl
from jax.experimental.pallas import tpu as pltpu
from jax.sharding import PartitionSpec as P

HD = 64
MESH = pl.DeviceIdType.MESH
BF = jnp.bfloat16
F32 = jnp.float32
VMEM_LIMIT = 64 * 1024 * 1024


def nn(a, b):
    return lax.dot_general(a, b, (((1,), (0,)), ((), ())), preferred_element_type=F32)


def nt(a, b):
    return lax.dot_general(a, b, (((1,), (1,)), ((), ())), preferred_element_type=F32)


def tn(a, b):
    return lax.dot_general(a, b, (((0,), (0,)), ((), ())), preferred_element_type=F32)


def place():
    dp, z = lax.axis_index("dp"), lax.axis_index("head")
    core, plane = dp % 2, dp // 2
    return core, plane % 2, plane // 2, z


def device(core, x, y, z):
    return ((y * 2 + x) * 2 + core, z)


def push(src, dst, send, recv, target):
    return pltpu.make_async_remote_copy(
        src_ref=src, dst_ref=dst, send_sem=send, recv_sem=recv, device_id=target, device_id_type=MESH
    )


def from_root(x, axis, root):
    mine = lax.axis_index(axis) == root
    return lax.psum(jnp.where(mine, x, jnp.zeros_like(x)), axis)


def layer_norm(values, gain_row, shift_row):
    center = values - jnp.mean(values, axis=-1, keepdims=True)
    spread = jnp.mean(center * center, axis=-1, keepdims=True)
    return center * lax.rsqrt(spread + 1e-05) * gain_row + shift_row


def gelu_tanh(values):
    return jax.nn.gelu(values, approximate=True)


def head_major(array, dim, dp_count, head_count):
    shape = array.shape
    size = shape[dim]
    split = array.reshape(
        shape[:dim] + (dp_count, head_count, size // (dp_count * head_count)) + shape[dim + 1 :]
    )
    return jnp.swapaxes(split, dim, dim + 1).reshape(shape)


def local(
    text,
    boundary,
    reset,
    memory_in,
    init_memory,
    w_qkv,
    b_qv,
    w_out,
    w_in,
    w_back,
    b_in,
    norm_gains,
    biases,
    cotangent,
):
    head_count = lax.axis_size("head")
    dp_count = lax.axis_size("dp")
    head_idx = lax.axis_index("head")
    batch_size = text.shape[0]
    width = text.shape[3]
    seg_rows = cotangent.shape[2]
    seg_len = seg_rows * head_count
    mem_rows = memory_in.shape[1]
    text_len = seg_len - 2 * mem_rows
    local_width = w_qkv.shape[2]
    local_heads = local_width // HD
    row_start = head_idx * seg_rows
    is_first = (head_idx == 0).astype(jnp.float32)
    is_final = (head_idx == head_count - 1).astype(jnp.float32)
    grad_dims = (1, 0, 0, 1, 1, 1)
    doc_ids = jnp.cumsum(boundary, axis=2)
    marks = jnp.full((batch_size, 2, mem_rows), -1, jnp.int32)
    labels = jnp.concatenate([marks, doc_ids, marks], axis=2)
    visible = (
        (labels[..., :, None] == labels[..., None, :])
        | (labels[..., :, None] < 0)
        | (labels[..., None, :] < 0)
    )
    bias_query = b_qv[0].reshape(local_width).astype(jnp.float32)
    bias_value = b_qv[1].reshape(local_width).astype(jnp.float32)
    shared = (
        lax.all_gather(w_in, ("dp", "head"), axis=1, tiled=True),
        lax.all_gather(w_back, ("dp", "head"), axis=0, tiled=True),
        lax.all_gather(b_in, ("dp", "head"), axis=0, tiled=True),
        lax.all_gather(norm_gains, ("dp", "head"), axis=1, tiled=True),
        lax.all_gather(biases, ("dp", "head"), axis=1, tiled=True),
        lax.all_gather(init_memory, ("dp", "head"), axis=1, tiled=True),
    )

    def fetch():
        return shared

    def attention_probs(query, key_rows, seg):
        scores = (
            jnp.einsum("sqhe,skhe->shqk", query, key_rows, preferred_element_type=jnp.float32)
            * 0.125
        )
        return jnp.where(visible[:, seg][:, None], scores, -1e30)

    def forward(seg, memory, ffn):
        w_in_all, w_back_all, b_in_all, gains_all, biases_all, unused = ffn
        gains_f = gains_all.astype(jnp.float32)
        biases_f = biases_all.astype(jnp.float32)
        local_text = lax.all_gather(text[:, seg], "head", axis=1, tiled=True)
        x_rows = jnp.concatenate([memory, local_text, memory], axis=1)
        mixed = jnp.einsum("srd,dce->srce", x_rows, w_qkv, preferred_element_type=jnp.float32)
        query = (
            (mixed[:, :, 0] + bias_query)
            .astype(jnp.bfloat16)
            .reshape(batch_size, seg_len, local_heads, HD)
        )
        key_rows = mixed[:, :, 1].astype(jnp.bfloat16).reshape(batch_size, seg_len, local_heads, HD)
        value = (
            (mixed[:, :, 2] + bias_value)
            .astype(jnp.bfloat16)
            .reshape(batch_size, seg_len, local_heads, HD)
        )
        masked = attention_probs(query, key_rows, seg)
        row_max = jnp.max(masked, axis=-1, keepdims=True)
        exp_terms = jnp.exp(masked - row_max)
        row_total = jnp.sum(exp_terms, axis=-1, keepdims=True)
        log_total = row_max + jnp.log(row_total)
        probs = (exp_terms / row_total).astype(jnp.bfloat16)
        attended = jnp.einsum("shqk,skhe->sqhe", probs, value, preferred_element_type=jnp.float32)
        attended = attended.astype(jnp.bfloat16).reshape(batch_size, seg_len, local_width)
        partial_out = jnp.einsum("srl,ld->srd", attended, w_out, preferred_element_type=jnp.float32)
        summed = lax.psum_scatter(
            partial_out.astype(jnp.bfloat16), "head", scatter_dimension=1, tiled=True
        ).astype(jnp.float32)
        own_rows = lax.dynamic_slice_in_dim(x_rows, row_start, seg_rows, 1).astype(jnp.float32)
        pre_norm = own_rows + summed + biases_f[1]
        hidden = layer_norm(pre_norm, gains_f[0], biases_f[0])
        hidden_low = hidden.astype(jnp.bfloat16)
        inner = jnp.einsum(
            "srd,df->srf", hidden_low, w_in_all, preferred_element_type=jnp.float32
        ) + b_in_all.astype(jnp.float32)
        active = gelu_tanh(inner).astype(jnp.bfloat16)
        outer = (
            jnp.einsum("srf,fd->srd", active, w_back_all, preferred_element_type=jnp.float32)
            + biases_f[2]
        )
        post_norm = hidden + outer
        result = layer_norm(post_norm, gains_f[1], biases_f[3])
        kept = (
            x_rows,
            query,
            key_rows,
            value,
            log_total,
            attended,
            pre_norm,
            hidden_low,
            inner,
            active,
            post_norm,
        )
        return (result, kept)

    def backward(seg, grad_out, kept, ffn):
        (
            x_rows,
            query,
            key_rows,
            value,
            log_total,
            attended,
            pre_norm,
            hidden_low,
            inner,
            active,
            post_norm,
        ) = kept
        w_in_all, w_back_all, b_in_all, gains_all, biases_all, unused = ffn
        gains_f = gains_all.astype(jnp.float32)
        biases_f = biases_all.astype(jnp.float32)
        unused_two, pull_two = jax.vjp(layer_norm, post_norm, gains_f[1], biases_f[3])
        grad_post, grad_gain_two, grad_shift_two = pull_two(grad_out)
        grad_outer = grad_post.astype(jnp.bfloat16)
        grad_ffn_bias = jnp.sum(grad_post, axis=(0, 1))
        grad_w_back = jnp.einsum(
            "srf,srd->fd", active, grad_outer, preferred_element_type=jnp.float32
        )
        grad_active = jnp.einsum(
            "srd,fd->srf", grad_outer, w_back_all, preferred_element_type=jnp.float32
        )
        unused_gelu, pull_gelu = jax.vjp(gelu_tanh, inner)
        grad_inner = pull_gelu(grad_active)[0].astype(jnp.bfloat16)
        grad_b_in = jnp.sum(grad_inner, axis=(0, 1), dtype=jnp.float32)
        grad_w_in = jnp.einsum(
            "srd,srf->df", hidden_low, grad_inner, preferred_element_type=jnp.float32
        )
        grad_hidden = grad_post + jnp.einsum(
            "srf,df->srd", grad_inner, w_in_all, preferred_element_type=jnp.float32
        )
        unused_one, pull_one = jax.vjp(layer_norm, pre_norm, gains_f[0], biases_f[0])
        grad_pre, grad_gain_one, grad_shift_one = pull_one(grad_hidden)
        grad_out_bias = jnp.sum(grad_pre, axis=(0, 1))
        grad_branch = lax.all_gather(grad_pre.astype(jnp.bfloat16), "head", axis=1, tiled=True)
        grad_w_out = jnp.einsum(
            "srl,srd->ld", attended, grad_branch, preferred_element_type=jnp.float32
        )
        grad_att = jnp.einsum("srd,ld->srl", grad_branch, w_out, preferred_element_type=jnp.float32)
        grad_att = grad_att.astype(jnp.bfloat16).reshape(batch_size, seg_len, local_heads, HD)
        masked = attention_probs(query, key_rows, seg)
        probs = jnp.exp(masked - log_total)
        grad_value = jnp.einsum(
            "shqk,sqhe->skhe",
            probs.astype(jnp.bfloat16),
            grad_att,
            preferred_element_type=jnp.float32,
        )
        grad_probs = jnp.einsum(
            "sqhe,skhe->shqk", grad_att, value, preferred_element_type=jnp.float32
        )
        grad_scores = probs * (grad_probs - jnp.sum(grad_probs * probs, axis=-1, keepdims=True))
        grad_scores = grad_scores.astype(jnp.bfloat16)
        grad_query = (
            jnp.einsum("shqk,skhe->sqhe", grad_scores, key_rows, preferred_element_type=jnp.float32)
            * 0.125
        )
        grad_key = (
            jnp.einsum("shqk,sqhe->skhe", grad_scores, query, preferred_element_type=jnp.float32)
            * 0.125
        )
        grad_mixed = jnp.stack([grad_query, grad_key, grad_value], axis=2).astype(jnp.bfloat16)
        grad_mixed = grad_mixed.reshape(batch_size, seg_len, 3, local_width)
        grad_bias_qv = jnp.stack(
            [
                jnp.sum(grad_mixed[:, :, 0], axis=(0, 1), dtype=jnp.float32),
                jnp.sum(grad_mixed[:, :, 2], axis=(0, 1), dtype=jnp.float32),
            ]
        ).reshape(2, local_heads, HD)
        grad_w_qkv = jnp.einsum(
            "srd,srce->dce", x_rows, grad_mixed, preferred_element_type=jnp.float32
        )
        grad_rows = jnp.einsum(
            "srce,dce->srd", grad_mixed, w_qkv, preferred_element_type=jnp.float32
        )
        placed = lax.dynamic_update_slice_in_dim(jnp.zeros_like(grad_rows), grad_pre, row_start, 1)
        grad_rows = grad_rows + placed
        grad_text_part = lax.psum_scatter(
            grad_rows[:, mem_rows : mem_rows + text_len].astype(jnp.bfloat16),
            "head",
            scatter_dimension=1,
            tiled=True,
        ).astype(jnp.float32)
        grad_memory = lax.psum(
            (grad_rows[:, :mem_rows] + grad_rows[:, seg_len - mem_rows :]).astype(jnp.bfloat16),
            "head",
        ).astype(jnp.float32)
        reset_flag = reset[:, seg] > 0
        grad_init = (
            jnp.sum(jnp.where(reset_flag[:, None, None], grad_memory, 0.0), axis=0) * is_first
        )
        ffn_grads = (
            grad_w_in,
            grad_w_back,
            grad_b_in,
            jnp.stack([grad_gain_one, grad_gain_two]),
            jnp.stack([grad_shift_one, grad_out_bias, grad_ffn_bias, grad_shift_two]),
            grad_init,
        )
        return (grad_text_part, grad_memory, (grad_w_qkv, grad_bias_qv, grad_w_out), ffn_grads)

    ffn_first = fetch()
    init_all = ffn_first[5]
    memory_one = jnp.where(reset[:, 0, None, None] > 0, init_all[None], memory_in)
    out_one, kept_one = forward(0, memory_one, ffn_first)
    tail_rows = out_one[:, seg_rows - mem_rows :].astype(jnp.bfloat16)
    carried = from_root(tail_rows, "head", head_count - 1)
    ffn_second = fetch()
    memory_two = jnp.where(reset[:, 1, None, None] > 0, ffn_second[5][None], carried)
    out_two, kept_two = forward(1, memory_two, ffn_second)
    activations = jnp.stack([out_one, out_two], axis=1).astype(jnp.bfloat16)
    ffn_third = fetch()
    text_two, memory_grad_two, attn_two, ffn_two = backward(
        1, cotangent[:, 1].astype(jnp.float32), kept_two, ffn_third
    )
    keep_flag = reset[:, 1, None, None] <= 0
    carried_grad = jnp.where(keep_flag, memory_grad_two, 0.0) * is_final
    grad_one = cotangent[:, 0].astype(jnp.float32) + jnp.concatenate(
        [jnp.zeros((batch_size, seg_rows - mem_rows, width), jnp.float32), carried_grad], axis=1
    )
    ffn_fourth = fetch()
    text_one, memory_grad_one, attn_one, ffn_one = backward(0, grad_one, kept_one, ffn_fourth)
    grads = jax.tree.map(lambda a, b: a + b, ffn_one, ffn_two)
    ffn_total = tuple((head_major(g, d, dp_count, head_count) for g, d in zip(grads, grad_dims)))
    partial_sums = (
        lax.psum_scatter(
            ffn_total[0].astype(jnp.bfloat16), "head", scatter_dimension=1, tiled=True
        ).astype(jnp.float32),
        lax.psum_scatter(
            ffn_total[1].astype(jnp.bfloat16), "head", scatter_dimension=0, tiled=True
        ).astype(jnp.float32),
        lax.psum_scatter(
            ffn_total[2].astype(jnp.bfloat16), "head", scatter_dimension=0, tiled=True
        ).astype(jnp.float32),
        lax.psum_scatter(
            ffn_total[3].astype(jnp.bfloat16), "head", scatter_dimension=1, tiled=True
        ).astype(jnp.float32),
        lax.psum_scatter(
            ffn_total[4].astype(jnp.bfloat16), "head", scatter_dimension=1, tiled=True
        ).astype(jnp.float32),
        lax.psum_scatter(
            ffn_total[5].astype(jnp.bfloat16), "head", scatter_dimension=1, tiled=True
        ).astype(jnp.float32),
    )
    reduced = (
        lax.psum_scatter(partial_sums[0], "dp", scatter_dimension=1, tiled=True),
        lax.psum_scatter(partial_sums[1], "dp", scatter_dimension=0, tiled=True),
        lax.psum_scatter(partial_sums[2], "dp", scatter_dimension=0, tiled=True),
        lax.psum_scatter(partial_sums[3], "dp", scatter_dimension=1, tiled=True),
        lax.psum_scatter(partial_sums[4], "dp", scatter_dimension=1, tiled=True),
        lax.psum_scatter(partial_sums[5], "dp", scatter_dimension=1, tiled=True),
    )
    attn_total = jax.tree.map(lambda a, b: a + b, attn_one, attn_two)
    grad_qkv, grad_bqv, grad_wout = (
        lax.psum_scatter(attn_total[0], "dp", scatter_dimension=0, tiled=True),
        lax.psum_scatter(attn_total[1], "dp", scatter_dimension=2, tiled=True),
        lax.psum_scatter(attn_total[2], "dp", scatter_dimension=1, tiled=True),
    )
    grad_text = jnp.stack([text_one, text_two], axis=1).astype(jnp.bfloat16)
    grad_win, grad_wback, grad_bin, grad_gains, grad_biases, grad_init = reduced
    return (
        activations,
        grad_text,
        grad_init,
        grad_qkv,
        grad_bqv,
        grad_wout,
        grad_win,
        grad_wback,
        grad_bin,
        grad_gains,
        grad_biases,
    )


class Refs:
    pass


def by_name(names, values):
    refs = Refs()
    for name, value in zip(names, values, strict=True):
        setattr(refs, name, value)
    return refs


def loop(count, body, unroll=1):
    def run(i, unused):
        body(i)
        return unused

    lax.fori_loop(0, count, run, 0, unroll=unroll)


def add_all(dst, *sources):
    def body(at):
        dst[at] = sum([src[at].astype(F32) for src in sources], dst[at].astype(F32)).astype(BF)

    if len(dst.shape) == 2:
        body(...)
    else:
        loop(dst.shape[0], body)


def as_column(row):
    n = row.shape[1]
    down = lax.broadcasted_iota(jnp.int32, (n, n), 0)
    across = lax.broadcasted_iota(jnp.int32, (n, n), 1)
    return jnp.sum(jnp.where(down == across, row, 0.0), axis=1, keepdims=True)


def norm(v):
    center = v - jnp.mean(v, axis=-1, keepdims=True)
    scale = lax.rsqrt(jnp.mean(center * center, axis=-1, keepdims=True) + 1e-05)
    return center * scale, scale


def pull_norm(g, hat, scale):
    m1 = jnp.mean(g, axis=-1, keepdims=True)
    m2 = jnp.mean(g * hat, axis=-1, keepdims=True)
    return scale * (g - m1 - hat * m2)


def row_sum(v):
    return jnp.sum(v, axis=0, keepdims=True)


def main_kernel(names, dp_count, head_count, *values):
    r_ = by_name(names, values)
    core, px, py, z = place()
    plane = py * 2 + px
    x_plane, y_plane = py * 2 + 1 - px, (1 - py) * 2 + px
    me = (plane * 2 + core) * head_count + z
    total = dp_count * head_count
    planes = dp_count // 2
    is_home = core == z // 2
    away = jnp.logical_not(is_home)
    sibling = device(1 - core, px, py, z)
    x_mate, y_mate = device(core, 1 - px, py, z), device(core, px, 1 - py, z)
    mirror = z // 2

    def from_end(i):
        return i + mirror * (head_count - 1 - 2 * i)

    depth = from_end(z)
    inside = depth == 1
    order = [from_end(i) for i in (depth, 1 - depth, 2, 3)]

    def order_at(n):
        return from_end(jnp.where(n == 0, depth, jnp.where(n == 1, 1 - depth, n)))

    x, qkv, pt, ot, wa, wf = r_.x, r_.qkv, r_.pt, r_.ot, r_.wa, r_.wf
    hf, acc, par = r_.hf, r_.acc, r_.par
    seg_len, width = x.shape[1], x.shape[2]
    hidden = r_.u.shape[2]
    heads = pt.shape[1]
    local = ot.shape[2]
    hid = r_.w_back.shape[0]
    lanes = r_.norm_gains.shape[1]
    mem_rows = r_.memory_in.shape[0]
    text_rows = r_.text.shape[1]
    per_block = local // HD
    step = seg_len // head_count
    piece = step // 2
    chunk = hidden // head_count
    tail = 16
    tail_at = pl.ds(seg_len - tail, tail)

    def rows(r):
        return pl.ds(pl.multiple_of(r * step, step), step)

    def cols(i):
        return pl.ds(pl.multiple_of(i * chunk, chunk), chunk)

    def head_rows(h, part):
        return pl.ds(pl.multiple_of((h % per_block) * HD + part * local, HD), HD)

    def column(i):
        h = core if i < head_count - 1 else 1 - core
        zt = (z + 1 + i) % head_count
        return (plane * 2 + h) * head_count + zt, device(h, px, py, zt)

    column_size = 2 * head_count - 1

    def sent_rows(count, sem):
        ref = wf.at[0, pl.ds(0, count)]
        push(ref, ref, sem, sem, sibling).wait_send()

    def got_rows(count, sem):
        ref = wf.at[0, pl.ds(0, count)]
        push(ref, ref, sem, sem, sibling).wait_recv()

    def when_not(cond, body):
        pl.when(jnp.logical_not(cond))(body)

    share = local
    half = share // 2

    def attention_out(i, which):
        zt = (z + 1 + i) % head_count
        at = pl.multiple_of((share * jnp.minimum(plane, planes - 2) if which == 0 else 0) + half * core, half)
        src = (r_.wq_t, r_.w_out)[which]
        return push(
            src.at[pl.ds(at, half)], wa.at[z % 2, pl.ds(pl.multiple_of(share * plane + half * core, half), half)],
            r_.att_s.at[i], r_.att_r.at[z % 2, core], device(z // 2, px, py, zt),
        )

    def attention_outs(do):
        for which, mine in enumerate((plane < planes - 1, plane == planes - 1)):

            def each():
                for i in range(head_count - 1):
                    do(attention_out(i, which))

            pl.when(mine)(each)

    def attention_in(k, h):
        span = pl.ds(pl.multiple_of(share * plane + half * h, half), half)
        return push(r_.w_out.at[pl.ds(0, half)], wa.at[k, span], r_.att_s.at[0], r_.att_r.at[k, h], sibling)

    def attention_plane(k, which):
        at, count, mate = (
            (share * plane, share, x_mate),
            (share * plane, share, y_mate),
            (share * x_plane, half, y_mate),
            (share * y_plane + half, half, x_mate),
        )[which]
        block = pl.ds(pl.multiple_of(at, half), count)
        return push(
            wa.at[k, block], wa.at[k, block], r_.plane_s.at[k, which], r_.plane_r.at[k, which], mate
        )

    own_attention = [
        pltpu.make_async_copy(r_.wq_t, wa.at[z % 2, pl.ds(0, 3 * local)], r_.local_sem.at[0]),
        pltpu.make_async_copy(r_.w_out, wa.at[z % 2, pl.ds(3 * local, local)], r_.local_sem.at[1]),
    ]
    foreign = [jnp.logical_not(is_home & (z % 2 == k)) for k in range(2)]

    def rows_src(a, j, h):
        src = r_.text_pad if a < 2 else r_.cotangent
        return src.at[j, a % 2, pl.ds(h * piece, piece)]

    def rows_dst(a, zs, h):
        dst = r_.text_all if a < 2 else r_.cot_all
        return dst.at[a % 2, pl.ds(pl.multiple_of(zs * step + h * piece, piece), piece)]

    def rows_out(a, j, h):
        return push(
            rows_src(a, j, h), rows_dst(a, z, h), r_.rows_s.at[a], r_.rows_r.at[a, z],
            device(h, px, py, 2 * core + j),
        )

    def rows_here(a, j, h):
        return pltpu.make_async_copy(rows_src(a, j, h), rows_dst(a, z, h), r_.here_sem.at[a])

    def rows_send(a):
        for j in range(2):
            for h in range(2):
                here = (core == h) & (z == 2 * core + j)
                pl.when(here)(lambda: rows_here(a, j, h).start())
                when_not(here, lambda: rows_out(a, j, h).start())

    def rows_forward(a, zs, h):
        ref = rows_dst(a, zs, h)
        return push(ref, ref, r_.fwd_s.at[a], r_.fwd_r.at[a], sibling)

    def rows_pass(a):
        for zs in range(head_count):
            here = is_home & (z == zs)
            pl.when(here)(lambda: rows_here(a, z % 2, core).wait())
            when_not(
                here,
                lambda: push(
                    rows_src(a, 0, 0), rows_dst(a, zs, core), r_.rows_s.at[a], r_.rows_r.at[a, zs], sibling
                ).wait_recv(),
            )
            rows_forward(a, zs, core).start()

    def rows_ready(a):
        got_rows(head_count * piece, r_.fwd_r.at[a])

    def rows_done(a):
        pl.when(is_home)(lambda: sent_rows(3 * piece, r_.rows_s.at[a]))
        pl.when(away)(lambda: sent_rows(4 * piece, r_.rows_s.at[a]))
        sent_rows(head_count * piece, r_.fwd_s.at[a])

    def hidden_block(p, zi):
        return pl.ds(pl.multiple_of((zi * planes + p) * hid, hid), hid)

    def ffn_push(zi, to, slot):
        ref = wf.at[:, hidden_block(plane, zi)]
        return push(ref, ref, r_.ffn_s.at[slot], r_.ffn_r.at[zi], device(core, px, py, to))

    ffn_hops = [(0, from_end(1 - depth)), (0, from_end(2)), (1, from_end(2)), (2, from_end(0)), (3, from_end(0))]

    def ffn_hop(i):
        which, to = ffn_hops[i]
        return ffn_push(order[which], to, i)

    def ffn_own():
        ffn_hop(0).start()
        pl.when(inside)(ffn_hop(1).start)

    def ffn_hop_on(n):
        ffn_push(order[n], z, 0).wait_recv()
        pl.when(inside)(ffn_hop(n + 1).start)

    def ffn_sent():
        ffn_hop(0).wait_send()

        def rest():
            for i in range(1, 5):
                ffn_hop(i).wait_send()

        pl.when(inside)(rest)

    def side(kind, zi, which):
        p, mate = (
            (plane, x_mate),
            (plane, y_mate),
            (x_plane, y_mate) if kind == 0 else (y_plane, x_mate),
        )[which]
        ref = wf.at[kind, hidden_block(p, zi)]
        return push(ref, ref, r_.side_s.at[0], r_.side_r.at[zi, kind, which], mate)

    def side_first(zi):
        for kind in range(2):
            side(kind, zi, 0).start()
            side(kind, zi, 1).start()

    def ffn_two(n):
        zi = order_at(n)
        side(0, zi, 0).wait_recv()
        side(0, zi, 2).start()
        side(1, zi, 1).wait_recv()
        side(1, zi, 2).start()

    def ffn_ready(n):
        zi = order_at(n)
        side(0, zi, 1).wait_recv()
        side(1, zi, 0).wait_recv()
        side(0, zi, 2).wait_recv()
        side(1, zi, 2).wait_recv()

    def small_out(i):
        return push(r_.small, r_.small_all.at[me], r_.small_s.at[0], r_.small_r.at[0], column(i)[1])

    every_small = r_.small_all.at[pl.ds(0, column_size)]
    smalls = push(every_small, every_small, r_.small_s.at[0], r_.small_r.at[0], sibling)

    def small_plane(i):
        p, mate = ((plane, x_mate), (plane, y_mate), (x_plane, y_mate))[i]
        ref = r_.small_all.at[pl.ds(p * 2 * head_count, 2 * head_count)]
        return push(ref, ref, r_.small_ps.at[i], r_.small_pr.at[i], mate)

    pair = [
        push(r_.seqf, r_.seqf_in, r_.pair_s.at[0], r_.pair_r.at[0], sibling),
        push(r_.memp, r_.memp_in, r_.pair_s.at[1], r_.pair_r.at[1], sibling),
    ]

    barrier = pltpu.get_barrier_semaphore()
    mates = [x_mate, y_mate] + [column(i)[1] for i in range(column_size)]
    for mate in mates:
        pl.semaphore_signal(barrier, inc=1, device_id=mate, device_id_type=MESH)
    early = [
        pltpu.make_async_copy(r_.w_in_t, wf.at[0, hidden_block(plane, z)], r_.early_sem.at[0]),
        pltpu.make_async_copy(r_.w_back, wf.at[1, hidden_block(plane, z)], r_.early_sem.at[1]),
        pltpu.make_async_copy(r_.text, r_.text_v, r_.early_sem.at[2]),
    ]
    for copy in early:
        copy.start()
    vtmp = r_.vtmp
    vtmp[...] = jnp.zeros_like(vtmp)
    vtmp[0:2, 0:lanes] = r_.norm_gains[...].astype(F32)
    vtmp[2:6, 0:lanes] = r_.biases[...].astype(F32)
    vtmp[6 : 6 + mem_rows, 0:lanes] = r_.init_memory[...].astype(F32)
    vtmp[0:1, 32 : 32 + hid] = r_.b_in[...].astype(F32)
    for b in range(per_block):
        pair_b = r_.b_qv[b].astype(F32)
        for part in range(2):
            vtmp[1 + part * per_block + b : 2 + part * per_block + b, 32 : 32 + HD] = pair_b[part : part + 1, :]
    r_.small[...] = vtmp[...].astype(BF)
    r_.small_all[me] = r_.small[...]
    pl.semaphore_wait(barrier, len(mates))

    for i in range(column_size):
        small_out(i).start()
    early[0].wait()
    early[1].wait()
    side_first(z)
    ffn_own()
    attention_outs(lambda c: c.start())

    def keep_own():
        for copy in own_attention:
            copy.start()

    pl.when(is_home)(keep_own)
    seqf = r_.seqf
    marks = r_.boundary[z % 2].astype(F32).astype(BF)
    text_len = marks.shape[1]
    n_from = lax.broadcasted_iota(jnp.int32, (text_len, seg_len), 0)
    n_to = lax.broadcasted_iota(jnp.int32, (text_len, seg_len), 1) - mem_rows
    counts = nn(marks, jnp.where(n_from <= n_to, 1.0, 0.0).astype(BF))
    at_row = lax.broadcasted_iota(jnp.int32, (2, seg_len), 1)
    seqf[...] = jnp.zeros_like(seqf)
    seqf[0:2, :] = jnp.where((at_row >= mem_rows) & (at_row < seg_len - mem_rows), counts, -1.0)
    for s in range(2):
        seqf[2 + s : 3 + s, :] = jnp.full((1, seg_len), r_.reset[z % 2, s].astype(F32))
    r_.memp[...] = jnp.zeros_like(r_.memp)
    both_in = r_.memory_in[...].astype(F32)
    r_.memp[0:mem_rows, :] = jnp.where(z % 2 == 0, both_in[:, 0, :], both_in[:, 1, :]).astype(BF)
    for copy in pair:
        copy.start()

    def pad_text(j):
        both = r_.text_v[j].astype(F32)
        for s in range(2):
            r_.text_pad[j, s, 0:text_rows, :] = both[:, s, :].astype(BF)
            r_.text_pad[j, s, text_rows:step, :] = jnp.zeros((step - text_rows, width), BF)

    early[2].wait()
    loop(2, pad_text)
    for ref in (r_.sg, r_.dinit, r_.dbin, r_.carry, r_.rs):
        ref[...] = jnp.zeros_like(ref)

    def attention_to_plane(k):
        for h in range(2):
            attention_in(k, h).wait_recv()
        attention_plane(k, 0).start()
        attention_plane(k, 1).start()

    def attention_across(k):
        attention_plane(k, 0).wait_recv()
        attention_plane(k, 2).start()
        attention_plane(k, 1).wait_recv()
        attention_plane(k, 3).start()

    smalls.wait_recv()
    small_plane(0).start()
    small_plane(1).start()
    ffn_two(0)
    ffn_hop_on(1)
    pl.when(inside)(lambda: ffn_hop_on(2))
    side_first(order[1])
    rows_send(0)
    small_plane(0).wait_recv()
    small_plane(2).start()
    for k in range(2):
        pl.when(foreign[k] & is_home)(lambda: attention_to_plane(k))
    ffn_two(1)
    for k in range(2):
        pl.when(foreign[k] & away)(lambda: attention_to_plane(k))

    for copy in pair:
        copy.wait_recv()
    small_plane(1).wait_recv()
    small_plane(2).wait_recv()
    for i in range(total):
        par[0:16, lanes * i : lanes * (i + 1)] = r_.small_all[i, 0:16, 0:lanes].astype(F32)
    for zi in range(head_count):
        for p in range(planes):
            at = (zi * planes + p) * hid
            line = r_.small_all[(2 * p + core) * head_count + zi].astype(F32)
            r_.bin_row[0:1, at : at + hid] = line[0:1, 32 : 32 + hid]
    r_.bqv[...] = jnp.zeros_like(r_.bqv)
    for k in range(2):
        lines = r_.small_all[2 * core + k].astype(F32)
        for part in range(2):
            for b in range(per_block):
                line = lines[1 + part * per_block + b : 2 + part * per_block + b, 32 : 32 + HD]
                at = 2 * part * local + b * HD
                r_.bqv[k, at : at + HD, :] = as_column(line)
    seq = jnp.where(is_home, seqf[...], r_.seqf_in[...])
    seqf_out = r_.seq
    seqf_out[...] = seq
    flags = [seqf_out[2 + s : 3 + s, 0:1] for s in range(2)]
    tail_row = lax.broadcasted_iota(jnp.int32, (tail, width), 0)
    is_mem = tail_row >= tail - mem_rows
    init_b = jnp.where(is_mem, par[...], 0.0)
    given = jnp.where(is_home, r_.memp[...].astype(F32), r_.memp_in[...].astype(F32))
    first_b = jnp.where(flags[0] > 0, init_b, pltpu.roll(given, tail - mem_rows, 0))
    r_.cur_b[...] = first_b.astype(BF)
    r_.cur_a[...] = pltpu.roll(first_b, mem_rows, 0).astype(BF)

    def take_rows(r):
        inside = lax.broadcasted_iota(jnp.int32, (step, seg_len), 0)
        nat = lax.broadcasted_iota(jnp.int32, (step, seg_len), 1)
        return jnp.where((nat == r * text_rows + inside + mem_rows) & (inside < text_rows), 1.0, 0.0).astype(BF)

    def place_rows(r):
        nat = lax.broadcasted_iota(jnp.int32, (step, seg_len), 0) + r * step
        pad = lax.broadcasted_iota(jnp.int32, (step, seg_len), 1)
        inside = pad & (step - 1)
        target = (pad // step) * text_rows + inside + mem_rows
        return jnp.where((nat == target) & (inside < text_rows), 1.0, 0.0).astype(BF)

    wide = 2 * step

    def half_span(i):
        return pl.ds(pl.multiple_of(i * wide, wide), wide), i

    def end_span(i):
        return pl.ds(pl.multiple_of(i * (seg_len - step), step), step), i

    def middle_span(i):
        return pl.ds(step, wide), 2

    def exchange(slot, span):
        at, n = span
        return push(
            r_.send_buf.at[slot, at], r_.recv_buf.at[slot, at], r_.send_sem.at[slot, n], r_.recv_sem.at[slot, n],
            sibling,
        )

    def give(slot, span, part):
        at = span[0]
        acc[at, :] = part
        r_.send_buf[slot, at, :] = part.astype(BF)
        exchange(slot, span).start()

    def taken(slot, at):
        return acc[at, :] + r_.recv_buf[slot, at, :].astype(F32)

    def by_quarter(slot, body):
        def one(r):
            exchange(slot, (rows(r), r)).wait()
            body(rows(r))

        loop(head_count, one)

    def by_half(slot, body):
        def one(r):
            pl.when(r % 2 == 0)(lambda: exchange(slot, half_span(r // 2)).wait())
            body(rows(r))

        loop(head_count, one)

    def keep_scale(first, seg, at, scale):
        pair_at = slice(2 * first, 2 * first + 2)
        lane = lax.broadcasted_iota(jnp.int32, (1, 2), 1)
        r_.rs[at, pair_at] = jnp.where(lane == seg, scale, r_.rs[at, pair_at])

    def kept_scale(first, seg, at):
        lane = lax.broadcasted_iota(jnp.int32, (1, 2), 1)
        both = r_.rs[at, 2 * first : 2 * first + 2]
        return jnp.sum(jnp.where(lane == seg, both, 0.0), axis=1, keepdims=True)

    def back_copy(which, seg, zt):
        src, dst = ((r_.y, r_.acts_o), (r_.text_all, r_.text_pad))[which]
        span = pl.ds(pl.multiple_of(zt * step + core * piece, piece), piece)
        return src.at[seg, span], dst.at[z % 2, seg, pl.ds(core * piece, piece)]

    def back_out(which, seg, i):
        zt = (z + i) % head_count
        src, dst = back_copy(which, seg, zt)
        return push(
            src, dst, r_.back_s.at[which, seg], r_.back_r.at[which, seg], device(z // 2, px, py, zt)
        )

    def back_here(which, seg):
        src, dst = back_copy(which, seg, z)
        return pltpu.make_async_copy(src, dst, r_.back_here_sem.at[which, seg])

    def back_send(which, seg):
        pl.when(is_home)(lambda: back_here(which, seg).start())
        pl.when(away)(lambda: back_out(which, seg, 0).start())
        for i in range(1, head_count):
            back_out(which, seg, i).start()

    def back_sent(which, seg):
        def home():
            back_here(which, seg).wait()
            sent_rows(3 * piece, r_.back_s.at[which, seg])
            got_rows(3 * piece, r_.back_r.at[which, seg])

        def not_home():
            sent_rows(4 * piece, r_.back_s.at[which, seg])
            got_rows(4 * piece, r_.back_r.at[which, seg])

        pl.when(is_home)(home)
        pl.when(away)(not_home)

    def tail_z(which, i):
        zt = (z + 1 + i) % head_count
        to = device(core, px, py, zt)
        dst = r_.factors.at[which, z, plane]
        return push(r_.factor_out.at[which, zt], dst, r_.tg_s.at[which], r_.tg_r.at[which, z], to)

    def tail_z_in(which, i):
        zs = (z + 1 + i) % head_count
        dst = r_.factors.at[which, zs, plane]
        return push(r_.factor_out.at[which, zs], dst, r_.tg_s.at[which], r_.tg_r.at[which, zs], sibling)

    def tail_plane(which, i):
        p, zs, to = (
            (plane, slice(None), x_mate), (plane, slice(None), y_mate),
            (x_plane, pl.ds(0, 2), y_mate), (y_plane, pl.ds(2, 2), x_mate),
        )[i]
        buf = r_.factors.at[which, zs, p]
        return push(buf, buf, r_.tg_s.at[which], r_.tg_r.at[which, head_count + i], to)

    def tail_pair(which):
        src = r_.factors.at[which, :, :, :, pl.ds(0, half_width)]
        return push(src, r_.factors_in.at[which], r_.tp_s.at[which], r_.tp_r.at[which], sibling)

    def tail_gather(which, stage):
        if stage == 0:
            for i in range(head_count - 1):
                tail_z(which, i).start()
            r_.factors[which, z, plane] = r_.factor_out[which, z]
        elif stage == 1:
            for i in range(head_count - 1):
                tail_z_in(which, i).wait_recv()
            tail_plane(which, 0).start()
            tail_plane(which, 1).start()
        elif stage == 2:
            for i in range(2):
                tail_plane(which, i).wait_recv()
                tail_plane(which, 2 + i).start()
        elif stage == 3:
            for i in range(2):
                tail_plane(which, 2 + i).wait_recv()
            tail_pair(which).start()
        else:
            sent_rows((head_count - 1 + 3 * head_count) * tail, r_.tg_s.at[which])

    half_width = width // 2

    def half_of(h):
        return pl.ds(pl.multiple_of(h * half_width, half_width), half_width)

    def tail_put(which, hidden_ref, units):
        part = hidden_ref[0, tail_at, half_of(core)]
        for zt in range(head_count):
            r_.factor_out[which, zt, :, 0:half_width] = part
            r_.factor_out[which, zt, :, half_width:] = units[:, zt * chunk : (zt + 1) * chunk]
        tail_gather(which, 0)

    def tail_products():
        down = lax.broadcasted_iota(jnp.int32, (chunk, 128), 0)
        across = lax.broadcasted_iota(jnp.int32, (chunk, 128), 1)
        pick = jnp.where((down == plane * hid + across) & (across < hid), 1.0, 0.0).astype(BF)
        all_rows = planes * head_count * tail
        units = [
            nn(r_.factors[which, :, :, :, half_width:].reshape(all_rows, chunk), pick).astype(BF) for which in range(2)
        ]
        for which in range(2):
            tail_pair(which).wait()
        out = []
        for kind in range(2):
            mine = tn(units[1 - kind], r_.factors[kind, :, :, :, 0:half_width].reshape(all_rows, half_width))[0:hid, :]
            theirs = tn(units[1 - kind], r_.factors_in[kind].reshape(all_rows, half_width))[0:hid, :]
            out.append((mine, theirs))
        return out

    def build(seg):
        def one(r):
            x[seg, rows(r), :] = nn(place_rows(r), r_.text_all[seg]).astype(BF)

        loop(head_count, one)

    def add_memory(seg):
        x[seg, 0:tail, :] = x[seg, 0:tail, :] + r_.cur_a[...]
        x[seg, tail_at, :] = x[seg, tail_at, :] + r_.cur_b[...]

    def make_mask(seg):
        right = r_.seq[pl.ds(seg, 1), :]
        left = as_column(right)
        acc[:, 0:seg_len] = jnp.where((left == right) | (left < 0) | (right < 0), 0.0, -1e30)

    def keep_projected(seg, j, at, value):
        value = value + r_.bqv[j]
        qkv[seg, j, 0:local, at] = (value[0:local, :] * 0.125).astype(BF)
        qkv[seg, j, local:, at] = value[local:, :].astype(BF)

    def project(seg):
        def one(j):
            keep_projected(seg, j, slice(None), nt(wa[j, 0 : 3 * local, :], x[seg]))

        loop(2, one)

    def project_ends(seg):
        both = jnp.concatenate([x[seg, 0:step, :], x[seg, seg_len - step :, :]], axis=0)

        def one(j):
            value = nt(wa[j, 0 : 3 * local, :], both)
            keep_projected(seg, j, slice(0, step), value[:, 0:step])
            keep_projected(seg, j, slice(seg_len - step, seg_len), value[:, step:])

        loop(2, one)

    def attend(seg):
        def one(h):
            j = h // per_block
            q, k, v = (qkv[seg, j, head_rows(h, part), :] for part in range(3))
            s = tn(k, q) + acc[:, 0:seg_len]
            e = jnp.exp(s - jnp.max(s, axis=0, keepdims=True))
            p = (e * (1.0 / jnp.sum(e, axis=0, keepdims=True))).astype(BF)
            pt[seg, h] = p
            ot[seg, j, head_rows(h, 0), :] = nn(v, p).astype(BF)

        loop(heads, one, unroll=3)

    def out_project(seg):
        def one(i):
            span = (rows(i), i)
            at = span[0]
            give(
                0, span, tn(ot[seg, 0, :, at], wa[0, 3 * local :, :]) + tn(ot[seg, 1, :, at], wa[1, 3 * local :, :])
            )

        loop(head_count, one)

    def norm_one(seg):
        def one(at):
            hat, scale = norm(x[seg, at, :].astype(F32) + taken(0, at) + par[3:4, :])
            r_.xh1[seg, at, :] = hat.astype(BF)
            keep_scale(0, seg, at, scale)
            h = hat * par[0:1, :] + par[2:3, :]
            hf[at, :] = h
            r_.hb[seg, at, :] = h.astype(BF)

        by_quarter(0, one)

    def inner(seg, at):
        v = nt(r_.hb[seg], wf[0, at, :]) + r_.bin_row[:, at]
        c0 = 0.7978845608028654
        sq = v * v
        th = jnp.tanh(v * (c0 + (c0 * 0.044715) * sq))
        up = 0.5 + 0.5 * th
        active = v * up
        r_.u[seg, :, at] = active.astype(BF)
        slope = up + active * (1.0 - up) * (2 * c0 + (6 * c0 * 0.044715) * sq)
        r_.gp[seg, :, at] = slope.astype(BF)

    def outer(seg):
        def one(i):
            span = (rows(i), i)
            give(1, span, nn(r_.u[seg, span[0], :], wf[1]))

        loop(head_count, one)

    def norm_two(seg):
        def one(at):
            hat, scale = norm(hf[at, :] + taken(1, at) + par[4:5, :])
            r_.xh2[seg, at, :] = hat.astype(BF)
            keep_scale(1, seg, at, scale)
            r_.y[seg, at, :] = (hat * par[1:2, :] + par[5:6, :]).astype(BF)

        by_quarter(1, one)

    def next_memory():
        last = r_.y[0, tail_at, :].astype(F32)
        memory = jnp.where(is_mem, jnp.where(flags[1] > 0, par[...], last), 0.0)
        r_.cur_b[...] = memory.astype(BF)
        r_.cur_a[...] = pltpu.roll(memory, mem_rows, 0).astype(BF)

    def pull_two_part(g_y, hat, scale):
        pre = pull_norm(g_y * par[1:2, :], hat, scale)
        r_.sg[1:2, :] += row_sum(g_y * hat)
        r_.sg[5:6, :] += row_sum(g_y)
        r_.sg[4:5, :] += row_sum(pre)
        return pre.astype(BF)

    def pull_two():
        def one(n):
            seg, r = 1 - n // head_count, n % head_count
            pl.when(n == head_count)(lambda: rows_ready(2))
            below = lax.broadcasted_iota(jnp.int32, (step, width), 0) + r * step
            held = (below >= seg_len - tail) & (seg == 0)
            g_y = jnp.where(held, 0.0, r_.cot_all[seg, rows(r), :].astype(F32))
            hat = r_.xh2[seg, rows(r), :].astype(F32)
            r_.xh2[seg, rows(r), :] = pull_two_part(g_y, hat, kept_scale(1, seg, rows(r)))

        loop(2 * head_count, one)

    def keep_tail():
        r_.xh2_t[...] = r_.xh2[0, tail_at, :]
        r_.gp_t[...] = r_.gp[0, tail_at, :]

    pl.when(inside)(lambda: ffn_hop_on(3))
    pl.when(depth == 0)(lambda: ffn_hop_on(2))
    for k in range(2):
        pl.when(foreign[k])(lambda: attention_across(k))
    side_first(order[2])
    rows_pass(0)
    rows_ready(0)
    build(0)
    add_memory(0)
    for k in range(2):

        def last_part():
            attention_plane(k, 2).wait_recv()
            attention_plane(k, 3).wait_recv()

        pl.when(foreign[k])(last_part)

    def kept_own():
        for copy in own_attention:
            copy.wait()

    pl.when(is_home)(kept_own)
    project(0)
    pl.when(depth == 0)(lambda: ffn_hop_on(3))
    side_first(order[3])
    rows_send(1)

    def forward(seg):
        make_mask(seg)
        attend(seg)

        def between():
            rows_pass(3)
            back_send(0, 0)

        pl.when(seg == 1)(between)
        out_project(seg)

        def rows_next():
            ffn_two(2)
            rows_send(3)
            rows_send(2)

        pl.when(seg == 0)(rows_next)
        norm_one(seg)

        def units(n):
            def start_two():
                ffn_two(3)
                rows_ready(1)
                build(1)
                project(1)

            def rows_on():
                rows_pass(1)

            pl.when(n == 2)(rows_on)
            pl.when(n == 3)(start_two)
            ffn_ready(n)
            inner(0, cols(order_at(n)))

        def wide_units():
            loop(2, lambda n: inner(1, pl.ds(pl.multiple_of(n * 2 * chunk, 2 * chunk), 2 * chunk)))

        pl.when(seg == 0)(lambda: loop(head_count, units))
        pl.when(seg == 1)(wide_units)
        outer(seg)
        pl.when(seg == 1)(lambda: rows_pass(2))
        norm_two(seg)

        def on_to_two():
            rows_done(0)
            rows_done(1)
            next_memory()
            add_memory(1)
            project_ends(1)
            tail_put(0, r_.hb, r_.u[0, tail_at, :])

        pl.when(seg == 0)(on_to_two)

    loop(2, forward)
    back_send(0, 1)
    rows_ready(3)

    def pull_tail():
        g_y = r_.cot_all[0, tail_at, :].astype(F32) + r_.carry[...]
        pre = pull_two_part(g_y, r_.xh2_t[...].astype(F32), kept_scale(1, 0, tail_at))
        r_.xh2[0, tail_at, :] = pre
        g_z = (nt(pre, wf[1]) * r_.gp_t[...].astype(F32)).astype(BF)
        r_.gp[0, tail_at, :] = g_z
        r_.dbin[0:1, :] += row_sum(g_z.astype(F32))
        tail_put(1, r_.xh2, g_z)

    def pull_inner(i):
        both = r_.xh2[...].reshape(2 * seg_len, width)
        g_u = nt(both, wf[1, cols(i), :])
        for seg in range(2):
            g_z = (g_u[seg * seg_len : (seg + 1) * seg_len, :] * r_.gp[seg, :, cols(i)].astype(F32)).astype(BF)
            r_.gp[seg, :, cols(i)] = g_z
            r_.dbin[0:1, cols(i)] += row_sum(g_z.astype(F32))

    def pull_hidden(seg):
        def one(i):
            span = half_span(i)
            give(0, span, nn(r_.gp[seg, span[0], :], wf[0]))

        loop(2, one)

    def pull_one(seg):
        def one(at):
            g_h = r_.xh2[seg, at, :].astype(F32) + taken(0, at)
            hat = r_.xh1[seg, at, :].astype(F32)
            pre = pull_norm(g_h * par[0:1, :], hat, kept_scale(0, seg, at))
            hf[at, :] = pre
            r_.xh1[seg, at, :] = pre.astype(BF)
            r_.sg[0:1, :] += row_sum(g_h * hat)
            r_.sg[2:3, :] += row_sum(g_h)
            r_.sg[3:4, :] += row_sum(pre)

        by_half(0, one)

        def out(j):
            r_.got[j] = nt(wa[j, 3 * local :, :], r_.xh1[seg]).astype(BF)

        loop(2, out)

    def pull_heads(seg):
        def one(h):
            j = h // per_block
            q, k, v = (qkv[seg, j, head_rows(h, part), :] for part in range(3))
            g_o = r_.got[j, head_rows(h, 0), :]
            p = pt[seg, h]
            d_v = nt(g_o, p).astype(BF)
            total_p = row_sum(g_o.astype(F32) * ot[seg, j, head_rows(h, 0), :].astype(F32))
            d_s = (p.astype(F32) * (tn(v, g_o) - total_p)).astype(BF)
            d_q = (nn(k, d_s) * 0.125).astype(BF)
            d_k = nt(q, d_s).astype(BF)
            for part, value in enumerate((d_q, d_k, d_v)):
                qkv[seg, j, head_rows(h, part), :] = value

        loop(heads, one, unroll=3)

    def pull_rows(seg, span):
        at = span[0]
        give(
            1, span,
            tn(qkv[seg, 0, :, at], wa[0, 0 : 3 * local, :]) + tn(qkv[seg, 1, :, at], wa[1, 0 : 3 * local, :]),
        )

    def pull_x(at):
        value = hf[at, :] + taken(1, at)
        acc[at, :] = value
        r_.send_buf[1, at, :] = value.astype(BF)

    def pull_memory(seg):
        both = pltpu.roll(acc[0:tail, :], tail - mem_rows, 0) + acc[seg_len - tail : seg_len, :]
        memory = jnp.where(is_mem, both, 0.0)
        r_.dinit[...] += jnp.where(flags[seg] > 0, memory, 0.0)
        if seg == 1:
            r_.carry[...] = jnp.where(flags[1] > 0, 0.0, memory)

    def text_grad(seg):
        def one(r):
            r_.text_all[seg, rows(r), :] = nn(take_rows(r), r_.send_buf[1]).astype(BF)

        loop(head_count, one)

    def cut(buf, kind, a, b):
        first, second = (px, py) if kind == 0 else (py, px)
        first = first if a == 0 else 1 - first
        second = second if b == 0 else 1 - second
        return buf.at[second, first] if kind == 0 else buf.at[first, second]

    def parts_of(name):
        return sums[name] if isinstance(name, str) else ffn_sum(name)

    sum_mates = ((x_mate, y_mate), (y_mate, x_mate))

    def sum_one(name, kind, b):
        buf, got, s, r = parts_of(name)(kind)
        return push(cut(buf, kind, 1, b), got[0].at[b], s, r.at[b], sum_mates[kind][0])

    def sum_two(name, kind):
        buf, got, s, r = parts_of(name)(kind)
        return push(cut(buf, kind, 0, 1), got[1], s, r.at[2], sum_mates[kind][1])

    def ffn_sum(d):
        zi = order_at(d)

        def parts(kind):
            return (
                r_.fsend.at[kind, zi], (r_.f_one.at[kind, zi], r_.f_two.at[kind, zi]),
                r_.sum_s.at[0], r_.fsum_r.at[kind, zi],
            )

        return parts

    sums = {}

    def attention_sum(n):
        def parts(kind):
            return (
                r_.asend.at[n, kind], (r_.a_one.at[n, kind], r_.a_two.at[n, kind]),
                r_.sum_s.at[1], r_.asum_r.at[n, kind],
            )

        return parts

    halves = ("a", "b", "c")
    for n, name in enumerate(halves):
        sums[name] = attention_sum(n)
    sums["v"] = lambda kind: (
        r_.vsend.at[kind], (r_.v_one.at[kind], r_.v_two.at[kind]), r_.sum_s.at[2], r_.vsum_r.at[kind]
    )

    def start_sum(name, which=((1, 0), (1, 1), (0, 0), (0, 1))):
        for b, kind in which:
            sum_one(name, kind, b).start()

    def travel(name, kinds=(0, 1)):
        for kind in kinds:
            buf, got, _, _ = parts_of(name)(kind)
            sum_one(name, kind, 1).wait_recv()
            add_all(cut(buf, kind, 0, 1), got[0].at[1])
            sum_two(name, kind).start()

    def end_plane(name):
        for kind in range(2):
            buf, got, _, _ = parts_of(name)(kind)
            sum_one(name, kind, 0).wait_recv()
            sum_two(name, kind).wait_recv()
            add_all(cut(buf, kind, 0, 0), got[0].at[0], got[1])

    def sums_sent():
        every = r_.fsend.at[:, pl.ds(0, 3)]
        push(every, every, r_.sum_s.at[0], r_.sum_s.at[0], sibling).wait_send()
        sent_rows(12 * hid_rows, r_.sum_s.at[1])
        every = r_.small_all.at[pl.ds(0, 12)]
        push(every, every, r_.sum_s.at[2], r_.sum_s.at[2], sibling).wait_send()

    def z_out(kind, d):
        slot = jnp.where(inside, jnp.where(d == 1, 0, jnp.where(d == 2, 4, 1)), jnp.where(d == 1, 0, d))
        to = from_end(jnp.where(inside, jnp.where(d == 1, 0, 2), 1))
        return push(
            cut(r_.fsend.at[kind, order_at(d)], kind, 0, 0), r_.f_z.at[kind, slot], r_.fz_s.at[kind, d],
            r_.fz_r.at[kind, slot], device(core, px, py, to),
        )

    def z_in(kind, slot):
        return push(
            cut(r_.fsend.at[kind, z], kind, 0, 0), r_.f_z.at[kind, slot], r_.fz_s.at[kind, 0], r_.fz_r.at[kind, slot],
            sibling,
        )

    def end_ffn(d):
        end_plane(d)

        def send():
            for kind in range(2):
                z_out(kind, d).start()

        if d > 0:
            pl.when(depth == 0)(send)

    def z_pass(d):
        def add_and_send():
            for kind in range(2):
                z_in(kind, d).wait_recv()
                add_all(cut(r_.fsend.at[kind, order_at(d)], kind, 0, 0), r_.f_z.at[kind, d])
                z_out(kind, d).start()

        pl.when(inside)(add_and_send)

    def last_out(name, k, h):
        buf, dst, s, r = last[name]
        return push(
            cut(buf.at[k], k, 0, 0).at[h], dst.at[z], s.at[k, h], r.at[z], device(h, px, py, 2 * core + k)
        )

    def last_here(name, k):
        buf, dst, _, _ = last[name]
        return pltpu.make_async_copy(cut(buf.at[k], k, 0, 0).at[core], dst.at[z], r_.last_sem.at["abcv".index(name)])

    last = {
        "a": (r_.asend.at[0], r_.a_z.at[0], r_.az_s.at[0], r_.az_r.at[0]),
        "b": (r_.asend.at[1], r_.a_z.at[1], r_.az_s.at[1], r_.az_r.at[1]),
        "c": (r_.asend.at[2], r_.a_z.at[2], r_.az_s.at[2], r_.az_r.at[2]),
        "v": (r_.vsend, r_.v_z, r_.vz_s, r_.vz_r),
    }

    def last_each(name, here_do, away_do):
        for k in range(2):
            for h in range(2):
                here = (core == h) & (z == 2 * core + k)
                if here_do is not None:
                    pl.when(here)(lambda: here_do(last_here(name, k)))
                when_not(here, lambda: away_do(last_out(name, k, h)))

    def last_total(name):
        buf, dst, s, r = last[name]
        for zs in range(head_count):
            here = is_home & (z == zs)
            pl.when(here)(lambda: last_here(name, 0).wait())
            when_not(
                here, lambda: push(buf.at[0, 0, 0, 0], dst.at[zs], s.at[0, 0], r.at[zs], sibling).wait_recv()
            )
        value = dst[0].astype(F32)
        for zs in range(1, head_count):
            value = value + dst[zs].astype(F32)
        return value

    def ffn_grads(d):
        i = order_at(d)

        def grads(kind, left, right):
            value = tn(left[0, :, cols(i)], right[0]) + tn(left[1, :, cols(i)], right[1])
            for p in range(planes):
                r_.fsend[kind, i, p // 2, p % 2] = value[p * hid : (p + 1) * hid, :].astype(BF)

        grads(1, r_.u, r_.xh2)
        pl.when(d >= 2)(lambda: start_sum(d, ((1, 1), (0, 1))))
        pull_inner(i)
        grads(0, r_.gp, r_.hb)
        pl.when(d == 2)(lambda: travel(3, (1,)))
        pl.when(d >= 2)(lambda: start_sum(d, ((1, 0), (0, 0))))
        pl.when(d == 1)(lambda: travel(3, (0,)))

    keep_tail()
    tail_gather(0, 1)
    pull_two()
    loop(head_count, lambda n: ffn_grads(head_count - 1 - n))
    dbin_pair = push(r_.dbin, r_.dbin_in, r_.pair_s.at[2], r_.pair_r.at[2], sibling)

    def backward(n):
        seg = 1 - n
        pull_hidden(seg)

        pull_one(seg)

        def first_events():
            travel(2)
            start_sum(1)
            start_sum(0)
            tail_gather(0, 2)

        pl.when(seg == 1)(first_events)
        pull_heads(seg)

        def segment_two():
            end_ffn(3)
            loop(2, lambda i: pull_rows(1, end_span(i)))

            def one(i):
                exchange(1, end_span(i)).wait()
                pull_x(end_span(i)[0])

            loop(2, one)
            pull_memory(1)
            pull_tail()
            dbin_pair.start()
            pull_rows(1, middle_span(0))
            z_pass(3)
            end_ffn(2)
            travel(1)
            exchange(1, middle_span(0)).wait()
            pull_x(middle_span(0)[0])
            text_grad(1)
            back_send(1, 1)

        pl.when(seg == 1)(segment_two)

    loop(2, backward)
    travel(0)
    z_pass(2)
    hid_rows = width // dp_count
    cut_rows = hid_rows // len(halves)

    def attention_grads(i):
        wide = width // 2
        span = pl.ds(pl.multiple_of(i * wide, wide), wide)
        xt = [x[s, :, span].T for s in range(2)]
        gt = [r_.xh1[s, :, span].T for s in range(2)]
        for k in range(2):
            qkv_g = nt(xt[0], qkv[0, k]) + nt(xt[1], qkv[1, k])
            out_g = nt(gt[0], ot[0, k]) + nt(gt[1], ot[1, k])
            for n in range(4 * len(halves)):
                at = slice(n * cut_rows, (n + 1) * cut_rows)
                b, part = n // len(halves), n % len(halves)
                r_.asend[part, k, i, b // 2, b % 2, :, 0 : 3 * local] = qkv_g[at, :].astype(BF)
                r_.asend[part, k, i, b // 2, b % 2, :, 3 * local :] = out_g[at, :].astype(BF)

    def both_planes(n):
        attention_grads(jnp.where(n == 0, 1 - py, py))

        def travelling():
            for name in halves:
                start_sum(name, ((1, 0), (1, 1)))

        pl.when(n == 0)(travelling)

    loop(2, both_planes)
    start_sum("a", ((0, 1), (0, 0)))
    tail_gather(1, 1)
    end_ffn(1)
    loop(2, lambda i: pull_rows(0, half_span(i)))
    by_half(1, pull_x)
    pull_memory(0)
    dbin_pair.wait()

    dbin_both = [jnp.where(core == h, r_.dbin[0:1, :], r_.dbin_in[0:1, :]) for h in range(2)]
    for k in range(2):
        r_.bqv[k] = sum(jnp.sum(qkv[s, k].astype(F32), axis=1, keepdims=True) for s in range(2))
    sg, dinit = r_.sg, r_.dinit
    r_.vec[...] = jnp.where(is_mem, dinit[...], 0.0)
    r_.vec[0:6, :] = sg[0:6, :]
    vtmp[...] = jnp.zeros_like(vtmp)

    def by_core(cut_of):
        return jnp.where(core == 0, cut_of(0), cut_of(1))

    qv_rows = [
        [
            jnp.sum(
                jnp.where(
                    lax.broadcasted_iota(jnp.int32, (HD, HD), 0) == lax.broadcasted_iota(jnp.int32, (HD, HD), 1),
                    r_.bqv[k, 2 * part * local + b * HD : 2 * part * local + (b + 1) * HD, :],
                    0.0,
                ),
                axis=0,
                keepdims=True,
            )
            for part in range(2)
            for b in range(per_block)
        ]
        for k in range(2)
    ]
    piece_b = HD // dp_count
    vec = r_.vec[...]

    def small_cut(k, p, h):
        dp_t = 2 * p + h

        def from_vec(c):
            at = (dp_t * head_count + 2 * c + k) * lanes
            return vec[:, at : at + lanes]

        def from_bin(c):
            at = ((2 * c + k) * planes + p) * hid
            return dbin_both[h][:, at : at + hid]

        vtmp[0:16, 0:lanes] = by_core(from_vec)
        vtmp[0:1, 32 : 32 + hid] = by_core(from_bin)
        for n, line in enumerate(qv_rows[k]):
            vtmp[1:2, 32 + n * piece_b : 32 + (n + 1) * piece_b] = line[:, dp_t * piece_b : (dp_t + 1) * piece_b]
        r_.vsend[k, p // 2, p % 2, h] = vtmp[...].astype(BF)

    for k in range(2):
        for p in range(planes):
            for h in range(2):
                small_cut(k, p, h)
    start_sum("v")
    end_ffn(0)
    z_pass(1)
    travel("a")
    start_sum("b", ((0, 1), (0, 0)))
    text_grad(0)
    back_send(1, 0)
    travel("b")
    start_sum("c", ((0, 1), (0, 0)))
    travel("c")
    travel("v")
    end_plane("a")
    last_each("a", lambda c: c.start(), lambda c: c.start())
    tail_gather(1, 2)
    end_plane("b")
    last_each("b", lambda c: c.start(), lambda c: c.start())
    end_plane("v")
    last_each("v", lambda c: c.start(), lambda c: c.start())
    end_plane("c")
    last_each("c", lambda c: c.start(), lambda c: c.start())

    results = (
        (r_.win_v, r_.win_o), (r_.wback_v, r_.wback_o), (r_.dt_v, r_.dt_o), (r_.dqkv_v, r_.dqkv_o),
        (r_.dwout_v, r_.dwout_o), (r_.dinit_v, r_.dinit_o), (r_.dbqv_v, r_.dbqv_o), (r_.dbin_v, r_.dbin_o),
        (r_.dgains_v, r_.dgains_o), (r_.dbiases_v, r_.dbiases_o),
    )

    def leave(n):
        return pltpu.make_async_copy(results[n][0], results[n][1], r_.leave_sem.at[n])

    tail_gather(0, 3)
    tail_gather(1, 3)
    extra = tail_products()
    for kind, out in enumerate((r_.win_v, r_.wback_v)):
        value = cut(r_.fsend.at[kind, z], kind, 0, 0)[...].astype(F32)
        z_in(kind, 0).wait_recv()
        out[...] = value + r_.f_z[kind, 0].astype(F32)

        def other_side():
            z_in(kind, 4).wait_recv()
            out[...] += r_.f_z[kind, 4].astype(F32)

        pl.when(inside)(other_side)
        out[:, half_of(core)] += extra[kind][0]
        out[:, half_of(1 - core)] += extra[kind][1]
        leave(kind).start()


    sums_sent()
    for d in range(1, head_count):
        for kind in range(2):
            z_out(kind, d).wait_send()
    for which in range(2):
        for seg in range(2):
            back_sent(which, seg)
    for a in range(2, 4):
        rows_done(a)
    attention_outs(lambda c: c.wait_send())
    ffn_sent()
    for which in range(2):
        tail_gather(which, 4)
    for copy in pair:
        copy.wait_send()
    for k in range(2):

        def sent():
            for which in range(4):
                attention_plane(k, which).wait_send()

        pl.when(foreign[k])(sent)
    every_side = wf.at[:, pl.ds(0, 3 * head_count * hid)]
    push(every_side, every_side, r_.side_s.at[0], r_.side_s.at[0], sibling).wait_send()
    smalls.wait_send()
    for i in range(3):
        small_plane(i).wait_send()
    for j in range(2):
        both = [r_.text_pad[j, s, 0:text_rows, :].astype(F32)[:, None, :] for s in range(2)]
        r_.dt_v[j] = jnp.concatenate(both, axis=1).astype(BF)
    leave(2).start()
    total_v = last_total("v")
    r_.dinit_v[...] = total_v[6 : 6 + mem_rows, 0:lanes]
    for b in range(per_block):
        for part in range(2):
            at = 32 + (part * per_block + b) * piece_b
            r_.dbqv_v[b, part : part + 1, :] = total_v[1:2, at : at + piece_b]
    r_.dbin_v[...] = total_v[0:1, 32 : 32 + hid]
    r_.dgains_v[...] = total_v[0:2, 0:lanes]
    r_.dbiases_v[...] = total_v[2:6, 0:lanes]
    for n in range(5, len(results)):
        leave(n).start()
    for n, name in enumerate(halves):
        part = last_total(name)
        at = slice(n * cut_rows, (n + 1) * cut_rows)
        for t in range(3):
            r_.dqkv_v[t, at, :] = part[:, t * local : (t + 1) * local]
        r_.out_rows[at, :] = part[:, 3 * local :]
    leave(3).start()
    r_.dwout_v[...] = r_.out_rows[...].T
    leave(4).start()
    for n in range(len(results)):
        leave(n).wait()
    for name in "abcv":
        last_each(name, None, lambda c: c.wait_send())


def vmem(*shape, dtype=BF):
    return pltpu.VMEM(shape, dtype)


def f32(*shape):
    return pltpu.VMEM(shape, F32)


def sds(*shape, dtype=BF):
    return jax.ShapeDtypeStruct(shape, dtype)


def dma(*shape):
    return pltpu.SemaphoreType.DMA(shape)


ANY = pl.BlockSpec(memory_space=pl.ANY)
INV = pl.BlockSpec(memory_space=pltpu.VMEM)
INS = pl.BlockSpec(memory_space=pltpu.SMEM)


def end_kernel(count, *refs):
    given, out, kept = refs[:count], refs[count : 2 * count], refs[2 * count : 3 * count]
    sem = refs[3 * count]
    parts = []
    for n in range(count):
        if len(given[n].shape) == 4:
            parts += [(n, (j, s)) for j in range(2) for s in range(2)] if n == 0 else [(n, (j,)) for j in range(2)]
        else:
            parts.append((n, ()))

    def part(ref, at):
        return ref.at[at] if at else ref

    loads = [
        pltpu.make_async_copy(part(given[n], at), part(kept[n], at), sem.at[0, i]) for i, (n, at) in enumerate(parts)
    ]
    stores = [
        pltpu.make_async_copy(part(kept[n], at), part(out[n], at), sem.at[1, i]) for i, (n, at) in enumerate(parts)
    ]
    for copy in loads:
        copy.start()
    for load, store in zip(loads, stores):
        load.wait()
        store.start()
    for copy in stores:
        copy.wait()


def by_chip(
    text, boundary, reset, memory_in, init_memory, w_qkv, b_qv, w_out, w_in, w_back, b_in, norm_gains, biases,
    cotangent,
):
    head_count = lax.axis_size("head")
    dp_count = lax.axis_size("dp")
    planes = dp_count // 2
    total = dp_count * head_count
    text_rows, width = text.shape[2], text.shape[3]
    block = cotangent.shape[2]
    seg_len = block * head_count
    mem_rows = memory_in.shape[1]
    local = w_qkv.shape[2]
    hid = w_in.shape[1]
    lanes = norm_gains.shape[1]
    heads = 2 * local // HD
    hidden = hid * planes * head_count
    share = width // dp_count

    inputs = dict(
        text=(text.transpose(0, 2, 1, 3), ANY),
        boundary=(boundary, INV),
        reset=(reset, INS),
        memory_in=(memory_in.transpose(1, 0, 2), INV),
        init_memory=(init_memory, INV),
        wq_t=(w_qkv.transpose(1, 2, 0).reshape(3 * local, width), ANY),
        w_out=(w_out, ANY),
        b_qv=(b_qv.transpose(1, 0, 2), INV),
        w_in_t=(w_in.T, ANY),
        w_back=(w_back, ANY),
        b_in=(b_in[None, :], INV),
        norm_gains=(norm_gains, INV),
        biases=(biases, INV),
        cotangent=(cotangent, ANY),
    )
    slice_b = HD // dp_count
    shapes = dict(
        acts=sds(2, 2, block, width),
        dt=sds(2, text_rows, 2, width),
        dinit=sds(mem_rows, lanes, dtype=F32),
        dqkv=sds(3, share, local, dtype=F32),
        dbqv=sds(local // HD, 2, slice_b, dtype=F32),
        dwout=sds(local, share, dtype=F32),
        win=sds(hid, width, dtype=F32),
        wback=sds(hid, width, dtype=F32),
        dbin=sds(1, hid, dtype=F32),
        dgains=sds(2, lanes, dtype=F32),
        dbiases=sds(4, lanes, dtype=F32),
    )
    outputs = {name + "_o": (shape, ANY) for name, shape in shapes.items()}
    staged = {name + "_v": pltpu.VMEM(shape.shape, shape.dtype) for name, shape in shapes.items() if name != "acts"}
    scratch = dict(
        text_pad=vmem(2, 2, block, width),
        text_v=vmem(2, text_rows, 2, width),
        early_sem=dma(3),
        text_all=vmem(2, seg_len, width),
        cot_all=vmem(2, seg_len, width),
        wa=vmem(2, 4 * local, width),
        wf=vmem(2, hidden, width),
        small=vmem(16, 128),
        small_all=vmem(total, 16, 128),
        seqf=f32(8, seg_len),
        seqf_in=f32(8, seg_len),
        seq=f32(8, seg_len),
        memp=vmem(16, width),
        memp_in=vmem(16, width),
        par=f32(16, width),
        bin_row=f32(1, hidden),
        bqv=f32(2, 3 * local, 1),
        x=vmem(2, seg_len, width),
        qkv=vmem(2, 2, 3 * local, seg_len),
        pt=vmem(2, heads, seg_len, seg_len),
        ot=vmem(2, 2, local, seg_len),
        hf=f32(seg_len, width),
        acc=f32(seg_len, width),
        xh1=vmem(2, seg_len, width),
        hb=vmem(2, seg_len, width),
        u=vmem(2, seg_len, hidden),
        gp=vmem(2, seg_len, hidden),
        xh2=vmem(2, seg_len, width),
        rs=f32(seg_len, 4),
        y=vmem(2, seg_len, width),
        got=vmem(2, local, seg_len),
        send_buf=vmem(2, seg_len, width),
        recv_buf=vmem(2, seg_len, width),
        cur_a=vmem(16, width),
        cur_b=vmem(16, width),
        carry=f32(16, width),
        xh2_t=vmem(16, width),
        gp_t=vmem(16, hidden),
        factor_out=vmem(2, head_count, 16, width // 2 + hidden // head_count),
        factors=vmem(2, head_count, planes, 16, width // 2 + hidden // head_count),
        factors_in=vmem(2, head_count, planes, 16, width // 2),
        sg=f32(8, width),
        dinit=f32(16, width),
        dbin=f32(8, hidden),
        dbin_in=f32(8, hidden),
        vec=f32(16, width),
        vtmp=f32(16, 128),
        fsend=vmem(2, head_count, 2, 2, hid, width),
        f_one=vmem(2, head_count, 2, hid, width),
        f_two=vmem(2, head_count, hid, width),
        f_z=vmem(2, head_count + 1, hid, width),
        asend=vmem(3, 2, 2, 2, 2, share // 3, width),
        a_one=vmem(3, 2, 2, 2, share // 3, width),
        a_two=vmem(3, 2, 2, share // 3, width),
        a_z=vmem(3, head_count, share // 3, width),
        out_rows=f32(share, local),
        vsend=vmem(2, 2, 2, 2, 16, 128),
        v_one=vmem(2, 2, 2, 16, 128),
        v_two=vmem(2, 2, 16, 128),
        v_z=vmem(head_count, 16, 128),
        small_s=dma(1),
        small_r=dma(1),
        small_ps=dma(3),
        small_pr=dma(3),
        pair_s=dma(3),
        pair_r=dma(3),
        att_s=dma(3),
        att_r=dma(2, 2),
        plane_s=dma(2, 4),
        plane_r=dma(2, 4),
        local_sem=dma(2),
        rows_s=dma(4),
        rows_r=dma(4, 4),
        here_sem=dma(4),
        fwd_s=dma(4),
        fwd_r=dma(4),
        ffn_s=dma(5),
        ffn_r=dma(4),
        side_s=dma(1),
        side_r=dma(4, 2, 3),
        send_sem=dma(2, 4),
        recv_sem=dma(2, 4),
        back_s=dma(2, 2),
        back_r=dma(2, 2),
        back_here_sem=dma(2, 2),
        sum_s=dma(3),
        fsum_r=dma(2, 4, 3),
        asum_r=dma(3, 2, 3),
        tg_s=dma(2),
        tg_r=dma(2, 8),
        tp_s=dma(2),
        tp_r=dma(2),
        vsum_r=dma(2, 3),
        fz_s=dma(2, 4),
        fz_r=dma(2, 5),
        az_s=dma(3, 2, 2),
        az_r=dma(3, 4),
        leave_sem=dma(10),
        vz_s=dma(2, 2),
        vz_r=dma(4),
        last_sem=dma(4),
    )
    scratch.update(staged)
    names = tuple(inputs) + tuple(outputs) + tuple(scratch)
    middle = pl.pallas_call(
        functools.partial(main_kernel, names, dp_count, head_count),
        out_shape=tuple(v[0] for v in outputs.values()),
        in_specs=[v[1] for v in inputs.values()],
        out_specs=tuple(v[1] for v in outputs.values()),
        scratch_shapes=list(scratch.values()),
        compiler_params=pltpu.CompilerParams(
            collective_id=0, has_side_effects=True, vmem_limit_bytes=VMEM_LIMIT
        ),
        name="layer",
    )(*(v[0] for v in inputs.values()))

    out = pl.pallas_call(
        functools.partial(end_kernel, len(shapes)),
        out_shape=tuple(shapes.values()),
        in_specs=[ANY] * len(shapes),
        out_specs=tuple([ANY] * len(shapes)),
        scratch_shapes=[pltpu.VMEM(shape.shape, shape.dtype) for shape in shapes.values()] + [dma(2, 16)],
        name="results",
    )(*middle)
    acts, d_text, d_init, d_qkv, d_bqv, d_wout, d_win, d_wback, d_bin, d_gains, d_biases = out
    return (
        acts, d_text.transpose(0, 2, 1, 3), d_init,
        d_qkv.transpose(1, 0, 2),
        d_bqv.transpose(1, 0, 2),
        d_wout, d_win.T, d_wback, d_bin[0], d_gains, d_biases,
    )


def solution(mesh):
    body = by_chip if mesh.shape["dp"] == 8 and mesh.shape["head"] == 4 else local
    return jax.shard_map(
        body,
        mesh=mesh,
        in_specs=(
            P("dp", None, "head", None),
            P("dp", None, None),
            P("dp", None),
            P("dp", None, None),
            P(None, ("dp", "head")),
            P(None, None, "head"),
            P(None, "head", None),
            P("head", None),
            P(None, ("dp", "head")),
            P(("dp", "head"), None),
            P(("dp", "head")),
            P(None, ("dp", "head")),
            P(None, ("dp", "head")),
            P("dp", None, "head", None),
        ),
        out_specs=(
            P("dp", None, "head", None),
            P("dp", None, "head", None),
            P(None, ("dp", "head")),
            P("dp", None, "head"),
            P(None, "head", "dp"),
            P("head", "dp"),
            P(None, ("dp", "head")),
            P(("dp", "head"), None),
            P(("dp", "head")),
            P(None, ("dp", "head")),
            P(None, ("dp", "head")),
        ),
        check_vma=False,
    )
```

```python
import functools

import jax
import jax.numpy as jnp
from jax import lax
from jax.experimental import pallas as pl
from jax.experimental.pallas import tpu as pltpu
from jax.sharding import PartitionSpec as P

HD = 64
MESH = pl.DeviceIdType.MESH
BF = jnp.bfloat16
F32 = jnp.float32
VMEM_LIMIT = 64 * 1024 * 1024


def nn(a, b):
    return lax.dot_general(a, b, (((1,), (0,)), ((), ())), preferred_element_type=F32)


def nt(a, b):
    return lax.dot_general(a, b, (((1,), (1,)), ((), ())), preferred_element_type=F32)


def tn(a, b):
    return lax.dot_general(a, b, (((0,), (0,)), ((), ())), preferred_element_type=F32)


def place():
    dp, z = lax.axis_index("dp"), lax.axis_index("head")
    core, plane = dp % 2, dp // 2
    return core, plane % 2, plane // 2, z


def device(core, x, y, z):
    return ((y * 2 + x) * 2 + core, z)


def push(src, dst, send, recv, target):
    return pltpu.make_async_remote_copy(
        src_ref=src, dst_ref=dst, send_sem=send, recv_sem=recv, device_id=target, device_id_type=MESH
    )


def from_root(x, axis, root):
    mine = lax.axis_index(axis) == root
    return lax.psum(jnp.where(mine, x, jnp.zeros_like(x)), axis)


def layer_norm(values, gain_row, shift_row):
    center = values - jnp.mean(values, axis=-1, keepdims=True)
    spread = jnp.mean(center * center, axis=-1, keepdims=True)
    return center * lax.rsqrt(spread + 1e-05) * gain_row + shift_row


def gelu_tanh(values):
    return jax.nn.gelu(values, approximate=True)


def head_major(array, dim, dp_count, head_count):
    shape = array.shape
    size = shape[dim]
    split = array.reshape(
        shape[:dim] + (dp_count, head_count, size // (dp_count * head_count)) + shape[dim + 1 :]
    )
    return jnp.swapaxes(split, dim, dim + 1).reshape(shape)


def local(
    text,
    boundary,
    reset,
    memory_in,
    init_memory,
    w_qkv,
    b_qv,
    w_out,
    w_in,
    w_back,
    b_in,
    norm_gains,
    biases,
    cotangent,
):
    head_count = lax.axis_size("head")
    dp_count = lax.axis_size("dp")
    head_idx = lax.axis_index("head")
    batch_size = text.shape[0]
    width = text.shape[3]
    seg_rows = cotangent.shape[2]
    seg_len = seg_rows * head_count
    mem_rows = memory_in.shape[1]
    text_len = seg_len - 2 * mem_rows
    local_width = w_qkv.shape[2]
    local_heads = local_width // HD
    row_start = head_idx * seg_rows
    is_first = (head_idx == 0).astype(jnp.float32)
    is_final = (head_idx == head_count - 1).astype(jnp.float32)
    grad_dims = (1, 0, 0, 1, 1, 1)
    doc_ids = jnp.cumsum(boundary, axis=2)
    marks = jnp.full((batch_size, 2, mem_rows), -1, jnp.int32)
    labels = jnp.concatenate([marks, doc_ids, marks], axis=2)
    visible = (
        (labels[..., :, None] == labels[..., None, :])
        | (labels[..., :, None] < 0)
        | (labels[..., None, :] < 0)
    )
    bias_query = b_qv[0].reshape(local_width).astype(jnp.float32)
    bias_value = b_qv[1].reshape(local_width).astype(jnp.float32)
    shared = (
        lax.all_gather(w_in, ("dp", "head"), axis=1, tiled=True),
        lax.all_gather(w_back, ("dp", "head"), axis=0, tiled=True),
        lax.all_gather(b_in, ("dp", "head"), axis=0, tiled=True),
        lax.all_gather(norm_gains, ("dp", "head"), axis=1, tiled=True),
        lax.all_gather(biases, ("dp", "head"), axis=1, tiled=True),
        lax.all_gather(init_memory, ("dp", "head"), axis=1, tiled=True),
    )

    def fetch():
        return shared

    def attention_probs(query, key_rows, seg):
        scores = (
            jnp.einsum("sqhe,skhe->shqk", query, key_rows, preferred_element_type=jnp.float32)
            * 0.125
        )
        return jnp.where(visible[:, seg][:, None], scores, -1e30)

    def forward(seg, memory, ffn):
        w_in_all, w_back_all, b_in_all, gains_all, biases_all, unused = ffn
        gains_f = gains_all.astype(jnp.float32)
        biases_f = biases_all.astype(jnp.float32)
        local_text = lax.all_gather(text[:, seg], "head", axis=1, tiled=True)
        x_rows = jnp.concatenate([memory, local_text, memory], axis=1)
        mixed = jnp.einsum("srd,dce->srce", x_rows, w_qkv, preferred_element_type=jnp.float32)
        query = (
            (mixed[:, :, 0] + bias_query)
            .astype(jnp.bfloat16)
            .reshape(batch_size, seg_len, local_heads, HD)
        )
        key_rows = mixed[:, :, 1].astype(jnp.bfloat16).reshape(batch_size, seg_len, local_heads, HD)
        value = (
            (mixed[:, :, 2] + bias_value)
            .astype(jnp.bfloat16)
            .reshape(batch_size, seg_len, local_heads, HD)
        )
        masked = attention_probs(query, key_rows, seg)
        row_max = jnp.max(masked, axis=-1, keepdims=True)
        exp_terms = jnp.exp(masked - row_max)
        row_total = jnp.sum(exp_terms, axis=-1, keepdims=True)
        log_total = row_max + jnp.log(row_total)
        probs = (exp_terms / row_total).astype(jnp.bfloat16)
        attended = jnp.einsum("shqk,skhe->sqhe", probs, value, preferred_element_type=jnp.float32)
        attended = attended.astype(jnp.bfloat16).reshape(batch_size, seg_len, local_width)
        partial_out = jnp.einsum("srl,ld->srd", attended, w_out, preferred_element_type=jnp.float32)
        summed = lax.psum_scatter(
            partial_out.astype(jnp.bfloat16), "head", scatter_dimension=1, tiled=True
        ).astype(jnp.float32)
        own_rows = lax.dynamic_slice_in_dim(x_rows, row_start, seg_rows, 1).astype(jnp.float32)
        pre_norm = own_rows + summed + biases_f[1]
        hidden = layer_norm(pre_norm, gains_f[0], biases_f[0])
        hidden_low = hidden.astype(jnp.bfloat16)
        inner = jnp.einsum(
            "srd,df->srf", hidden_low, w_in_all, preferred_element_type=jnp.float32
        ) + b_in_all.astype(jnp.float32)
        active = gelu_tanh(inner).astype(jnp.bfloat16)
        outer = (
            jnp.einsum("srf,fd->srd", active, w_back_all, preferred_element_type=jnp.float32)
            + biases_f[2]
        )
        post_norm = hidden + outer
        result = layer_norm(post_norm, gains_f[1], biases_f[3])
        kept = (
            x_rows,
            query,
            key_rows,
            value,
            log_total,
            attended,
            pre_norm,
            hidden_low,
            inner,
            active,
            post_norm,
        )
        return (result, kept)

    def backward(seg, grad_out, kept, ffn):
        (
            x_rows,
            query,
            key_rows,
            value,
            log_total,
            attended,
            pre_norm,
            hidden_low,
            inner,
            active,
            post_norm,
        ) = kept
        w_in_all, w_back_all, b_in_all, gains_all, biases_all, unused = ffn
        gains_f = gains_all.astype(jnp.float32)
        biases_f = biases_all.astype(jnp.float32)
        unused_two, pull_two = jax.vjp(layer_norm, post_norm, gains_f[1], biases_f[3])
        grad_post, grad_gain_two, grad_shift_two = pull_two(grad_out)
        grad_outer = grad_post.astype(jnp.bfloat16)
        grad_ffn_bias = jnp.sum(grad_post, axis=(0, 1))
        grad_w_back = jnp.einsum(
            "srf,srd->fd", active, grad_outer, preferred_element_type=jnp.float32
        )
        grad_active = jnp.einsum(
            "srd,fd->srf", grad_outer, w_back_all, preferred_element_type=jnp.float32
        )
        unused_gelu, pull_gelu = jax.vjp(gelu_tanh, inner)
        grad_inner = pull_gelu(grad_active)[0].astype(jnp.bfloat16)
        grad_b_in = jnp.sum(grad_inner, axis=(0, 1), dtype=jnp.float32)
        grad_w_in = jnp.einsum(
            "srd,srf->df", hidden_low, grad_inner, preferred_element_type=jnp.float32
        )
        grad_hidden = grad_post + jnp.einsum(
            "srf,df->srd", grad_inner, w_in_all, preferred_element_type=jnp.float32
        )
        unused_one, pull_one = jax.vjp(layer_norm, pre_norm, gains_f[0], biases_f[0])
        grad_pre, grad_gain_one, grad_shift_one = pull_one(grad_hidden)
        grad_out_bias = jnp.sum(grad_pre, axis=(0, 1))
        grad_branch = lax.all_gather(grad_pre.astype(jnp.bfloat16), "head", axis=1, tiled=True)
        grad_w_out = jnp.einsum(
            "srl,srd->ld", attended, grad_branch, preferred_element_type=jnp.float32
        )
        grad_att = jnp.einsum("srd,ld->srl", grad_branch, w_out, preferred_element_type=jnp.float32)
        grad_att = grad_att.astype(jnp.bfloat16).reshape(batch_size, seg_len, local_heads, HD)
        masked = attention_probs(query, key_rows, seg)
        probs = jnp.exp(masked - log_total)
        grad_value = jnp.einsum(
            "shqk,sqhe->skhe",
            probs.astype(jnp.bfloat16),
            grad_att,
            preferred_element_type=jnp.float32,
        )
        grad_probs = jnp.einsum(
            "sqhe,skhe->shqk", grad_att, value, preferred_element_type=jnp.float32
        )
        grad_scores = probs * (grad_probs - jnp.sum(grad_probs * probs, axis=-1, keepdims=True))
        grad_scores = grad_scores.astype(jnp.bfloat16)
        grad_query = (
            jnp.einsum("shqk,skhe->sqhe", grad_scores, key_rows, preferred_element_type=jnp.float32)
            * 0.125
        )
        grad_key = (
            jnp.einsum("shqk,sqhe->skhe", grad_scores, query, preferred_element_type=jnp.float32)
            * 0.125
        )
        grad_mixed = jnp.stack([grad_query, grad_key, grad_value], axis=2).astype(jnp.bfloat16)
        grad_mixed = grad_mixed.reshape(batch_size, seg_len, 3, local_width)
        grad_bias_qv = jnp.stack(
            [
                jnp.sum(grad_mixed[:, :, 0], axis=(0, 1), dtype=jnp.float32),
                jnp.sum(grad_mixed[:, :, 2], axis=(0, 1), dtype=jnp.float32),
            ]
        ).reshape(2, local_heads, HD)
        grad_w_qkv = jnp.einsum(
            "srd,srce->dce", x_rows, grad_mixed, preferred_element_type=jnp.float32
        )
        grad_rows = jnp.einsum(
            "srce,dce->srd", grad_mixed, w_qkv, preferred_element_type=jnp.float32
        )
        placed = lax.dynamic_update_slice_in_dim(jnp.zeros_like(grad_rows), grad_pre, row_start, 1)
        grad_rows = grad_rows + placed
        grad_text_part = lax.psum_scatter(
            grad_rows[:, mem_rows : mem_rows + text_len].astype(jnp.bfloat16),
            "head",
            scatter_dimension=1,
            tiled=True,
        ).astype(jnp.float32)
        grad_memory = lax.psum(
            (grad_rows[:, :mem_rows] + grad_rows[:, seg_len - mem_rows :]).astype(jnp.bfloat16),
            "head",
        ).astype(jnp.float32)
        reset_flag = reset[:, seg] > 0
        grad_init = (
            jnp.sum(jnp.where(reset_flag[:, None, None], grad_memory, 0.0), axis=0) * is_first
        )
        ffn_grads = (
            grad_w_in,
            grad_w_back,
            grad_b_in,
            jnp.stack([grad_gain_one, grad_gain_two]),
            jnp.stack([grad_shift_one, grad_out_bias, grad_ffn_bias, grad_shift_two]),
            grad_init,
        )
        return (grad_text_part, grad_memory, (grad_w_qkv, grad_bias_qv, grad_w_out), ffn_grads)

    ffn_first = fetch()
    init_all = ffn_first[5]
    memory_one = jnp.where(reset[:, 0, None, None] > 0, init_all[None], memory_in)
    out_one, kept_one = forward(0, memory_one, ffn_first)
    tail_rows = out_one[:, seg_rows - mem_rows :].astype(jnp.bfloat16)
    carried = from_root(tail_rows, "head", head_count - 1)
    ffn_second = fetch()
    memory_two = jnp.where(reset[:, 1, None, None] > 0, ffn_second[5][None], carried)
    out_two, kept_two = forward(1, memory_two, ffn_second)
    activations = jnp.stack([out_one, out_two], axis=1).astype(jnp.bfloat16)
    ffn_third = fetch()
    text_two, memory_grad_two, attn_two, ffn_two = backward(
        1, cotangent[:, 1].astype(jnp.float32), kept_two, ffn_third
    )
    keep_flag = reset[:, 1, None, None] <= 0
    carried_grad = jnp.where(keep_flag, memory_grad_two, 0.0) * is_final
    grad_one = cotangent[:, 0].astype(jnp.float32) + jnp.concatenate(
        [jnp.zeros((batch_size, seg_rows - mem_rows, width), jnp.float32), carried_grad], axis=1
    )
    ffn_fourth = fetch()
    text_one, memory_grad_one, attn_one, ffn_one = backward(0, grad_one, kept_one, ffn_fourth)
    grads = jax.tree.map(lambda a, b: a + b, ffn_one, ffn_two)
    ffn_total = tuple((head_major(g, d, dp_count, head_count) for g, d in zip(grads, grad_dims)))
    partial_sums = (
        lax.psum_scatter(
            ffn_total[0].astype(jnp.bfloat16), "head", scatter_dimension=1, tiled=True
        ).astype(jnp.float32),
        lax.psum_scatter(
            ffn_total[1].astype(jnp.bfloat16), "head", scatter_dimension=0, tiled=True
        ).astype(jnp.float32),
        lax.psum_scatter(
            ffn_total[2].astype(jnp.bfloat16), "head", scatter_dimension=0, tiled=True
        ).astype(jnp.float32),
        lax.psum_scatter(
            ffn_total[3].astype(jnp.bfloat16), "head", scatter_dimension=1, tiled=True
        ).astype(jnp.float32),
        lax.psum_scatter(
            ffn_total[4].astype(jnp.bfloat16), "head", scatter_dimension=1, tiled=True
        ).astype(jnp.float32),
        lax.psum_scatter(
            ffn_total[5].astype(jnp.bfloat16), "head", scatter_dimension=1, tiled=True
        ).astype(jnp.float32),
    )
    reduced = (
        lax.psum_scatter(partial_sums[0], "dp", scatter_dimension=1, tiled=True),
        lax.psum_scatter(partial_sums[1], "dp", scatter_dimension=0, tiled=True),
        lax.psum_scatter(partial_sums[2], "dp", scatter_dimension=0, tiled=True),
        lax.psum_scatter(partial_sums[3], "dp", scatter_dimension=1, tiled=True),
        lax.psum_scatter(partial_sums[4], "dp", scatter_dimension=1, tiled=True),
        lax.psum_scatter(partial_sums[5], "dp", scatter_dimension=1, tiled=True),
    )
    attn_total = jax.tree.map(lambda a, b: a + b, attn_one, attn_two)
    grad_qkv, grad_bqv, grad_wout = (
        lax.psum_scatter(attn_total[0], "dp", scatter_dimension=0, tiled=True),
        lax.psum_scatter(attn_total[1], "dp", scatter_dimension=2, tiled=True),
        lax.psum_scatter(attn_total[2], "dp", scatter_dimension=1, tiled=True),
    )
    grad_text = jnp.stack([text_one, text_two], axis=1).astype(jnp.bfloat16)
    grad_win, grad_wback, grad_bin, grad_gains, grad_biases, grad_init = reduced
    return (
        activations,
        grad_text,
        grad_init,
        grad_qkv,
        grad_bqv,
        grad_wout,
        grad_win,
        grad_wback,
        grad_bin,
        grad_gains,
        grad_biases,
    )


class Refs:
    pass


def by_name(names, values):
    refs = Refs()
    for name, value in zip(names, values, strict=True):
        setattr(refs, name, value)
    return refs


def loop(count, body, unroll=1):
    def run(i, unused):
        body(i)
        return unused

    lax.fori_loop(0, count, run, 0, unroll=unroll)


def add_all(dst, *sources):
    def body(at):
        dst[at] = sum([src[at].astype(F32) for src in sources], dst[at].astype(F32)).astype(BF)

    if len(dst.shape) == 2:
        body(...)
    else:
        loop(dst.shape[0], body)


def as_column(row):
    n = row.shape[1]
    down = lax.broadcasted_iota(jnp.int32, (n, n), 0)
    across = lax.broadcasted_iota(jnp.int32, (n, n), 1)
    return jnp.sum(jnp.where(down == across, row, 0.0), axis=1, keepdims=True)


def norm(v):
    center = v - jnp.mean(v, axis=-1, keepdims=True)
    scale = lax.rsqrt(jnp.mean(center * center, axis=-1, keepdims=True) + 1e-05)
    return center * scale, scale


def pull_norm(g, hat, scale):
    m1 = jnp.mean(g, axis=-1, keepdims=True)
    m2 = jnp.mean(g * hat, axis=-1, keepdims=True)
    return scale * (g - m1 - hat * m2)


def row_sum(v):
    return jnp.sum(v, axis=0, keepdims=True)


def main_kernel(names, dp_count, head_count, *values):
    r_ = by_name(names, values)
    core, px, py, z = place()
    plane = py * 2 + px
    x_plane, y_plane = py * 2 + 1 - px, (1 - py) * 2 + px
    me = (plane * 2 + core) * head_count + z
    total = dp_count * head_count
    planes = dp_count // 2
    is_home = core == z // 2
    away = jnp.logical_not(is_home)
    sibling = device(1 - core, px, py, z)
    x_mate, y_mate = device(core, 1 - px, py, z), device(core, px, 1 - py, z)
    mirror = z // 2

    def from_end(i):
        return i + mirror * (head_count - 1 - 2 * i)

    depth = from_end(z)
    inside = depth == 1
    order = [from_end(i) for i in (depth, 1 - depth, 2, 3)]

    def order_at(n):
        return from_end(jnp.where(n == 0, depth, jnp.where(n == 1, 1 - depth, n)))

    x, qkv, pt, ot, wa, wf = r_.x, r_.qkv, r_.pt, r_.ot, r_.wa, r_.wf
    hf, acc, par = r_.hf, r_.acc, r_.par
    seg_len, width = x.shape[1], x.shape[2]
    hidden = r_.u.shape[2]
    heads = pt.shape[1]
    local = ot.shape[2]
    hid = r_.w_back.shape[0]
    lanes = r_.norm_gains.shape[1]
    mem_rows = r_.memory_in.shape[0]
    text_rows = r_.text.shape[1]
    per_block = local // HD
    step = seg_len // head_count
    piece = step // 2
    chunk = hidden // head_count
    tail = 16
    tail_at = pl.ds(seg_len - tail, tail)

    def rows(r):
        return pl.ds(pl.multiple_of(r * step, step), step)

    def cols(i):
        return pl.ds(pl.multiple_of(i * chunk, chunk), chunk)

    def head_rows(h, part):
        return pl.ds(pl.multiple_of((h % per_block) * HD + part * local, HD), HD)

    def column(i):
        h = core if i < head_count - 1 else 1 - core
        zt = (z + 1 + i) % head_count
        return (plane * 2 + h) * head_count + zt, device(h, px, py, zt)

    column_size = 2 * head_count - 1

    def sent_rows(count, sem):
        ref = wf.at[0, pl.ds(0, count)]
        push(ref, ref, sem, sem, sibling).wait_send()

    def got_rows(count, sem):
        ref = wf.at[0, pl.ds(0, count)]
        push(ref, ref, sem, sem, sibling).wait_recv()

    def when_not(cond, body):
        pl.when(jnp.logical_not(cond))(body)

    share = local
    half = share // 2

    def attention_out(i, which):
        zt = (z + 1 + i) % head_count
        at = pl.multiple_of((share * jnp.minimum(plane, planes - 2) if which == 0 else 0) + half * core, half)
        src = (r_.wq_t, r_.w_out)[which]
        return push(
            src.at[pl.ds(at, half)], wa.at[z % 2, pl.ds(pl.multiple_of(share * plane + half * core, half), half)],
            r_.att_s.at[i], r_.att_r.at[z % 2, core], device(z // 2, px, py, zt),
        )

    def attention_outs(do):
        for which, mine in enumerate((plane < planes - 1, plane == planes - 1)):

            def each():
                for i in range(head_count - 1):
                    do(attention_out(i, which))

            pl.when(mine)(each)

    def attention_in(k, h):
        span = pl.ds(pl.multiple_of(share * plane + half * h, half), half)
        return push(r_.w_out.at[pl.ds(0, half)], wa.at[k, span], r_.att_s.at[0], r_.att_r.at[k, h], sibling)

    def attention_plane(k, which):
        at, count, mate = (
            (share * plane, share, x_mate),
            (share * plane, share, y_mate),
            (share * x_plane, half, y_mate),
            (share * y_plane + half, half, x_mate),
        )[which]
        block = pl.ds(pl.multiple_of(at, half), count)
        return push(
            wa.at[k, block], wa.at[k, block], r_.plane_s.at[k, which], r_.plane_r.at[k, which], mate
        )

    own_attention = [
        pltpu.make_async_copy(r_.wq_t, wa.at[z % 2, pl.ds(0, 3 * local)], r_.local_sem.at[0]),
        pltpu.make_async_copy(r_.w_out, wa.at[z % 2, pl.ds(3 * local, local)], r_.local_sem.at[1]),
    ]
    foreign = [jnp.logical_not(is_home & (z % 2 == k)) for k in range(2)]

    def rows_src(a, j, h):
        src = r_.text_pad if a < 2 else r_.cotangent
        return src.at[j, a % 2, pl.ds(h * piece, piece)]

    def rows_dst(a, zs, h):
        dst = r_.text_all if a < 2 else r_.cot_all
        return dst.at[a % 2, pl.ds(pl.multiple_of(zs * step + h * piece, piece), piece)]

    def rows_out(a, j, h):
        return push(
            rows_src(a, j, h), rows_dst(a, z, h), r_.rows_s.at[a], r_.rows_r.at[a, z],
            device(h, px, py, 2 * core + j),
        )

    def rows_here(a, j, h):
        return pltpu.make_async_copy(rows_src(a, j, h), rows_dst(a, z, h), r_.here_sem.at[a])

    def rows_send(a):
        for j in range(2):
            for h in range(2):
                here = (core == h) & (z == 2 * core + j)
                pl.when(here)(lambda: rows_here(a, j, h).start())
                when_not(here, lambda: rows_out(a, j, h).start())

    def rows_forward(a, zs, h):
        ref = rows_dst(a, zs, h)
        return push(ref, ref, r_.fwd_s.at[a], r_.fwd_r.at[a], sibling)

    def rows_pass(a):
        for zs in range(head_count):
            here = is_home & (z == zs)
            pl.when(here)(lambda: rows_here(a, z % 2, core).wait())
            when_not(
                here,
                lambda: push(
                    rows_src(a, 0, 0), rows_dst(a, zs, core), r_.rows_s.at[a], r_.rows_r.at[a, zs], sibling
                ).wait_recv(),
            )
            rows_forward(a, zs, core).start()

    def rows_ready(a):
        got_rows(head_count * piece, r_.fwd_r.at[a])

    def rows_done(a):
        pl.when(is_home)(lambda: sent_rows(3 * piece, r_.rows_s.at[a]))
        pl.when(away)(lambda: sent_rows(4 * piece, r_.rows_s.at[a]))
        sent_rows(head_count * piece, r_.fwd_s.at[a])

    def hidden_block(p, zi):
        return pl.ds(pl.multiple_of((zi * planes + p) * hid, hid), hid)

    def ffn_push(zi, to, slot):
        ref = wf.at[:, hidden_block(plane, zi)]
        return push(ref, ref, r_.ffn_s.at[slot], r_.ffn_r.at[zi], device(core, px, py, to))

    ffn_hops = [(0, from_end(1 - depth)), (0, from_end(2)), (1, from_end(2)), (2, from_end(0)), (3, from_end(0))]

    def ffn_hop(i):
        which, to = ffn_hops[i]
        return ffn_push(order[which], to, i)

    def ffn_own():
        ffn_hop(0).start()
        pl.when(inside)(ffn_hop(1).start)

    def ffn_hop_on(n):
        ffn_push(order[n], z, 0).wait_recv()
        pl.when(inside)(ffn_hop(n + 1).start)

    def ffn_sent():
        ffn_hop(0).wait_send()

        def rest():
            for i in range(1, 5):
                ffn_hop(i).wait_send()

        pl.when(inside)(rest)

    def side(kind, zi, which):
        p, mate = (
            (plane, x_mate),
            (plane, y_mate),
            (x_plane, y_mate) if kind == 0 else (y_plane, x_mate),
        )[which]
        ref = wf.at[kind, hidden_block(p, zi)]
        return push(ref, ref, r_.side_s.at[0], r_.side_r.at[zi, kind, which], mate)

    def side_first(zi):
        for kind in range(2):
            side(kind, zi, 0).start()
            side(kind, zi, 1).start()

    def ffn_two(n):
        zi = order_at(n)
        side(0, zi, 0).wait_recv()
        side(0, zi, 2).start()
        side(1, zi, 1).wait_recv()
        side(1, zi, 2).start()

    def ffn_ready(n):
        zi = order_at(n)
        side(0, zi, 1).wait_recv()
        side(1, zi, 0).wait_recv()
        side(0, zi, 2).wait_recv()
        side(1, zi, 2).wait_recv()

    def small_out(i):
        return push(r_.small, r_.small_all.at[me], r_.small_s.at[0], r_.small_r.at[0], column(i)[1])

    every_small = r_.small_all.at[pl.ds(0, column_size)]
    smalls = push(every_small, every_small, r_.small_s.at[0], r_.small_r.at[0], sibling)

    def small_plane(i):
        p, mate = ((plane, x_mate), (plane, y_mate), (x_plane, y_mate))[i]
        ref = r_.small_all.at[pl.ds(p * 2 * head_count, 2 * head_count)]
        return push(ref, ref, r_.small_ps.at[i], r_.small_pr.at[i], mate)

    pair = [
        push(r_.seqf, r_.seqf_in, r_.pair_s.at[0], r_.pair_r.at[0], sibling),
        push(r_.memp, r_.memp_in, r_.pair_s.at[1], r_.pair_r.at[1], sibling),
    ]

    barrier = pltpu.get_barrier_semaphore()
    mates = [x_mate, y_mate] + [column(i)[1] for i in range(column_size)]
    for mate in mates:
        pl.semaphore_signal(barrier, inc=1, device_id=mate, device_id_type=MESH)
    early = [
        pltpu.make_async_copy(r_.w_in_t, wf.at[0, hidden_block(plane, z)], r_.early_sem.at[0]),
        pltpu.make_async_copy(r_.w_back, wf.at[1, hidden_block(plane, z)], r_.early_sem.at[1]),
        pltpu.make_async_copy(r_.text, r_.text_v, r_.early_sem.at[2]),
    ]
    for copy in early:
        copy.start()
    vtmp = r_.vtmp
    vtmp[...] = jnp.zeros_like(vtmp)
    vtmp[0:2, 0:lanes] = r_.norm_gains[...].astype(F32)
    vtmp[2:6, 0:lanes] = r_.biases[...].astype(F32)
    vtmp[6 : 6 + mem_rows, 0:lanes] = r_.init_memory[...].astype(F32)
    vtmp[0:1, 32 : 32 + hid] = r_.b_in[...].astype(F32)
    for b in range(per_block):
        pair_b = r_.b_qv[b].astype(F32)
        for part in range(2):
            vtmp[1 + part * per_block + b : 2 + part * per_block + b, 32 : 32 + HD] = pair_b[part : part + 1, :]
    r_.small[...] = vtmp[...].astype(BF)
    r_.small_all[me] = r_.small[...]
    pl.semaphore_wait(barrier, len(mates))

    for i in range(column_size):
        small_out(i).start()
    early[0].wait()
    early[1].wait()
    side_first(z)
    ffn_own()
    attention_outs(lambda c: c.start())

    def keep_own():
        for copy in own_attention:
            copy.start()

    pl.when(is_home)(keep_own)
    seqf = r_.seqf
    marks = r_.boundary[z % 2].astype(F32).astype(BF)
    text_len = marks.shape[1]
    n_from = lax.broadcasted_iota(jnp.int32, (text_len, seg_len), 0)
    n_to = lax.broadcasted_iota(jnp.int32, (text_len, seg_len), 1) - mem_rows
    counts = nn(marks, jnp.where(n_from <= n_to, 1.0, 0.0).astype(BF))
    at_row = lax.broadcasted_iota(jnp.int32, (2, seg_len), 1)
    seqf[...] = jnp.zeros_like(seqf)
    seqf[0:2, :] = jnp.where((at_row >= mem_rows) & (at_row < seg_len - mem_rows), counts, -1.0)
    for s in range(2):
        seqf[2 + s : 3 + s, :] = jnp.full((1, seg_len), r_.reset[z % 2, s].astype(F32))
    r_.memp[...] = jnp.zeros_like(r_.memp)
    both_in = r_.memory_in[...].astype(F32)
    r_.memp[0:mem_rows, :] = jnp.where(z % 2 == 0, both_in[:, 0, :], both_in[:, 1, :]).astype(BF)
    for copy in pair:
        copy.start()

    def pad_text(j):
        both = r_.text_v[j].astype(F32)
        for s in range(2):
            r_.text_pad[j, s, 0:text_rows, :] = both[:, s, :].astype(BF)
            r_.text_pad[j, s, text_rows:step, :] = jnp.zeros((step - text_rows, width), BF)

    early[2].wait()
    loop(2, pad_text)
    for ref in (r_.sg, r_.dinit, r_.dbin, r_.carry, r_.rs):
        ref[...] = jnp.zeros_like(ref)

    def attention_to_plane(k):
        for h in range(2):
            attention_in(k, h).wait_recv()
        attention_plane(k, 0).start()
        attention_plane(k, 1).start()

    def attention_across(k):
        attention_plane(k, 0).wait_recv()
        attention_plane(k, 2).start()
        attention_plane(k, 1).wait_recv()
        attention_plane(k, 3).start()

    smalls.wait_recv()
    small_plane(0).start()
    small_plane(1).start()
    ffn_two(0)
    ffn_hop_on(1)
    pl.when(inside)(lambda: ffn_hop_on(2))
    side_first(order[1])
    rows_send(0)
    small_plane(0).wait_recv()
    small_plane(2).start()
    for k in range(2):
        pl.when(foreign[k] & is_home)(lambda: attention_to_plane(k))
    ffn_two(1)
    for k in range(2):
        pl.when(foreign[k] & away)(lambda: attention_to_plane(k))

    for copy in pair:
        copy.wait_recv()
    small_plane(1).wait_recv()
    small_plane(2).wait_recv()
    for i in range(total):
        par[0:16, lanes * i : lanes * (i + 1)] = r_.small_all[i, 0:16, 0:lanes].astype(F32)
    for zi in range(head_count):
        for p in range(planes):
            at = (zi * planes + p) * hid
            line = r_.small_all[(2 * p + core) * head_count + zi].astype(F32)
            r_.bin_row[0:1, at : at + hid] = line[0:1, 32 : 32 + hid]
    r_.bqv[...] = jnp.zeros_like(r_.bqv)
    for k in range(2):
        lines = r_.small_all[2 * core + k].astype(F32)
        for part in range(2):
            for b in range(per_block):
                line = lines[1 + part * per_block + b : 2 + part * per_block + b, 32 : 32 + HD]
                at = 2 * part * local + b * HD
                r_.bqv[k, at : at + HD, :] = as_column(line)
    seq = jnp.where(is_home, seqf[...], r_.seqf_in[...])
    seqf_out = r_.seq
    seqf_out[...] = seq
    flags = [seqf_out[2 + s : 3 + s, 0:1] for s in range(2)]
    tail_row = lax.broadcasted_iota(jnp.int32, (tail, width), 0)
    is_mem = tail_row >= tail - mem_rows
    init_b = jnp.where(is_mem, par[...], 0.0)
    given = jnp.where(is_home, r_.memp[...].astype(F32), r_.memp_in[...].astype(F32))
    first_b = jnp.where(flags[0] > 0, init_b, pltpu.roll(given, tail - mem_rows, 0))
    r_.cur_b[...] = first_b.astype(BF)
    r_.cur_a[...] = pltpu.roll(first_b, mem_rows, 0).astype(BF)

    def take_rows(r):
        inside = lax.broadcasted_iota(jnp.int32, (step, seg_len), 0)
        nat = lax.broadcasted_iota(jnp.int32, (step, seg_len), 1)
        return jnp.where((nat == r * text_rows + inside + mem_rows) & (inside < text_rows), 1.0, 0.0).astype(BF)

    def place_rows(r):
        nat = lax.broadcasted_iota(jnp.int32, (step, seg_len), 0) + r * step
        pad = lax.broadcasted_iota(jnp.int32, (step, seg_len), 1)
        inside = pad & (step - 1)
        target = (pad // step) * text_rows + inside + mem_rows
        return jnp.where((nat == target) & (inside < text_rows), 1.0, 0.0).astype(BF)

    wide = 2 * step

    def half_span(i):
        return pl.ds(pl.multiple_of(i * wide, wide), wide), i

    def end_span(i):
        return pl.ds(pl.multiple_of(i * (seg_len - step), step), step), i

    def middle_span(i):
        return pl.ds(step, wide), 2

    def exchange(slot, span):
        at, n = span
        return push(
            r_.send_buf.at[slot, at], r_.recv_buf.at[slot, at], r_.send_sem.at[slot, n], r_.recv_sem.at[slot, n],
            sibling,
        )

    def give(slot, span, part):
        at = span[0]
        acc[at, :] = part
        r_.send_buf[slot, at, :] = part.astype(BF)
        exchange(slot, span).start()

    def taken(slot, at):
        return acc[at, :] + r_.recv_buf[slot, at, :].astype(F32)

    def by_quarter(slot, body):
        def one(r):
            exchange(slot, (rows(r), r)).wait()
            body(rows(r))

        loop(head_count, one)

    def by_half(slot, body):
        def one(r):
            pl.when(r % 2 == 0)(lambda: exchange(slot, half_span(r // 2)).wait())
            body(rows(r))

        loop(head_count, one)

    def keep_scale(first, seg, at, scale):
        pair_at = slice(2 * first, 2 * first + 2)
        lane = lax.broadcasted_iota(jnp.int32, (1, 2), 1)
        r_.rs[at, pair_at] = jnp.where(lane == seg, scale, r_.rs[at, pair_at])

    def kept_scale(first, seg, at):
        lane = lax.broadcasted_iota(jnp.int32, (1, 2), 1)
        both = r_.rs[at, 2 * first : 2 * first + 2]
        return jnp.sum(jnp.where(lane == seg, both, 0.0), axis=1, keepdims=True)

    def back_copy(which, seg, zt):
        src, dst = ((r_.y, r_.acts_o), (r_.text_all, r_.text_pad))[which]
        span = pl.ds(pl.multiple_of(zt * step + core * piece, piece), piece)
        return src.at[seg, span], dst.at[z % 2, seg, pl.ds(core * piece, piece)]

    def back_out(which, seg, i):
        zt = (z + i) % head_count
        src, dst = back_copy(which, seg, zt)
        return push(
            src, dst, r_.back_s.at[which, seg], r_.back_r.at[which, seg], device(z // 2, px, py, zt)
        )

    def back_here(which, seg):
        src, dst = back_copy(which, seg, z)
        return pltpu.make_async_copy(src, dst, r_.back_here_sem.at[which, seg])

    def back_send(which, seg):
        pl.when(is_home)(lambda: back_here(which, seg).start())
        pl.when(away)(lambda: back_out(which, seg, 0).start())
        for i in range(1, head_count):
            back_out(which, seg, i).start()

    def back_sent(which, seg):
        def home():
            back_here(which, seg).wait()
            sent_rows(3 * piece, r_.back_s.at[which, seg])
            got_rows(3 * piece, r_.back_r.at[which, seg])

        def not_home():
            sent_rows(4 * piece, r_.back_s.at[which, seg])
            got_rows(4 * piece, r_.back_r.at[which, seg])

        pl.when(is_home)(home)
        pl.when(away)(not_home)

    def tail_z(which, i):
        zt = (z + 1 + i) % head_count
        to = device(core, px, py, zt)
        dst = r_.factors.at[which, z, plane]
        return push(r_.factor_out.at[which, zt], dst, r_.tg_s.at[which], r_.tg_r.at[which, z], to)

    def tail_z_in(which, i):
        zs = (z + 1 + i) % head_count
        dst = r_.factors.at[which, zs, plane]
        return push(r_.factor_out.at[which, zs], dst, r_.tg_s.at[which], r_.tg_r.at[which, zs], sibling)

    def tail_plane(which, i):
        p, zs, to = (
            (plane, slice(None), x_mate), (plane, slice(None), y_mate),
            (x_plane, pl.ds(0, 2), y_mate), (y_plane, pl.ds(2, 2), x_mate),
        )[i]
        buf = r_.factors.at[which, zs, p]
        return push(buf, buf, r_.tg_s.at[which], r_.tg_r.at[which, head_count + i], to)

    def tail_pair(which):
        src = r_.factors.at[which, :, :, :, pl.ds(0, half_width)]
        return push(src, r_.factors_in.at[which], r_.tp_s.at[which], r_.tp_r.at[which], sibling)

    def tail_gather(which, stage):
        if stage == 0:
            for i in range(head_count - 1):
                tail_z(which, i).start()
            r_.factors[which, z, plane] = r_.factor_out[which, z]
        elif stage == 1:
            for i in range(head_count - 1):
                tail_z_in(which, i).wait_recv()
            tail_plane(which, 0).start()
            tail_plane(which, 1).start()
        elif stage == 2:
            for i in range(2):
                tail_plane(which, i).wait_recv()
                tail_plane(which, 2 + i).start()
        elif stage == 3:
            for i in range(2):
                tail_plane(which, 2 + i).wait_recv()
            tail_pair(which).start()
        else:
            sent_rows((head_count - 1 + 3 * head_count) * tail, r_.tg_s.at[which])

    half_width = width // 2

    def half_of(h):
        return pl.ds(pl.multiple_of(h * half_width, half_width), half_width)

    def tail_put(which, hidden_ref, units):
        part = hidden_ref[0, tail_at, half_of(core)]
        for zt in range(head_count):
            r_.factor_out[which, zt, :, 0:half_width] = part
            r_.factor_out[which, zt, :, half_width:] = units[:, zt * chunk : (zt + 1) * chunk]
        tail_gather(which, 0)

    def tail_products():
        down = lax.broadcasted_iota(jnp.int32, (chunk, 128), 0)
        across = lax.broadcasted_iota(jnp.int32, (chunk, 128), 1)
        pick = jnp.where((down == plane * hid + across) & (across < hid), 1.0, 0.0).astype(BF)
        all_rows = planes * head_count * tail
        units = [
            nn(r_.factors[which, :, :, :, half_width:].reshape(all_rows, chunk), pick).astype(BF) for which in range(2)
        ]
        for which in range(2):
            tail_pair(which).wait()
        out = []
        for kind in range(2):
            mine = tn(units[1 - kind], r_.factors[kind, :, :, :, 0:half_width].reshape(all_rows, half_width))[0:hid, :]
            theirs = tn(units[1 - kind], r_.factors_in[kind].reshape(all_rows, half_width))[0:hid, :]
            out.append((mine, theirs))
        return out

    def build(seg):
        def one(r):
            x[seg, rows(r), :] = nn(place_rows(r), r_.text_all[seg]).astype(BF)

        loop(head_count, one)

    def add_memory(seg):
        x[seg, 0:tail, :] = x[seg, 0:tail, :] + r_.cur_a[...]
        x[seg, tail_at, :] = x[seg, tail_at, :] + r_.cur_b[...]

    def make_mask(seg):
        right = r_.seq[pl.ds(seg, 1), :]
        left = as_column(right)
        acc[:, 0:seg_len] = jnp.where((left == right) | (left < 0) | (right < 0), 0.0, -1e30)

    def keep_projected(seg, j, at, value):
        value = value + r_.bqv[j]
        qkv[seg, j, 0:local, at] = (value[0:local, :] * 0.125).astype(BF)
        qkv[seg, j, local:, at] = value[local:, :].astype(BF)

    def project(seg):
        def one(j):
            keep_projected(seg, j, slice(None), nt(wa[j, 0 : 3 * local, :], x[seg]))

        loop(2, one)

    def project_ends(seg):
        both = jnp.concatenate(
            [x[seg, 0:tail, :], jnp.zeros((step - 2 * tail, width), BF), x[seg, seg_len - tail :, :]], axis=0
        )

        def one(j):
            value = nt(wa[j, 0 : 3 * local, :], both)
            keep_projected(seg, j, slice(0, tail), value[:, 0:tail])
            keep_projected(seg, j, slice(seg_len - tail, seg_len), value[:, step - tail :])

        loop(2, one)

    def attend(seg):
        def one(h):
            j = h // per_block
            q, k, v = (qkv[seg, j, head_rows(h, part), :] for part in range(3))
            s = tn(k, q) + acc[:, 0:seg_len]
            e = jnp.exp(s - jnp.max(s, axis=0, keepdims=True))
            p = (e * (1.0 / jnp.sum(e, axis=0, keepdims=True))).astype(BF)
            pt[seg, h] = p
            ot[seg, j, head_rows(h, 0), :] = nn(v, p).astype(BF)

        loop(heads, one, unroll=3)

    def out_project(seg):
        def one(i):
            span = (rows(i), i)
            at = span[0]
            give(
                0, span, tn(ot[seg, 0, :, at], wa[0, 3 * local :, :]) + tn(ot[seg, 1, :, at], wa[1, 3 * local :, :])
            )

        loop(head_count, one)

    def norm_one(seg):
        def one(at):
            hat, scale = norm(x[seg, at, :].astype(F32) + taken(0, at) + par[3:4, :])
            r_.xh1[seg, at, :] = hat.astype(BF)
            keep_scale(0, seg, at, scale)
            h = hat * par[0:1, :] + par[2:3, :]
            hf[at, :] = h
            r_.hb[seg, at, :] = h.astype(BF)

        by_quarter(0, one)

    def inner(seg, at):
        v = nt(r_.hb[seg], wf[0, at, :]) + r_.bin_row[:, at]
        c0 = 0.7978845608028654
        sq = v * v
        th = jnp.tanh(v * (c0 + (c0 * 0.044715) * sq))
        up = 0.5 + 0.5 * th
        active = v * up
        r_.u[seg, :, at] = active.astype(BF)
        slope = up + active * (1.0 - up) * (2 * c0 + (6 * c0 * 0.044715) * sq)
        r_.gp[seg, :, at] = slope.astype(BF)

    def outer_part(n):
        def one(i):
            at = cols(order_at(n))
            span = half_span(i)[0]
            part = nn(r_.u[0, span, at], wf[1, at, :])
            acc[span, :] = jnp.where(n == 0, part, acc[span, :] + part)

        loop(2, one)

    def outer_last():
        def one(i):
            at = cols(order[head_count - 1])
            span = (rows(i), i)
            give(1, span, acc[span[0], :] + nn(r_.u[0, span[0], at], wf[1, at, :]))

        loop(head_count, one)

    def outer(seg):
        def one(i):
            span = (rows(i), i)
            give(1, span, nn(r_.u[seg, span[0], :], wf[1]))

        loop(head_count, one)

    def norm_two(seg):
        def one(at):
            hat, scale = norm(hf[at, :] + taken(1, at) + par[4:5, :])
            r_.xh2[seg, at, :] = hat.astype(BF)
            keep_scale(1, seg, at, scale)
            r_.y[seg, at, :] = (hat * par[1:2, :] + par[5:6, :]).astype(BF)

        by_quarter(1, one)

    def next_memory():
        last = r_.y[0, tail_at, :].astype(F32)
        memory = jnp.where(is_mem, jnp.where(flags[1] > 0, par[...], last), 0.0)
        r_.cur_b[...] = memory.astype(BF)
        r_.cur_a[...] = pltpu.roll(memory, mem_rows, 0).astype(BF)

    def pull_two_part(g_y, hat, scale):
        pre = pull_norm(g_y * par[1:2, :], hat, scale)
        r_.sg[1:2, :] += row_sum(g_y * hat)
        r_.sg[5:6, :] += row_sum(g_y)
        r_.sg[4:5, :] += row_sum(pre)
        return pre.astype(BF)

    def pull_two():
        def one(n):
            seg, r = 1 - n // head_count, n % head_count
            pl.when(n == head_count)(lambda: rows_ready(2))
            below = lax.broadcasted_iota(jnp.int32, (step, width), 0) + r * step
            held = (below >= seg_len - tail) & (seg == 0)
            g_y = jnp.where(held, 0.0, r_.cot_all[seg, rows(r), :].astype(F32))
            hat = r_.xh2[seg, rows(r), :].astype(F32)
            r_.xh2[seg, rows(r), :] = pull_two_part(g_y, hat, kept_scale(1, seg, rows(r)))

        loop(2 * head_count, one)

    def keep_tail():
        r_.xh2_t[...] = r_.xh2[0, tail_at, :]
        r_.gp_t[...] = r_.gp[0, tail_at, :]

    pl.when(inside)(lambda: ffn_hop_on(3))
    pl.when(depth == 0)(lambda: ffn_hop_on(2))
    for k in range(2):
        pl.when(foreign[k])(lambda: attention_across(k))
    side_first(order[2])
    rows_pass(0)
    rows_ready(0)
    build(0)
    add_memory(0)
    for k in range(2):

        def last_part():
            attention_plane(k, 2).wait_recv()
            attention_plane(k, 3).wait_recv()

        pl.when(foreign[k])(last_part)

    def kept_own():
        for copy in own_attention:
            copy.wait()

    pl.when(is_home)(kept_own)
    project(0)
    pl.when(depth == 0)(lambda: ffn_hop_on(3))
    side_first(order[3])
    rows_send(1)

    def forward(seg):
        make_mask(seg)
        attend(seg)

        def between():
            rows_pass(3)
            back_send(0, 0)

        pl.when(seg == 1)(between)
        out_project(seg)

        def rows_next():
            ffn_two(2)
            rows_send(3)
            rows_send(2)

        pl.when(seg == 0)(rows_next)
        norm_one(seg)

        def units(n):
            def start_two():
                ffn_two(3)
                rows_ready(1)
                build(1)
                project(1)

            def rows_on():
                rows_pass(1)

            pl.when(n == 2)(rows_on)
            pl.when(n == 3)(start_two)
            ffn_ready(n)
            inner(0, cols(order_at(n)))
            pl.when(n < head_count - 1)(lambda: outer_part(n))

        def wide_units():
            loop(2, lambda n: inner(1, pl.ds(pl.multiple_of(n * 2 * chunk, 2 * chunk), 2 * chunk)))

        pl.when(seg == 0)(lambda: loop(head_count, units))
        pl.when(seg == 1)(wide_units)
        pl.when(seg == 0)(outer_last)
        pl.when(seg == 1)(lambda: outer(1))
        pl.when(seg == 1)(lambda: rows_pass(2))
        norm_two(seg)

        def on_to_two():
            rows_done(0)
            rows_done(1)
            next_memory()
            add_memory(1)
            project_ends(1)
            tail_put(0, r_.hb, r_.u[0, tail_at, :])

        pl.when(seg == 0)(on_to_two)

    loop(2, forward)
    back_send(0, 1)
    rows_ready(3)

    def pull_tail():
        g_y = r_.cot_all[0, tail_at, :].astype(F32) + r_.carry[...]
        pre = pull_two_part(g_y, r_.xh2_t[...].astype(F32), kept_scale(1, 0, tail_at))
        r_.xh2[0, tail_at, :] = pre
        g_z = (nt(pre, wf[1]) * r_.gp_t[...].astype(F32)).astype(BF)
        r_.gp[0, tail_at, :] = g_z
        r_.dbin[0:1, :] += row_sum(g_z.astype(F32))
        tail_put(1, r_.xh2, g_z)

    def pull_inner(i):
        both = r_.xh2[...].reshape(2 * seg_len, width)
        g_u = nt(both, wf[1, cols(i), :])
        for seg in range(2):
            g_z = (g_u[seg * seg_len : (seg + 1) * seg_len, :] * r_.gp[seg, :, cols(i)].astype(F32)).astype(BF)
            r_.gp[seg, :, cols(i)] = g_z
            r_.dbin[0:1, cols(i)] += row_sum(g_z.astype(F32))

    def pull_hidden(seg):
        def one(i):
            span = half_span(i)
            give(0, span, nn(r_.gp[seg, span[0], :], wf[0]))

        loop(2, one)

    def pull_one(seg):
        def one(at):
            g_h = r_.xh2[seg, at, :].astype(F32) + taken(0, at)
            hat = r_.xh1[seg, at, :].astype(F32)
            pre = pull_norm(g_h * par[0:1, :], hat, kept_scale(0, seg, at))
            hf[at, :] = pre
            r_.xh1[seg, at, :] = pre.astype(BF)
            r_.sg[0:1, :] += row_sum(g_h * hat)
            r_.sg[2:3, :] += row_sum(g_h)
            r_.sg[3:4, :] += row_sum(pre)

        by_half(0, one)

        def out(j):
            r_.got[j] = nt(wa[j, 3 * local :, :], r_.xh1[seg]).astype(BF)

        loop(2, out)

    def pull_heads(seg):
        def one(h):
            j = h // per_block
            q, k, v = (qkv[seg, j, head_rows(h, part), :] for part in range(3))
            g_o = r_.got[j, head_rows(h, 0), :]
            p = pt[seg, h]
            d_v = nt(g_o, p).astype(BF)
            total_p = row_sum(g_o.astype(F32) * ot[seg, j, head_rows(h, 0), :].astype(F32))
            d_s = (p.astype(F32) * (tn(v, g_o) - total_p)).astype(BF)
            d_q = (nn(k, d_s) * 0.125).astype(BF)
            d_k = nt(q, d_s).astype(BF)
            for part, value in enumerate((d_q, d_k, d_v)):
                qkv[seg, j, head_rows(h, part), :] = value

        loop(heads, one, unroll=3)

    def pull_rows(seg, span):
        at = span[0]
        give(
            1, span,
            tn(qkv[seg, 0, :, at], wa[0, 0 : 3 * local, :]) + tn(qkv[seg, 1, :, at], wa[1, 0 : 3 * local, :]),
        )

    def pull_x(at):
        value = hf[at, :] + taken(1, at)
        acc[at, :] = value
        r_.send_buf[1, at, :] = value.astype(BF)

    def pull_memory(seg):
        both = pltpu.roll(acc[0:tail, :], tail - mem_rows, 0) + acc[seg_len - tail : seg_len, :]
        memory = jnp.where(is_mem, both, 0.0)
        r_.dinit[...] += jnp.where(flags[seg] > 0, memory, 0.0)
        if seg == 1:
            r_.carry[...] = jnp.where(flags[1] > 0, 0.0, memory)

    def text_grad(seg):
        def one(r):
            r_.text_all[seg, rows(r), :] = nn(take_rows(r), r_.send_buf[1]).astype(BF)

        loop(head_count, one)

    def cut(buf, kind, a, b):
        first, second = (px, py) if kind == 0 else (py, px)
        first = first if a == 0 else 1 - first
        second = second if b == 0 else 1 - second
        return buf.at[second, first] if kind == 0 else buf.at[first, second]

    def parts_of(name):
        return sums[name] if isinstance(name, str) else ffn_sum(name)

    sum_mates = ((x_mate, y_mate), (y_mate, x_mate))

    def sum_one(name, kind, b):
        buf, got, s, r = parts_of(name)(kind)
        return push(cut(buf, kind, 1, b), got[0].at[b], s, r.at[b], sum_mates[kind][0])

    def sum_two(name, kind):
        buf, got, s, r = parts_of(name)(kind)
        return push(cut(buf, kind, 0, 1), got[1], s, r.at[2], sum_mates[kind][1])

    def ffn_sum(d):
        zi = order_at(d)

        def parts(kind):
            return (
                r_.fsend.at[kind, zi], (r_.f_one.at[kind, zi], r_.f_two.at[kind, zi]),
                r_.sum_s.at[0], r_.fsum_r.at[kind, zi],
            )

        return parts

    sums = {}

    def attention_sum(n):
        def parts(kind):
            return (
                r_.asend.at[n, kind], (r_.a_one.at[n, kind], r_.a_two.at[n, kind]),
                r_.sum_s.at[1], r_.asum_r.at[n, kind],
            )

        return parts

    halves = tuple("abc")
    for n, name in enumerate(halves):
        sums[name] = attention_sum(n)
    sums["v"] = lambda kind: (
        r_.vsend.at[kind], (r_.v_one.at[kind], r_.v_two.at[kind]), r_.sum_s.at[2], r_.vsum_r.at[kind]
    )

    def start_sum(name, which=((1, 0), (1, 1), (0, 0), (0, 1))):
        for b, kind in which:
            sum_one(name, kind, b).start()

    def travel(name, kinds=(0, 1)):
        for kind in kinds:
            buf, got, _, _ = parts_of(name)(kind)
            sum_one(name, kind, 1).wait_recv()
            add_all(cut(buf, kind, 0, 1), got[0].at[1])
            sum_two(name, kind).start()

    def end_plane(name):
        for kind in range(2):
            buf, got, _, _ = parts_of(name)(kind)
            sum_one(name, kind, 0).wait_recv()
            sum_two(name, kind).wait_recv()
            add_all(cut(buf, kind, 0, 0), got[0].at[0], got[1])

    def sums_sent():
        every = r_.fsend.at[:, pl.ds(0, 3)]
        push(every, every, r_.sum_s.at[0], r_.sum_s.at[0], sibling).wait_send()
        sent_rows(12 * hid_rows, r_.sum_s.at[1])
        every = r_.small_all.at[pl.ds(0, 12)]
        push(every, every, r_.sum_s.at[2], r_.sum_s.at[2], sibling).wait_send()

    def z_out(kind, d):
        slot = jnp.where(inside, jnp.where(d == 1, 0, jnp.where(d == 2, 4, 1)), jnp.where(d == 1, 0, d))
        to = from_end(jnp.where(inside, jnp.where(d == 1, 0, 2), 1))
        return push(
            cut(r_.fsend.at[kind, order_at(d)], kind, 0, 0), r_.f_z.at[kind, slot], r_.fz_s.at[0],
            r_.fz_r.at[kind, slot], device(core, px, py, to),
        )

    def z_in(kind, slot):
        return push(
            cut(r_.fsend.at[kind, z], kind, 0, 0), r_.f_z.at[kind, slot], r_.fz_s.at[0], r_.fz_r.at[kind, slot],
            sibling,
        )

    def end_ffn(d):
        end_plane(d)

        def send():
            for kind in range(2):
                z_out(kind, d).start()

        if d > 0:
            pl.when(depth == 0)(send)

    def z_pass(d):
        def add_and_send():
            for kind in range(2):
                z_in(kind, d).wait_recv()
                add_all(cut(r_.fsend.at[kind, order_at(d)], kind, 0, 0), r_.f_z.at[kind, d])
                z_out(kind, d).start()

        pl.when(inside)(add_and_send)

    def last_out(name, k, h):
        buf, dst, s, r = last[name]
        return push(
            cut(buf.at[k], k, 0, 0).at[h], dst.at[z], s.at[k, h], r.at[z], device(h, px, py, 2 * core + k)
        )

    def last_here(name, k):
        buf, dst, _, _ = last[name]
        return pltpu.make_async_copy(cut(buf.at[k], k, 0, 0).at[core], dst.at[z], r_.last_sem.at["abcdefv".index(name)])

    last = {
        "v": (r_.vsend, r_.v_z, r_.vz_s, r_.vz_r),
    }
    for n, name in enumerate(halves):
        last[name] = (r_.asend.at[n], r_.a_z.at[n], r_.az_s.at[n], r_.az_r.at[n])

    def last_each(name, here_do, away_do):
        for k in range(2):
            for h in range(2):
                here = (core == h) & (z == 2 * core + k)
                if here_do is not None:
                    pl.when(here)(lambda: here_do(last_here(name, k)))
                when_not(here, lambda: away_do(last_out(name, k, h)))

    def last_total(name):
        buf, dst, s, r = last[name]
        for zs in range(head_count):
            here = is_home & (z == zs)
            pl.when(here)(lambda: last_here(name, 0).wait())
            when_not(
                here, lambda: push(buf.at[0, 0, 0, 0], dst.at[zs], s.at[0, 0], r.at[zs], sibling).wait_recv()
            )
        value = dst[0].astype(F32)
        for zs in range(1, head_count):
            value = value + dst[zs].astype(F32)
        return value

    def ffn_grads(d):
        i = order_at(d)

        def grads(kind, left, right):
            value = tn(left[0, :, cols(i)], right[0]) + tn(left[1, :, cols(i)], right[1])
            for p in range(planes):
                r_.fsend[kind, i, p // 2, p % 2] = value[p * hid : (p + 1) * hid, :].astype(BF)

        grads(1, r_.u, r_.xh2)
        pl.when(d >= 2)(lambda: start_sum(d, ((1, 1), (0, 1))))
        pull_inner(i)
        grads(0, r_.gp, r_.hb)
        pl.when(d == 2)(lambda: travel(3, (1,)))
        pl.when(d >= 2)(lambda: start_sum(d, ((1, 0), (0, 0))))
        pl.when(d == 1)(lambda: travel(3, (0,)))

    keep_tail()
    pull_two()
    tail_gather(0, 1)
    loop(head_count, lambda n: ffn_grads(head_count - 1 - n))
    dbin_pair = push(r_.dbin, r_.dbin_in, r_.pair_s.at[2], r_.pair_r.at[2], sibling)

    def backward(n):
        seg = 1 - n
        pull_hidden(seg)

        pull_one(seg)

        def first_events():
            travel(2)
            start_sum(1)
            start_sum(0)
            tail_gather(0, 2)

        pl.when(seg == 1)(first_events)
        pull_heads(seg)

        def segment_two():
            end_ffn(3)
            loop(2, lambda i: pull_rows(1, end_span(i)))

            def one(i):
                exchange(1, end_span(i)).wait()
                pull_x(end_span(i)[0])

            loop(2, one)
            pull_memory(1)
            pull_tail()
            dbin_pair.start()
            pull_rows(1, middle_span(0))
            z_pass(3)
            end_ffn(2)
            travel(1)
            exchange(1, middle_span(0)).wait()
            pull_x(middle_span(0)[0])
            text_grad(1)
            back_send(1, 1)

        pl.when(seg == 1)(segment_two)

    loop(2, backward)
    travel(0)
    z_pass(2)
    hid_rows = width // dp_count
    cut_rows = hid_rows // len(halves)

    def attention_grads(i):
        wide = width // 2
        span = pl.ds(pl.multiple_of(i * wide, wide), wide)
        xt = [x[s, :, span].T for s in range(2)]
        gt = [r_.xh1[s, :, span].T for s in range(2)]
        for k in range(2):
            qkv_g = nt(xt[0], qkv[0, k]) + nt(xt[1], qkv[1, k])
            out_g = nt(gt[0], ot[0, k]) + nt(gt[1], ot[1, k])
            for n in range(4 * len(halves)):
                at = slice(n * cut_rows, (n + 1) * cut_rows)
                b, part = n // len(halves), n % len(halves)
                r_.asend[part, k, i, b // 2, b % 2, :, 0 : 3 * local] = qkv_g[at, :].astype(BF)
                r_.asend[part, k, i, b // 2, b % 2, :, 3 * local :] = out_g[at, :].astype(BF)

    def both_planes(n):
        attention_grads(jnp.where(n == 0, 1 - py, py))

        def travelling():
            for name in halves:
                start_sum(name, ((1, 0), (1, 1)))
            end_ffn(1)

        pl.when(n == 0)(travelling)

    loop(2, lambda i: pull_rows(0, half_span(i)))
    loop(2, both_planes)
    start_sum("a", ((0, 1), (0, 0)))
    z_pass(1)
    by_half(1, pull_x)
    text_grad(0)
    back_send(1, 0)
    tail_gather(1, 1)
    pull_memory(0)
    dbin_pair.wait()

    dbin_both = [jnp.where(core == h, r_.dbin[0:1, :], r_.dbin_in[0:1, :]) for h in range(2)]
    for k in range(2):
        r_.bqv[k] = sum(jnp.sum(qkv[s, k].astype(F32), axis=1, keepdims=True) for s in range(2))
    sg, dinit = r_.sg, r_.dinit
    r_.vec[...] = jnp.where(is_mem, dinit[...], 0.0)
    r_.vec[0:6, :] = sg[0:6, :]
    vtmp[...] = jnp.zeros_like(vtmp)

    def by_core(cut_of):
        return jnp.where(core == 0, cut_of(0), cut_of(1))

    qv_rows = [
        [
            jnp.sum(
                jnp.where(
                    lax.broadcasted_iota(jnp.int32, (HD, HD), 0) == lax.broadcasted_iota(jnp.int32, (HD, HD), 1),
                    r_.bqv[k, 2 * part * local + b * HD : 2 * part * local + (b + 1) * HD, :],
                    0.0,
                ),
                axis=0,
                keepdims=True,
            )
            for part in range(2)
            for b in range(per_block)
        ]
        for k in range(2)
    ]
    piece_b = HD // dp_count
    vec = r_.vec[...]

    def small_cut(k, p, h):
        dp_t = 2 * p + h

        def from_vec(c):
            at = (dp_t * head_count + 2 * c + k) * lanes
            return vec[:, at : at + lanes]

        def from_bin(c):
            at = ((2 * c + k) * planes + p) * hid
            return dbin_both[h][:, at : at + hid]

        vtmp[0:16, 0:lanes] = by_core(from_vec)
        vtmp[0:1, 32 : 32 + hid] = by_core(from_bin)
        for n, line in enumerate(qv_rows[k]):
            vtmp[1:2, 32 + n * piece_b : 32 + (n + 1) * piece_b] = line[:, dp_t * piece_b : (dp_t + 1) * piece_b]
        r_.vsend[k, p // 2, p % 2, h] = vtmp[...].astype(BF)

    for k in range(2):
        for p in range(planes):
            for h in range(2):
                small_cut(k, p, h)
    start_sum("v")
    end_ffn(0)
    for n, name in enumerate(halves):
        travel(name)
        if n + 1 < len(halves):
            start_sum(halves[n + 1], ((0, 1), (0, 0)))
    travel("v")
    for n, name in enumerate(halves):
        if n == len(halves) - 1:
            end_plane("v")
            last_each("v", lambda c: c.start(), lambda c: c.start())
        end_plane(name)
        last_each(name, lambda c: c.start(), lambda c: c.start())
        if n == 1:
            tail_gather(1, 2)

    results = (
        (r_.win_v, r_.win_o), (r_.wback_v, r_.wback_o), (r_.dt_v, r_.dt_o), (r_.dqkv_v, r_.dqkv_o),
        (r_.dwout_v, r_.dwout_o), (r_.dinit_v, r_.dinit_o), (r_.dbqv_v, r_.dbqv_o), (r_.dbin_v, r_.dbin_o),
        (r_.dgains_v, r_.dgains_o), (r_.dbiases_v, r_.dbiases_o),
    )

    def leave(n):
        return pltpu.make_async_copy(results[n][0], results[n][1], r_.leave_sem.at[n])

    tail_gather(0, 3)
    tail_gather(1, 3)
    extra = tail_products()
    for kind, out in enumerate((r_.win_v, r_.wback_v)):
        value = cut(r_.fsend.at[kind, z], kind, 0, 0)[...].astype(F32)
        z_in(kind, 0).wait_recv()
        out[...] = value + r_.f_z[kind, 0].astype(F32)

        def other_side():
            z_in(kind, 4).wait_recv()
            out[...] += r_.f_z[kind, 4].astype(F32)

        pl.when(inside)(other_side)
        out[:, half_of(core)] += extra[kind][0]
        out[:, half_of(1 - core)] += extra[kind][1]
        leave(kind).start()


    sums_sent()
    sent_rows(2 * (head_count - 1) * hid, r_.fz_s.at[0])
    for which in range(2):
        for seg in range(2):
            back_sent(which, seg)
    for a in range(2, 4):
        rows_done(a)
    attention_outs(lambda c: c.wait_send())
    ffn_sent()
    for which in range(2):
        tail_gather(which, 4)
    for copy in pair:
        copy.wait_send()
    for k in range(2):

        def sent():
            for which in range(4):
                attention_plane(k, which).wait_send()

        pl.when(foreign[k])(sent)
    every_side = wf.at[:, pl.ds(0, 3 * head_count * hid)]
    push(every_side, every_side, r_.side_s.at[0], r_.side_s.at[0], sibling).wait_send()
    smalls.wait_send()
    for i in range(3):
        small_plane(i).wait_send()
    for j in range(2):
        both = [r_.text_pad[j, s, 0:text_rows, :].astype(F32)[:, None, :] for s in range(2)]
        r_.dt_v[j] = jnp.concatenate(both, axis=1).astype(BF)
    leave(2).start()
    total_v = last_total("v")
    r_.dinit_v[...] = total_v[6 : 6 + mem_rows, 0:lanes]
    for b in range(per_block):
        for part in range(2):
            at = 32 + (part * per_block + b) * piece_b
            r_.dbqv_v[b, part : part + 1, :] = total_v[1:2, at : at + piece_b]
    r_.dbin_v[...] = total_v[0:1, 32 : 32 + hid]
    r_.dgains_v[...] = total_v[0:2, 0:lanes]
    r_.dbiases_v[...] = total_v[2:6, 0:lanes]
    for n in range(5, len(results)):
        leave(n).start()
    for n, name in enumerate(halves):
        part = last_total(name)
        at = slice(n * cut_rows, (n + 1) * cut_rows)
        for t in range(3):
            r_.dqkv_v[t, at, :] = part[:, t * local : (t + 1) * local]
        r_.out_rows[at, :] = part[:, 3 * local :]
    leave(3).start()
    r_.dwout_v[...] = r_.out_rows[...].T
    leave(4).start()
    for n in range(len(results)):
        leave(n).wait()
    for name in halves + ("v",):
        last_each(name, None, lambda c: c.wait_send())


def vmem(*shape, dtype=BF):
    return pltpu.VMEM(shape, dtype)


def f32(*shape):
    return pltpu.VMEM(shape, F32)


def sds(*shape, dtype=BF):
    return jax.ShapeDtypeStruct(shape, dtype)


def dma(*shape):
    return pltpu.SemaphoreType.DMA(shape)


ANY = pl.BlockSpec(memory_space=pl.ANY)
INV = pl.BlockSpec(memory_space=pltpu.VMEM)
INS = pl.BlockSpec(memory_space=pltpu.SMEM)


def end_kernel(count, *refs):
    given, out, kept = refs[:count], refs[count : 2 * count], refs[2 * count : 3 * count]
    sem = refs[3 * count]
    parts = []
    for n in range(count):
        if len(given[n].shape) == 4:
            parts += [(n, (j, s)) for j in range(2) for s in range(2)] if n == 0 else [(n, (j,)) for j in range(2)]
        else:
            parts.append((n, ()))

    def part(ref, at):
        return ref.at[at] if at else ref

    loads = [
        pltpu.make_async_copy(part(given[n], at), part(kept[n], at), sem.at[0, i]) for i, (n, at) in enumerate(parts)
    ]
    stores = [
        pltpu.make_async_copy(part(kept[n], at), part(out[n], at), sem.at[1, i]) for i, (n, at) in enumerate(parts)
    ]
    for copy in loads:
        copy.start()
    for load, store in zip(loads, stores):
        load.wait()
        store.start()
    for copy in stores:
        copy.wait()


def by_chip(
    text, boundary, reset, memory_in, init_memory, w_qkv, b_qv, w_out, w_in, w_back, b_in, norm_gains, biases,
    cotangent,
):
    head_count = lax.axis_size("head")
    dp_count = lax.axis_size("dp")
    planes = dp_count // 2
    total = dp_count * head_count
    text_rows, width = text.shape[2], text.shape[3]
    block = cotangent.shape[2]
    seg_len = block * head_count
    mem_rows = memory_in.shape[1]
    local = w_qkv.shape[2]
    hid = w_in.shape[1]
    lanes = norm_gains.shape[1]
    heads = 2 * local // HD
    hidden = hid * planes * head_count
    share = width // dp_count

    inputs = dict(
        text=(text.transpose(0, 2, 1, 3), ANY),
        boundary=(boundary, INV),
        reset=(reset, INS),
        memory_in=(memory_in.transpose(1, 0, 2), INV),
        init_memory=(init_memory, INV),
        wq_t=(w_qkv.transpose(1, 2, 0).reshape(3 * local, width), ANY),
        w_out=(w_out, ANY),
        b_qv=(b_qv.transpose(1, 0, 2), INV),
        w_in_t=(w_in.T, ANY),
        w_back=(w_back, ANY),
        b_in=(b_in[None, :], INV),
        norm_gains=(norm_gains, INV),
        biases=(biases, INV),
        cotangent=(cotangent, ANY),
    )
    slice_b = HD // dp_count
    shapes = dict(
        acts=sds(2, 2, block, width),
        dt=sds(2, text_rows, 2, width),
        dinit=sds(mem_rows, lanes, dtype=F32),
        dqkv=sds(3, share, local, dtype=F32),
        dbqv=sds(local // HD, 2, slice_b, dtype=F32),
        dwout=sds(local, share, dtype=F32),
        win=sds(hid, width, dtype=F32),
        wback=sds(hid, width, dtype=F32),
        dbin=sds(1, hid, dtype=F32),
        dgains=sds(2, lanes, dtype=F32),
        dbiases=sds(4, lanes, dtype=F32),
    )
    outputs = {name + "_o": (shape, ANY) for name, shape in shapes.items()}
    staged = {name + "_v": pltpu.VMEM(shape.shape, shape.dtype) for name, shape in shapes.items() if name != "acts"}
    scratch = dict(
        text_pad=vmem(2, 2, block, width),
        text_v=vmem(2, text_rows, 2, width),
        early_sem=dma(3),
        text_all=vmem(2, seg_len, width),
        cot_all=vmem(2, seg_len, width),
        wa=vmem(2, 4 * local, width),
        wf=vmem(2, hidden, width),
        small=vmem(16, 128),
        small_all=vmem(total, 16, 128),
        seqf=f32(8, seg_len),
        seqf_in=f32(8, seg_len),
        seq=f32(8, seg_len),
        memp=vmem(16, width),
        memp_in=vmem(16, width),
        par=f32(16, width),
        bin_row=f32(1, hidden),
        bqv=f32(2, 3 * local, 1),
        x=vmem(2, seg_len, width),
        qkv=vmem(2, 2, 3 * local, seg_len),
        pt=vmem(2, heads, seg_len, seg_len),
        ot=vmem(2, 2, local, seg_len),
        hf=f32(seg_len, width),
        acc=f32(seg_len, width),
        xh1=vmem(2, seg_len, width),
        hb=vmem(2, seg_len, width),
        u=vmem(2, seg_len, hidden),
        gp=vmem(2, seg_len, hidden),
        xh2=vmem(2, seg_len, width),
        rs=f32(seg_len, 4),
        y=vmem(2, seg_len, width),
        got=vmem(2, local, seg_len),
        send_buf=vmem(2, seg_len, width),
        recv_buf=vmem(2, seg_len, width),
        cur_a=vmem(16, width),
        cur_b=vmem(16, width),
        carry=f32(16, width),
        xh2_t=vmem(16, width),
        gp_t=vmem(16, hidden),
        factor_out=vmem(2, head_count, 16, width // 2 + hidden // head_count),
        factors=vmem(2, head_count, planes, 16, width // 2 + hidden // head_count),
        factors_in=vmem(2, head_count, planes, 16, width // 2),
        sg=f32(8, width),
        dinit=f32(16, width),
        dbin=f32(8, hidden),
        dbin_in=f32(8, hidden),
        vec=f32(16, width),
        vtmp=f32(16, 128),
        fsend=vmem(2, head_count, 2, 2, hid, width),
        f_one=vmem(2, head_count, 2, hid, width),
        f_two=vmem(2, head_count, hid, width),
        f_z=vmem(2, head_count + 1, hid, width),
        asend=vmem(3, 2, 2, 2, 2, share // 3, width),
        a_one=vmem(3, 2, 2, 2, share // 3, width),
        a_two=vmem(3, 2, 2, share // 3, width),
        a_z=vmem(3, head_count, share // 3, width),
        out_rows=f32(share, local),
        vsend=vmem(2, 2, 2, 2, 16, 128),
        v_one=vmem(2, 2, 2, 16, 128),
        v_two=vmem(2, 2, 16, 128),
        v_z=vmem(head_count, 16, 128),
        small_s=dma(1),
        small_r=dma(1),
        small_ps=dma(3),
        small_pr=dma(3),
        pair_s=dma(3),
        pair_r=dma(3),
        att_s=dma(3),
        att_r=dma(2, 2),
        plane_s=dma(2, 4),
        plane_r=dma(2, 4),
        local_sem=dma(2),
        rows_s=dma(4),
        rows_r=dma(4, 4),
        here_sem=dma(4),
        fwd_s=dma(4),
        fwd_r=dma(4),
        ffn_s=dma(5),
        ffn_r=dma(4),
        side_s=dma(1),
        side_r=dma(4, 2, 3),
        send_sem=dma(2, 4),
        recv_sem=dma(2, 4),
        back_s=dma(2, 2),
        back_r=dma(2, 2),
        back_here_sem=dma(2, 2),
        sum_s=dma(3),
        fsum_r=dma(2, 4, 3),
        asum_r=dma(3, 2, 3),
        tg_s=dma(2),
        tg_r=dma(2, 8),
        tp_s=dma(2),
        tp_r=dma(2),
        vsum_r=dma(2, 3),
        fz_s=dma(1),
        fz_r=dma(2, 5),
        az_s=dma(3, 2, 2),
        az_r=dma(3, 4),
        leave_sem=dma(10),
        vz_s=dma(2, 2),
        vz_r=dma(4),
        last_sem=dma(7),
    )
    scratch.update(staged)
    names = tuple(inputs) + tuple(outputs) + tuple(scratch)
    middle = pl.pallas_call(
        functools.partial(main_kernel, names, dp_count, head_count),
        out_shape=tuple(v[0] for v in outputs.values()),
        in_specs=[v[1] for v in inputs.values()],
        out_specs=tuple(v[1] for v in outputs.values()),
        scratch_shapes=list(scratch.values()),
        compiler_params=pltpu.CompilerParams(
            collective_id=0, has_side_effects=True, vmem_limit_bytes=VMEM_LIMIT
        ),
        name="layer",
    )(*(v[0] for v in inputs.values()))

    out = pl.pallas_call(
        functools.partial(end_kernel, len(shapes)),
        out_shape=tuple(shapes.values()),
        in_specs=[ANY] * len(shapes),
        out_specs=tuple([ANY] * len(shapes)),
        scratch_shapes=[pltpu.VMEM(shape.shape, shape.dtype) for shape in shapes.values()] + [dma(2, 16)],
        name="results",
    )(*middle)
    acts, d_text, d_init, d_qkv, d_bqv, d_wout, d_win, d_wback, d_bin, d_gains, d_biases = out
    return (
        acts, d_text.transpose(0, 2, 1, 3), d_init,
        d_qkv.transpose(1, 0, 2),
        d_bqv.transpose(1, 0, 2),
        d_wout, d_win.T, d_wback, d_bin[0], d_gains, d_biases,
    )


def solution(mesh):
    body = by_chip if mesh.shape["dp"] == 8 and mesh.shape["head"] == 4 else local
    return jax.shard_map(
        body,
        mesh=mesh,
        in_specs=(
            P("dp", None, "head", None),
            P("dp", None, None),
            P("dp", None),
            P("dp", None, None),
            P(None, ("dp", "head")),
            P(None, None, "head"),
            P(None, "head", None),
            P("head", None),
            P(None, ("dp", "head")),
            P(("dp", "head"), None),
            P(("dp", "head")),
            P(None, ("dp", "head")),
            P(None, ("dp", "head")),
            P("dp", None, "head", None),
        ),
        out_specs=(
            P("dp", None, "head", None),
            P("dp", None, "head", None),
            P(None, ("dp", "head")),
            P("dp", None, "head"),
            P(None, "head", "dp"),
            P("head", "dp"),
            P(None, ("dp", "head")),
            P(("dp", "head"), None),
            P(("dp", "head")),
            P(None, ("dp", "head")),
            P(None, ("dp", "head")),
        ),
        check_vma=False,
    )
```
